128 devices in a mesh: dp: 4 (over x), vocab: 32 (over z, y, core).
Axes of the slice: x: 4, y: 4, z: 4, core: 2. Of those that a mesh axis runs over, the one named last changes fastest.
Arguments:
- token_ids: int32 [128, 128], P('dp'), may hold values from 0 to 50256
- seq_lengths: int32 [128], P('dp'), may hold values from 1 to 128, as said below
- loss_positions: int32 [128, 16], P('dp'), may hold values from 0 to 127, as said below
- target_ids: int32 [128, 16], P('dp'), may hold values from 0 to 50256
- block_of_slot: int32 [768], replicated, may hold values from 0 to 767, as said below
- matrices: float32 [768, 128, 128], P(('dp', 'vocab'))
- left_stats: float32 [768, 128, 128], P(('dp', 'vocab'))
- right_stats: float32 [768, 128, 128], P(('dp', 'vocab'))
- left_roots: float32 [768, 128, 128], P(('dp', 'vocab'))
- right_roots: float32 [768, 128, 128], P(('dp', 'vocab'))
- vocab_table: float32 [51200, 1024], P('vocab', 'dp')
- table_m: float32 [51200, 1024], P('vocab', 'dp')
- table_v: float32 [51200, 1024], P('vocab', 'dp')
- positions_table: float32 [128, 1024], replicated, may hold values from -0.6 to 0.6
- pos_m: float32 [128, 1024], replicated
- pos_v: float32 [128, 1024], replicated
- vectors: float32 [14, 1024], replicated
- vectors_m: float32 [14, 1024], replicated
- vectors_v: float32 [14, 1024], replicated
Outputs:
- loss_value: float32 [], replicated
- grad_norm: float32 [], replicated
- matrices_new: float32 [768, 128, 128], P(('dp', 'vocab'))
- left_new: float32 [768, 128, 128], P(('dp', 'vocab'))
- right_new: float32 [768, 128, 128], P(('dp', 'vocab'))
- matrices_grad: float32 [768, 128, 128], P(('dp', 'vocab'))
- vocab_table_new: float32 [51200, 1024], P('vocab', 'dp')
- table_m_new: float32 [51200, 1024], P('vocab', 'dp')
- table_v_new: float32 [51200, 1024], P('vocab', 'dp')
- positions_new: float32 [128, 1024], replicated
- pos_m_new: float32 [128, 1024], replicated
- pos_v_new: float32 [128, 1024], replicated
- vectors_new: float32 [14, 1024], replicated
- vectors_m_new: float32 [14, 1024], replicated
- vectors_v_new: float32 [14, 1024], replicated
The draws below stay inside these ranges and needn't reach their ends.
Inputs may be any that keep to these rules, and one draw needn't show every extreme that they name: `seq_lengths`: the last sequence has all 128 slots live. `loss_positions`: distinct within each sequence. `block_of_slot`: a permutation of the 768 blocks.
All inputs are finite; a program needn't handle non-finite values.
Results may differ from the reference program's by a relative error of at most 0.014.
Values may be sent and summed in bfloat16 or wider, within the bound.
A program may use at most 256 MiB of HBM per device.

```python
import math
import jax
import jax.numpy as jnp
import numpy as np
from jax import lax

D = 1024
HEADS = 16
HEAD_DIM = 64
FF = 4096
VOCAB_REAL = 50257
VOCAB = 51200
LAYERS = 1
BLOCK = 128
STEP = 10
SEQ_LEN = 128
LOSS_DEV = 16
SEQS = 128
BLOCKS = 768
PARAMS = 65157120
N_DP = 4
N_VOCAB = 32


def slot_order(key):
    return jax.random.permutation(jax.random.fold_in(key, 97), BLOCKS).astype(jnp.int32)


def grad_entry(factor):
    return factor * 0.05 / math.sqrt(PARAMS)


def first_moment(key, shape_all, factor):
    return jax.random.normal(key, shape_all, jnp.float32) * (0.11 * grad_entry(factor))


def second_moment(key, shape_all, factor):
    spread = jnp.exp(jax.random.uniform(key, shape_all, jnp.float32, 0.0, math.log(4.0)))
    return spread * (0.001 * grad_entry(factor) ** 2)


def stat_level():
    return 0.0526 * BLOCK * grad_entry(1.0) ** 2


def stat_matrix(key, level):
    diag_key, noise_key = jax.random.split(key)
    diagonal = jnp.exp(jax.random.uniform(diag_key, (BLOCKS, BLOCK), jnp.float32, 0.0, math.log(4.0)))
    noise = jax.random.normal(noise_key, (BLOCKS, BLOCK, BLOCK), jnp.float32)
    mixed = (noise + jnp.swapaxes(noise, 1, 2)) * (0.45 / math.sqrt(BLOCK))
    return level * (mixed + jnp.eye(BLOCK, dtype=jnp.float32)[None] * diagonal[:, :, None])


def draw_block_of_slot(key, part):
    return slot_order(key)


def draw_matrices(key, part):
    slot_blocks = slot_order(key)
    key = jax.random.fold_in(key, 2)
    quarter = (D // BLOCK) ** 2
    within = slot_blocks % (12 * quarter)
    scaling = jnp.where(within < 3 * quarter, D ** (-0.5), jnp.where(within < 4 * quarter, 3.0 * D ** (-0.5), jnp.where(within < 8 * quarter, D ** (-0.5), 1.5 * FF ** (-0.5))))
    return jax.random.normal(key, (BLOCKS, BLOCK, BLOCK), jnp.float32) * scaling[:, None, None]


def draw_left_stats(key, part):
    key = jax.random.fold_in(key, 3)
    return stat_matrix(key, stat_level())


def draw_right_stats(key, part):
    key = jax.random.fold_in(key, 4)
    return stat_matrix(key, stat_level())


def draw_left_roots(key, part):
    key = jax.random.fold_in(key, 5)
    return stat_matrix(key, stat_level() ** (-0.25))


def draw_right_roots(key, part):
    key = jax.random.fold_in(key, 6)
    return stat_matrix(key, stat_level() ** (-0.25))


def draw_seq_lengths(key, part):
    key = jax.random.fold_in(key, 7)
    index_all = jnp.arange(SEQS, dtype=jnp.int32)
    along_vocab = index_all % N_VOCAB
    along_data = index_all // N_VOCAB
    percent = 30 + 35 * along_vocab // max(N_VOCAB - 1, 1) + 35 * along_data // max(N_DP - 1, 1)
    jitter = jax.random.randint(key, (SEQS,), 85, 101)
    jitter = jnp.where(index_all == SEQS - 1, 100, jitter)
    return jnp.maximum(1, SEQ_LEN * percent * jitter // 10000).astype(jnp.int32)


def draw_loss_positions(key, part):
    key = jax.random.fold_in(key, 8)
    seq_keys = jax.random.split(key, SEQS)
    shuffled = jax.vmap(lambda single: jax.random.permutation(single, SEQ_LEN))(seq_keys)
    return shuffled[:, :LOSS_DEV].astype(jnp.int32)


def draw_vocab_table(key, part):
    key = jax.random.fold_in(key, 9)
    top_scale = 3.0
    row_index = jnp.arange(VOCAB, dtype=jnp.float32)
    scaling = (1.0 + (top_scale - 1.0) * row_index / VOCAB) / math.sqrt(D)
    values = jax.random.normal(key, (VOCAB, D), jnp.float32) * scaling[:, None]
    return jnp.where((row_index < VOCAB_REAL)[:, None], values, 0.0)


def draw_vectors(key, part):
    key = jax.random.fold_in(key, 10)
    row_index = jnp.arange(12 * LAYERS + 2)
    in_layer = row_index % 12
    is_gain = (row_index < 12 * LAYERS) & ((in_layer == 0) | (in_layer == 5)) | (row_index == 12 * LAYERS)
    noise = jax.random.normal(key, (12 * LAYERS + 2, D), jnp.float32)
    return jnp.where(is_gain[:, None], 1.0 + 0.1 * jnp.clip(noise, -3.0, 3.0), 0.1 * noise)


def draw_table_m(key, part):
    key = jax.random.fold_in(key, 11)
    return first_moment(key, (VOCAB, D), 1.0)


def draw_table_v(key, part):
    key = jax.random.fold_in(key, 12)
    return second_moment(key, (VOCAB, D), 6.0)


def draw_pos_m(key, part):
    key = jax.random.fold_in(key, 13)
    return first_moment(key, (SEQ_LEN, D), 1.0)


def draw_pos_v(key, part):
    key = jax.random.fold_in(key, 14)
    return second_moment(key, (SEQ_LEN, D), 1.0)


def draw_vectors_m(key, part):
    key = jax.random.fold_in(key, 15)
    return first_moment(key, (12 * LAYERS + 2, D), 5.0)


def draw_vectors_v(key, part):
    key = jax.random.fold_in(key, 16)
    return second_moment(key, (12 * LAYERS + 2, D), 5.0)


def set_ends(entries, key, least, largest):
    longest = entries.shape.index(max(entries.shape))
    spots = []
    for shift in (0, 1):
        where = [jax.random.randint(jax.random.fold_in(key, axis), (), 0, length) for axis, length in enumerate(entries.shape)]
        where[longest] = (where[longest] + shift) % entries.shape[longest]
        spots.append(tuple(where))
    return entries.at[spots[0]].set(least).at[spots[1]].set(largest)


def cumulative_ranks(number_of, lean):
    portions = [(1 << 20) // math.isqrt(rank ** lean) + 1 for rank in range(1, number_of + 1)]
    width = 1 + sum(portions) // (1 << 30)
    return np.cumsum(np.array([max(1, weight // width) for weight in portions]))


def ranked(own_key, extent, count, lean):
    table = cumulative_ranks(count, lean)
    pick = jax.random.randint(jax.random.fold_in(own_key, 1), extent, 0, int(table[count - 1]))
    grade = jnp.searchsorted(jnp.asarray(table, jnp.int32), pick, side="right")
    return jax.random.permutation(jax.random.fold_in(own_key, 2), count)[grade].astype(jnp.int32)


def centred(key, dims, width, most, held_as=jnp.bfloat16):
    values = width * jax.random.normal(key, dims, jnp.float32)
    return jnp.clip(values, min=-most, max=most).astype(held_as)


def setup_inputs(seed: int = 0) -> dict:
    seeds = jax.random.split(jax.random.key(seed), 20)
    return {
        "token_ids": set_ends(ranked(seeds[0], (SEQS, SEQ_LEN), VOCAB_REAL, 2), jax.random.fold_in(seeds[0], 3), 0, VOCAB_REAL - 1).astype(jnp.int32),
        "seq_lengths": draw_seq_lengths(jax.random.fold_in(seeds[19], 71), 0),
        "loss_positions": draw_loss_positions(jax.random.fold_in(seeds[19], 71), 0),
        "target_ids": set_ends(ranked(seeds[3], (SEQS, LOSS_DEV), VOCAB_REAL, 2), jax.random.fold_in(seeds[3], 3), 0, VOCAB_REAL - 1).astype(jnp.int32),
        "block_of_slot": draw_block_of_slot(jax.random.fold_in(seeds[19], 71), 0),
        "matrices": draw_matrices(jax.random.fold_in(seeds[19], 71), 0),
        "left_stats": draw_left_stats(jax.random.fold_in(seeds[19], 71), 0),
        "right_stats": draw_right_stats(jax.random.fold_in(seeds[19], 71), 0),
        "left_roots": draw_left_roots(jax.random.fold_in(seeds[19], 71), 0),
        "right_roots": draw_right_roots(jax.random.fold_in(seeds[19], 71), 0),
        "vocab_table": draw_vocab_table(jax.random.fold_in(seeds[19], 71), 0),
        "table_m": draw_table_m(jax.random.fold_in(seeds[19], 71), 0),
        "table_v": draw_table_v(jax.random.fold_in(seeds[19], 71), 0),
        "positions_table": centred(seeds[13], (SEQ_LEN, D), 0.1, 0.6, jnp.float32),
        "pos_m": draw_pos_m(jax.random.fold_in(seeds[19], 71), 0),
        "pos_v": draw_pos_v(jax.random.fold_in(seeds[19], 71), 0),
        "vectors": draw_vectors(jax.random.fold_in(seeds[19], 71), 0),
        "vectors_m": draw_vectors_m(jax.random.fold_in(seeds[19], 71), 0),
        "vectors_v": draw_vectors_v(jax.random.fold_in(seeds[19], 71), 0),
    }


@jax.custom_vjp
def low(v):
    return lax.optimization_barrier(v.astype(jnp.bfloat16)).astype(jnp.float32)

@jax.custom_vjp
def low_back(v):
    return v

def low_keep(v):
    return (low(v), None)

def low_pass(kept, grad):
    return (grad,)

def back_keep(v):
    return (v, None)

def back_low(kept, grad):
    return (low(grad),)
low.defvjp(low_keep, low_pass)
low_back.defvjp(back_keep, back_low)
LN_EPS = 1e-05
CLIP_LEVEL = 0.05
BETA_ONE = 0.9
BETA_TWO = 0.999
ADAM_EPS = 1e-08
STAT_DECAY = 0.95
SHAMPOO_RATE = 0.03
TABLE_RATE = 0.15
POS_RATE = 0.05
VECTOR_RATE = 0.25
DECAY_RATE = 0.1
NEG_FILL = -1e+30
GELU_C = 0.7978845608028654
HIGH = lax.Precision.HIGHEST

def matmul(left, right):
    return jnp.dot(left, right, precision=HIGH, preferred_element_type=jnp.float32)

def layer_norm(values, gain_row, shift_row):
    center = values - lax.optimization_barrier(jnp.mean(values, -1, keepdims=True))
    spread = lax.optimization_barrier(jnp.mean(center * center, -1, keepdims=True))
    return center * lax.rsqrt(spread + LN_EPS) * gain_row + shift_row

def gelu(values):
    return 0.5 * values * (1.0 + jnp.tanh(GELU_C * (values + 0.044715 * values * values * values)))

def from_blocks(blocks, height, across):
    block_side = blocks.shape[-1]
    shaped = blocks.reshape(height // block_side, across // block_side, block_side, block_side)
    return shaped.transpose(0, 2, 1, 3).reshape(height, across)

def unpack(blocks):
    square = (D // BLOCK) ** 2
    result = []
    for layer_idx in range(LAYERS):
        part_blocks = blocks[layer_idx * 12 * square:(layer_idx + 1) * 12 * square]
        result.append((from_blocks(part_blocks[:3 * square], D, 3 * D), from_blocks(part_blocks[3 * square:4 * square], D, D), from_blocks(part_blocks[4 * square:8 * square], D, FF), from_blocks(part_blocks[8 * square:], FF, D)))
    return result

def attention(queries, keys_in, values_in, own_length):
    seq_len = queries.shape[0]
    q_heads = queries.reshape(seq_len, HEADS, HEAD_DIM).transpose(1, 0, 2)
    k_heads = keys_in.reshape(seq_len, HEADS, HEAD_DIM).transpose(1, 0, 2)
    v_heads = values_in.reshape(seq_len, HEADS, HEAD_DIM).transpose(1, 0, 2)
    raw_scores = jnp.einsum('hqd,hkd->hqk', q_heads, k_heads, precision=HIGH)
    scores = low_back(raw_scores * HEAD_DIM ** (-0.5))
    query_pos = jnp.arange(seq_len)[:, None]
    key_pos = jnp.arange(seq_len)[None, :]
    allowed = (key_pos <= query_pos) & (key_pos < own_length)
    masked = jnp.where(allowed[None], scores, NEG_FILL)
    probs = jax.nn.softmax(masked, axis=-1)
    mixed = jnp.einsum('hqk,hkd->hqd', low(probs), v_heads, precision=HIGH)
    return mixed.transpose(1, 0, 2).reshape(seq_len, D)

def block_forward(hidden, own_length, w_qkv, w_proj, w_fc, w_out, vec_rows):
    normed_one = low(layer_norm(hidden, vec_rows[0], vec_rows[1]))
    qkv_bias = jnp.concatenate([vec_rows[2], jnp.zeros_like(vec_rows[2]), vec_rows[3]])
    qkv_all = low_back(low(matmul(normed_one, w_qkv) + qkv_bias))
    attended = low_back(low(attention(qkv_all[:, :D], qkv_all[:, D:2 * D], qkv_all[:, 2 * D:], own_length)))
    middle = hidden + low_back(matmul(attended, w_proj) + vec_rows[4])
    normed_two = low(layer_norm(middle, vec_rows[5], vec_rows[6]))
    pre_act = low_back(matmul(normed_two, w_fc) + vec_rows[7:11].reshape(-1))
    activated = low(gelu(pre_act))
    return middle + low_back(matmul(activated, w_out) + vec_rows[11])

def forward(table_f, pos_f, vec_f, blocks_f, token_ids, seq_lengths, loss_positions, target_ids):
    weights = unpack(low(blocks_f))
    table_low = low(table_f)
    hidden = low_back(table_low[token_ids]) + pos_f[None]
    for layer_idx in range(LAYERS):
        w_qkv, w_proj, w_fc, w_out = weights[layer_idx]
        vec_rows = vec_f[12 * layer_idx:12 * layer_idx + 12]

        def one_seq(single, length_one):
            return block_forward(single, length_one, w_qkv, w_proj, w_fc, w_out, vec_rows)
        hidden = jax.vmap(one_seq)(hidden, seq_lengths)
    selected = jnp.take_along_axis(hidden, loss_positions[:, :, None], axis=1)
    head_in = low(layer_norm(selected, vec_f[12 * LAYERS], vec_f[12 * LAYERS + 1])).reshape(-1, D)
    logits = low_back(matmul(head_in, table_low.T))
    columns = jnp.arange(VOCAB)
    masked = jnp.where(columns[None] < VOCAB_REAL, logits, NEG_FILL)
    row_top = lax.optimization_barrier(jnp.max(masked, -1, keepdims=True))
    log_total = row_top[:, 0] + jnp.log(lax.optimization_barrier(jnp.sum(jnp.exp(masked - row_top), -1)))
    picked = jnp.take_along_axis(logits, target_ids.reshape(-1, 1), axis=1)[:, 0]
    counted = (loss_positions < seq_lengths[:, None]).reshape(-1).astype(jnp.float32)
    return jnp.sum((log_total - picked) * counted)

def adamw(weight, moment_one, moment_two, grad_in, rate, decay):
    new_one = BETA_ONE * moment_one + (1.0 - BETA_ONE) * grad_in
    new_two = BETA_TWO * moment_two + (1.0 - BETA_TWO) * grad_in * grad_in
    hat_one = new_one / (1.0 - BETA_ONE ** STEP)
    hat_two = new_two / (1.0 - BETA_TWO ** STEP)
    new_weight = weight - rate * (hat_one / (jnp.sqrt(hat_two) + ADAM_EPS) + decay * weight)
    return (new_weight, new_one, new_two)

def reference(token_ids, seq_lengths, loss_positions, target_ids, block_of_slot, matrices, left_stats, right_stats, left_roots, right_roots, vocab_table, table_m, table_v, positions_table, pos_m, pos_v, vectors, vectors_m, vectors_v):
    inverse = jnp.argsort(block_of_slot).astype(jnp.int32)
    blocks = matrices[inverse]

    def objective(table_f, pos_f, vec_f, blocks_f):
        return forward(table_f, pos_f, vec_f, blocks_f, token_ids, seq_lengths, loss_positions, target_ids)
    loss_value, pull = jax.vjp(objective, vocab_table, positions_table, vectors, blocks)
    g_table, g_pos, g_vec, g_blocks = pull(jnp.full((), 1.0 / (SEQS * LOSS_DEV), jnp.float32))
    g_slots = g_blocks[block_of_slot]
    squares = jnp.sum(g_slots * g_slots) + jnp.sum(g_table * g_table) + jnp.sum(g_pos * g_pos) + jnp.sum(g_vec * g_vec)
    grad_norm = jnp.sqrt(squares)
    clip_factor = CLIP_LEVEL / jnp.maximum(grad_norm, CLIP_LEVEL)
    matrices_grad = g_slots * clip_factor
    left_new = STAT_DECAY * left_stats + (1.0 - STAT_DECAY) * jnp.einsum('bij,bkj->bik', matrices_grad, matrices_grad, precision=HIGH)
    right_new = STAT_DECAY * right_stats + (1.0 - STAT_DECAY) * jnp.einsum('bji,bjk->bik', matrices_grad, matrices_grad, precision=HIGH)
    left_part = jnp.einsum('bij,bjk->bik', left_roots, matrices_grad, precision=HIGH)
    precond = jnp.einsum('bij,bjk->bik', left_part, right_roots, precision=HIGH)
    matrices_new = matrices - SHAMPOO_RATE * (precond + DECAY_RATE * matrices)
    table_new, table_m_new, table_v_new = adamw(vocab_table, table_m, table_v, g_table * clip_factor, TABLE_RATE, DECAY_RATE)
    positions_new, pos_m_new, pos_v_new = adamw(positions_table, pos_m, pos_v, g_pos * clip_factor, POS_RATE, DECAY_RATE)
    vectors_new, vectors_m_new, vectors_v_new = adamw(vectors, vectors_m, vectors_v, g_vec * clip_factor, VECTOR_RATE, 0.0)
    return (loss_value, grad_norm, matrices_new, left_new, right_new, matrices_grad, table_new, table_m_new, table_v_new, positions_new, pos_m_new, pos_v_new, vectors_new, vectors_m_new, vectors_v_new)
```

```python
import jax
import jax.numpy as jnp
import numpy as np
from jax import lax
from jax.experimental import pallas as pl
from jax.experimental.pallas import tpu as pltpu
from jax.sharding import PartitionSpec as P

D = 1024
HEADS = 16
HEAD_DIM = 64
FF = 4096
VOCAB_REAL = 50257
LAYERS = 1
BLOCK = 128
STEP = 10


LN_EPS = 1e-05
CLIP_LEVEL = 0.05
BETA_ONE = 0.9
BETA_TWO = 0.999
ADAM_EPS = 1e-08
STAT_DECAY = 0.95
SHAMPOO_RATE = 0.03
TABLE_RATE = 0.15
POS_RATE = 0.05
VECTOR_RATE = 0.25
DECAY_RATE = 0.1
NEG_FILL = -1e30
GELU_C = 0.7978845608028654
HIGH = lax.Precision.HIGHEST


def gelu(values):
    return 0.5 * values * (1.0 + jnp.tanh(GELU_C * (values + 0.044715 * values * values * values)))


def dot_nt(left, right):
    return lax.dot_general(
        left, right, (((1,), (1,)), ((), ())), preferred_element_type=jnp.float32
    )


def dot_tn(left, right):
    return lax.dot_general(
        left, right, (((0,), (0,)), ((), ())), preferred_element_type=jnp.float32
    )


def adamw(weight, moment_one, moment_two, grad_in, rate, decay):
    new_one = BETA_ONE * moment_one + (1.0 - BETA_ONE) * grad_in
    new_two = BETA_TWO * moment_two + (1.0 - BETA_TWO) * grad_in * grad_in
    hat_one = new_one / (1.0 - BETA_ONE**STEP)
    hat_two = new_two / (1.0 - BETA_TWO**STEP)
    new_weight = weight - rate * (hat_one / (jnp.sqrt(hat_two) + ADAM_EPS) + decay * weight)
    return (new_weight, new_one, new_two)


TABLE_CHUNKS = 20
MESH_IDS = pl.DeviceIdType.MESH
ANY = pl.BlockSpec(memory_space=pl.ANY)
VMEM = pl.BlockSpec(memory_space=pltpu.VMEM)
N_DP = 4
N_VOCAB = 32
SIDE = 4
X, Y, Z, CORE = range(4)
ORDERS = ((X, Y, Z), (Y, Z, X), (Z, X, Y))
SLOTS = 6


def coordinates():
    across = lax.axis_index("dp")
    inner = lax.axis_index("vocab")
    return (across, (inner // 2) % SIDE, inner // (2 * SIDE), inner % 2)


def moved(place, axis, step):
    shifted = list(place)
    shifted[axis] = (place[axis] + step) % (2 if axis == CORE else SIDE)
    return tuple(shifted)


def device_of(place):
    return (place[X], (place[Z] * SIDE + place[Y]) * 2 + place[CORE])


def greet(place, axes, far_axes):
    barrier = pltpu.get_barrier_semaphore()
    others = [moved(place, CORE, 1)]
    for axis in axes:
        others += [moved(place, axis, 1), moved(place, axis, -1)]
    for axis in far_axes:
        others.append(moved(place, axis, 2))
    for other in others:
        pl.semaphore_signal(
            barrier, inc=1, device_id=device_of(other), device_id_type=MESH_IDS
        )
    pl.semaphore_wait(barrier, len(others))


class Wires:
    def __init__(self, send_sems, recv_sems):
        self.send_sems, self.recv_sems, self.used = send_sems, recv_sems, 0
        self.sent = []

    def send(self, source, target, place):
        copy = pltpu.make_async_remote_copy(
            src_ref=source,
            dst_ref=target,
            send_sem=self.send_sems.at[self.used],
            recv_sem=self.recv_sems.at[self.used],
            device_id=device_of(place),
            device_id_type=MESH_IDS,
        )
        self.used += 1
        copy.start()
        self.sent.append(copy)
        return copy

    def drain(self):
        for copy in self.sent:
            copy.wait_send()


def add_blocks(target, sources, count):
    @pl.loop(0, count)
    def _(i):
        total = target[i].astype(jnp.float32)
        for source in sources:
            total += source[i].astype(jnp.float32)
        target[i] = total.astype(target.dtype)


class RingGather:
    def __init__(self, wires, place, axis, piece, half):
        self.wires, self.place, self.axis = wires, place, axis
        self.piece, self.half = piece, half
        self.mine = place[axis]

    def start(self):
        mine = self.piece(self.mine)
        self.up = self.wires.send(mine, mine, moved(self.place, self.axis, 1))
        self.down = self.wires.send(mine, mine, moved(self.place, self.axis, -1))

    def forward(self):
        self.up.wait_recv()
        lower = self.half((self.mine + 3) % SIDE, 0)
        self.far_up = self.wires.send(lower, lower, moved(self.place, self.axis, 1))
        self.down.wait_recv()
        upper = self.half((self.mine + 1) % SIDE, 1)
        self.far_down = self.wires.send(upper, upper, moved(self.place, self.axis, -1))

    def finish(self):
        self.far_up.wait_recv()
        self.far_down.wait_recv()


class DirectGather:
    def __init__(self, wires, place, axis, piece):
        self.wires, self.place, self.axis, self.piece = wires, place, axis, piece

    def start(self):
        mine = self.piece(self.place[self.axis])
        self.copies = [
            self.wires.send(mine, mine, moved(self.place, self.axis, step)) for step in (1, 2, 3)
        ]

    def finish(self):
        for copy in self.copies:
            copy.wait_recv()


class RingReduce:
    def __init__(self, wires, place, axis, piece, half, count, half_in, whole_in):
        self.wires, self.place, self.axis = wires, place, axis
        self.piece, self.half, self.count = piece, half, count
        self.half_in, self.whole_in = half_in, whole_in
        self.mine = place[axis]

    def start(self):
        far = (self.mine + 2) % SIDE
        up, down = moved(self.place, self.axis, 1), moved(self.place, self.axis, -1)
        self.far_up = self.wires.send(self.half(far, 0), self.half_in.at[0], up)
        self.far_down = self.wires.send(self.half(far, 1), self.half_in.at[1], down)

    def forward(self):
        after, before = (self.mine + 1) % SIDE, (self.mine + 3) % SIDE
        up, down = moved(self.place, self.axis, 1), moved(self.place, self.axis, -1)
        self.far_up.wait_recv()
        add_blocks(self.half(after, 0), [self.half_in.at[0]], self.count // 2)
        self.up = self.wires.send(self.piece(after), self.whole_in.at[0], up)
        self.far_down.wait_recv()
        add_blocks(self.half(before, 1), [self.half_in.at[1]], self.count // 2)
        self.down = self.wires.send(self.piece(before), self.whole_in.at[1], down)

    def arrive(self):
        self.up.wait_recv()
        self.down.wait_recv()

    def finish(self):
        self.arrive()
        add_blocks(
            self.piece(self.mine), [self.whole_in.at[0], self.whole_in.at[1]], self.count
        )


class DirectReduce:
    def __init__(self, wires, place, axis, piece, count, landing):
        self.wires, self.place, self.axis = wires, place, axis
        self.piece, self.count, self.landing = piece, count, landing

    def start(self):
        mine = self.place[self.axis]
        self.copies = [
            self.wires.send(
                self.piece((mine + step) % SIDE),
                self.landing.at[step - 1],
                moved(self.place, self.axis, step),
            )
            for step in (1, 2, 3)
        ]

    def arrive(self):
        for copy in self.copies:
            copy.wait_recv()

    def finish(self):
        self.arrive()
        add_blocks(
            self.piece(self.place[self.axis]),
            [self.landing.at[step] for step in range(3)],
            self.count,
        )


def block_ring(place, part, phase, at):
    first_axis, second_axis, third_axis = ORDERS[part]
    k1, k2, k3 = place[first_axis], place[second_axis], place[third_axis]
    if phase == 0:
        return (
            lambda j: at(k3, 8 * k2 + 2 * j, 2),
            lambda j, h: at(k3, 8 * k2 + 2 * j + h, 1),
        )
    if phase == 1:
        return (lambda j: at(k3, 8 * j, 8), lambda j, h: at(k3, 8 * j + 4 * h, 4))
    return (lambda j: at(j, 0, 32), lambda j, h: at(j, 16 * h, 16))


def start_kernel(
    ids_ref,
    own_ref,
    table_ref,
    positions_ref,
    full_ref,
    table_full_ref,
    hidden_ref,
    table_pad,
    ids_all,
    parts,
    sibling_in,
    half_in,
    whole_in,
    landing,
    ready,
    arrived,
    send_sems,
    recv_sems,
    local_sems,
):
    place = coordinates()
    core = place[CORE]
    across = place[X]
    sibling = moved(place, CORE, 1)
    wires = Wires(send_sems, recv_sems)
    own_copies = []
    for part in range(3):
        k1, k2, k3 = (place[axis] for axis in ORDERS[part])
        own_copies.append(
            pltpu.make_async_copy(
                own_ref.at[part],
                full_ref.at[part, core, k3, pl.ds(8 * k2 + 2 * k1, 2)],
                local_sems.at[part],
            )
        )
    own_copies.append(
        pltpu.make_async_copy(table_ref, table_full_ref.at[across], local_sems.at[3])
    )
    for copy in own_copies:
        copy.start()
    ids_all[across] = ids_ref[...]
    greet(place, (X, Y, Z), (X, Y, Z))
    ids_ring = DirectGather(wires, place, X, lambda j: ids_all.at[j])
    ids_ring.start()
    rings = []
    for phase in range(3):
        row = []
        for part in range(3):
            piece, half = block_ring(
                place,
                part,
                phase,
                lambda k3, first, count, part=part: full_ref.at[
                    part, core, k3, pl.ds(first, count)
                ],
            )
            row.append(RingGather(wires, place, ORDERS[part][phase], piece, half))
        rings.append(row)
    for copy, ring in zip(own_copies, rings[0]):
        copy.wait()
        ring.start()
    own_copies[3].wait()
    table_ring = RingGather(
        wires,
        place,
        X,
        lambda j: table_full_ref.at[j],
        lambda j, h: table_full_ref.at[j, pl.ds(800 * h, 800)],
    )
    rows = table_ref.shape[0]
    table_pad[pl.ds(0, rows)] = table_ref[...]
    padding = table_pad.shape[0] - rows
    table_pad[pl.ds(rows, padding)] = jnp.zeros((padding, table_pad.shape[1]), jnp.bfloat16)
    base = (lax.axis_index("vocab") * rows).astype(jnp.float32)
    tiles = table_pad.shape[0] // 128
    lane = lax.broadcasted_iota(jnp.int32, (128, 128), 1).astype(jnp.float32)

    def look_up(group):
        part = group // 2

        @pl.loop(0, 8)
        def _(quad):
            hot_rows = []
            for which in range(4):
                ids = ids_all[group, pl.ds(4 * quad + which, 1), :].astype(jnp.float32) - base
                column = jnp.transpose(jnp.broadcast_to(ids, (128, 128)))
                hot_rows.append(
                    jnp.concatenate(
                        [
                            jnp.where(column == lane + 128.0 * tile, 1.0, 0.0).astype(jnp.bfloat16)
                            for tile in range(tiles)
                        ],
                        1,
                    )
                )
            found = jnp.dot(
                jnp.concatenate(hot_rows, 0), table_pad[...], preferred_element_type=jnp.float32
            ).astype(jnp.bfloat16)
            at_z = quad // 2
            for which in range(4):
                at_y = 2 * (quad % 2) + which // 2
                first, second = (at_z, at_y) if part == 0 else (at_y, at_z)
                parts[part, which % 2, first, 2 * second + group % 2] = found[
                    128 * which : 128 * which + 128
                ]

    def to_sibling(part):
        return wires.send(parts.at[part, 1 - core], sibling_in.at[part], sibling)

    lookup_axes = ((Z, Y), (Y, Z))
    lookup_rings, lookup_ends = [], []
    for part in range(2):
        first_axis, second_axis = lookup_axes[part]
        lookup_rings.append(
            RingReduce(
                wires,
                place,
                first_axis,
                lambda j, part=part: parts.at[part, core, j],
                lambda j, h, part=part: parts.at[part, core, j, pl.ds(4 * h, 4)],
                8,
                half_in.at[part],
                whole_in.at[part],
            )
        )
        lookup_ends.append(
            DirectReduce(
                wires,
                place,
                second_axis,
                lambda j, part=part, k=place[first_axis]: parts.at[part, core, k, pl.ds(2 * j, 2)],
                2,
                landing.at[part],
            )
        )
    ids_ring.finish()
    for ring in rings[0]:
        ring.forward()
    for ring, later in zip(rings[0], rings[1]):
        ring.finish()
        later.start()
    look_up(0)
    for ring in rings[1]:
        ring.forward()
    look_up(1)
    siblings = [to_sibling(0)]
    for ring, later in zip(rings[1], rings[2]):
        ring.finish()
        later.start()
    table_ring.start()
    block_siblings = []
    for part in range(3):
        own = full_ref.at[part, core, place[ORDERS[part][2]]]
        block_siblings.append(wires.send(own, own, sibling))
    look_up(2)
    look_up(3)
    siblings.append(to_sibling(1))

    def add_sibling(part):
        siblings[part].wait_recv()
        for j in range(4):
            add_blocks(parts.at[part, core, j], [sibling_in.at[part, j]], 8)
        lookup_rings[part].start()

    add_sibling(0)
    add_sibling(1)
    table_ring.forward()
    for ring in lookup_rings:
        ring.forward()
    for ring in rings[2]:
        ring.forward()
    for part in range(3):
        k3 = place[ORDERS[part][2]]
        for step in (1, 3):
            piece = full_ref.at[part, core, (k3 + step) % SIDE]
            block_siblings.append(wires.send(piece, piece, sibling))
    for ring, end in zip(lookup_rings, lookup_ends):
        ring.finish()
        end.start()
    for part in range(2):
        end = lookup_ends[part]
        end.arrive()
        first_axis, second_axis = lookup_axes[part]
        for which in range(2):
            total = parts[part, core, place[first_axis], 2 * place[second_axis] + which].astype(
                jnp.float32
            )
            for step in range(3):
                total += landing[part, step, which].astype(jnp.float32)
            ready[2 * part + which] = total.astype(jnp.bfloat16)
    swaps = []
    for step in (1, 2, 3):
        there = moved(place, X, step)
        swaps.append(wires.send(ready.at[there[X]], arrived.at[across], there))
    arrived[across] = ready[across]
    for copy in swaps:
        copy.wait_recv()
    for source in range(4):
        columns = pl.ds(256 * source, 256)
        hidden_ref[:, columns] = (
            arrived[source].astype(jnp.float32) + positions_ref[:, columns]
        )
    table_ring.finish()
    for part in range(3):
        rings[2][part].finish()
        far = full_ref.at[part, core, (place[ORDERS[part][2]] + 2) % SIDE]
        block_siblings.append(wires.send(far, far, sibling))
    for copy in block_siblings:
        copy.wait_recv()
    wires.drain()


def start_call(token_ids, own_blocks, table_low, positions_table):
    rows, width = table_low.shape
    padded = -(-rows // 128) * 128
    bf16 = jnp.bfloat16
    return pl.pallas_call(
        start_kernel,
        name="gather_and_look_up",
        out_shape=(
            jax.ShapeDtypeStruct((3, 2, SIDE, 32, BLOCK, BLOCK), bf16),
            jax.ShapeDtypeStruct((N_DP, rows, width), bf16),
            jax.ShapeDtypeStruct(positions_table.shape, jnp.float32),
        ),
        in_specs=[VMEM, ANY, VMEM, VMEM],
        out_specs=(ANY, ANY, VMEM),
        scratch_shapes=[
            pltpu.VMEM((padded, width), bf16),
            pltpu.VMEM((N_DP,) + token_ids.shape, jnp.int32),
            pltpu.VMEM((2, 2, SIDE, 8, 128, width), bf16),
            pltpu.VMEM((2, SIDE, 8, 128, width), bf16),
            pltpu.VMEM((2, 2, 4, 128, width), bf16),
            pltpu.VMEM((2, 2, 8, 128, width), bf16),
            pltpu.VMEM((2, 3, 2, 128, width), bf16),
            pltpu.VMEM((N_DP, 128, width), bf16),
            pltpu.VMEM((N_DP, 128, width), bf16),
            pltpu.SemaphoreType.DMA((80,)),
            pltpu.SemaphoreType.DMA((80,)),
            pltpu.SemaphoreType.DMA((4,)),
        ],
        compiler_params=pltpu.CompilerParams(
            collective_id=1, has_side_effects=True, vmem_limit_bytes=60 << 20
        ),
    )(token_ids, own_blocks, table_low, positions_table)


def head_kernel(
    head_in_ref,
    table_ref,
    target_ref,
    counted_ref,
    d_head_ref,
    table_grad_ref,
    loss_ref,
    pieces,
    rows_in,
    logits,
    d_logits,
    stats,
    stats_in,
    d_rows,
    d_sibling,
    d_first,
    d_second,
    send_sems,
    recv_sems,
):
    place = coordinates()
    core = place[CORE]
    sibling = moved(place, CORE, 1)
    wires = Wires(send_sems, recv_sems)
    own, width = head_in_ref.shape
    half_width = width // 2
    feature_axes = ((Y, Z), (Z, Y))
    for part in range(2):
        near, far = (place[axis] for axis in feature_axes[part])
        pieces[part, core, far, near] = head_in_ref[
            :, part * half_width : (part + 1) * half_width
        ]
    greet(place, (Y, Z), (Y, Z))
    first_rings, second_rings = [], []
    for part in range(2):
        near_axis, far_axis = feature_axes[part]
        first_rings.append(
            DirectGather(
                wires,
                place,
                near_axis,
                lambda j, part=part, k=place[far_axis]: pieces.at[part, core, k, j],
            )
        )
        second_rings.append(
            DirectGather(wires, place, far_axis, lambda j, part=part: pieces.at[part, core, j])
        )
    for ring in first_rings:
        ring.start()
    for ring, later in zip(first_rings, second_rings):
        ring.finish()
        later.start()
    crossing = []
    for part in range(2):
        second_rings[part].finish()
        mine = pieces.at[part, core]
        crossing.append(wires.send(mine, mine, sibling))
    for copy in crossing:
        copy.wait_recv()
    for index in range(32):
        at_z, at_y, at_core = index // 8, index // 2 % SIDE, index % 2
        rows_in[own * index : own * (index + 1), :half_width] = pieces[0, at_core, at_z, at_y]
        rows_in[own * index : own * (index + 1), half_width:] = pieces[1, at_core, at_y, at_z]

    groups, rows, group_width = table_ref.shape
    count = rows_in.shape[0]
    chunk = rows // 4
    base = lax.axis_index("vocab") * rows
    row_iota = lax.broadcasted_iota(jnp.int32, (chunk, count), 0)
    target = target_ref[...]
    counted = counted_ref[...]

    def logit_chunk(index, top):
        at = pl.ds(pl.multiple_of(index * chunk, chunk), chunk)
        total = jnp.zeros((chunk, count), jnp.float32)
        for group in range(groups):
            total += lax.dot_general(
                table_ref[group, at],
                rows_in[:, group * group_width : (group + 1) * group_width],
                (((1,), (1,)), ((), ())),
                preferred_element_type=jnp.float32,
            )
        total = jnp.where(row_iota + (base + index * chunk) < VOCAB_REAL, total, NEG_FILL)
        logits[at] = total
        return jnp.maximum(top, jnp.max(total, 0, keepdims=True))

    local_top = lax.fori_loop(
        0, 4, logit_chunk, jnp.full((1, count), NEG_FILL, jnp.float32)
    )

    def exp_chunk(index, carry):
        total, pick = carry
        at = pl.ds(pl.multiple_of(index * chunk, chunk), chunk)
        values = logits[at]
        hits = row_iota + (base + index * chunk) == target
        pick += jnp.sum(jnp.where(hits, values, 0.0), 0, keepdims=True)
        values = jnp.exp(values - local_top)
        logits[at] = values
        return total + jnp.sum(values, 0, keepdims=True), pick

    zero_row = jnp.zeros((1, count), jnp.float32)
    local_total, pick = lax.fori_loop(0, 4, exp_chunk, (zero_row, zero_row))
    lanes = count // 4
    top = jnp.concatenate([local_top[:, lanes * i : lanes * (i + 1)] for i in range(4)], 0)
    total = jnp.concatenate([local_total[:, lanes * i : lanes * (i + 1)] for i in range(4)], 0)
    for phase, (axis, steps) in enumerate(((CORE, (1,)), (Y, (1, 2, 3)), (Z, (1, 2, 3)))):
        stats[phase] = jnp.concatenate([top, total], 0)
        copies = [
            wires.send(stats.at[phase], stats_in.at[phase, step - 1], moved(place, axis, step))
            for step in steps
        ]
        for copy in copies:
            copy.wait_recv()
        tops, totals = [top], [total]
        for step in steps:
            received = stats_in[phase, step - 1]
            tops.append(received[:4])
            totals.append(received[4:])
        top = tops[0]
        for other in tops[1:]:
            top = jnp.maximum(top, other)
        total = sum(part * jnp.exp(part_top - top) for part, part_top in zip(totals, tops))
    log_total = top + jnp.log(total)
    log_total = jnp.concatenate([log_total[i : i + 1] for i in range(4)], 1)
    first_device = (lax.axis_index("vocab") == 0).astype(jnp.float32)
    loss_ref[...] = (first_device * log_total - pick) * counted
    weight = counted / (N_DP * N_VOCAB * own)
    scale = jnp.exp(local_top - log_total) * weight

    @pl.loop(0, 4)
    def _(index):
        at = pl.ds(pl.multiple_of(index * chunk, chunk), chunk)
        hits = row_iota + (base + index * chunk) == target
        d_logits[at] = (logits[at] * scale - jnp.where(hits, weight, 0.0)).astype(jnp.bfloat16)

    for side in range(2):
        lowered = d_logits[:, 256 * side : 256 * (side + 1)]
        for group in range(groups):
            rows_grad = lax.dot_general(
                lowered,
                table_ref[group],
                (((0,), (0,)), ((), ())),
                preferred_element_type=jnp.float32,
            ).astype(jnp.bfloat16)
            part, column = group // 2, group % 2 * group_width
            for index in range(16):
                inner = 16 * side + index
                at_z, at_y, at_core = inner // 8, inner // 2 % SIDE, inner % 2
                first, second = (at_z, at_y) if part == 0 else (at_y, at_z)
                d_rows[part, at_core, first, second, :, column : column + group_width] = (
                    rows_grad[own * index : own * (index + 1)]
                )
    crossing = [
        wires.send(d_rows.at[part, 1 - core], d_sibling.at[part], sibling) for part in range(2)
    ]
    reduce_axes = ((Z, Y), (Y, Z))
    first_rings, second_rings = [], []
    for part in range(2):
        first_axis, second_axis = reduce_axes[part]
        crossing[part].wait_recv()
        for j in range(4):
            add_blocks(d_rows.at[part, core, j], [d_sibling.at[part, j]], 4)
        first_rings.append(
            DirectReduce(
                wires,
                place,
                first_axis,
                lambda j, part=part: d_rows.at[part, core, j],
                4,
                d_first.at[part],
            )
        )
        second_rings.append(
            DirectReduce(
                wires,
                place,
                second_axis,
                lambda j, part=part, k=place[first_axis]: d_rows.at[part, core, k, j],
                1,
                d_second.at[part],
            )
        )
        first_rings[part].start()

    def table_grad_chunk(index):
        at = pl.ds(pl.multiple_of(index * chunk, chunk), chunk)
        blocks_in_chunk = chunk // table_grad_ref.shape[2]
        for group in range(groups):
            product = jnp.dot(
                d_logits[at],
                rows_in[:, group * group_width : (group + 1) * group_width],
                preferred_element_type=jnp.float32,
            ).astype(jnp.bfloat16)
            table_grad_ref[group, pl.ds(index * blocks_in_chunk, blocks_in_chunk)] = (
                product.reshape((blocks_in_chunk,) + table_grad_ref.shape[2:])
            )

    @pl.loop(0, 2)
    def _(index):
        table_grad_chunk(index)

    for ring, later in zip(first_rings, second_rings):
        ring.finish()
        later.start()

    @pl.loop(2, 4)
    def _(index):
        table_grad_chunk(index)

    for part in range(2):
        second_rings[part].arrive()
        first_axis, second_axis = reduce_axes[part]
        total = d_rows[part, core, place[first_axis], place[second_axis]].astype(jnp.float32)
        for step in range(3):
            total += d_second[part, step].astype(jnp.float32)
        d_head_ref[:, part * half_width : (part + 1) * half_width] = total
    wires.drain()


def head_call(head_in, table_full, target_row, counted_row):
    groups, rows, group_width = table_full.shape
    own, width = head_in.shape
    count = target_row.shape[1]
    half = width // 2
    bf16 = jnp.bfloat16
    return pl.pallas_call(
        head_kernel,
        name="head",
        out_shape=(
            jax.ShapeDtypeStruct((own, width), jnp.float32),
            jax.ShapeDtypeStruct((groups, TABLE_CHUNKS, rows // TABLE_CHUNKS, group_width), bf16),
            jax.ShapeDtypeStruct((1, count), jnp.float32),
        ),
        in_specs=[VMEM] * 4,
        out_specs=(VMEM,) * 3,
        scratch_shapes=[
            pltpu.VMEM((2, 2, SIDE, SIDE, own, half), bf16),
            pltpu.VMEM((count, width), bf16),
            pltpu.VMEM((rows, count), jnp.float32),
            pltpu.VMEM((rows, count), bf16),
            pltpu.VMEM((3, 8, count // 4), jnp.float32),
            pltpu.VMEM((3, 3, 8, count // 4), jnp.float32),
            pltpu.VMEM((2, 2, SIDE, SIDE, own, half), bf16),
            pltpu.VMEM((2, SIDE, SIDE, own, half), bf16),
            pltpu.VMEM((2, 3, SIDE, own, half), bf16),
            pltpu.VMEM((2, 3, own, half), bf16),
            pltpu.SemaphoreType.DMA((40,)),
            pltpu.SemaphoreType.DMA((40,)),
        ],
        compiler_params=pltpu.CompilerParams(
            collective_id=2, has_side_effects=True, vmem_limit_bytes=60 << 20
        ),
    )(head_in, table_full, target_row, counted_row)


def finish_kernel(
    grads_ref,
    small_ref,
    head_grad_ref,
    d_embed_ref,
    ids_ref,
    loss_ref,
    grads_out_ref,
    table_grad_ref,
    final_ref,
    sums,
    sibling_in,
    half_a,
    whole_a,
    half_b,
    whole_b,
    half_c,
    whole_c,
    small_sums,
    small_sibling,
    small_a,
    small_b,
    small_c,
    table_sums,
    table_half,
    table_whole,
    embeds,
    ids_all,
    send_sems,
    recv_sems,
    local_sems,
):
    place = coordinates()
    core = place[CORE]
    across = place[X]
    sibling = moved(place, CORE, 1)
    wires = Wires(send_sems, recv_sems)
    loads = []

    def load(source, target):
        copy = pltpu.make_async_copy(source, target, local_sems.at[len(loads)])
        copy.start()
        loads.append(copy)
        return copy

    third = [place[ORDERS[part][2]] for part in range(3)]
    table_load = load(head_grad_ref, table_sums)
    block_loads = {}
    for step in (2, 1, 3, 0):
        for part in range(3):
            j = (third[part] + step) % SIDE
            block_loads[part, step] = load(grads_ref.at[part, core, j], sums.at[part, j])
    small_load = load(small_ref.at[core], small_sums)

    width = table_grad_ref.shape[1]
    embed_axes = ((Y, Z), (Z, Y))
    source_part = across // 2
    near = place[Y] * (1 - source_part) + place[Z] * source_part
    far = place[Z] * (1 - source_part) + place[Y] * source_part
    landing = embeds.at[source_part, core, far, 2 * near + across % 2]
    own_columns = pl.ds(pl.multiple_of(across * width, width), width)
    landing[...] = d_embed_ref[:, own_columns]
    ids_all[across] = ids_ref[...]
    greet(place, (X, Y, Z), (X, Y, Z))
    swaps = []
    for step in (1, 2, 3):
        there = moved(place, X, step)
        columns = pl.ds(pl.multiple_of(there[X] * width, width), width)
        swaps.append(wires.send(d_embed_ref.at[:, columns], landing, there))
    ids_ring = DirectGather(wires, place, X, lambda j: ids_all.at[j])
    ids_ring.start()
    small_crossing = wires.send(small_ref.at[1 - core], small_sibling, sibling)
    crossings = {}
    for step in (2, 1, 3, 0):
        for part in range(3):
            j = (third[part] + step) % SIDE
            crossings[part, step] = wires.send(
                grads_ref.at[part, 1 - core, j], sibling_in.at[part, j], sibling
            )

    embed_first, embed_second = [], []
    for part in range(2):
        near_axis, far_axis = embed_axes[part]
        embed_first.append(
            DirectGather(
                wires,
                place,
                near_axis,
                lambda j, part=part, k=place[far_axis]: embeds.at[part, core, k, pl.ds(2 * j, 2)],
            )
        )
        embed_second.append(
            RingGather(
                wires,
                place,
                far_axis,
                lambda j, part=part: embeds.at[part, core, j],
                lambda j, h, part=part: embeds.at[part, core, j, pl.ds(4 * h, 4)],
            )
        )
    table_ring = RingReduce(
        wires,
        place,
        X,
        lambda j: table_sums.at[j],
        lambda j, h: table_sums.at[j, pl.ds(TABLE_CHUNKS // 2 * h, TABLE_CHUNKS // 2)],
        TABLE_CHUNKS,
        table_half,
        table_whole,
    )
    rings = []
    for phase, (half_in, whole_in) in enumerate(
        ((half_c, whole_c), (half_b, whole_b), (half_a, whole_a))
    ):
        row = []
        for part in range(3):
            piece, half = block_ring(
                place,
                part,
                phase,
                lambda k3, first, count, part=part: sums.at[part, k3, pl.ds(first, count)],
            )
            row.append(
                RingReduce(
                    wires,
                    place,
                    ORDERS[part][phase],
                    piece,
                    half,
                    (2, 8, 32)[phase],
                    half_in.at[part],
                    whole_in.at[part],
                )
            )
        rings.append(row)
    small_rings = [
        DirectReduce(wires, place, Z, lambda j: small_sums.at[j], 16, small_a),
        DirectReduce(
            wires, place, Y, lambda j: small_sums.at[place[Z], pl.ds(4 * j, 4)], 4, small_b
        ),
        DirectReduce(
            wires, place, X, lambda j: small_sums.at[place[Z], pl.ds(4 * place[Y] + j, 1)], 1, small_c
        ),
    ]

    for copy in swaps:
        copy.wait_recv()
    for ring in embed_first:
        ring.start()
    table_load.wait()
    table_ring.start()

    def add_crossing(part, step):
        j = (third[part] + step) % SIDE
        block_loads[part, step].wait()
        crossings[part, step].wait_recv()
        add_blocks(sums.at[part, j], [sibling_in.at[part, j]], 32)

    small_load.wait()
    small_crossing.wait_recv()
    for j in range(4):
        add_blocks(small_sums.at[j], [small_sibling.at[j]], 16)
    for ring, later in zip(embed_first, embed_second):
        ring.finish()
        later.start()
    small_rings[0].start()
    for part in range(3):
        add_crossing(part, 2)
        rings[2][part].start()
    for ring in embed_second:
        ring.forward()
    for part in range(3):
        add_crossing(part, 1)
        add_crossing(part, 3)
    embed_siblings = []
    for part in range(2):
        k = place[embed_axes[part][1]]
        for step in (0, 1, 3):
            piece = embeds.at[part, core, (k + step) % SIDE]
            embed_siblings.append(wires.send(piece, piece, sibling))
    table_ring.forward()
    for ring in rings[2]:
        ring.forward()
    for part in range(3):
        add_crossing(part, 0)
    for part in range(2):
        embed_second[part].finish()
        k = place[embed_axes[part][1]]
        piece = embeds.at[part, core, (k + 2) % SIDE]
        embed_siblings.append(wires.send(piece, piece, sibling))
    ids_ring.finish()
    small_rings[0].finish()
    small_rings[1].start()

    rows = table_grad_ref.shape[0]
    chunk = rows // 4
    base = lax.axis_index("vocab") * rows
    row_iota = lax.broadcasted_iota(jnp.int32, (chunk, 512), 0)

    @pl.loop(0, 4)
    def _(index):
        at = pl.ds(pl.multiple_of(index * chunk, chunk), chunk)
        table_grad_ref[at] = jnp.zeros((chunk, width), jnp.float32)

    def scatter_rows(part, at_core):
        @pl.loop(0, 8)
        def _(index):
            at_far, pair = index // 2, index % 2
            values = embeds[part, at_core, at_far, pl.ds(4 * pair, 4)].reshape(512, width)
            ids = []
            for which in range(4):
                at_near = 2 * pair + which // 2
                at_z, at_y = (at_far, at_near) if part == 0 else (at_near, at_far)
                inner = (at_z * SIDE + at_y) * 2 + at_core
                ids.append(ids_all[2 * part + which % 2, pl.ds(inner, 1), :])
            ids = jnp.concatenate(ids, 1) - base

            @pl.loop(0, 4)
            def _(row):
                at = pl.ds(pl.multiple_of(row * chunk, chunk), chunk)
                hot = jnp.where(row_iota + row * chunk == ids, 1.0, 0.0).astype(jnp.bfloat16)
                table_grad_ref[at] += jnp.dot(hot, values, preferred_element_type=jnp.float32)

    scatter_rows(0, core)
    table_ring.arrive()
    table_block = rows // TABLE_CHUNKS

    @pl.loop(0, TABLE_CHUNKS)
    def _(index):
        at = pl.ds(pl.multiple_of(index * table_block, table_block), table_block)
        table_grad_ref[at] += (
            table_sums[across, index].astype(jnp.float32)
            + table_whole[0, index].astype(jnp.float32)
            + table_whole[1, index].astype(jnp.float32)
        )

    scatter_rows(1, core)
    small_rings[1].finish()
    small_rings[2].start()
    for ring, later in zip(rings[2], rings[1]):
        ring.finish()
        later.start()
    for copy in embed_siblings:
        copy.wait_recv()
    scatter_rows(0, 1 - core)
    for ring in rings[1]:
        ring.forward()
    scatter_rows(1, 1 - core)
    for ring, later in zip(rings[1], rings[0]):
        ring.finish()
        later.start()
    small_rings[2].finish()
    table_squares = jnp.zeros((1, width), jnp.float32)
    for index in range(4):
        values = table_grad_ref[index * chunk : (index + 1) * chunk]
        table_squares += jnp.sum(values * values, 0, keepdims=True)
    squares = table_squares[:, :128] + table_squares[:, 128:]
    for ring in rings[0]:
        ring.forward()
    for part in range(3):
        rings[0][part].arrive()
        k1, k2, k3 = (place[axis] for axis in ORDERS[part])
        for which in range(2):
            total = sums[part, k3, 8 * k2 + 2 * k1 + which].astype(jnp.float32)
            for side in range(2):
                total += whole_c[part, side, which].astype(jnp.float32)
            grads_out_ref[part, which] = total
            squares += jnp.sum(total * total, 0, keepdims=True)
    loss = sum(loss_ref[:, 128 * index : 128 * (index + 1)] for index in range(4))
    own_small = small_sums[place[Z], 4 * place[Y] + across].astype(jnp.float32)
    final_ref[0, core, place[Z], place[Y], across] = own_small[:8]
    final_ref[1, core, across, place[Z], place[Y]] = jnp.concatenate(
        [own_small[8:9], squares, loss, jnp.zeros((5, 128), jnp.float32)], 0
    )
    lead = [(0, core), (1, core)]
    orders = (((X, Y, Z)), (Y, Z, X))
    for phase in range(3):
        gathers = []
        for part in range(2):
            first_axis, second_axis, third_axis = orders[part]
            keys = (place[third_axis], place[second_axis])[: 2 - phase]
            gathers.append(
                DirectGather(
                    wires,
                    place,
                    orders[part][phase],
                    lambda j, key=lead[part] + keys: final_ref.at[key + (j,)],
                )
            )
        for gather in gathers:
            gather.start()
        for gather in gathers:
            gather.finish()
    copies = []
    for part in range(2):
        mine = final_ref.at[part, core]
        copies.append(wires.send(mine, mine, sibling))
    for copy in copies:
        copy.wait_recv()
    wires.drain()


def finish_call(grads, small, head_grad, d_embed, token_ids, loss_row):
    bf16 = jnp.bfloat16
    groups, chunks, chunk_rows, width = head_grad.shape
    rows = chunks * chunk_rows
    block = (BLOCK, BLOCK)
    return pl.pallas_call(
        finish_kernel,
        name="reduce_and_scatter",
        out_shape=(
            jax.ShapeDtypeStruct((3, 2) + block, jnp.float32),
            jax.ShapeDtypeStruct((rows, width), jnp.float32),
            jax.ShapeDtypeStruct((2, 2, SIDE, SIDE, SIDE, 8, 128), jnp.float32),
        ),
        in_specs=[ANY, ANY, ANY, VMEM, VMEM, VMEM],
        out_specs=(VMEM,) * 3,
        scratch_shapes=[
            pltpu.VMEM((3, SIDE, 32) + block, bf16),
            pltpu.VMEM((3, SIDE, 32) + block, bf16),
            pltpu.VMEM((3, 2, 16) + block, bf16),
            pltpu.VMEM((3, 2, 32) + block, bf16),
            pltpu.VMEM((3, 2, 4) + block, bf16),
            pltpu.VMEM((3, 2, 8) + block, bf16),
            pltpu.VMEM((3, 2, 1) + block, bf16),
            pltpu.VMEM((3, 2, 2) + block, bf16),
            pltpu.VMEM((SIDE, 16, 16, 128), bf16),
            pltpu.VMEM((SIDE, 16, 16, 128), bf16),
            pltpu.VMEM((3, 16, 16, 128), bf16),
            pltpu.VMEM((3, 4, 16, 128), bf16),
            pltpu.VMEM((3, 1, 16, 128), bf16),
            pltpu.VMEM(head_grad.shape, bf16),
            pltpu.VMEM((2, chunks // 2, chunk_rows, width), bf16),
            pltpu.VMEM((2, chunks, chunk_rows, width), bf16),
            pltpu.VMEM((2, 2, SIDE, 8, 128, width), bf16),
            pltpu.VMEM((N_DP,) + token_ids.shape, jnp.int32),
            pltpu.SemaphoreType.DMA((128,)),
            pltpu.SemaphoreType.DMA((128,)),
            pltpu.SemaphoreType.DMA((14,)),
        ],
        compiler_params=pltpu.CompilerParams(
            collective_id=3, has_side_effects=True, vmem_limit_bytes=63 << 20
        ),
    )(grads, small, head_grad, d_embed, token_ids, loss_row)


def row_mean(values):
    return jnp.mean(values, -1, keepdims=True)


def normalized(values):
    center = values - row_mean(values)
    scale = lax.rsqrt(row_mean(center * center) + LN_EPS)
    return center * scale, scale


def norm_backward(d_normed, hat, scale, gain):
    d_hat = d_normed * gain
    d_values = scale * (d_hat - row_mean(d_hat) - hat * row_mean(d_hat * hat))
    d_gain = jnp.sum(d_normed * hat, 0, keepdims=True)
    return d_values, d_gain, jnp.sum(d_normed, 0, keepdims=True)


def lane_range(first, count):
    return pl.ds(pl.multiple_of(first, 128), count)


QKV, PROJ, FC, OUT = (0, 24), (192, 8), (256, 32), (512, 8)


def load_blocks(full_ref, blocks, sems):
    share = blocks.shape[0] // 8
    copies = []
    for index in range(8):
        part = pl.ds(index * share, share)
        copies.append(pltpu.make_async_copy(full_ref.at[part], blocks.at[part], sems.at[index]))
        copies[-1].start()
    return copies


def weight_tiles(blocks, where_ref, matrix, row, rows, column, columns):
    first, in_row = matrix
    return jnp.concatenate(
        [
            jnp.concatenate(
                [
                    blocks[where_ref[first + (row + i) * in_row + column + j]]
                    for j in range(columns)
                ],
                1,
            )
            for i in range(rows)
        ],
        0,
    )


def selected_rows(ref, at_ref, count):
    return jnp.concatenate([ref[pl.ds(at_ref[i], 1), :] for i in range(count)], 0)


def pair_masks(count):
    lane = lax.broadcasted_iota(jnp.int32, (2 * count, 2 * HEAD_DIM), 1)
    row = lax.broadcasted_iota(jnp.int32, (2 * count, 2 * HEAD_DIM), 0)
    return (lane < HEAD_DIM) == (row < count)


def doubled(values, own_lanes):
    both = jnp.concatenate([values, values], 0)
    return jnp.where(own_lanes, both.astype(jnp.float32), 0.0).astype(jnp.bfloat16)


def folded(values, count):
    lane = lax.broadcasted_iota(jnp.int32, (count, 2 * HEAD_DIM), 1)
    return jnp.where(lane < HEAD_DIM, values[:count], values[count:])


def forward_kernel(
    where_ref,
    at_ref,
    length_ref,
    full_ref,
    hidden_ref,
    vec_ref,
    head_in_ref,
    query_ref,
    kv_ref,
    probs_ref,
    attended_ref,
    middle_ref,
    pre_act_ref,
    last_ref,
    blocks,
    normed_rows,
    activated,
    sems,
):
    copies = load_blocks(full_ref, blocks, sems)
    count = head_in_ref.shape[0]
    bf16 = jnp.bfloat16
    hat, _ = normalized(hidden_ref[...])
    normed_rows[...] = hat * vec_ref[0:1] + vec_ref[1:2]
    normed_one = normed_rows[...].astype(bf16)
    normed_own = selected_rows(normed_rows, at_ref, count).astype(bf16)
    for copy in copies:
        copy.wait()

    @pl.loop(0, 4)
    def _(tile):
        at = lane_range(256 * tile, 256)
        weight = weight_tiles(blocks, where_ref, QKV, 0, 8, 2 * tile, 2)
        product = jnp.dot(normed_own, weight, preferred_element_type=jnp.float32)
        query_ref[:, at] = (product + vec_ref[2:3, at]).astype(bf16)

    @pl.loop(0, 4)
    def _(tile):
        at = lane_range(256 * tile, 256)
        weight = weight_tiles(blocks, where_ref, QKV, 0, 8, 8 + 2 * tile, 2)
        product = jnp.dot(normed_one, weight, preferred_element_type=jnp.float32)
        kv_ref[:, at] = product.astype(bf16)

    @pl.loop(0, 4)
    def _(tile):
        weight = weight_tiles(blocks, where_ref, QKV, 0, 8, 16 + 2 * tile, 2)
        product = jnp.dot(normed_one, weight, preferred_element_type=jnp.float32)
        bias = vec_ref[3:4, lane_range(256 * tile, 256)]
        kv_ref[:, lane_range(D + 256 * tile, 256)] = (product + bias).astype(bf16)

    own_lanes = pair_masks(count)
    pairs = HEADS // 2
    seq_len = hidden_ref.shape[0]
    row = lax.broadcasted_iota(jnp.int32, (count, seq_len), 0)
    key = lax.broadcasted_iota(jnp.int32, (count, seq_len), 1)
    last_key = jnp.zeros((count, seq_len), jnp.int32)
    for i in range(count):
        last_key = jnp.where(row == i, jnp.minimum(at_ref[i], length_ref[0] - 1), last_key)
    allowed = jnp.concatenate([key <= last_key] * 2, 0)
    for pair in range(pairs):
        lanes = slice(128 * pair, 128 * pair + 128)
        values_at = slice(D + 128 * pair, D + 128 * pair + 128)
        scores = dot_nt(doubled(query_ref[:, lanes], own_lanes), kv_ref[:, lanes]) * HEAD_DIM ** (
            -0.5
        )
        scores = jnp.where(allowed, scores, NEG_FILL)
        exps = jnp.exp(scores - jnp.max(scores, -1, keepdims=True))
        probs = exps / jnp.sum(exps, -1, keepdims=True)
        probs_ref[2 * count * pair : 2 * count * (pair + 1)] = probs
        mixed = jnp.dot(
            probs.astype(bf16), kv_ref[:, values_at], preferred_element_type=jnp.float32
        )
        attended_ref[:, lanes] = folded(mixed, count).astype(bf16)

    attended = attended_ref[...]
    middle_ref[...] = selected_rows(hidden_ref, at_ref, count) + vec_ref[4:5]

    @pl.loop(0, 4)
    def _(tile):
        weight = weight_tiles(blocks, where_ref, PROJ, 0, 8, 2 * tile, 2)
        middle_ref[:, lane_range(256 * tile, 256)] += jnp.dot(
            attended, weight, preferred_element_type=jnp.float32
        )

    middle = middle_ref[...]
    hat, _ = normalized(middle)
    normed_two = (hat * vec_ref[5:6] + vec_ref[6:7]).astype(bf16)

    @pl.loop(0, 16)
    def _(tile):
        at = lane_range(256 * tile, 256)
        weight = weight_tiles(blocks, where_ref, FC, 0, 8, 2 * tile, 2)
        bias = vec_ref[pl.ds(7 + tile // 4, 1), lane_range(256 * (tile % 4), 256)]
        pre_act = jnp.dot(normed_two, weight, preferred_element_type=jnp.float32) + bias
        pre_act_ref[:, at] = pre_act
        activated[:, at] = gelu(pre_act).astype(bf16)

    last_ref[...] = middle + vec_ref[11:12]

    @pl.loop(0, 16)
    def _(index):
        tile, depth = index // 4, index % 4
        weight = weight_tiles(blocks, where_ref, OUT, 8 * depth, 8, 2 * tile, 2)
        last_ref[:, lane_range(256 * tile, 256)] += jnp.dot(
            activated[:, lane_range(1024 * depth, 1024)],
            weight,
            preferred_element_type=jnp.float32,
        )

    hat, _ = normalized(last_ref[...])
    head_in_ref[...] = (hat * vec_ref[12:13] + vec_ref[13:14]).astype(bf16)


def forward_call(where, positions, length, full, hidden, vectors):
    count = positions.shape[0]
    seq_len = hidden.shape[0]
    bf16 = jnp.bfloat16
    shape = jax.ShapeDtypeStruct
    return pl.pallas_call(
        forward_kernel,
        name="layer_forward",
        out_shape=(
            shape((count, D), bf16),
            shape((count, D), bf16),
            shape((seq_len, 2 * D), bf16),
            shape((HEADS * count, seq_len), jnp.float32),
            shape((count, D), bf16),
            shape((count, D), jnp.float32),
            shape((count, FF), jnp.float32),
            shape((count, D), jnp.float32),
        ),
        grid_spec=pltpu.PrefetchScalarGridSpec(
            num_scalar_prefetch=3,
            grid=(),
            in_specs=[ANY, VMEM, VMEM],
            out_specs=(VMEM,) * 8,
            scratch_shapes=[
                pltpu.VMEM(full.shape, bf16),
                pltpu.VMEM(hidden.shape, jnp.float32),
                pltpu.VMEM((count, FF), bf16),
                pltpu.SemaphoreType.DMA((8,)),
            ],
        ),
        compiler_params=pltpu.CompilerParams(vmem_limit_bytes=48 << 20),
    )(where, positions, length, full, hidden, vectors)


def gelu_slope(values):
    cube = 0.044715 * values * values
    bent = jnp.tanh(GELU_C * (values + cube * values))
    return 0.5 * (1.0 + bent) + 0.5 * values * (1.0 - bent * bent) * GELU_C * (1.0 + 3.0 * cube)


def backward_kernel(
    where_ref,
    at_ref,
    full_ref,
    hidden_ref,
    vec_ref,
    query_ref,
    kv_ref,
    probs_ref,
    attended_ref,
    middle_ref,
    pre_act_ref,
    last_ref,
    d_head_ref,
    grads_ref,
    small_ref,
    d_embed_ref,
    blocks,
    grad_blocks,
    activated,
    d_pre,
    normed,
    rows_out,
    d_qkv,
    spread,
    query_grads,
    vec_grads,
    sems,
    grad_sem,
):
    copies = load_blocks(full_ref, blocks, sems)
    count = d_head_ref.shape[0]
    bf16 = jnp.bfloat16

    def weight_grad(matrix, rows, left_ref, right):
        first, in_row = matrix

        @pl.loop(0, rows)
        def _(row):
            left = left_ref[:, lane_range(128 * row, 128)]
            for column in range(0, in_row, 2):
                product = dot_tn(left, right[:, 128 * column : 128 * column + 256]).astype(bf16)
                for side in range(2):
                    index = first + row * in_row + column + side
                    grad_blocks[index] = product[:, 128 * side : 128 * side + 128]
                    pltpu.make_async_copy(
                        grad_blocks.at[index], grads_ref.at[where_ref[index]], grad_sem
                    ).start()

    hat, scale = normalized(last_ref[...])
    d_last, vec_grads[12:13], vec_grads[13:14] = norm_backward(
        d_head_ref[...], hat, scale, vec_ref[12:13]
    )
    d_branch = d_last.astype(bf16)
    vec_grads[11:12] = jnp.sum(d_branch.astype(jnp.float32), 0, keepdims=True)
    activated[...] = gelu(pre_act_ref[...]).astype(bf16)
    weight_grad(OUT, 32, activated, d_branch)
    for copy in copies:
        copy.wait()

    @pl.loop(0, 16)
    def _(tile):
        at = lane_range(256 * tile, 256)
        weight = weight_tiles(blocks, where_ref, OUT, 2 * tile, 2, 0, 8)
        lowered = (dot_nt(d_branch, weight) * gelu_slope(pre_act_ref[:, at])).astype(bf16)
        d_pre[:, at] = lowered
        vec_grads[pl.ds(7 + tile // 4, 1), lane_range(256 * (tile % 4), 256)] = jnp.sum(
            lowered.astype(jnp.float32), 0, keepdims=True
        )

    hat, scale = normalized(middle_ref[...])
    normed[pl.ds(0, count)] = (hat * vec_ref[5:6] + vec_ref[6:7]).astype(bf16)
    weight_grad(FC, 8, normed.at[pl.ds(0, count)], d_pre[...])
    rows_out[...] = jnp.zeros(rows_out.shape, jnp.float32)

    @pl.loop(0, 16)
    def _(index):
        tile, depth = index // 4, index % 4
        weight = weight_tiles(blocks, where_ref, FC, 2 * tile, 2, 8 * depth, 8)
        rows_out[pl.ds(0, count), lane_range(256 * tile, 256)] += dot_nt(
            d_pre[:, lane_range(1024 * depth, 1024)], weight
        )

    d_middle, vec_grads[5:6], vec_grads[6:7] = norm_backward(
        rows_out[pl.ds(0, count)], hat, scale, vec_ref[5:6]
    )
    d_middle = d_middle + d_last
    d_proj = d_middle.astype(bf16)
    vec_grads[4:5] = jnp.sum(d_proj.astype(jnp.float32), 0, keepdims=True)
    weight_grad(PROJ, 8, attended_ref, d_proj)

    @pl.loop(0, 4)
    def _(tile):
        weight = weight_tiles(blocks, where_ref, PROJ, 2 * tile, 2, 0, 8)
        rows_out[pl.ds(0, count), lane_range(256 * tile, 256)] = dot_nt(d_proj, weight)

    own_lanes = pair_masks(count)
    spread[...] = jnp.zeros(spread.shape, jnp.float32)
    for pair in range(HEADS // 2):
        lanes = slice(128 * pair, 128 * pair + 128)
        values_at = slice(D + 128 * pair, D + 128 * pair + 128)
        d_mixed = doubled(rows_out[0:count, lanes].astype(bf16), own_lanes)
        probs = probs_ref[2 * count * pair : 2 * count * (pair + 1)]
        d_probs = dot_nt(d_mixed, kv_ref[:, values_at])
        inner = jnp.sum(probs * d_probs, -1, keepdims=True)
        d_scores = (probs * (d_probs - inner)).astype(bf16)
        d_values = dot_tn(probs.astype(bf16), d_mixed).astype(bf16)
        d_keys = dot_tn(d_scores, doubled(query_ref[:, lanes], own_lanes)) * HEAD_DIM ** (-0.5)
        d_query = jnp.dot(d_scores, kv_ref[:, lanes], preferred_element_type=jnp.float32)
        d_query = (folded(d_query, count) * HEAD_DIM ** (-0.5)).astype(bf16).astype(jnp.float32)
        vec_grads[2:3, lanes] = jnp.sum(d_query, 0, keepdims=True)
        vec_grads[3:4, lanes] = jnp.sum(d_values.astype(jnp.float32), 0, keepdims=True)
        query_grads[:, lanes] = d_query
        d_qkv[:, D + 128 * pair : D + 128 * pair + 128] = d_keys.astype(bf16)
        d_qkv[:, 2 * D + 128 * pair : 2 * D + 128 * pair + 128] = d_values
    for i in range(count):
        spread[pl.ds(at_ref[i], 1), :] = query_grads[i : i + 1, :]
    d_qkv[:, :D] = spread[...].astype(bf16)
    hat, scale = normalized(hidden_ref[...])
    normed[...] = (hat * vec_ref[0:1] + vec_ref[1:2]).astype(bf16)
    weight_grad(QKV, 8, normed, d_qkv)
    rows_out[...] = jnp.zeros(rows_out.shape, jnp.float32)

    @pl.loop(0, 12)
    def _(index):
        tile, depth = index // 3, index % 3
        weight = weight_tiles(blocks, where_ref, QKV, 2 * tile, 2, 8 * depth, 8)
        rows_out[:, lane_range(256 * tile, 256)] += dot_nt(
            d_qkv[:, lane_range(1024 * depth, 1024)], weight
        )

    d_hidden, vec_grads[0:1], vec_grads[1:2] = norm_backward(
        rows_out[...], hat, scale, vec_ref[0:1]
    )
    rows_out[...] = d_hidden
    for i in range(count):
        rows_out[pl.ds(at_ref[i], 1), :] += d_middle[i : i + 1]
    d_embed_ref[...] = rows_out[...].astype(bf16)
    vec_rows = vec_ref.shape[0]
    for index in range(small_ref.shape[0]):
        group, tile = index // 8, index % 8
        lanes = slice(128 * tile, 128 * tile + 128)
        vec_row = (
            vec_grads[group : group + 1, lanes]
            if group < vec_rows
            else jnp.zeros((1, 128), jnp.float32)
        )
        small_ref[index] = jnp.concatenate(
            [rows_out[8 * group : 8 * group + 8, lanes], vec_row, jnp.zeros((7, 128), jnp.float32)],
            0,
        ).astype(bf16)
    pltpu.make_async_copy(grad_blocks, grads_ref, grad_sem).wait()


def backward_call(where, positions, full, hidden, vectors, cache, d_head):
    count = positions.shape[0]
    bf16 = jnp.bfloat16
    shape = jax.ShapeDtypeStruct
    return pl.pallas_call(
        backward_kernel,
        name="layer_backward",
        out_shape=(
            shape(full.shape, bf16),
            shape((N_DP * N_VOCAB, 16, 128), bf16),
            shape(hidden.shape, bf16),
        ),
        grid_spec=pltpu.PrefetchScalarGridSpec(
            num_scalar_prefetch=2,
            grid=(),
            in_specs=[ANY] + [VMEM] * 10,
            out_specs=(ANY, VMEM, VMEM),
            scratch_shapes=[
                pltpu.VMEM(full.shape, bf16),
                pltpu.VMEM(full.shape, bf16),
                pltpu.VMEM((count, FF), bf16),
                pltpu.VMEM((count, FF), bf16),
                pltpu.VMEM(hidden.shape, bf16),
                pltpu.VMEM(hidden.shape, jnp.float32),
                pltpu.VMEM((hidden.shape[0], 3 * D), bf16),
                pltpu.VMEM(hidden.shape, jnp.float32),
                pltpu.VMEM((count, D), jnp.float32),
                pltpu.VMEM((16, D), jnp.float32),
                pltpu.SemaphoreType.DMA((8,)),
                pltpu.SemaphoreType.DMA,
            ],
        ),
        compiler_params=pltpu.CompilerParams(vmem_limit_bytes=62 << 20),
    )(where, positions, full, hidden, vectors, *cache, d_head)


def slot_places():
    slot = np.arange(N_DP * N_VOCAB * SLOTS)
    device, own = slot // SLOTS, slot % SLOTS
    inner = device % N_VOCAB
    place = (device // N_VOCAB, inner // 2 % SIDE, inner // (2 * SIDE), inner % 2)
    part = own // 2
    result = np.zeros_like(slot)
    for which, (first, second, third) in enumerate(ORDERS):
        index = which * 2 + place[CORE]
        for axis in (third, second, first):
            index = index * SIDE + place[axis]
        result = np.where(part == which, index * 2 + own % 2, result)
    return result.astype(np.int32)


def per_device(
    token_ids,
    seq_lengths,
    loss_positions,
    target_ids,
    block_of_slot,
    matrices,
    left_stats,
    right_stats,
    left_roots,
    right_roots,
    vocab_table,
    table_m,
    table_v,
    positions_table,
    pos_m,
    pos_v,
    vectors,
    vectors_m,
    vectors_v,
):
    vocab_index = lax.axis_index("vocab")
    slots = block_of_slot.shape[0]
    block_iota = jnp.arange(slots, dtype=jnp.int32)
    where = jnp.sum(
        jnp.where(block_of_slot[None, :] == block_iota[:, None], slot_places()[None, :], 0),
        1,
        dtype=jnp.int32,
    )
    own_blocks = matrices.astype(jnp.bfloat16).reshape(3, 2, BLOCK, BLOCK)
    table_low = vocab_table.astype(jnp.bfloat16)
    full, table_full, hidden = start_call(token_ids, own_blocks, table_low, positions_table)
    full_blocks = full.reshape(slots, BLOCK, BLOCK)
    own_length = lax.dynamic_index_in_dim(seq_lengths, vocab_index)
    own_positions = lax.dynamic_index_in_dim(loss_positions, vocab_index, keepdims=False)
    counted = (loss_positions < seq_lengths[:, None]).astype(jnp.float32).reshape(1, -1)
    head_in, *cache = forward_call(where, own_positions, own_length, full_blocks, hidden, vectors)
    d_head_in, head_grad, loss_row = head_call(
        head_in, table_full, target_ids.reshape(1, -1), counted
    )
    grad_blocks, small, d_embed = backward_call(
        where, own_positions, full_blocks, hidden, vectors, cache, d_head_in
    )
    owned_grads, table_grad_own, final = finish_call(
        grad_blocks.reshape(full.shape[:3] + (32, BLOCK, BLOCK)),
        small.reshape(2, SIDE, 16, 16, 128),
        head_grad,
        d_embed,
        token_ids,
        loss_row,
    )
    owned_grads = owned_grads.reshape(SLOTS, BLOCK, BLOCK)
    pos_grad = final[0].reshape(16, 8, 8, 128).transpose(0, 2, 1, 3).reshape(positions_table.shape)
    rest = final[1].transpose(0, 2, 3, 1, 4, 5).reshape(N_DP * N_VOCAB, 8, 128)
    vec_sum = rest[: 8 * vectors.shape[0], 0].reshape(vectors.shape)
    squares_all = jnp.sum(rest[:, 1])
    loss_value = jnp.sum(rest[:, 2])
    grad_norm = jnp.sqrt(squares_all + jnp.sum(pos_grad * pos_grad) + jnp.sum(vec_sum * vec_sum))
    clip_factor = CLIP_LEVEL / jnp.maximum(grad_norm, CLIP_LEVEL)
    matrices_grad = owned_grads * clip_factor
    left_new = STAT_DECAY * left_stats + (1.0 - STAT_DECAY) * jnp.einsum(
        "bij,bkj->bik", matrices_grad, matrices_grad, precision=HIGH
    )
    right_new = STAT_DECAY * right_stats + (1.0 - STAT_DECAY) * jnp.einsum(
        "bji,bjk->bik", matrices_grad, matrices_grad, precision=HIGH
    )
    left_part = jnp.einsum("bij,bjk->bik", left_roots, matrices_grad, precision=HIGH)
    precond = jnp.einsum("bij,bjk->bik", left_part, right_roots, precision=HIGH)
    matrices_new = matrices - SHAMPOO_RATE * (precond + DECAY_RATE * matrices)
    table_new, table_m_new, table_v_new = adamw(
        vocab_table, table_m, table_v, table_grad_own * clip_factor, TABLE_RATE, DECAY_RATE
    )
    positions_new, pos_m_new, pos_v_new = adamw(
        positions_table, pos_m, pos_v, pos_grad * clip_factor, POS_RATE, DECAY_RATE
    )
    vectors_new, vectors_m_new, vectors_v_new = adamw(
        vectors, vectors_m, vectors_v, vec_sum * clip_factor, VECTOR_RATE, 0.0
    )
    return (
        loss_value,
        grad_norm,
        matrices_new,
        left_new,
        right_new,
        matrices_grad,
        table_new,
        table_m_new,
        table_v_new,
        positions_new,
        pos_m_new,
        pos_v_new,
        vectors_new,
        vectors_m_new,
        vectors_v_new,
    )


def solution(mesh):
    in_specs = (
        P("dp", None),
        P("dp"),
        P("dp", None),
        P("dp", None),
        P(),
        P(("dp", "vocab"), None, None),
        P(("dp", "vocab"), None, None),
        P(("dp", "vocab"), None, None),
        P(("dp", "vocab"), None, None),
        P(("dp", "vocab"), None, None),
        P("vocab", "dp"),
        P("vocab", "dp"),
        P("vocab", "dp"),
        P(),
        P(),
        P(),
        P(),
        P(),
        P(),
    )
    out_specs = (
        P(),
        P(),
        P(("dp", "vocab"), None, None),
        P(("dp", "vocab"), None, None),
        P(("dp", "vocab"), None, None),
        P(("dp", "vocab"), None, None),
        P("vocab", "dp"),
        P("vocab", "dp"),
        P("vocab", "dp"),
        P(),
        P(),
        P(),
        P(),
        P(),
        P(),
    )
    return jax.shard_map(
        per_device, mesh=mesh, in_specs=in_specs, out_specs=out_specs, check_vma=False
    )
```

```python
import jax
import jax.numpy as jnp
import numpy as np
from jax import lax
from jax.experimental import pallas as pl
from jax.experimental.pallas import tpu as pltpu
from jax.sharding import PartitionSpec as P

D = 1024
HEADS = 16
HEAD_DIM = 64
FF = 4096
VOCAB_REAL = 50257
LAYERS = 1
BLOCK = 128
STEP = 10


LN_EPS = 1e-05
CLIP_LEVEL = 0.05
BETA_ONE = 0.9
BETA_TWO = 0.999
ADAM_EPS = 1e-08
STAT_DECAY = 0.95
SHAMPOO_RATE = 0.03
TABLE_RATE = 0.15
POS_RATE = 0.05
VECTOR_RATE = 0.25
DECAY_RATE = 0.1
NEG_FILL = -1e30
GELU_C = 0.7978845608028654
HIGH = lax.Precision.HIGHEST


def gelu(values):
    return 0.5 * values * (1.0 + jnp.tanh(GELU_C * (values + 0.044715 * values * values * values)))


def dot_nt(left, right):
    return lax.dot_general(
        left, right, (((1,), (1,)), ((), ())), preferred_element_type=jnp.float32
    )


def dot_tn(left, right):
    return lax.dot_general(
        left, right, (((0,), (0,)), ((), ())), preferred_element_type=jnp.float32
    )


VMEM_BYTES = 63 << 20
MESH_IDS = pl.DeviceIdType.MESH
ANY = pl.BlockSpec(memory_space=pl.ANY)
VMEM = pl.BlockSpec(memory_space=pltpu.VMEM)
N_DP = 4
N_VOCAB = 32
SIDE = 4
X, Y, Z, CORE = range(4)
ORDERS = ((X, Y, Z), (Y, Z, X), (Z, X, Y))
SLOTS = 6


def coordinates():
    across = lax.axis_index("dp")
    inner = lax.axis_index("vocab")
    return (across, (inner // 2) % SIDE, inner // (2 * SIDE), inner % 2)


def moved(place, axis, step):
    shifted = list(place)
    shifted[axis] = (place[axis] + step) % (2 if axis == CORE else SIDE)
    return tuple(shifted)


def device_of(place):
    return (place[X], (place[Z] * SIDE + place[Y]) * 2 + place[CORE])


def rings_of(place, axes):
    others = [moved(place, CORE, 1)]
    return others + [moved(place, axis, step) for axis in axes for step in (1, 2, 3)]


def greet(others):
    barrier = pltpu.get_barrier_semaphore()
    for other in others:
        pl.semaphore_signal(
            barrier, inc=1, device_id=device_of(other), device_id_type=MESH_IDS
        )
    pl.semaphore_wait(barrier, len(others))


def lane_range(first, count):
    return pl.ds(pl.multiple_of(first, 128), count)


class Wires:
    def __init__(self, send_sems, recv_sems):
        self.send_sems, self.recv_sems, self.used = send_sems, recv_sems, 0
        self.sent = []

    def slot(self):
        self.used += 1
        return self.used - 1

    def copy(self, source, target, place, send_slot, recv_slot):
        return pltpu.make_async_remote_copy(
            src_ref=source,
            dst_ref=target,
            send_sem=self.send_sems.at[send_slot],
            recv_sem=self.recv_sems.at[recv_slot],
            device_id=device_of(place),
            device_id_type=MESH_IDS,
        )

    def send(self, source, target, place, bundle=None):
        recv_slot = self.slot()
        copy = self.copy(source, target, place, recv_slot if bundle is None else bundle, recv_slot)
        copy.start()
        if bundle is None:
            self.sent.append(copy)
        return copy

    def send_all(self, source, target, place, bundle):
        self.copy(source, target, place, bundle, bundle).start()

    def whole(self, ref, place, bundle):
        return self.copy(ref, ref, place, bundle, bundle)

    def settle(self, latest=0):
        done = len(self.sent) - latest
        for copy in self.sent[:done]:
            copy.wait_send()
        self.sent = self.sent[done:]


def add_blocks(target, sources, count):
    @pl.loop(0, count)
    def _(i):
        total = target[i].astype(jnp.float32)
        for source in sources:
            total += source[i].astype(jnp.float32)
        target[i] = total.astype(target.dtype)


class RingGather:
    def __init__(self, wires, place, axis, piece, half, own=None):
        self.wires, self.place, self.axis = wires, place, axis
        self.piece, self.half = piece, half
        self.mine = place[axis]
        self.own = self.piece(self.mine) if own is None else own

    def start(self):
        mine = self.piece(self.mine)
        self.up = self.wires.send(self.own, mine, moved(self.place, self.axis, 1))
        self.down = self.wires.send(self.own, mine, moved(self.place, self.axis, -1))

    def forward(self):
        self.up.wait_recv()
        lower = self.half((self.mine + 3) % SIDE, 0)
        self.far_up = self.wires.send(lower, lower, moved(self.place, self.axis, 1))
        self.down.wait_recv()
        upper = self.half((self.mine + 1) % SIDE, 1)
        self.far_down = self.wires.send(upper, upper, moved(self.place, self.axis, -1))

    def finish(self):
        self.far_up.wait_recv()
        self.far_down.wait_recv()


class DirectGather:
    def __init__(self, wires, place, axis, piece, own=None):
        self.wires, self.place, self.axis, self.piece = wires, place, axis, piece
        self.own = self.piece(place[axis]) if own is None else own

    def start(self):
        mine = self.piece(self.place[self.axis])
        self.copies = [
            self.wires.send(self.own, mine, moved(self.place, self.axis, step))
            for step in (1, 2, 3)
        ]

    def finish(self):
        for copy in self.copies:
            copy.wait_recv()


class RingReduce:
    def __init__(self, wires, place, axis, piece, half, count, half_in, whole_in):
        self.wires, self.place, self.axis = wires, place, axis
        self.piece, self.half, self.count = piece, half, count
        self.half_in, self.whole_in = half_in, whole_in
        self.mine = place[axis]

    def start(self):
        far = (self.mine + 2) % SIDE
        up, down = moved(self.place, self.axis, 1), moved(self.place, self.axis, -1)
        self.far_up = self.wires.send(self.half(far, 0), self.half_in.at[0], up)
        self.far_down = self.wires.send(self.half(far, 1), self.half_in.at[1], down)

    def forward(self):
        after, before = (self.mine + 1) % SIDE, (self.mine + 3) % SIDE
        up, down = moved(self.place, self.axis, 1), moved(self.place, self.axis, -1)
        self.far_up.wait_recv()
        add_blocks(self.half(after, 0), [self.half_in.at[0]], self.count // 2)
        self.up = self.wires.send(self.piece(after), self.whole_in.at[0], up)
        self.far_down.wait_recv()
        add_blocks(self.half(before, 1), [self.half_in.at[1]], self.count // 2)
        self.down = self.wires.send(self.piece(before), self.whole_in.at[1], down)

    def arrive(self):
        self.up.wait_recv()
        self.down.wait_recv()

    def finish(self):
        self.arrive()
        add_blocks(
            self.piece(self.mine), [self.whole_in.at[0], self.whole_in.at[1]], self.count
        )


class DirectReduce:
    def __init__(self, wires, place, axis, piece, count, landing):
        self.wires, self.place, self.axis = wires, place, axis
        self.piece, self.count, self.landing = piece, count, landing

    def start(self):
        mine = self.place[self.axis]
        self.copies = [
            self.wires.send(
                self.piece((mine + step) % SIDE),
                self.landing.at[step - 1],
                moved(self.place, self.axis, step),
            )
            for step in (1, 2, 3)
        ]

    def arrive(self):
        for copy in self.copies:
            copy.wait_recv()

    def finish(self):
        self.arrive()
        add_blocks(
            self.piece(self.place[self.axis]),
            [self.landing.at[step] for step in range(3)],
            self.count,
        )


class RowGather:
    def __init__(self, wires, place, axis, first, row):
        self.wires, self.place, self.axis = wires, place, axis
        self.row, self.mine, self.first = row, place[axis], first
        self.up, self.down, self.far = [], [], {}
        self.bundles = [wires.slot() for _ in range(3)]

    def of(self, piece, index):
        return self.row((self.mine + piece) % SIDE, (self.first + (0, 1, 3, 2)[index]) % SIDE)

    def send(self, index):
        mine = self.of(0, index)
        up, down = moved(self.place, self.axis, 1), moved(self.place, self.axis, -1)
        self.up.append(self.wires.send(mine, mine, up, self.bundles[0]))
        self.down.append(self.wires.send(mine, mine, down, self.bundles[1]))

    def forward(self, index):
        upward = index < 2
        (self.up if upward else self.down)[index].wait_recv()
        passed = self.of(3 if upward else 1, index)
        step = 1 if upward else -1
        target = moved(self.place, self.axis, step)
        self.far[index] = self.wires.send(passed, passed, target, self.bundles[2])
        return passed

    def take(self, index):
        (self.down if index < 2 else self.up)[index].wait_recv()
        return self.of(1 if index < 2 else 3, index)

    def take_far(self, index):
        self.far[index].wait_recv()
        return self.of(2, index)

    def settle(self, piece):
        for bundle in self.bundles:
            self.wires.whole(piece, self.place, bundle).wait_send()


class QuarterReduce(RingReduce):
    def start(self, chunk):
        far = (self.mine + 2) % SIDE
        up, down = moved(self.place, self.axis, 1), moved(self.place, self.axis, -1)
        size = self.count // 4
        landing = pl.ds(chunk * size, size)
        if chunk == 0:
            self.far_ups, self.far_downs = [], []
        self.far_ups.append(
            self.wires.send(self.half(far, chunk), self.half_in.at[0, landing], up)
        )
        self.far_downs.append(
            self.wires.send(self.half(far, 2 + chunk), self.half_in.at[1, landing], down)
        )

    def forward(self):
        after, before = (self.mine + 1) % SIDE, (self.mine + 3) % SIDE
        up, down = moved(self.place, self.axis, 1), moved(self.place, self.axis, -1)
        size = self.count // 4
        for chunk, copy in enumerate(self.far_ups):
            copy.wait_recv()
            landed = self.half_in.at[0, pl.ds(chunk * size, size)]
            add_blocks(self.half(after, chunk), [landed], size)
        self.up = self.wires.send(self.piece(after), self.whole_in.at[0], up)
        for chunk, copy in enumerate(self.far_downs):
            copy.wait_recv()
            landed = self.half_in.at[1, pl.ds(chunk * size, size)]
            add_blocks(self.half(before, 2 + chunk), [landed], size)
        self.down = self.wires.send(self.piece(before), self.whole_in.at[1], down)


def block_ring(place, part, phase, at):
    first_axis, second_axis, third_axis = ORDERS[part]
    k1, k2, k3 = place[first_axis], place[second_axis], place[third_axis]
    if phase == 0:
        return (
            lambda j: at(k3, 8 * k2 + 2 * j, 2),
            lambda j, h: at(k3, 8 * k2 + 2 * j + h, 1),
        )
    if phase == 1:
        return (lambda j: at(k3, 8 * j, 8), lambda j, h: at(k3, 8 * j + 4 * h, 4))
    return (lambda j: at(j, 0, 32), lambda j, q: at(j, 8 * q, 8))


def start_kernel(
    ids_ref,
    matrices_ref,
    table_ref,
    positions_ref,
    full_ref,
    table_full_ref,
    hidden_ref,
    own_low,
    table_pad,
    ids_all,
    parts,
    sibling_in,
    half_in,
    whole_in,
    landing,
    ready,
    arrived,
    send_sems,
    recv_sems,
    local_sems,
):
    place = coordinates()
    core = place[CORE]
    across = place[X]
    sibling = moved(place, CORE, 1)
    wires = Wires(send_sems, recv_sems)
    own_low[...] = matrices_ref[...].astype(jnp.bfloat16).reshape(own_low.shape)
    own_copies = []
    for part in range(3):
        k1, k2, k3 = (place[axis] for axis in ORDERS[part])
        own_copies.append(
            pltpu.make_async_copy(
                own_low.at[part],
                full_ref.at[part, core, k3, pl.ds(8 * k2 + 2 * k1, 2)],
                local_sems.at[part],
            )
        )
        own_copies[-1].start()
    ids_all[across] = ids_ref[...]
    greet(rings_of(place, (X, Y, Z)))
    rings = [[], [], []]
    for part in range(3):

        def at(k3, first, count, part=part):
            return full_ref.at[part, core, k3, pl.ds(first, count)]

        first_axis, second_axis, third_axis = ORDERS[part]
        piece, _ = block_ring(place, part, 0, at)
        rings[0].append(DirectGather(wires, place, first_axis, piece, own_low.at[part]))
        piece, half = block_ring(place, part, 1, at)
        rings[1].append(RingGather(wires, place, second_axis, piece, half))
        rings[2].append(
            RowGather(
                wires,
                place,
                third_axis,
                place[second_axis],
                lambda j, row, at=at: at(j, 8 * row, 8),
            )
        )
    on_z, on_x, on_y = rings[2]
    ids_ring = DirectGather(wires, place, X, lambda j: ids_all.at[j])
    ids_ring.start()
    for ring in rings[0]:
        ring.start()
    rows = table_ref.shape[0]
    table_pad[pl.ds(0, rows)] = table_ref[...].astype(jnp.bfloat16)
    padding = table_pad.shape[0] - rows
    table_pad[pl.ds(rows, padding)] = jnp.zeros((padding, table_pad.shape[1]), jnp.bfloat16)
    table_low = table_pad.at[pl.ds(0, rows)]
    own_copies.append(
        pltpu.make_async_copy(table_low, table_full_ref.at[across], local_sems.at[3])
    )
    own_copies[-1].start()
    table_ring = RowGather(
        wires,
        place,
        X,
        0,
        lambda j, row: table_full_ref.at[j, pl.ds(rows // SIDE * row, rows // SIDE)],
    )
    own_copies[3].wait()
    table_ring.send(0)
    base = (lax.axis_index("vocab") * rows).astype(jnp.float32)
    tiles = table_pad.shape[0] // 128
    lane = lax.broadcasted_iota(jnp.int32, (128, 128), 1).astype(jnp.float32)

    def group_of(part, which):
        return 2 * ((across // 2 + part) % 2) + which

    def look_up(part, side):
        group = group_of(part, side)

        @pl.loop(0, 8)
        def _(quad):
            hot_rows = []
            for which in range(4):
                ids = ids_all[group, pl.ds(4 * quad + which, 1), :].astype(jnp.float32) - base
                column = jnp.transpose(jnp.broadcast_to(ids, (128, 128)))
                hot_rows.append(
                    jnp.concatenate(
                        [
                            jnp.where(column == lane + 128.0 * tile, 1.0, 0.0).astype(jnp.bfloat16)
                            for tile in range(tiles)
                        ],
                        1,
                    )
                )
            found = jnp.dot(
                jnp.concatenate(hot_rows, 0), table_pad[...], preferred_element_type=jnp.float32
            ).astype(jnp.bfloat16)
            at_z = quad // 2
            for which in range(4):
                at_y = 2 * (quad % 2) + which // 2
                first, second = (at_z, at_y) if part == 0 else (at_y, at_z)
                parts[part, which % 2, first, 2 * second + side] = found[
                    128 * which : 128 * which + 128
                ]

    def to_sibling(part):
        return wires.send(parts.at[part, 1 - core], sibling_in.at[part], sibling)

    lookup_axes = ((Z, Y), (Y, Z))
    lookup_rings, lookup_ends = [], []
    for part in range(2):
        first_axis, second_axis = lookup_axes[part]
        lookup_rings.append(
            RingReduce(
                wires,
                place,
                first_axis,
                lambda j, part=part: parts.at[part, core, j],
                lambda j, h, part=part: parts.at[part, core, j, pl.ds(4 * h, 4)],
                8,
                half_in.at[part],
                whole_in.at[part],
            )
        )
        lookup_ends.append(
            DirectReduce(
                wires,
                place,
                second_axis,
                lambda j, part=part, k=place[first_axis]: parts.at[part, core, k, pl.ds(2 * j, 2)],
                2,
                landing.at[part],
            )
        )

    def add_sibling(part):
        siblings[part].wait_recv()
        for j in range(4):
            add_blocks(parts.at[part, core, j], [sibling_in.at[part, j]], 8)
        lookup_rings[part].start()

    def take_result(part):
        lookup_ends[part].arrive()
        first_axis, second_axis = lookup_axes[part]
        for which in range(2):
            total = parts[part, core, place[first_axis], 2 * place[second_axis] + which].astype(
                jnp.float32
            )
            for step in range(3):
                total += landing[part, step, which].astype(jnp.float32)
            ready[group_of(part, which)] = total.astype(jnp.bfloat16)

    shares = [wires.slot() for _ in range(3)]

    def share(part, ref):
        wires.send_all(ref, ref, sibling, shares[part])

    look_up(0, across % 2)
    ids_ring.finish()
    for copy in own_copies[:3]:
        copy.wait()
    for ring, later in zip(rings[0], rings[1]):
        ring.finish()
        later.start()
    for ring in rings[2]:
        ring.send(0)
    look_up(0, 1 - across % 2)
    siblings = [to_sibling(0)]
    for ring in rings[1]:
        ring.forward()
    for ring in rings[2]:
        ring.send(1)
    look_up(1, 0)
    add_sibling(0)
    for ring in rings[1]:
        ring.finish()
    for ring in rings[2]:
        ring.send(2)
    on_y.send(3)
    on_x.send(3)
    for index in (1, 2, 3):
        table_ring.send(index)
    look_up(1, 1)
    siblings.append(to_sibling(1))
    lookup_rings[0].forward()
    on_z.send(3)
    add_sibling(1)
    for part in range(3):
        share(part, full_ref.at[part, core, place[ORDERS[part][2]]])
    lookup_rings[1].forward()
    lookup_rings[0].finish()
    lookup_ends[0].start()
    share(0, on_z.forward(0))
    share(0, on_z.forward(2))
    share(1, on_x.forward(0))
    share(1, on_x.forward(2))
    lookup_rings[1].finish()
    lookup_ends[1].start()
    share(1, on_x.forward(1))
    share(1, on_x.forward(3))
    for index in (0, 2, 1, 3):
        share(2, on_y.forward(index))
    share(0, on_z.forward(1))
    share(0, on_z.forward(3))
    take_result(0)
    take_result(1)
    swaps = []
    for step in (1, 2, 3):
        there = moved(place, X, step)
        swaps.append(wires.send(ready.at[there[X]], arrived.at[across], there))
    arrived[across] = ready[across]
    for index in (0, 2, 1, 3):
        table_ring.forward(index)
    for part in range(3):
        for index in range(4):
            share(part, rings[2][part].take(index))
    for copy in swaps:
        copy.wait_recv()
    for source in range(4):
        columns = pl.ds(256 * source, 256)
        hidden_ref[:, columns] = (
            arrived[source].astype(jnp.float32) + positions_ref[:, columns]
        )
    for index in range(4):
        table_ring.take(index)
    wires.settle()
    for index in (0, 2, 1, 3):
        for part in range(3):
            share(part, rings[2][part].take_far(index))
    for index in range(4):
        table_ring.take_far(index)
    table_ring.settle(table_full_ref.at[across])
    for part in range(3):
        rings[2][part].settle(full_ref.at[part, core, 0])
        wires.whole(full_ref.at[part, core], sibling, shares[part]).wait()


def start_call(token_ids, matrices, vocab_table, positions_table):
    rows, width = vocab_table.shape
    padded = -(-rows // 128) * 128
    bf16 = jnp.bfloat16
    return pl.pallas_call(
        start_kernel,
        name="gather_and_look_up",
        out_shape=(
            jax.ShapeDtypeStruct((3, 2, SIDE, 32, BLOCK, BLOCK), bf16),
            jax.ShapeDtypeStruct((N_DP, rows, width), bf16),
            jax.ShapeDtypeStruct(positions_table.shape, jnp.float32),
        ),
        in_specs=[VMEM] * 4,
        out_specs=(ANY, ANY, VMEM),
        scratch_shapes=[
            pltpu.VMEM((3, 2, BLOCK, BLOCK), bf16),
            pltpu.VMEM((padded, width), bf16),
            pltpu.VMEM((N_DP,) + token_ids.shape, jnp.int32),
            pltpu.VMEM((2, 2, SIDE, 8, 128, width), bf16),
            pltpu.VMEM((2, SIDE, 8, 128, width), bf16),
            pltpu.VMEM((2, 2, 4, 128, width), bf16),
            pltpu.VMEM((2, 2, 8, 128, width), bf16),
            pltpu.VMEM((2, 3, 2, 128, width), bf16),
            pltpu.VMEM((N_DP, 128, width), bf16),
            pltpu.VMEM((N_DP, 128, width), bf16),
            pltpu.SemaphoreType.DMA((140,)),
            pltpu.SemaphoreType.DMA((140,)),
            pltpu.SemaphoreType.DMA((4,)),
        ],
        compiler_params=pltpu.CompilerParams(
            collective_id=1, has_side_effects=True, vmem_limit_bytes=VMEM_BYTES
        ),
    )(token_ids, matrices, vocab_table, positions_table)


def head_kernel(
    head_in_ref,
    table_ref,
    target_ref,
    at_ref,
    length_ref,
    d_head_ref,
    own_grad_ref,
    next_grad_ref,
    far_grad_ref,
    last_grad_ref,
    loss_ref,
    table,
    table_grads,
    pieces,
    rows_in,
    logits,
    d_logits,
    stats,
    d_rows,
    d_sibling,
    d_first,
    d_second,
    send_sems,
    recv_sems,
    local_sems,
):
    place = coordinates()
    table_load = pltpu.make_async_copy(table_ref, table, local_sems.at[4])
    table_load.start()
    core = place[CORE]
    sibling = moved(place, CORE, 1)
    wires = Wires(send_sems, recv_sems)
    own, width = head_in_ref.shape
    half_width = width // 2
    feature_axes = ((Y, Z), (Z, Y))
    for part in range(2):
        near, far = (place[axis] for axis in feature_axes[part])
        pieces[part, core, far, near] = head_in_ref[
            :, part * half_width : (part + 1) * half_width
        ]
    vocab_group = [
        moved(moved(moved(place, Y, near), Z, far), CORE, side)
        for near in range(SIDE)
        for far in range(SIDE)
        for side in range(2)
    ][1:]
    greet(vocab_group)
    first_rings, second_rings = [], []
    for part in range(2):
        near_axis, far_axis = feature_axes[part]
        first_rings.append(
            DirectGather(
                wires,
                place,
                near_axis,
                lambda j, part=part, k=place[far_axis]: pieces.at[part, core, k, j],
            )
        )
        second_rings.append(
            DirectGather(wires, place, far_axis, lambda j, part=part: pieces.at[part, core, j])
        )
    for ring in first_rings:
        ring.start()
    seqs = target_ref.shape[1]
    column = lax.broadcasted_iota(jnp.int32, (seqs, seqs * own), 1)
    row = lax.broadcasted_iota(jnp.int32, (seqs, seqs * own), 0)
    own_seq = jnp.where(column // own == row, 1.0, 0.0)
    slot = lax.broadcasted_iota(jnp.int32, (own, seqs * own), 0)
    slot_column = lax.broadcasted_iota(jnp.int32, (own, seqs * own), 1)
    own_slot = slot_column % own == slot

    def laid_end_to_end(values):
        wide = jnp.dot(
            values.astype(jnp.float32), own_seq, precision=HIGH, preferred_element_type=jnp.float32
        )
        return jnp.sum(jnp.where(own_slot, wide, 0.0), 0, keepdims=True)

    target = laid_end_to_end(target_ref[...]).astype(jnp.int32)
    lengths = jnp.dot(
        length_ref[...].astype(jnp.float32),
        own_seq,
        precision=HIGH,
        preferred_element_type=jnp.float32,
    )
    counted = (laid_end_to_end(at_ref[...]) < lengths).astype(jnp.float32)
    for ring, later in zip(first_rings, second_rings):
        ring.finish()
        later.start()
    crossing = []
    for part in range(2):
        second_rings[part].finish()
        mine = pieces.at[part, core]
        crossing.append(wires.send(mine, mine, sibling))
    for copy in crossing:
        copy.wait_recv()
    for index in range(32):
        at_z, at_y, at_core = index // 8, index // 2 % SIDE, index % 2
        rows_in[own * index : own * (index + 1), :half_width] = pieces[0, at_core, at_z, at_y]
        rows_in[own * index : own * (index + 1), half_width:] = pieces[1, at_core, at_y, at_z]

    table_load.wait()
    groups, rows, group_width = table.shape
    count = rows_in.shape[0]
    chunk = rows // 4
    base = lax.axis_index("vocab") * rows
    row_iota = lax.broadcasted_iota(jnp.int32, (chunk, count), 0)

    def logit_chunk(index, top):
        at = pl.ds(pl.multiple_of(index * chunk, chunk), chunk)
        total = jnp.zeros((chunk, count), jnp.float32)
        for group in range(groups):
            total += lax.dot_general(
                table[group, at],
                rows_in[:, group * group_width : (group + 1) * group_width],
                (((1,), (1,)), ((), ())),
                preferred_element_type=jnp.float32,
            )
        total = jnp.where(row_iota + (base + index * chunk) < VOCAB_REAL, total, NEG_FILL)
        logits[at] = total
        return jnp.maximum(top, jnp.max(total, 0, keepdims=True))

    local_top = lax.fori_loop(
        0, 4, logit_chunk, jnp.full((1, count), NEG_FILL, jnp.float32)
    )

    def exp_chunk(index, carry):
        total, pick = carry
        at = pl.ds(pl.multiple_of(index * chunk, chunk), chunk)
        values = logits[at]
        hits = row_iota + (base + index * chunk) == target
        pick += jnp.sum(jnp.where(hits, values, 0.0), 0, keepdims=True)
        values = jnp.exp(values - local_top)
        logits[at] = values
        return total + jnp.sum(values, 0, keepdims=True), pick

    zero_row = jnp.zeros((1, count), jnp.float32)
    local_total, pick = lax.fori_loop(0, 4, exp_chunk, (zero_row, zero_row))
    lanes = count // 4
    top = jnp.concatenate([local_top[:, lanes * i : lanes * (i + 1)] for i in range(4)], 0)
    total = jnp.concatenate([local_total[:, lanes * i : lanes * (i + 1)] for i in range(4)], 0)
    mine = stats.at[lax.axis_index("vocab")]
    mine[...] = jnp.concatenate([top, total], 0)
    bundle = wires.slot()
    for other in vocab_group:
        wires.send_all(mine, mine, other, bundle)
    wires.whole(stats.at[pl.ds(0, len(vocab_group))], sibling, bundle).wait()
    top = jnp.max(stats[:, :4], 0)
    total = jnp.sum(stats[:, 4:] * jnp.exp(stats[:, :4] - top[None]), 0)
    log_total = top + jnp.log(total)
    log_total = jnp.concatenate([log_total[i : i + 1] for i in range(4)], 1)
    first_device = (lax.axis_index("vocab") == 0).astype(jnp.float32)
    loss_ref[...] = (first_device * log_total - pick) * counted
    weight = counted / (N_DP * N_VOCAB * own)
    scale = jnp.exp(local_top - log_total) * weight

    @pl.loop(0, 4)
    def _(index):
        at = pl.ds(pl.multiple_of(index * chunk, chunk), chunk)
        hits = row_iota + (base + index * chunk) == target
        d_logits[at] = (logits[at] * scale - jnp.where(hits, weight, 0.0)).astype(jnp.bfloat16)

    for side in range(2):
        lowered = d_logits[:, 256 * side : 256 * (side + 1)]
        for group in range(groups):
            rows_grad = lax.dot_general(
                lowered,
                table[group],
                (((0,), (0,)), ((), ())),
                preferred_element_type=jnp.float32,
            ).astype(jnp.bfloat16)
            part, column = group // 2, group % 2 * group_width
            for index in range(16):
                inner = 16 * side + index
                at_z, at_y, at_core = inner // 8, inner // 2 % SIDE, inner % 2
                first, second = (at_z, at_y) if part == 0 else (at_y, at_z)
                d_rows[part, at_core, first, second, :, column : column + group_width] = (
                    rows_grad[own * index : own * (index + 1)]
                )
    crossing = [
        wires.send(d_rows.at[part, 1 - core], d_sibling.at[part], sibling) for part in range(2)
    ]
    reduce_axes = ((Z, Y), (Y, Z))
    first_rings, second_rings = [], []
    for part in range(2):
        first_axis, second_axis = reduce_axes[part]
        crossing[part].wait_recv()
        for j in range(4):
            add_blocks(d_rows.at[part, core, j], [d_sibling.at[part, j]], 4)
        first_rings.append(
            DirectReduce(
                wires,
                place,
                first_axis,
                lambda j, part=part: d_rows.at[part, core, j],
                4,
                d_first.at[part],
            )
        )
        second_rings.append(
            DirectReduce(
                wires,
                place,
                second_axis,
                lambda j, part=part, k=place[first_axis]: d_rows.at[part, core, k, j],
                1,
                d_second.at[part],
            )
        )
        first_rings[part].start()

    grad_refs = (own_grad_ref, next_grad_ref, far_grad_ref, last_grad_ref)
    stores = []

    def table_grad(step):
        group = (place[X] + step) % N_DP
        columns = lane_range(group * group_width, group_width)

        @pl.loop(0, 4)
        def _(index):
            at = pl.ds(pl.multiple_of(index * chunk, chunk), chunk)
            product = jnp.dot(
                d_logits[at], rows_in[:, columns], preferred_element_type=jnp.float32
            ).astype(jnp.bfloat16)
            table_grads[step, at] = product

        stores.append(
            pltpu.make_async_copy(table_grads.at[step], grad_refs[step], local_sems.at[step])
        )
        stores[-1].start()

    table_grad(1)
    table_grad(2)
    for ring, later in zip(first_rings, second_rings):
        ring.finish()
        later.start()
    table_grad(3)
    table_grad(0)
    for part in range(2):
        second_rings[part].arrive()
        first_axis, second_axis = reduce_axes[part]
        total = d_rows[part, core, place[first_axis], place[second_axis]].astype(jnp.float32)
        for step in range(3):
            total += d_second[part, step].astype(jnp.float32)
        d_head_ref[:, part * half_width : (part + 1) * half_width] = total
    wires.settle()
    for copy in stores:
        copy.wait()


def head_call(head_in, table_full, targets, positions, lengths):
    groups, rows, group_width = table_full.shape
    own, width = head_in.shape
    count = targets.size
    half = width // 2
    bf16 = jnp.bfloat16
    return pl.pallas_call(
        head_kernel,
        name="head",
        out_shape=(
            jax.ShapeDtypeStruct((own, width), jnp.float32),
            *[jax.ShapeDtypeStruct((rows, group_width), bf16)] * groups,
            jax.ShapeDtypeStruct((1, count), jnp.float32),
        ),
        in_specs=[VMEM, ANY, VMEM, VMEM, VMEM],
        out_specs=(VMEM,) + (ANY,) * groups + (VMEM,),
        scratch_shapes=[
            pltpu.VMEM(table_full.shape, bf16),
            pltpu.VMEM(table_full.shape, bf16),
            pltpu.VMEM((2, 2, SIDE, SIDE, own, half), bf16),
            pltpu.VMEM((count, width), bf16),
            pltpu.VMEM((rows, count), jnp.float32),
            pltpu.VMEM((rows, count), bf16),
            pltpu.VMEM((N_VOCAB, 8, count // 4), jnp.float32),
            pltpu.VMEM((2, 2, SIDE, SIDE, own, half), bf16),
            pltpu.VMEM((2, SIDE, SIDE, own, half), bf16),
            pltpu.VMEM((2, 3, SIDE, own, half), bf16),
            pltpu.VMEM((2, 3, own, half), bf16),
            pltpu.SemaphoreType.DMA((40,)),
            pltpu.SemaphoreType.DMA((40,)),
            pltpu.SemaphoreType.DMA((5,)),
        ],
        compiler_params=pltpu.CompilerParams(
            collective_id=2, has_side_effects=True, vmem_limit_bytes=VMEM_BYTES
        ),
    )(head_in, table_full, targets, positions, lengths)


def finish_kernel(
    grads_ref,
    small_ref,
    own_grad_ref,
    next_grad_ref,
    far_grad_ref,
    last_grad_ref,
    d_embed_ref,
    ids_ref,
    loss_ref,
    grads_out_ref,
    table_grad_ref,
    final_ref,
    totals_ref,
    sums,
    sibling_in,
    half_a,
    whole_a,
    half_b,
    whole_b,
    whole_c,
    small_sums,
    small_sibling,
    small_a,
    small_b,
    small_c,
    table_parts,
    embeds,
    ids_all,
    totals_all,
    send_sems,
    recv_sems,
    local_sems,
):
    place = coordinates()
    core = place[CORE]
    across = place[X]
    sibling = moved(place, CORE, 1)
    wires = Wires(send_sems, recv_sems)
    loads = []

    def load(source, target):
        copy = pltpu.make_async_copy(source, target, local_sems.at[len(loads)])
        copy.start()
        loads.append(copy)
        return copy

    third = [place[ORDERS[part][2]] for part in range(3)]
    small_load = load(small_ref.at[core], small_sums)
    block_loads = {}
    for step in (2, 1, 3, 0):
        for part in range(3):
            j = (third[part] + step) % SIDE
            block_loads[part, step] = load(grads_ref.at[part, core, j], sums.at[part, j])
    table_loads = [
        load(ref, table_parts.at[index])
        for index, ref in enumerate((own_grad_ref, next_grad_ref, far_grad_ref, last_grad_ref))
    ]

    width = table_grad_ref.shape[1]
    embed_axes = ((Y, Z), (Z, Y))
    source_part = across // 2
    near = place[Y] * (1 - source_part) + place[Z] * source_part
    far = place[Z] * (1 - source_part) + place[Y] * source_part
    landing = embeds.at[source_part, core, far, 2 * near + across % 2]
    own_columns = pl.ds(pl.multiple_of(across * width, width), width)
    landing[...] = d_embed_ref[:, own_columns]
    ids_all[across] = ids_ref[...]
    line = [
        moved(moved(place, X, step), CORE, side) for step in range(SIDE) for side in range(2)
    ][1:]
    plane = [
        moved(moved(place, Y, step), Z, other) for step in range(SIDE) for other in range(SIDE)
    ][1:]
    greet(line + plane)
    swaps = []
    for step in (1, 2, 3):
        there = moved(place, X, step)
        columns = pl.ds(pl.multiple_of(there[X] * width, width), width)
        swaps.append(wires.send(d_embed_ref.at[:, columns], landing, there))
    ids_ring = DirectGather(wires, place, X, lambda j: ids_all.at[j])
    ids_ring.start()
    small_crossing = wires.send(small_ref.at[1 - core], small_sibling, sibling)
    crossings = {}
    for step in (2, 1, 3, 0):
        for part in range(3):
            j = (third[part] + step) % SIDE
            crossings[part, step] = wires.send(
                grads_ref.at[part, 1 - core, j], sibling_in.at[part, j], sibling
            )

    embed_first, embed_second = [], []
    for part in range(2):
        near_axis, far_axis = embed_axes[part]
        embed_first.append(
            RingGather(
                wires,
                place,
                near_axis,
                lambda j, part=part, k=place[far_axis]: embeds.at[part, core, k, pl.ds(2 * j, 2)],
                lambda j, h, part=part, k=place[far_axis]: embeds.at[
                    part, core, k, pl.ds(2 * j + h, 1)
                ],
            )
        )
        embed_second.append(
            RingGather(
                wires,
                place,
                far_axis,
                lambda j, part=part: embeds.at[part, core, j],
                lambda j, h, part=part: embeds.at[part, core, j, pl.ds(4 * h, 4)],
            )
        )
    first_rings, middle_rings, last_rings = [], [], []
    for part in range(3):

        def at(k3, first, count, part=part):
            return sums.at[part, k3, pl.ds(first, count)]

        last_axis, middle_axis, first_axis = ORDERS[part]
        piece, half = block_ring(place, part, 2, at)
        first_rings.append(
            QuarterReduce(
                wires, place, first_axis, piece, half, 32, half_a.at[part], whole_a.at[part]
            )
        )
        piece, half = block_ring(place, part, 1, at)
        middle_rings.append(
            RingReduce(
                wires, place, middle_axis, piece, half, 8, half_b.at[part], whole_b.at[part]
            )
        )
        piece, _ = block_ring(place, part, 0, at)
        last_rings.append(DirectReduce(wires, place, last_axis, piece, 2, whole_c.at[part]))
    small_rings = [
        DirectReduce(wires, place, Z, lambda j: small_sums.at[j], 16, small_a),
        DirectReduce(
            wires, place, Y, lambda j: small_sums.at[place[Z], pl.ds(4 * j, 4)], 4, small_b
        ),
        DirectReduce(
            wires, place, X, lambda j: small_sums.at[place[Z], pl.ds(4 * place[Y] + j, 1)], 1, small_c
        ),
    ]

    def add_crossing(part, step):
        j = (third[part] + step) % SIDE
        block_loads[part, step].wait()
        crossings[part, step].wait_recv()
        add_blocks(sums.at[part, j], [sibling_in.at[part, j]], 32)

    embed_siblings = []

    def share(part, step):
        piece = embeds.at[part, core, (place[embed_axes[part][1]] + step) % SIDE]
        embed_siblings.append(wires.send(piece, piece, sibling))

    rows = table_grad_ref.shape[0]
    chunk = rows // 4
    base = lax.axis_index("vocab") * rows
    row_iota = lax.broadcasted_iota(jnp.int32, (chunk, 512), 0)

    def scatter_rows(part, at_core, step):
        at_far = (place[embed_axes[part][1]] + step) % SIDE

        @pl.loop(0, 2)
        def _(pair):
            values = embeds[part, at_core, at_far, pl.ds(4 * pair, 4)].reshape(512, width)
            ids = []
            for which in range(4):
                at_near = 2 * pair + which // 2
                at_z, at_y = (at_far, at_near) if part == 0 else (at_near, at_far)
                inner = (at_z * SIDE + at_y) * 2 + at_core
                ids.append(ids_all[2 * part + which % 2, pl.ds(inner, 1), :])
            ids = jnp.concatenate(ids, 1) - base

            @pl.loop(0, 4)
            def _(row):
                at = pl.ds(pl.multiple_of(row * chunk, chunk), chunk)
                hot = jnp.where(row_iota + row * chunk == ids, 1.0, 0.0).astype(jnp.bfloat16)
                table_grad_ref[at] += jnp.dot(hot, values, preferred_element_type=jnp.float32)

    lead = ((0, core), (1, core))
    orders = ((X, Y, Z), (Y, Z, X))
    gathers = []
    for phase in range(3):
        row = []
        for part in range(2):
            _, second_axis, third_axis = orders[part]
            keys = (place[third_axis], place[second_axis])[: 2 - phase]
            row.append(
                DirectGather(
                    wires,
                    place,
                    orders[part][phase],
                    lambda j, key=lead[part] + keys: final_ref.at[key + (j,)],
                )
            )
        gathers.append(row)

    small_load.wait()
    small_crossing.wait_recv()
    for j in range(4):
        add_blocks(small_sums.at[j], [small_sibling.at[j]], 16)
    for part in range(3):
        add_crossing(part, 2)
        first_rings[part].start(0)
    for copy in swaps:
        copy.wait_recv()
    for ring in embed_first:
        ring.start()
    small_rings[0].start()
    for part in range(3):
        add_crossing(part, 1)
    for ring in embed_first:
        ring.forward()
    for part in range(3):
        first_rings[part].start(1)
    for ring, later in zip(embed_first, embed_second):
        ring.finish()
        later.start()
    small_rings[0].finish()
    small_rings[1].start()
    share(0, 0)
    share(1, 0)
    for part in range(3):
        add_crossing(part, 3)
    ids_ring.finish()
    for copy in table_loads:
        copy.wait()

    @pl.loop(0, rows // 80)
    def _(index):
        at = pl.ds(pl.multiple_of(index * 80, 80), 80)
        total = table_parts[0, at].astype(jnp.float32)
        for step in range(1, N_DP):
            total += table_parts[step, at].astype(jnp.float32)
        table_grad_ref[at] = total

    scatter_rows(0, core, 0)
    scatter_rows(1, core, 0)
    for part in range(3):
        add_crossing(part, 0)
    for ring in first_rings:
        ring.forward()
    for copy in embed_siblings:
        copy.wait_recv()
    embed_siblings.clear()
    scatter_rows(0, 1 - core, 0)
    scatter_rows(1, 1 - core, 0)
    for part in range(2):
        embed_second[part].forward()
        share(part, 1)
        share(part, 3)
    small_rings[1].finish()
    small_rings[2].start()
    for part in range(2):
        scatter_rows(part, core, 1)
        scatter_rows(part, core, 3)
    for copy in embed_siblings:
        copy.wait_recv()
    embed_siblings.clear()
    for part in range(2):
        scatter_rows(part, 1 - core, 1)
        scatter_rows(part, 1 - core, 3)
    small_rings[2].finish()
    own_small = small_sums[place[Z], 4 * place[Y] + across].astype(jnp.float32)
    final_ref[0, core, place[Z], place[Y], across] = own_small[:8]
    final_ref[1, core, across, place[Z], place[Y]] = jnp.concatenate(
        [own_small[8:9], jnp.zeros((7, 128), jnp.float32)], 0
    )
    wires.settle(17)
    for ring, later in zip(first_rings, middle_rings):
        ring.finish()
        later.start()
    for gather in gathers[0]:
        gather.start()
    for part in range(2):
        embed_second[part].finish()
        share(part, 2)
    scatter_rows(0, core, 2)
    for ring in middle_rings:
        ring.forward()
    for gather, later in zip(gathers[0], gathers[1]):
        gather.finish()
        later.start()
    scatter_rows(1, core, 2)
    for copy in embed_siblings:
        copy.wait_recv()
    scatter_rows(0, 1 - core, 2)
    for ring, later in zip(middle_rings, last_rings):
        ring.finish()
        later.start()
    for gather, later in zip(gathers[1], gathers[2]):
        gather.finish()
        later.start()
    scatter_rows(1, 1 - core, 2)
    table_squares = jnp.zeros((1, width), jnp.float32)
    for index in range(4):
        values = table_grad_ref[index * chunk : (index + 1) * chunk]
        table_squares += jnp.sum(values * values, 0, keepdims=True)
    squares = table_squares[:, :128] + table_squares[:, 128:]
    for part in range(3):
        last_rings[part].arrive()
        k1, k2, k3 = (place[axis] for axis in ORDERS[part])
        for which in range(2):
            total = sums[part, k3, 8 * k2 + 2 * k1 + which].astype(jnp.float32)
            for step in range(3):
                total += whole_c[part, step, which].astype(jnp.float32)
            grads_out_ref[part, which] = total
            squares += jnp.sum(total * total, 0, keepdims=True)
    final_siblings = []
    for part in range(2):
        gathers[2][part].finish()
        mine = final_ref.at[part, core]
        final_siblings.append(wires.send(mine, mine, sibling))
    loss = sum(loss_ref[:, 128 * index : 128 * (index + 1)] for index in range(4))
    totals = jnp.concatenate([squares, loss, jnp.zeros((6, 128), jnp.float32)], 0)
    for phase, (own, others) in enumerate(
        ((2 * across + core, line), (SIDE * place[Z] + place[Y], plane))
    ):
        mine = totals_all.at[phase, own]
        mine[...] = totals
        bundle = wires.slot()
        for other in others:
            wires.send_all(mine, mine, other, bundle)
        wires.whole(totals_all.at[phase, pl.ds(0, len(others))], sibling, bundle).wait()
        totals = totals_all[phase, 0]
        for index in range(1, len(others) + 1):
            totals += totals_all[phase, index]
    totals_ref[...] = totals
    for copy in final_siblings:
        copy.wait_recv()
    wires.settle()


def finish_call(grads, small, head_grads, d_embed, token_ids, loss_row):
    bf16 = jnp.bfloat16
    rows, width = head_grads[0].shape
    block = (BLOCK, BLOCK)
    return pl.pallas_call(
        finish_kernel,
        name="reduce_and_scatter",
        out_shape=(
            jax.ShapeDtypeStruct((3, 2) + block, jnp.float32),
            jax.ShapeDtypeStruct((rows, width), jnp.float32),
            jax.ShapeDtypeStruct((2, 2, SIDE, SIDE, SIDE, 8, 128), jnp.float32),
            jax.ShapeDtypeStruct((8, 128), jnp.float32),
        ),
        in_specs=[ANY] * 6 + [VMEM] * 3,
        out_specs=(VMEM,) * 4,
        scratch_shapes=[
            pltpu.VMEM((3, SIDE, 32) + block, bf16),
            pltpu.VMEM((3, SIDE, 32) + block, bf16),
            pltpu.VMEM((3, 2, 16) + block, bf16),
            pltpu.VMEM((3, 2, 32) + block, bf16),
            pltpu.VMEM((3, 2, 4) + block, bf16),
            pltpu.VMEM((3, 2, 8) + block, bf16),
            pltpu.VMEM((3, 3, 2) + block, bf16),
            pltpu.VMEM((SIDE, 16, 16, 128), bf16),
            pltpu.VMEM((SIDE, 16, 16, 128), bf16),
            pltpu.VMEM((3, 16, 16, 128), bf16),
            pltpu.VMEM((3, 4, 16, 128), bf16),
            pltpu.VMEM((3, 1, 16, 128), bf16),
            pltpu.VMEM((N_DP, rows, width), bf16),
            pltpu.VMEM((2, 2, SIDE, 8, 128, width), bf16),
            pltpu.VMEM((N_DP,) + token_ids.shape, jnp.int32),
            pltpu.VMEM((2, SIDE * SIDE, 8, 128), jnp.float32),
            pltpu.SemaphoreType.DMA((160,)),
            pltpu.SemaphoreType.DMA((160,)),
            pltpu.SemaphoreType.DMA((17,)),
        ],
        compiler_params=pltpu.CompilerParams(
            collective_id=3, has_side_effects=True, vmem_limit_bytes=VMEM_BYTES
        ),
    )(grads, small, *head_grads, d_embed, token_ids, loss_row)


def row_mean(values):
    return jnp.mean(values, -1, keepdims=True)


def normalized(values):
    center = values - row_mean(values)
    scale = lax.rsqrt(row_mean(center * center) + LN_EPS)
    return center * scale, scale


def norm_backward(d_normed, hat, scale, gain):
    d_hat = d_normed * gain
    d_values = scale * (d_hat - row_mean(d_hat) - hat * row_mean(d_hat * hat))
    d_gain = jnp.sum(d_normed * hat, 0, keepdims=True)
    return d_values, d_gain, jnp.sum(d_normed, 0, keepdims=True)


QKV, PROJ, FC, OUT = (0, 24), (192, 8), (256, 32), (512, 8)


def load_blocks(full_ref, blocks, sems):
    share = blocks.shape[0] // 8
    copies = []
    for index in range(8):
        part = pl.ds(index * share, share)
        copies.append(pltpu.make_async_copy(full_ref.at[part], blocks.at[part], sems.at[index]))
        copies[-1].start()
    return copies


def weight_tiles(blocks, where_ref, matrix, row, rows, column, columns):
    first, in_row = matrix
    return jnp.concatenate(
        [
            jnp.concatenate(
                [
                    blocks[where_ref[first + (row + i) * in_row + column + j]]
                    for j in range(columns)
                ],
                1,
            )
            for i in range(rows)
        ],
        0,
    )


def selected_rows(ref, positions):
    return jnp.concatenate([ref[pl.ds(position, 1), :] for position in positions], 0)


def pair_masks(count):
    lane = lax.broadcasted_iota(jnp.int32, (2 * count, 2 * HEAD_DIM), 1)
    row = lax.broadcasted_iota(jnp.int32, (2 * count, 2 * HEAD_DIM), 0)
    return (lane < HEAD_DIM) == (row < count)


def doubled(values, own_lanes):
    both = jnp.concatenate([values, values], 0)
    return jnp.where(own_lanes, both.astype(jnp.float32), 0.0).astype(jnp.bfloat16)


def folded(values, count):
    lane = lax.broadcasted_iota(jnp.int32, (count, 2 * HEAD_DIM), 1)
    return jnp.where(lane < HEAD_DIM, values[:count], values[count:])


def forward_kernel(
    where_ref,
    at_ref,
    length_ref,
    full_ref,
    hidden_ref,
    vec_ref,
    head_in_ref,
    query_ref,
    kv_ref,
    probs_ref,
    attended_ref,
    middle_ref,
    pre_act_ref,
    last_ref,
    blocks,
    normed_rows,
    activated,
    sems,
):
    copies = load_blocks(full_ref, blocks, sems)
    count = head_in_ref.shape[0]
    bf16 = jnp.bfloat16
    own = lax.axis_index("vocab")
    positions = [at_ref[i, own] for i in range(count)]
    length = length_ref[own]
    hat, _ = normalized(hidden_ref[...])
    normed_rows[...] = hat * vec_ref[0:1] + vec_ref[1:2]
    normed_one = normed_rows[...].astype(bf16)
    normed_own = selected_rows(normed_rows, positions).astype(bf16)
    for copy in copies:
        copy.wait()

    @pl.loop(0, 4)
    def _(tile):
        at = lane_range(256 * tile, 256)
        weight = weight_tiles(blocks, where_ref, QKV, 0, 8, 2 * tile, 2)
        product = jnp.dot(normed_own, weight, preferred_element_type=jnp.float32)
        query_ref[:, at] = (product + vec_ref[2:3, at]).astype(bf16)

    @pl.loop(0, 4)
    def _(tile):
        at = lane_range(256 * tile, 256)
        weight = weight_tiles(blocks, where_ref, QKV, 0, 8, 8 + 2 * tile, 2)
        product = jnp.dot(normed_one, weight, preferred_element_type=jnp.float32)
        kv_ref[:, at] = product.astype(bf16)

    @pl.loop(0, 4)
    def _(tile):
        weight = weight_tiles(blocks, where_ref, QKV, 0, 8, 16 + 2 * tile, 2)
        product = jnp.dot(normed_one, weight, preferred_element_type=jnp.float32)
        bias = vec_ref[3:4, lane_range(256 * tile, 256)]
        kv_ref[:, lane_range(D + 256 * tile, 256)] = (product + bias).astype(bf16)

    own_lanes = pair_masks(count)
    pairs = HEADS // 2
    seq_len = hidden_ref.shape[0]
    row = lax.broadcasted_iota(jnp.int32, (count, seq_len), 0)
    key = lax.broadcasted_iota(jnp.int32, (count, seq_len), 1)
    last_key = jnp.zeros((count, seq_len), jnp.int32)
    for i in range(count):
        last_key = jnp.where(row == i, jnp.minimum(positions[i], length - 1), last_key)
    allowed = jnp.concatenate([key <= last_key] * 2, 0)
    for pair in range(pairs):
        lanes = slice(128 * pair, 128 * pair + 128)
        values_at = slice(D + 128 * pair, D + 128 * pair + 128)
        scores = dot_nt(doubled(query_ref[:, lanes], own_lanes), kv_ref[:, lanes]) * HEAD_DIM ** (
            -0.5
        )
        scores = jnp.where(allowed, scores, NEG_FILL)
        exps = jnp.exp(scores - jnp.max(scores, -1, keepdims=True))
        probs = exps / jnp.sum(exps, -1, keepdims=True)
        probs_ref[2 * count * pair : 2 * count * (pair + 1)] = probs
        mixed = jnp.dot(
            probs.astype(bf16), kv_ref[:, values_at], preferred_element_type=jnp.float32
        )
        attended_ref[:, lanes] = folded(mixed, count).astype(bf16)

    attended = attended_ref[...]
    middle_ref[...] = selected_rows(hidden_ref, positions) + vec_ref[4:5]

    @pl.loop(0, 4)
    def _(tile):
        weight = weight_tiles(blocks, where_ref, PROJ, 0, 8, 2 * tile, 2)
        middle_ref[:, lane_range(256 * tile, 256)] += jnp.dot(
            attended, weight, preferred_element_type=jnp.float32
        )

    middle = middle_ref[...]
    hat, _ = normalized(middle)
    normed_two = (hat * vec_ref[5:6] + vec_ref[6:7]).astype(bf16)

    @pl.loop(0, 16)
    def _(tile):
        at = lane_range(256 * tile, 256)
        weight = weight_tiles(blocks, where_ref, FC, 0, 8, 2 * tile, 2)
        bias = vec_ref[pl.ds(7 + tile // 4, 1), lane_range(256 * (tile % 4), 256)]
        pre_act = jnp.dot(normed_two, weight, preferred_element_type=jnp.float32) + bias
        pre_act_ref[:, at] = pre_act
        activated[:, at] = gelu(pre_act).astype(bf16)

    last_ref[...] = middle + vec_ref[11:12]

    @pl.loop(0, 16)
    def _(index):
        tile, depth = index // 4, index % 4
        weight = weight_tiles(blocks, where_ref, OUT, 8 * depth, 8, 2 * tile, 2)
        last_ref[:, lane_range(256 * tile, 256)] += jnp.dot(
            activated[:, lane_range(1024 * depth, 1024)],
            weight,
            preferred_element_type=jnp.float32,
        )

    hat, _ = normalized(last_ref[...])
    head_in_ref[...] = (hat * vec_ref[12:13] + vec_ref[13:14]).astype(bf16)


def forward_call(where, positions, lengths, full, hidden, vectors):
    count = positions.shape[0]
    seq_len = hidden.shape[0]
    bf16 = jnp.bfloat16
    shape = jax.ShapeDtypeStruct
    return pl.pallas_call(
        forward_kernel,
        name="layer_forward",
        out_shape=(
            shape((count, D), bf16),
            shape((count, D), bf16),
            shape((seq_len, 2 * D), bf16),
            shape((HEADS * count, seq_len), jnp.float32),
            shape((count, D), bf16),
            shape((count, D), jnp.float32),
            shape((count, FF), jnp.float32),
            shape((count, D), jnp.float32),
        ),
        grid_spec=pltpu.PrefetchScalarGridSpec(
            num_scalar_prefetch=3,
            grid=(),
            in_specs=[ANY, VMEM, VMEM],
            out_specs=(VMEM,) * 8,
            scratch_shapes=[
                pltpu.VMEM(full.shape, bf16),
                pltpu.VMEM(hidden.shape, jnp.float32),
                pltpu.VMEM((count, FF), bf16),
                pltpu.SemaphoreType.DMA((8,)),
            ],
        ),
        compiler_params=pltpu.CompilerParams(vmem_limit_bytes=VMEM_BYTES),
    )(where, positions, lengths, full, hidden, vectors)


def gelu_slope(values):
    cube = 0.044715 * values * values
    bent = jnp.tanh(GELU_C * (values + cube * values))
    return 0.5 * (1.0 + bent) + 0.5 * values * (1.0 - bent * bent) * GELU_C * (1.0 + 3.0 * cube)


def backward_kernel(
    where_ref,
    at_ref,
    full_ref,
    hidden_ref,
    vec_ref,
    query_ref,
    kv_ref,
    probs_ref,
    attended_ref,
    middle_ref,
    pre_act_ref,
    last_ref,
    d_head_ref,
    grads_ref,
    small_ref,
    d_embed_ref,
    blocks,
    grad_blocks,
    activated,
    d_pre,
    normed,
    rows_out,
    d_qkv,
    spread,
    query_grads,
    vec_grads,
    sems,
    grad_sem,
):
    copies = load_blocks(full_ref, blocks, sems)
    count = d_head_ref.shape[0]
    bf16 = jnp.bfloat16
    own = lax.axis_index("vocab")
    positions = [at_ref[i, own] for i in range(count)]

    def weight_grad(matrix, rows, left_ref, right, together=4):
        first, in_row = matrix

        @pl.loop(0, rows // together)
        def _(group):
            left = left_ref[:, lane_range(128 * together * group, 128 * together)]
            for column in range(0, in_row, 2):
                product = dot_tn(left, right[:, 128 * column : 128 * column + 256]).astype(bf16)
                for inner in range(2 * together):
                    row, side = inner // 2, inner % 2
                    index = first + (group * together + row) * in_row + column + side
                    grad_blocks[index] = product[
                        128 * row : 128 * row + 128, 128 * side : 128 * side + 128
                    ]
                    pltpu.make_async_copy(
                        grad_blocks.at[index], grads_ref.at[where_ref[index]], grad_sem
                    ).start()

    hat, scale = normalized(last_ref[...])
    d_last, vec_grads[12:13], vec_grads[13:14] = norm_backward(
        d_head_ref[...], hat, scale, vec_ref[12:13]
    )
    d_branch = d_last.astype(bf16)
    vec_grads[11:12] = jnp.sum(d_branch.astype(jnp.float32), 0, keepdims=True)
    activated[...] = gelu(pre_act_ref[...]).astype(bf16)
    weight_grad(OUT, 32, activated, d_branch)
    for copy in copies:
        copy.wait()

    @pl.loop(0, 16)
    def _(tile):
        at = lane_range(256 * tile, 256)
        weight = weight_tiles(blocks, where_ref, OUT, 2 * tile, 2, 0, 8)
        lowered = (dot_nt(d_branch, weight) * gelu_slope(pre_act_ref[:, at])).astype(bf16)
        d_pre[:, at] = lowered
        vec_grads[pl.ds(7 + tile // 4, 1), lane_range(256 * (tile % 4), 256)] = jnp.sum(
            lowered.astype(jnp.float32), 0, keepdims=True
        )

    hat, scale = normalized(middle_ref[...])
    normed[pl.ds(0, count)] = (hat * vec_ref[5:6] + vec_ref[6:7]).astype(bf16)
    weight_grad(FC, 8, normed.at[pl.ds(0, count)], d_pre[...])
    rows_out[...] = jnp.zeros(rows_out.shape, jnp.float32)

    @pl.loop(0, 16)
    def _(index):
        tile, depth = index // 4, index % 4
        weight = weight_tiles(blocks, where_ref, FC, 2 * tile, 2, 8 * depth, 8)
        rows_out[pl.ds(0, count), lane_range(256 * tile, 256)] += dot_nt(
            d_pre[:, lane_range(1024 * depth, 1024)], weight
        )

    d_middle, vec_grads[5:6], vec_grads[6:7] = norm_backward(
        rows_out[pl.ds(0, count)], hat, scale, vec_ref[5:6]
    )
    d_middle = d_middle + d_last
    d_proj = d_middle.astype(bf16)
    vec_grads[4:5] = jnp.sum(d_proj.astype(jnp.float32), 0, keepdims=True)
    weight_grad(PROJ, 8, attended_ref, d_proj)

    @pl.loop(0, 4)
    def _(tile):
        weight = weight_tiles(blocks, where_ref, PROJ, 2 * tile, 2, 0, 8)
        rows_out[pl.ds(0, count), lane_range(256 * tile, 256)] = dot_nt(d_proj, weight)

    own_lanes = pair_masks(count)
    spread[...] = jnp.zeros(spread.shape, jnp.float32)
    for pair in range(HEADS // 2):
        lanes = slice(128 * pair, 128 * pair + 128)
        values_at = slice(D + 128 * pair, D + 128 * pair + 128)
        d_mixed = doubled(rows_out[0:count, lanes].astype(bf16), own_lanes)
        probs = probs_ref[2 * count * pair : 2 * count * (pair + 1)]
        d_probs = dot_nt(d_mixed, kv_ref[:, values_at])
        inner = jnp.sum(probs * d_probs, -1, keepdims=True)
        d_scores = (probs * (d_probs - inner)).astype(bf16)
        d_values = dot_tn(probs.astype(bf16), d_mixed).astype(bf16)
        d_keys = dot_tn(d_scores, doubled(query_ref[:, lanes], own_lanes)) * HEAD_DIM ** (-0.5)
        d_query = jnp.dot(d_scores, kv_ref[:, lanes], preferred_element_type=jnp.float32)
        d_query = (folded(d_query, count) * HEAD_DIM ** (-0.5)).astype(bf16).astype(jnp.float32)
        vec_grads[2:3, lanes] = jnp.sum(d_query, 0, keepdims=True)
        vec_grads[3:4, lanes] = jnp.sum(d_values.astype(jnp.float32), 0, keepdims=True)
        query_grads[:, lanes] = d_query
        d_qkv[:, D + 128 * pair : D + 128 * pair + 128] = d_keys.astype(bf16)
        d_qkv[:, 2 * D + 128 * pair : 2 * D + 128 * pair + 128] = d_values
    for i in range(count):
        spread[pl.ds(positions[i], 1), :] = query_grads[i : i + 1, :]
    d_qkv[:, :D] = spread[...].astype(bf16)
    hat, scale = normalized(hidden_ref[...])
    normed[...] = (hat * vec_ref[0:1] + vec_ref[1:2]).astype(bf16)
    weight_grad(QKV, 8, normed, d_qkv)
    rows_out[...] = jnp.zeros(rows_out.shape, jnp.float32)

    @pl.loop(0, 12)
    def _(index):
        tile, depth = index // 3, index % 3
        weight = weight_tiles(blocks, where_ref, QKV, 2 * tile, 2, 8 * depth, 8)
        rows_out[:, lane_range(256 * tile, 256)] += dot_nt(
            d_qkv[:, lane_range(1024 * depth, 1024)], weight
        )

    d_hidden, vec_grads[0:1], vec_grads[1:2] = norm_backward(
        rows_out[...], hat, scale, vec_ref[0:1]
    )
    rows_out[...] = d_hidden
    for i in range(count):
        rows_out[pl.ds(positions[i], 1), :] += d_middle[i : i + 1]
    d_embed_ref[...] = rows_out[...].astype(bf16)
    vec_rows = vec_ref.shape[0]
    for index in range(small_ref.shape[0]):
        group, tile = index // 8, index % 8
        lanes = slice(128 * tile, 128 * tile + 128)
        vec_row = (
            vec_grads[group : group + 1, lanes]
            if group < vec_rows
            else jnp.zeros((1, 128), jnp.float32)
        )
        small_ref[index] = jnp.concatenate(
            [rows_out[8 * group : 8 * group + 8, lanes], vec_row, jnp.zeros((7, 128), jnp.float32)],
            0,
        ).astype(bf16)
    pltpu.make_async_copy(grad_blocks, grads_ref, grad_sem).wait()


def backward_call(where, positions, full, hidden, vectors, cache, d_head):
    count = positions.shape[0]
    bf16 = jnp.bfloat16
    shape = jax.ShapeDtypeStruct
    return pl.pallas_call(
        backward_kernel,
        name="layer_backward",
        out_shape=(
            shape(full.shape, bf16),
            shape((N_DP * N_VOCAB, 16, 128), bf16),
            shape(hidden.shape, bf16),
        ),
        grid_spec=pltpu.PrefetchScalarGridSpec(
            num_scalar_prefetch=2,
            grid=(),
            in_specs=[ANY] + [VMEM] * 10,
            out_specs=(ANY, VMEM, VMEM),
            scratch_shapes=[
                pltpu.VMEM(full.shape, bf16),
                pltpu.VMEM(full.shape, bf16),
                pltpu.VMEM((count, FF), bf16),
                pltpu.VMEM((count, FF), bf16),
                pltpu.VMEM(hidden.shape, bf16),
                pltpu.VMEM(hidden.shape, jnp.float32),
                pltpu.VMEM((hidden.shape[0], 3 * D), bf16),
                pltpu.VMEM(hidden.shape, jnp.float32),
                pltpu.VMEM((count, D), jnp.float32),
                pltpu.VMEM((16, D), jnp.float32),
                pltpu.SemaphoreType.DMA((8,)),
                pltpu.SemaphoreType.DMA,
            ],
        ),
        compiler_params=pltpu.CompilerParams(vmem_limit_bytes=VMEM_BYTES),
    )(where, positions, full, hidden, vectors, *cache, d_head)


def adam_step(weight, moment_one, moment_two, grad_in, rate, decay):
    new_one = BETA_ONE * moment_one + (1.0 - BETA_ONE) * grad_in
    new_two = BETA_TWO * moment_two + (1.0 - BETA_TWO) * grad_in * grad_in
    hat_one = new_one * (1.0 / (1.0 - BETA_ONE**STEP))
    hat_two = new_two * (1.0 / (1.0 - BETA_TWO**STEP))
    change = hat_one / (jnp.sqrt(hat_two) + ADAM_EPS)
    if decay:
        change = change + decay * weight
    return weight - rate * change, new_one, new_two


def high_dot(left, right, contract=((1,), (0,))):
    return lax.dot_general(
        left, right, (contract, ((), ())), precision=HIGH, preferred_element_type=jnp.float32
    )


def update_kernel(*refs):
    names = 18
    sources, targets = refs[:names], refs[names : names + 14]
    buffers = refs[names + 14 : names + 14 + names]
    results = refs[names + 14 + names : names + 28 + names]
    vec_grad, load_sems, store_sems = refs[names + 28 + names :]
    loads = [
        pltpu.make_async_copy(source, buffer, load_sems.at[index])
        for index, (source, buffer) in enumerate(zip(sources, buffers))
    ]
    for copy in loads:
        copy.start()
    stores = []

    def store(index, at=None):
        source, target = results[index], targets[index]
        if at is not None:
            source, target = source.at[at], target.at[at]
        copy = pltpu.make_async_copy(source, target, store_sems.at[len(stores)])
        copy.start()
        stores.append(copy)

    totals, final, grads, matrices, left_stats, right_stats, left_roots, right_roots = buffers[:8]
    table_grad, table, table_m, table_v = buffers[8:12]
    positions, pos_m, pos_v, vectors, vectors_m, vectors_v = buffers[12:]
    scalars, matrices_new, left_new, right_new, matrices_grad = results[:5]
    for copy in loads[:2]:
        copy.wait()
    row_squares = jnp.zeros((8, 128), jnp.float32)
    for part in range(2):
        for core in range(2):
            values = final[part, core].reshape(SIDE**3, 8, 128)
            row_squares += jnp.sum(values * values, 0)
    squares = jnp.sum(totals[0:1]) + jnp.sum(row_squares)
    loss = jnp.sum(totals[1:2])
    norm = jnp.sqrt(jnp.full((1, 128), squares, jnp.float32))
    clip = CLIP_LEVEL / jnp.maximum(norm, CLIP_LEVEL)
    scalars[...] = jnp.concatenate(
        [jnp.full((1, 128), loss, jnp.float32), norm, jnp.zeros((6, 128), jnp.float32)], 0
    )
    store(0)
    for copy in loads[2:8]:
        copy.wait()

    @pl.loop(0, SLOTS, unroll=3)
    def _(slot):
        grad = grads[slot // 2, slot % 2] * clip
        matrices_grad[slot] = grad
        left_new[slot] = STAT_DECAY * left_stats[slot] + (1.0 - STAT_DECAY) * high_dot(
            grad, grad, ((1,), (1,))
        )
        right_new[slot] = STAT_DECAY * right_stats[slot] + (1.0 - STAT_DECAY) * high_dot(
            grad, grad, ((0,), (0,))
        )
        stepped = high_dot(high_dot(left_roots[slot], grad), right_roots[slot])
        weight = matrices[slot]
        matrices_new[slot] = weight - SHAMPOO_RATE * (stepped + DECAY_RATE * weight)

    for index in range(1, 5):
        store(index)
    for copy in loads[8:12]:
        copy.wait()
    rows, width = table.shape
    wide_clip = jnp.concatenate([clip] * (width // 128), 1)
    chunk = rows // 4
    for index in range(4):

        @pl.loop(0, chunk // 80)
        def _(inner):
            at = pl.ds(pl.multiple_of(index * chunk + inner * 80, 80), 80)
            grad = table_grad[at] * wide_clip
            stepped = adam_step(
                table[at], table_m[at], table_v[at], grad, TABLE_RATE, DECAY_RATE
            )
            for order, value in enumerate(stepped):
                results[5 + order][at] = value

        for order in range(3):
            store(5 + order, pl.ds(index * chunk, chunk))
    for copy in loads[12:]:
        copy.wait()
    tiles = D // 128
    for index in range(N_DP * N_VOCAB):
        at_core, rest = index // 64, index % 64
        at_z, at_y, at_x = rest // 16, rest // 4 % 4, rest % 4
        group, lanes = index // tiles, slice(128 * (index % tiles), 128 * (index % tiles) + 128)
        at = slice(8 * group, 8 * group + 8)
        stepped = adam_step(
            positions[at, lanes],
            pos_m[at, lanes],
            pos_v[at, lanes],
            final[0, at_core, at_z, at_y, at_x] * clip,
            POS_RATE,
            DECAY_RATE,
        )
        for order, value in enumerate(stepped):
            results[8 + order][at, lanes] = value
        if group < vectors.shape[0]:
            vec_grad[group : group + 1, lanes] = (
                final[1, at_core, at_x, at_z, at_y, 0:1] * clip
            )
    for index in range(8, 11):
        store(index)
    stepped = adam_step(
        vectors[...], vectors_m[...], vectors_v[...], vec_grad[...], VECTOR_RATE, 0.0
    )
    for order, value in enumerate(stepped):
        results[11 + order][...] = value
        store(11 + order)
    for copy in stores:
        copy.wait()


def update_call(totals, final, grads, blocks, table_grad, table, positions, vectors):
    sources = [totals, final, grads, *blocks, table_grad, *table, *positions, *vectors]
    shape = lambda array: jax.ShapeDtypeStruct(array.shape, jnp.float32)
    targets = [shape(totals)] + [shape(blocks[0])] * 4
    targets += [shape(array) for array in (*table, *positions, *vectors)]
    return pl.pallas_call(
        update_kernel,
        name="optimizer_update",
        out_shape=tuple(targets),
        in_specs=[ANY] * len(sources),
        out_specs=(ANY,) * len(targets),
        scratch_shapes=[pltpu.VMEM(array.shape, jnp.float32) for array in sources]
        + [pltpu.VMEM(target.shape, jnp.float32) for target in targets]
        + [
            pltpu.VMEM(vectors[0].shape, jnp.float32),
            pltpu.SemaphoreType.DMA((len(sources),)),
            pltpu.SemaphoreType.DMA((len(targets) + 9,)),
        ],
        compiler_params=pltpu.CompilerParams(vmem_limit_bytes=VMEM_BYTES),
    )(*sources)


def slot_places():
    slot = np.arange(N_DP * N_VOCAB * SLOTS)
    device, own = slot // SLOTS, slot % SLOTS
    inner = device % N_VOCAB
    place = (device // N_VOCAB, inner // 2 % SIDE, inner // (2 * SIDE), inner % 2)
    part = own // 2
    result = np.zeros_like(slot)
    for which, (first, second, third) in enumerate(ORDERS):
        index = which * 2 + place[CORE]
        for axis in (third, second, first):
            index = index * SIDE + place[axis]
        result = np.where(part == which, index * 2 + own % 2, result)
    return result.astype(np.int32)


def per_device(
    token_ids,
    seq_lengths,
    loss_positions,
    target_ids,
    block_of_slot,
    matrices,
    left_stats,
    right_stats,
    left_roots,
    right_roots,
    vocab_table,
    table_m,
    table_v,
    positions_table,
    pos_m,
    pos_v,
    vectors,
    vectors_m,
    vectors_v,
):
    slots = block_of_slot.shape[0]
    block_iota = jnp.arange(slots, dtype=jnp.int32)
    where = jnp.sum(
        jnp.where(block_of_slot[None, :] == block_iota[:, None], slot_places()[None, :], 0),
        1,
        dtype=jnp.int32,
    )
    full, table_full, hidden = start_call(token_ids, matrices, vocab_table, positions_table)
    full_blocks = full.reshape(slots, BLOCK, BLOCK)
    positions = loss_positions.T
    head_in, *cache = forward_call(
        where, positions, seq_lengths, full_blocks, hidden, vectors
    )
    d_head_in, *head_grads, loss_row = head_call(
        head_in, table_full, target_ids.T, positions, seq_lengths.reshape(1, -1)
    )
    for step in range(1, N_DP):
        head_grads[step] = lax.ppermute(
            head_grads[step], "dp", [(i, (i + step) % N_DP) for i in range(N_DP)]
        )
    grad_blocks, small, d_embed = backward_call(
        where, positions, full_blocks, hidden, vectors, cache, d_head_in
    )
    owned_grads, table_grad_own, final, totals = finish_call(
        grad_blocks.reshape(full.shape[:3] + (32, BLOCK, BLOCK)),
        small.reshape(2, SIDE, 16, 16, 128),
        head_grads,
        d_embed,
        token_ids,
        loss_row,
    )
    scalars, *updated = update_call(
        totals,
        final,
        owned_grads,
        (matrices, left_stats, right_stats, left_roots, right_roots),
        table_grad_own,
        (vocab_table, table_m, table_v),
        (positions_table, pos_m, pos_v),
        (vectors, vectors_m, vectors_v),
    )
    return (scalars[0, 0], scalars[1, 0], *updated)


def solution(mesh):
    in_specs = (
        P("dp", None),
        P("dp"),
        P("dp", None),
        P("dp", None),
        P(),
        P(("dp", "vocab"), None, None),
        P(("dp", "vocab"), None, None),
        P(("dp", "vocab"), None, None),
        P(("dp", "vocab"), None, None),
        P(("dp", "vocab"), None, None),
        P("vocab", "dp"),
        P("vocab", "dp"),
        P("vocab", "dp"),
        P(),
        P(),
        P(),
        P(),
        P(),
        P(),
    )
    out_specs = (
        P(),
        P(),
        P(("dp", "vocab"), None, None),
        P(("dp", "vocab"), None, None),
        P(("dp", "vocab"), None, None),
        P(("dp", "vocab"), None, None),
        P("vocab", "dp"),
        P("vocab", "dp"),
        P("vocab", "dp"),
        P(),
        P(),
        P(),
        P(),
        P(),
        P(),
    )
    return jax.shard_map(
        per_device, mesh=mesh, in_specs=in_specs, out_specs=out_specs, check_vma=False
    )
```

```python
import jax
import jax.numpy as jnp
import numpy as np
from jax import lax
from jax.experimental import pallas as pl
from jax.experimental.pallas import tpu as pltpu
from jax.sharding import PartitionSpec as P

D = 1024
HEADS = 16
HEAD_DIM = 64
FF = 4096
VOCAB_REAL = 50257
LAYERS = 1
BLOCK = 128
STEP = 10


LN_EPS = 1e-05
CLIP_LEVEL = 0.05
BETA_ONE = 0.9
BETA_TWO = 0.999
ADAM_EPS = 1e-08
STAT_DECAY = 0.95
SHAMPOO_RATE = 0.03
TABLE_RATE = 0.15
POS_RATE = 0.05
VECTOR_RATE = 0.25
DECAY_RATE = 0.1
NEG_FILL = -1e30
GELU_C = 0.7978845608028654
HIGH = lax.Precision.HIGHEST


def gelu(values):
    return 0.5 * values * (1.0 + jnp.tanh(GELU_C * (values + 0.044715 * values * values * values)))


def dot_nt(left, right):
    return lax.dot_general(
        left, right, (((1,), (1,)), ((), ())), preferred_element_type=jnp.float32
    )


def dot_tn(left, right):
    return lax.dot_general(
        left, right, (((0,), (0,)), ((), ())), preferred_element_type=jnp.float32
    )


VMEM_BYTES = 63 << 20
TABLE_CHUNKS = 20
MESH_IDS = pl.DeviceIdType.MESH
ANY = pl.BlockSpec(memory_space=pl.ANY)
VMEM = pl.BlockSpec(memory_space=pltpu.VMEM)
N_DP = 4
N_VOCAB = 32
SIDE = 4
X, Y, Z, CORE = range(4)
ORDERS = ((X, Y, Z), (Y, Z, X), (Z, X, Y))
SLOTS = 6


def coordinates():
    across = lax.axis_index("dp")
    inner = lax.axis_index("vocab")
    return (across, (inner // 2) % SIDE, inner // (2 * SIDE), inner % 2)


def moved(place, axis, step):
    shifted = list(place)
    shifted[axis] = (place[axis] + step) % (2 if axis == CORE else SIDE)
    return tuple(shifted)


def device_of(place):
    return (place[X], (place[Z] * SIDE + place[Y]) * 2 + place[CORE])


def rings_of(place, axes):
    others = [moved(place, CORE, 1)]
    return others + [moved(place, axis, step) for axis in axes for step in (1, 2, 3)]


def greet(others):
    for other in others:
        pl.semaphore_signal(
            pltpu.get_barrier_semaphore(),
            inc=1,
            device_id=device_of(other),
            device_id_type=MESH_IDS,
        )


def await_greetings(others):
    pl.semaphore_wait(pltpu.get_barrier_semaphore(), len(others))


class Wires:
    def __init__(self, send_sems, recv_sems):
        self.send_sems, self.recv_sems, self.used = send_sems, recv_sems, 0
        self.sent = []

    def slot(self):
        self.used += 1
        return self.used - 1

    def copy(self, source, target, place, send_slot, recv_slot):
        return pltpu.make_async_remote_copy(
            src_ref=source,
            dst_ref=target,
            send_sem=self.send_sems.at[send_slot],
            recv_sem=self.recv_sems.at[recv_slot],
            device_id=device_of(place),
            device_id_type=MESH_IDS,
        )

    def send(self, source, target, place, bundle=None):
        recv_slot = self.slot()
        copy = self.copy(source, target, place, recv_slot if bundle is None else bundle, recv_slot)
        copy.start()
        if bundle is None:
            self.sent.append(copy)
        return copy

    def send_all(self, source, target, place, bundle):
        self.copy(source, target, place, bundle, bundle).start()

    def whole(self, ref, place, bundle):
        return self.copy(ref, ref, place, bundle, bundle)

    def settle(self, latest=0):
        done = len(self.sent) - latest
        for copy in self.sent[:done]:
            copy.wait_send()
        self.sent = self.sent[done:]


def lane_range(first, count):
    return pl.ds(pl.multiple_of(first, 128), count)


def add_blocks(target, sources, count):
    @pl.loop(0, count)
    def _(i):
        at = i if len(target.shape) == 3 else lane_range(128 * i, 128)
        total = target[at].astype(jnp.float32)
        for source in sources:
            total += source[at].astype(jnp.float32)
        target[at] = total.astype(target.dtype)


class RingGather:
    def __init__(self, wires, place, axis, piece, half, own=None):
        self.wires, self.place, self.axis = wires, place, axis
        self.piece, self.half = piece, half
        self.mine = place[axis]
        self.own = self.piece(self.mine) if own is None else own

    def start(self):
        mine = self.piece(self.mine)
        self.up = self.wires.send(self.own, mine, moved(self.place, self.axis, 1))
        self.down = self.wires.send(self.own, mine, moved(self.place, self.axis, -1))

    def forward(self):
        self.up.wait_recv()
        lower = self.half((self.mine + 3) % SIDE, 0)
        self.far_up = self.wires.send(lower, lower, moved(self.place, self.axis, 1))
        self.down.wait_recv()
        upper = self.half((self.mine + 1) % SIDE, 1)
        self.far_down = self.wires.send(upper, upper, moved(self.place, self.axis, -1))

    def finish(self):
        self.far_up.wait_recv()
        self.far_down.wait_recv()


class DirectGather:
    def __init__(self, wires, place, axis, piece, own=None):
        self.wires, self.place, self.axis, self.piece = wires, place, axis, piece
        self.own = self.piece(place[axis]) if own is None else own

    def start(self):
        mine = self.piece(self.place[self.axis])
        self.copies = [
            self.wires.send(self.own, mine, moved(self.place, self.axis, step))
            for step in (1, 2, 3)
        ]

    def finish(self):
        for copy in self.copies:
            copy.wait_recv()


class RingReduce:
    def __init__(self, wires, place, axis, piece, half, count, half_in, whole_in):
        self.wires, self.place, self.axis = wires, place, axis
        self.piece, self.half, self.count = piece, half, count
        self.half_in, self.whole_in = half_in, whole_in
        self.mine = place[axis]

    def start(self):
        far = (self.mine + 2) % SIDE
        up, down = moved(self.place, self.axis, 1), moved(self.place, self.axis, -1)
        self.far_up = self.wires.send(self.half(far, 0), self.half_in.at[0], up)
        self.far_down = self.wires.send(self.half(far, 1), self.half_in.at[1], down)

    def forward(self):
        after, before = (self.mine + 1) % SIDE, (self.mine + 3) % SIDE
        up, down = moved(self.place, self.axis, 1), moved(self.place, self.axis, -1)
        self.far_up.wait_recv()
        add_blocks(self.half(after, 0), [self.half_in.at[0]], self.count // 2)
        self.up = self.wires.send(self.piece(after), self.whole_in.at[0], up)
        self.far_down.wait_recv()
        add_blocks(self.half(before, 1), [self.half_in.at[1]], self.count // 2)
        self.down = self.wires.send(self.piece(before), self.whole_in.at[1], down)

    def arrive(self):
        self.up.wait_recv()
        self.down.wait_recv()

    def finish(self):
        self.arrive()
        add_blocks(
            self.piece(self.mine), [self.whole_in.at[0], self.whole_in.at[1]], self.count
        )


class DirectReduce:
    def __init__(self, wires, place, axis, piece, count, landing):
        self.wires, self.place, self.axis = wires, place, axis
        self.piece, self.count, self.landing = piece, count, landing

    def start(self):
        mine = self.place[self.axis]
        self.copies = [
            self.wires.send(
                self.piece((mine + step) % SIDE),
                self.landing.at[step - 1],
                moved(self.place, self.axis, step),
            )
            for step in (1, 2, 3)
        ]

    def arrive(self):
        for copy in self.copies:
            copy.wait_recv()

    def finish(self):
        self.arrive()
        add_blocks(
            self.piece(self.place[self.axis]),
            [self.landing.at[step] for step in range(3)],
            self.count,
        )


class RowGather:
    def __init__(self, wires, place, axis, first, row):
        self.wires, self.place, self.axis = wires, place, axis
        self.row, self.mine, self.first = row, place[axis], first
        self.up, self.down, self.far = [], [], {}
        self.bundles = [wires.slot() for _ in range(3)]

    def of(self, piece, index):
        return self.row((self.mine + piece) % SIDE, (self.first + (0, 1, 3, 2)[index]) % SIDE)

    def send(self, index):
        mine = self.of(0, index)
        up, down = moved(self.place, self.axis, 1), moved(self.place, self.axis, -1)
        self.up.append(self.wires.send(mine, mine, up, self.bundles[0]))
        self.down.append(self.wires.send(mine, mine, down, self.bundles[1]))

    def forward(self, index):
        upward = index < 2
        (self.up if upward else self.down)[index].wait_recv()
        passed = self.of(3 if upward else 1, index)
        step = 1 if upward else -1
        target = moved(self.place, self.axis, step)
        self.far[index] = self.wires.send(passed, passed, target, self.bundles[2])
        return passed

    def take(self, index):
        (self.down if index < 2 else self.up)[index].wait_recv()
        return self.of(1 if index < 2 else 3, index)

    def take_far(self, index):
        self.far[index].wait_recv()
        return self.of(2, index)

    def settle(self, piece):
        for bundle in self.bundles:
            self.wires.whole(piece, self.place, bundle).wait_send()


class QuarterReduce(RingReduce):
    def start(self, chunk):
        far = (self.mine + 2) % SIDE
        up, down = moved(self.place, self.axis, 1), moved(self.place, self.axis, -1)
        size = self.count // 4
        landing = pl.ds(chunk * size, size)
        if chunk == 0:
            self.far_ups, self.far_downs, self.wholes = [], [], []
        self.far_ups.append(
            self.wires.send(self.half(far, 2 * chunk), self.half_in.at[0, landing], up)
        )
        self.far_downs.append(
            self.wires.send(self.half(far, 2 * chunk + 1), self.half_in.at[1, landing], down)
        )

    def send_quarter(self, piece, quarter, side):
        size = self.count // 4
        landing = self.whole_in.at[side, pl.ds(quarter * size, size)]
        there = moved(self.place, self.axis, 1 if side == 0 else -1)
        self.wholes.append(self.wires.send(self.half(piece, quarter), landing, there))

    def start_near(self):
        after, before = (self.mine + 1) % SIDE, (self.mine + 3) % SIDE
        for quarter in (0, 2):
            self.send_quarter(after, quarter + 1, 0)
            self.send_quarter(before, quarter, 1)

    def forward(self):
        after, before = (self.mine + 1) % SIDE, (self.mine + 3) % SIDE
        size = self.count // 4
        for chunk in range(2):
            landed = pl.ds(chunk * size, size)
            self.far_ups[chunk].wait_recv()
            add_blocks(self.half(after, 2 * chunk), [self.half_in.at[0, landed]], size)
            self.send_quarter(after, 2 * chunk, 0)
            self.far_downs[chunk].wait_recv()
            add_blocks(self.half(before, 2 * chunk + 1), [self.half_in.at[1, landed]], size)
            self.send_quarter(before, 2 * chunk + 1, 1)

    def arrive(self):
        for copy in self.wholes:
            copy.wait_recv()


def block_ring(place, part, phase, at):
    first_axis, second_axis, third_axis = ORDERS[part]
    k1, k2, k3 = place[first_axis], place[second_axis], place[third_axis]
    if phase == 0:
        return (
            lambda j: at(k3, 8 * k2 + 2 * j, 2),
            lambda j, h: at(k3, 8 * k2 + 2 * j + h, 1),
        )
    if phase == 1:
        return (lambda j: at(k3, 8 * j, 8), lambda j, h: at(k3, 8 * j + 4 * h, 4))
    return (lambda j: at(j, 0, 32), lambda j, q: at(j, 8 * q, 8))


def gather_phase(
    place,
    wires,
    others,
    ids_ref,
    matrices_ref,
    table_ref,
    positions_ref,
    blocks,
    table,
    hidden_ref,
    own_low,
    table_pad,
    ids_all,
    parts,
    sibling_in,
    half_in,
    whole_in,
    landing,
    ready,
    arrived,
    local_sems,
):
    core = place[CORE]
    across = place[X]
    sibling = moved(place, CORE, 1)

    def blocks_at(part, side, k3, first, count):
        start = ((2 * part + side) * SIDE + k3) * 32 + first
        return blocks.at[pl.ds(start, count)]

    own_low[...] = matrices_ref[...].astype(jnp.bfloat16).reshape(own_low.shape)
    for part in range(3):
        k1, k2, k3 = (place[axis] for axis in ORDERS[part])
        first = ((2 * part + core) * SIDE + k3) * 32 + 8 * k2 + 2 * k1
        for which in range(2):
            blocks[first + which] = own_low[part, which]
    ids_all[across] = ids_ref[...]
    table[across] = table_ref[...].astype(jnp.bfloat16)
    rings = [[], [], []]
    for part in range(3):

        def at(k3, first, count, part=part):
            return blocks_at(part, core, k3, first, count)

        first_axis, second_axis, third_axis = ORDERS[part]
        piece, _ = block_ring(place, part, 0, at)
        rings[0].append(DirectGather(wires, place, first_axis, piece, own_low.at[part]))
        piece, half = block_ring(place, part, 1, at)
        rings[1].append(RingGather(wires, place, second_axis, piece, half))
        rings[2].append(
            RowGather(
                wires,
                place,
                third_axis,
                place[second_axis],
                lambda j, row, at=at: at(j, 8 * row, 8),
            )
        )
    on_z, on_x, on_y = rings[2]
    ids_ring = DirectGather(wires, place, X, lambda j: ids_all.at[j])
    rows = table_ref.shape[0]
    table_pad[pl.ds(0, rows)] = table_ref[...].astype(jnp.bfloat16)
    padding = table_pad.shape[0] - rows
    table_pad[pl.ds(rows, padding)] = jnp.zeros((padding, table_pad.shape[1]), jnp.bfloat16)
    table_ring = RowGather(
        wires,
        place,
        X,
        0,
        lambda j, row: table.at[j, pl.ds(rows // SIDE * row, rows // SIDE)],
    )
    base = (lax.axis_index("vocab") * rows).astype(jnp.float32)
    tiles = table_pad.shape[0] // 128
    lane = lax.broadcasted_iota(jnp.int32, (128, 128), 1).astype(jnp.float32)

    def group_of(part, which):
        return 2 * ((across // 2 + part) % 2) + which

    def look_up(part, side, half):
        group = group_of(part, side)

        @pl.loop(4 * half, 4 * half + 4)
        def _(quad):
            hot_rows = []
            for which in range(4):
                ids = ids_all[group, pl.ds(4 * quad + which, 1), :].astype(jnp.float32) - base
                column = jnp.transpose(jnp.broadcast_to(ids, (128, 128)))
                hot_rows.append(
                    jnp.concatenate(
                        [
                            jnp.where(column == lane + 128.0 * tile, 1.0, 0.0).astype(jnp.bfloat16)
                            for tile in range(tiles)
                        ],
                        1,
                    )
                )
            found = jnp.dot(
                jnp.concatenate(hot_rows, 0), table_pad[...], preferred_element_type=jnp.float32
            ).astype(jnp.bfloat16)
            at_z = quad // 2
            for which in range(4):
                at_y = 2 * (quad % 2) + which // 2
                first, second = (at_z, at_y) if part == 0 else (at_y, at_z)
                at = lookup_rows(part, which % 2, first, 2 * second + side, 1)
                parts[at] = found[128 * which : 128 * which + 128]

    def lookup_rows(part, side, first, index, count):
        start = ((2 * part + side) * SIDE + first) * 8 + index
        return lane_range(128 * start, 128 * count)

    def to_sibling(part):
        crossing = parts.at[lookup_rows(part, 1 - core, 0, 0, 32)]
        return wires.send(crossing, sibling_in.at[part], sibling)

    lookup_axes = ((Z, Y), (Y, Z))
    lookup_rings, lookup_ends = [], []
    for part in range(2):
        first_axis, second_axis = lookup_axes[part]
        lookup_rings.append(
            RingReduce(
                wires,
                place,
                first_axis,
                lambda j, part=part: parts.at[lookup_rows(part, core, j, 0, 8)],
                lambda j, h, part=part: parts.at[lookup_rows(part, core, j, 4 * h, 4)],
                8,
                half_in.at[part],
                whole_in.at[part],
            )
        )
        lookup_ends.append(
            DirectReduce(
                wires,
                place,
                second_axis,
                lambda j, part=part, k=place[first_axis]: parts.at[
                    lookup_rows(part, core, k, 2 * j, 2)
                ],
                2,
                landing.at[part],
            )
        )

    def add_sibling(part):
        siblings[part].wait_recv()
        add_blocks(parts.at[lookup_rows(part, core, 0, 0, 32)], [sibling_in.at[part]], 32)
        lookup_rings[part].start()

    def take_result(part):
        lookup_ends[part].arrive()
        first_axis, second_axis = lookup_axes[part]
        for which in range(2):
            at = lookup_rows(part, core, place[first_axis], 2 * place[second_axis] + which, 1)
            total = parts[at].astype(jnp.float32)
            for step in range(3):
                total += landing[part, step, 128 * which : 128 * which + 128].astype(jnp.float32)
            ready[group_of(part, which)] = total.astype(jnp.bfloat16)

    shares = [wires.slot() for _ in range(3)]

    def share(part, ref):
        wires.send_all(ref, ref, sibling, shares[part])

    own_side = across % 2
    await_greetings(others)
    ids_ring.start()
    for ring in rings[0]:
        ring.start()
    table_ring.send(0)
    look_up(0, own_side, 0)
    look_up(0, own_side, 1)
    for ring, later in zip(rings[0], rings[1]):
        ring.finish()
        later.start()
    for ring in rings[2]:
        ring.send(0)
    ids_ring.finish()
    look_up(0, 1 - own_side, 0)
    look_up(0, 1 - own_side, 1)
    siblings = [to_sibling(0)]
    look_up(1, 0, 0)
    for ring in rings[1]:
        ring.forward()
    look_up(1, 0, 1)
    add_sibling(0)
    for ring in (on_y, on_x, on_z):
        ring.send(1)
    look_up(1, 1, 0)
    look_up(1, 1, 1)
    siblings.append(to_sibling(1))
    for ring in rings[1]:
        ring.finish()
    on_y.send(2)
    on_x.send(2)
    lookup_rings[0].forward()
    add_sibling(1)
    on_z.send(2)
    on_x.send(3)
    table_ring.send(1)
    for part in range(3):
        share(part, blocks_at(part, core, place[ORDERS[part][2]], 0, 32))
    lookup_rings[1].forward()
    share(1, on_x.forward(0))
    share(1, on_x.forward(2))
    lookup_rings[0].finish()
    lookup_ends[0].start()
    on_z.send(3)
    on_y.send(3)
    share(1, on_x.forward(1))
    share(1, on_x.forward(3))
    table_ring.send(2)
    table_ring.send(3)
    lookup_rings[1].finish()
    lookup_ends[1].start()
    for ring_part, ring in ((0, on_z), (2, on_y)):
        for index in (0, 2):
            share(ring_part, ring.forward(index))
    take_result(0)
    for ring_part, ring in ((0, on_z), (2, on_y)):
        for index in (1, 3):
            share(ring_part, ring.forward(index))
    take_result(1)
    swaps = []
    for step in (1, 2, 3):
        there = moved(place, X, step)
        swaps.append(wires.send(ready.at[there[X]], arrived.at[across], there))
    arrived[across] = ready[across]
    for part in range(3):
        for index in range(4):
            share(part, rings[2][part].take(index))
    for copy in swaps:
        copy.wait_recv()
    for source in range(4):
        columns = pl.ds(256 * source, 256)
        hidden_ref[:, columns] = (
            arrived[source].astype(jnp.float32) + positions_ref[:, columns]
        )
    table_ring.forward(0)
    table_ring.forward(2)
    for index in (0, 2, 1, 3):
        for part in range(3):
            share(part, rings[2][part].take_far(index))
    for index in (1, 3):
        table_ring.forward(index)
    for part in range(3):
        rings[2][part].settle(blocks.at[pl.ds(0, 32)])
        wires.whole(blocks.at[pl.ds(0, 128)], sibling, shares[part]).wait()
    return table_ring


def head_phase(
    place,
    wires,
    vocab_group,
    table_ring,
    head_in_ref,
    table,
    target_ref,
    at_ref,
    length_ref,
    d_head_ref,
    table_grad_ref,
    loss_ref,
    table_grads,
    pieces,
    rows_in,
    logits,
    d_logits,
    stats,
    d_rows,
    d_sibling,
    d_first,
    d_second,
    local_sems,
):
    core = place[CORE]
    sibling = moved(place, CORE, 1)
    own, width = head_in_ref.shape
    half_width = width // 2
    feature_axes = ((Y, Z), (Z, Y))
    for part in range(2):
        near, far = (place[axis] for axis in feature_axes[part])
        pieces[part, core, far, near] = head_in_ref[
            :, part * half_width : (part + 1) * half_width
        ]
    first_rings, second_rings = [], []
    for part in range(2):
        near_axis, far_axis = feature_axes[part]
        first_rings.append(
            DirectGather(
                wires,
                place,
                near_axis,
                lambda j, part=part, k=place[far_axis]: pieces.at[part, core, k, j],
            )
        )
        second_rings.append(
            DirectGather(wires, place, far_axis, lambda j, part=part: pieces.at[part, core, j])
        )
    for ring in first_rings:
        ring.start()
    seqs = target_ref.shape[1]
    column = lax.broadcasted_iota(jnp.int32, (seqs, seqs * own), 1)
    row = lax.broadcasted_iota(jnp.int32, (seqs, seqs * own), 0)
    own_seq = jnp.where(column // own == row, 1.0, 0.0)
    slot = lax.broadcasted_iota(jnp.int32, (own, seqs * own), 0)
    slot_column = lax.broadcasted_iota(jnp.int32, (own, seqs * own), 1)
    own_slot = slot_column % own == slot

    def laid_end_to_end(values):
        wide = jnp.dot(
            values.astype(jnp.float32), own_seq, precision=HIGH, preferred_element_type=jnp.float32
        )
        return jnp.sum(jnp.where(own_slot, wide, 0.0), 0, keepdims=True)

    target = laid_end_to_end(target_ref[...]).astype(jnp.int32)
    lengths = jnp.dot(
        length_ref[...].astype(jnp.float32),
        own_seq,
        precision=HIGH,
        preferred_element_type=jnp.float32,
    )
    counted = (laid_end_to_end(at_ref[...]) < lengths).astype(jnp.float32)
    wires.settle(12)
    for ring, later in zip(first_rings, second_rings):
        ring.finish()
        later.start()
    crossing = []
    for part in range(2):
        second_rings[part].finish()
        mine = pieces.at[part, core]
        crossing.append(wires.send(mine, mine, sibling))
    for copy in crossing:
        copy.wait_recv()
    for index in range(32):
        at_z, at_y, at_core = index // 8, index // 2 % SIDE, index % 2
        rows_in[own * index : own * (index + 1), :half_width] = pieces[0, at_core, at_z, at_y]
        rows_in[own * index : own * (index + 1), half_width:] = pieces[1, at_core, at_y, at_z]

    for index in range(4):
        table_ring.take(index)
        table_ring.take_far(index)
    table_ring.settle(table.at[0])
    groups, rows, group_width = table.shape
    count = rows_in.shape[0]
    chunk = rows // 4
    base = lax.axis_index("vocab") * rows
    row_iota = lax.broadcasted_iota(jnp.int32, (chunk, count), 0)

    def logit_chunk(index, top):
        at = pl.ds(pl.multiple_of(index * chunk, chunk), chunk)
        total = jnp.zeros((chunk, count), jnp.float32)
        for group in range(groups):
            total += lax.dot_general(
                table[group, at],
                rows_in[:, group * group_width : (group + 1) * group_width],
                (((1,), (1,)), ((), ())),
                preferred_element_type=jnp.float32,
            )
        total = jnp.where(row_iota + (base + index * chunk) < VOCAB_REAL, total, NEG_FILL)
        logits[at] = total
        return jnp.maximum(top, jnp.max(total, 0, keepdims=True))

    local_top = lax.fori_loop(
        0, 4, logit_chunk, jnp.full((1, count), NEG_FILL, jnp.float32)
    )

    def exp_chunk(index, carry):
        total, pick = carry
        at = pl.ds(pl.multiple_of(index * chunk, chunk), chunk)
        values = logits[at]
        hits = row_iota + (base + index * chunk) == target
        pick += jnp.sum(jnp.where(hits, values, 0.0), 0, keepdims=True)
        values = jnp.exp(values - local_top)
        logits[at] = values
        return total + jnp.sum(values, 0, keepdims=True), pick

    zero_row = jnp.zeros((1, count), jnp.float32)
    local_total, pick = lax.fori_loop(0, 4, exp_chunk, (zero_row, zero_row))
    lanes = count // 4
    top = jnp.concatenate([local_top[:, lanes * i : lanes * (i + 1)] for i in range(4)], 0)
    total = jnp.concatenate([local_total[:, lanes * i : lanes * (i + 1)] for i in range(4)], 0)
    mine = stats.at[lax.axis_index("vocab")]
    mine[...] = jnp.concatenate([top, total], 0)
    bundle = wires.slot()
    for other in vocab_group:
        wires.send_all(mine, mine, other, bundle)
    wires.whole(stats.at[pl.ds(0, len(vocab_group))], sibling, bundle).wait()
    top = jnp.max(stats[:, :4], 0)
    total = jnp.sum(stats[:, 4:] * jnp.exp(stats[:, :4] - top[None]), 0)
    log_total = top + jnp.log(total)
    log_total = jnp.concatenate([log_total[i : i + 1] for i in range(4)], 1)
    first_device = (lax.axis_index("vocab") == 0).astype(jnp.float32)
    loss_ref[...] = (first_device * log_total - pick) * counted
    weight = counted / (N_DP * N_VOCAB * own)
    scale = jnp.exp(local_top - log_total) * weight

    @pl.loop(0, 4)
    def _(index):
        at = pl.ds(pl.multiple_of(index * chunk, chunk), chunk)
        hits = row_iota + (base + index * chunk) == target
        d_logits[at] = (logits[at] * scale - jnp.where(hits, weight, 0.0)).astype(jnp.bfloat16)

    for side in range(2):
        lowered = d_logits[:, 256 * side : 256 * (side + 1)]
        for group in range(groups):
            rows_grad = lax.dot_general(
                lowered,
                table[group],
                (((0,), (0,)), ((), ())),
                preferred_element_type=jnp.float32,
            ).astype(jnp.bfloat16)
            part, column = group // 2, group % 2 * group_width
            for index in range(16):
                inner = 16 * side + index
                at_z, at_y, at_core = inner // 8, inner // 2 % SIDE, inner % 2
                first, second = (at_z, at_y) if part == 0 else (at_y, at_z)
                d_rows[part, at_core, first, second, :, column : column + group_width] = (
                    rows_grad[own * index : own * (index + 1)]
                )
    crossing = [
        wires.send(d_rows.at[part, 1 - core], d_sibling.at[part], sibling) for part in range(2)
    ]
    reduce_axes = ((Z, Y), (Y, Z))
    first_rings, second_rings = [], []
    for part in range(2):
        first_axis, second_axis = reduce_axes[part]
        crossing[part].wait_recv()
        for j in range(4):
            add_blocks(d_rows.at[part, core, j], [d_sibling.at[part, j]], 4)
        first_rings.append(
            DirectReduce(
                wires,
                place,
                first_axis,
                lambda j, part=part: d_rows.at[part, core, j],
                4,
                d_first.at[part],
            )
        )
        second_rings.append(
            DirectReduce(
                wires,
                place,
                second_axis,
                lambda j, part=part, k=place[first_axis]: d_rows.at[part, core, k, j],
                1,
                d_second.at[part],
            )
        )
        first_rings[part].start()

    stores = []

    def table_grad(group):
        @pl.loop(0, 4)
        def _(index):
            at = pl.ds(pl.multiple_of(index * chunk, chunk), chunk)
            product = jnp.dot(
                d_logits[at],
                rows_in[:, group * group_width : (group + 1) * group_width],
                preferred_element_type=jnp.float32,
            ).astype(jnp.bfloat16)
            table_grads[pl.ds(pl.multiple_of(group * rows + index * chunk, chunk), chunk)] = product

        at = pl.ds(group * rows, rows)
        stores.append(
            pltpu.make_async_copy(table_grads.at[at], table_grad_ref.at[at], local_sems.at[group])
        )
        stores[-1].start()

    table_grad(0)
    table_grad(1)
    for ring, later in zip(first_rings, second_rings):
        ring.finish()
        later.start()
    table_grad(2)
    table_grad(3)
    wires.settle(6)
    for part in range(2):
        second_rings[part].arrive()
        first_axis, second_axis = reduce_axes[part]
        total = d_rows[part, core, place[first_axis], place[second_axis]].astype(jnp.float32)
        for step in range(3):
            total += d_second[part, step].astype(jnp.float32)
        d_head_ref[:, part * half_width : (part + 1) * half_width] = total
    return stores


def finish_kernel(
    grads_ref,
    small_ref,
    head_grad_ref,
    d_embed_ref,
    ids_ref,
    loss_ref,
    grads_out_ref,
    table_grad_ref,
    final_ref,
    totals_ref,
    sums,
    sibling_in,
    half_a,
    whole_a,
    half_b,
    whole_b,
    whole_c,
    small_sums,
    small_sibling,
    small_a,
    small_b,
    small_c,
    table_sums,
    table_half,
    table_whole,
    embeds,
    ids_all,
    totals_all,
    send_sems,
    recv_sems,
    local_sems,
):
    place = coordinates()
    core = place[CORE]
    across = place[X]
    sibling = moved(place, CORE, 1)
    wires = Wires(send_sems, recv_sems)
    loads = []

    def load(source, target):
        copy = pltpu.make_async_copy(source, target, local_sems.at[len(loads)])
        copy.start()
        loads.append(copy)
        return copy

    third = [place[ORDERS[part][2]] for part in range(3)]
    small_load = load(small_ref.at[core], small_sums)
    block_loads = {}
    for step in (2, 1, 3, 0):
        for part in range(3):
            j = (third[part] + step) % SIDE
            block_loads[part, step] = load(grads_ref.at[part, core, j], sums.at[part, j])
    table_load = load(head_grad_ref, table_sums)

    width = table_grad_ref.shape[1]
    embed_axes = ((Y, Z), (Z, Y))
    source_part = across // 2
    near = place[Y] * (1 - source_part) + place[Z] * source_part
    far = place[Z] * (1 - source_part) + place[Y] * source_part
    landing = embeds.at[source_part, core, far, 2 * near + across % 2]
    own_columns = pl.ds(pl.multiple_of(across * width, width), width)
    landing[...] = d_embed_ref[:, own_columns]
    ids_all[across] = ids_ref[...]
    line = [
        moved(moved(place, X, step), CORE, side) for step in range(SIDE) for side in range(2)
    ][1:]
    plane = [
        moved(moved(place, Y, step), Z, other) for step in range(SIDE) for other in range(SIDE)
    ][1:]
    greet(line + plane)
    await_greetings(line + plane)
    swaps = []
    for step in (1, 2, 3):
        there = moved(place, X, step)
        columns = pl.ds(pl.multiple_of(there[X] * width, width), width)
        swaps.append(wires.send(d_embed_ref.at[:, columns], landing, there))
    ids_ring = DirectGather(wires, place, X, lambda j: ids_all.at[j])
    ids_ring.start()
    small_crossing = wires.send(small_ref.at[1 - core], small_sibling, sibling)
    crossings = {}
    for step, half in ((2, 0), (2, 1), (1, None), (3, None), (0, None)):
        for part in range(3):
            j = (third[part] + step) % SIDE
            source, target = grads_ref.at[part, 1 - core, j], sibling_in.at[part, j]
            if half is not None:
                source, target = source.at[pl.ds(16 * half, 16)], target.at[pl.ds(16 * half, 16)]
            crossings[part, step, half] = wires.send(source, target, sibling)

    embed_first, embed_second = [], []
    for part in range(2):
        near_axis, far_axis = embed_axes[part]
        embed_first.append(
            RingGather(
                wires,
                place,
                near_axis,
                lambda j, part=part, k=place[far_axis]: embeds.at[part, core, k, pl.ds(2 * j, 2)],
                lambda j, h, part=part, k=place[far_axis]: embeds.at[
                    part, core, k, pl.ds(2 * j + h, 1)
                ],
            )
        )
        embed_second.append(
            RingGather(
                wires,
                place,
                far_axis,
                lambda j, part=part: embeds.at[part, core, j],
                lambda j, h, part=part: embeds.at[part, core, j, pl.ds(4 * h, 4)],
            )
        )
    first_rings, middle_rings, last_rings = [], [], []
    for part in range(3):

        def at(k3, first, count, part=part):
            return sums.at[part, k3, pl.ds(first, count)]

        last_axis, middle_axis, first_axis = ORDERS[part]
        piece, half = block_ring(place, part, 2, at)
        first_rings.append(
            QuarterReduce(
                wires, place, first_axis, piece, half, 32, half_a.at[part], whole_a.at[part]
            )
        )
        piece, half = block_ring(place, part, 1, at)
        middle_rings.append(
            RingReduce(
                wires, place, middle_axis, piece, half, 8, half_b.at[part], whole_b.at[part]
            )
        )
        piece, _ = block_ring(place, part, 0, at)
        last_rings.append(DirectReduce(wires, place, last_axis, piece, 2, whole_c.at[part]))
    table_ring = QuarterReduce(
        wires,
        place,
        X,
        lambda j: table_sums.at[j],
        lambda j, q: table_sums.at[j, pl.ds(TABLE_CHUNKS // 4 * q, TABLE_CHUNKS // 4)],
        TABLE_CHUNKS,
        table_half,
        table_whole,
    )
    small_rings = [
        DirectReduce(wires, place, Z, lambda j: small_sums.at[j], 16, small_a),
        DirectReduce(
            wires, place, Y, lambda j: small_sums.at[place[Z], pl.ds(4 * j, 4)], 4, small_b
        ),
        DirectReduce(
            wires, place, X, lambda j: small_sums.at[place[Z], pl.ds(4 * place[Y] + j, 1)], 1, small_c
        ),
    ]

    def add_crossing(part, step, half=None):
        j = (third[part] + step) % SIDE
        if not half:
            block_loads[part, step].wait()
        crossings[part, step, half].wait_recv()
        at = pl.ds(0, 32) if half is None else pl.ds(16 * half, 16)
        add_blocks(
            sums.at[part, j, at], [sibling_in.at[part, j, at]], 32 if half is None else 16
        )

    embed_siblings = []

    def share(part, step):
        piece = embeds.at[part, core, (place[embed_axes[part][1]] + step) % SIDE]
        embed_siblings.append(wires.send(piece, piece, sibling))

    rows = table_grad_ref.shape[0]
    chunk = rows // 4
    base = lax.axis_index("vocab") * rows
    row_iota = lax.broadcasted_iota(jnp.int32, (chunk, 512), 0)

    def scatter_rows(part, at_core, step):
        at_far = (place[embed_axes[part][1]] + step) % SIDE

        @pl.loop(0, 2)
        def _(pair):
            values = embeds[part, at_core, at_far, pl.ds(4 * pair, 4)].reshape(512, width)
            ids = []
            for which in range(4):
                at_near = 2 * pair + which // 2
                at_z, at_y = (at_far, at_near) if part == 0 else (at_near, at_far)
                inner = (at_z * SIDE + at_y) * 2 + at_core
                ids.append(ids_all[2 * part + which % 2, pl.ds(inner, 1), :])
            ids = jnp.concatenate(ids, 1) - base

            @pl.loop(0, 4)
            def _(row):
                at = pl.ds(pl.multiple_of(row * chunk, chunk), chunk)
                hot = jnp.where(row_iota + row * chunk == ids, 1.0, 0.0).astype(jnp.bfloat16)
                table_grad_ref[at] += jnp.dot(hot, values, preferred_element_type=jnp.float32)

    lead = ((0, core), (1, core))
    orders = ((X, Y, Z), (Y, Z, X))
    gathers = []
    for phase in range(3):
        row = []
        for part in range(2):
            _, second_axis, third_axis = orders[part]
            keys = (place[third_axis], place[second_axis])[: 2 - phase]
            row.append(
                DirectGather(
                    wires,
                    place,
                    orders[part][phase],
                    lambda j, key=lead[part] + keys: final_ref.at[key + (j,)],
                )
            )
        gathers.append(row)

    for part in range(3):
        add_crossing(part, 2, 0)
        first_rings[part].start(0)
    for copy in swaps:
        copy.wait_recv()
    for ring in embed_first:
        ring.start()
    table_load.wait()
    table_ring.start(0)
    table_ring.start(1)
    small_load.wait()
    small_crossing.wait_recv()
    for j in range(4):
        add_blocks(small_sums.at[j], [small_sibling.at[j]], 16)
    small_rings[0].start()
    for part in range(3):
        add_crossing(part, 2, 1)
    for ring in embed_first:
        ring.forward()
    for part in range(3):
        first_rings[part].start(1)
    for part in range(3):
        add_crossing(part, 1)
    for ring, later in zip(embed_first, embed_second):
        ring.finish()
        later.start()
    small_rings[0].finish()
    small_rings[1].start()
    share(0, 0)
    share(1, 0)
    for part in range(3):
        add_crossing(part, 3)
    for part in range(3):
        first_rings[part].start_near()
    table_ring.start_near()
    ids_ring.finish()

    @pl.loop(0, 4)
    def _(index):
        at = pl.ds(pl.multiple_of(index * chunk, chunk), chunk)
        table_grad_ref[at] = jnp.zeros((chunk, width), jnp.float32)

    scatter_rows(0, core, 0)
    scatter_rows(1, core, 0)
    for ring in first_rings:
        ring.forward()
    for part in range(3):
        add_crossing(part, 0)
    for copy in embed_siblings:
        copy.wait_recv()
    embed_siblings.clear()
    scatter_rows(0, 1 - core, 0)
    scatter_rows(1, 1 - core, 0)
    for part in range(2):
        embed_second[part].forward()
        share(part, 1)
        share(part, 3)
    small_rings[1].finish()
    small_rings[2].start()
    table_ring.forward()
    for part in range(2):
        scatter_rows(part, core, 1)
        scatter_rows(part, core, 3)
    for copy in embed_siblings:
        copy.wait_recv()
    embed_siblings.clear()
    for part in range(2):
        scatter_rows(part, 1 - core, 1)
        scatter_rows(part, 1 - core, 3)
    wires.settle(32)
    for ring, later in zip(first_rings, middle_rings):
        ring.finish()
        later.start()
    small_rings[2].finish()
    own_small = small_sums[place[Z], 4 * place[Y] + across].astype(jnp.float32)
    final_ref[0, core, place[Z], place[Y], across] = own_small[:8]
    final_ref[1, core, across, place[Z], place[Y]] = jnp.concatenate(
        [own_small[8:9], jnp.zeros((7, 128), jnp.float32)], 0
    )
    for gather in gathers[0]:
        gather.start()
    for part in range(2):
        embed_second[part].finish()
        share(part, 2)
    scatter_rows(0, core, 2)
    for ring in middle_rings:
        ring.forward()
    for gather, later in zip(gathers[0], gathers[1]):
        gather.finish()
        later.start()
    scatter_rows(1, core, 2)
    for copy in embed_siblings:
        copy.wait_recv()
    scatter_rows(0, 1 - core, 2)
    for ring, later in zip(middle_rings, last_rings):
        ring.finish()
        later.start()
    for gather, later in zip(gathers[1], gathers[2]):
        gather.finish()
        later.start()
    scatter_rows(1, 1 - core, 2)
    table_ring.arrive()
    table_block = rows // TABLE_CHUNKS

    @pl.loop(0, TABLE_CHUNKS)
    def _(index):
        at = pl.ds(pl.multiple_of(index * table_block, table_block), table_block)
        table_grad_ref[at] += (
            table_sums[across, index].astype(jnp.float32)
            + table_whole[0, index].astype(jnp.float32)
            + table_whole[1, index].astype(jnp.float32)
        )

    table_squares = jnp.zeros((1, width), jnp.float32)
    for index in range(4):
        values = table_grad_ref[index * chunk : (index + 1) * chunk]
        table_squares += jnp.sum(values * values, 0, keepdims=True)
    squares = table_squares[:, :128] + table_squares[:, 128:]
    for part in range(3):
        last_rings[part].arrive()
        k1, k2, k3 = (place[axis] for axis in ORDERS[part])
        for which in range(2):
            total = sums[part, k3, 8 * k2 + 2 * k1 + which].astype(jnp.float32)
            for step in range(3):
                total += whole_c[part, step, which].astype(jnp.float32)
            grads_out_ref[part, which] = total
            squares += jnp.sum(total * total, 0, keepdims=True)
    final_siblings = []
    for part in range(2):
        gathers[2][part].finish()
        mine = final_ref.at[part, core]
        final_siblings.append(wires.send(mine, mine, sibling))
    loss = sum(loss_ref[:, 128 * index : 128 * (index + 1)] for index in range(4))
    totals = jnp.concatenate([squares, loss, jnp.zeros((6, 128), jnp.float32)], 0)
    for phase, (own, others) in enumerate(
        ((2 * across + core, line), (SIDE * place[Z] + place[Y], plane))
    ):
        mine = totals_all.at[phase, own]
        mine[...] = totals
        bundle = wires.slot()
        for other in others:
            wires.send_all(mine, mine, other, bundle)
        wires.whole(totals_all.at[phase, pl.ds(0, len(others))], sibling, bundle).wait()
        totals = totals_all[phase, 0]
        for index in range(1, len(others) + 1):
            totals += totals_all[phase, index]
    totals_ref[...] = totals
    for copy in final_siblings:
        copy.wait_recv()
    wires.settle()


def finish_call(grads, small, head_grad, d_embed, token_ids, loss_row):
    bf16 = jnp.bfloat16
    _, chunks, chunk_rows, width = head_grad.shape
    rows = chunks * chunk_rows
    block = (BLOCK, BLOCK)
    return pl.pallas_call(
        finish_kernel,
        name="reduce_and_scatter",
        out_shape=(
            jax.ShapeDtypeStruct((3, 2) + block, jnp.float32),
            jax.ShapeDtypeStruct((rows, width), jnp.float32),
            jax.ShapeDtypeStruct((2, 2, SIDE, SIDE, SIDE, 8, 128), jnp.float32),
            jax.ShapeDtypeStruct((8, 128), jnp.float32),
        ),
        in_specs=[ANY] * 3 + [VMEM] * 3,
        out_specs=(VMEM,) * 4,
        scratch_shapes=[
            pltpu.VMEM((3, SIDE, 32) + block, bf16),
            pltpu.VMEM((3, SIDE, 32) + block, bf16),
            pltpu.VMEM((3, 2, 16) + block, bf16),
            pltpu.VMEM((3, 2, 32) + block, bf16),
            pltpu.VMEM((3, 2, 4) + block, bf16),
            pltpu.VMEM((3, 2, 8) + block, bf16),
            pltpu.VMEM((3, 3, 2) + block, bf16),
            pltpu.VMEM((SIDE, 16, 16, 128), bf16),
            pltpu.VMEM((SIDE, 16, 16, 128), bf16),
            pltpu.VMEM((3, 16, 16, 128), bf16),
            pltpu.VMEM((3, 4, 16, 128), bf16),
            pltpu.VMEM((3, 1, 16, 128), bf16),
            pltpu.VMEM(head_grad.shape, bf16),
            pltpu.VMEM((2, chunks // 2, chunk_rows, width), bf16),
            pltpu.VMEM((2, chunks, chunk_rows, width), bf16),
            pltpu.VMEM((2, 2, SIDE, 8, 128, width), bf16),
            pltpu.VMEM((N_DP,) + token_ids.shape, jnp.int32),
            pltpu.VMEM((2, SIDE * SIDE, 8, 128), jnp.float32),
            pltpu.SemaphoreType.DMA((160,)),
            pltpu.SemaphoreType.DMA((160,)),
            pltpu.SemaphoreType.DMA((17,)),
        ],
        compiler_params=pltpu.CompilerParams(
            collective_id=3, has_side_effects=True, vmem_limit_bytes=VMEM_BYTES
        ),
    )(grads, small, head_grad, d_embed, token_ids, loss_row)


def row_mean(values):
    return jnp.mean(values, -1, keepdims=True)


def normalized(values):
    center = values - row_mean(values)
    scale = lax.rsqrt(row_mean(center * center) + LN_EPS)
    return center * scale, scale


def norm_backward(d_normed, hat, scale, gain):
    d_hat = d_normed * gain
    d_values = scale * (d_hat - row_mean(d_hat) - hat * row_mean(d_hat * hat))
    d_gain = jnp.sum(d_normed * hat, 0, keepdims=True)
    return d_values, d_gain, jnp.sum(d_normed, 0, keepdims=True)


QKV, PROJ, FC, OUT = (0, 24), (192, 8), (256, 32), (512, 8)


def load_blocks(full_ref, blocks, sems):
    share = blocks.shape[0] // 8
    copies = []
    for index in range(8):
        part = pl.ds(index * share, share)
        copies.append(pltpu.make_async_copy(full_ref.at[part], blocks.at[part], sems.at[index]))
        copies[-1].start()
    return copies


def weight_tiles(blocks, where_ref, matrix, row, rows, column, columns):
    first, in_row = matrix
    return jnp.concatenate(
        [
            jnp.concatenate(
                [
                    blocks[where_ref[first + (row + i) * in_row + column + j]]
                    for j in range(columns)
                ],
                1,
            )
            for i in range(rows)
        ],
        0,
    )


def selected_rows(ref, positions):
    return jnp.concatenate([ref[pl.ds(position, 1), :] for position in positions], 0)


def pair_masks(count):
    lane = lax.broadcasted_iota(jnp.int32, (2 * count, 2 * HEAD_DIM), 1)
    row = lax.broadcasted_iota(jnp.int32, (2 * count, 2 * HEAD_DIM), 0)
    return (lane < HEAD_DIM) == (row < count)


def doubled(values, own_lanes):
    both = jnp.concatenate([values, values], 0)
    return jnp.where(own_lanes, both.astype(jnp.float32), 0.0).astype(jnp.bfloat16)


def folded(values, count):
    lane = lax.broadcasted_iota(jnp.int32, (count, 2 * HEAD_DIM), 1)
    return jnp.where(lane < HEAD_DIM, values[:count], values[count:])


def forward_phase(
    where_ref,
    at_ref,
    length_ref,
    hidden_ref,
    vec_ref,
    head_in_ref,
    query_ref,
    kv_ref,
    probs_ref,
    attended_ref,
    middle_ref,
    pre_act_ref,
    last_ref,
    blocks,
    normed_rows,
    activated,
):
    count = head_in_ref.shape[0]
    bf16 = jnp.bfloat16
    own = lax.axis_index("vocab")
    positions = [at_ref[i, own] for i in range(count)]
    length = length_ref[own]
    hat, _ = normalized(hidden_ref[...])
    normed_rows[...] = hat * vec_ref[0:1] + vec_ref[1:2]
    normed_one = normed_rows[...].astype(bf16)
    normed_own = selected_rows(normed_rows, positions).astype(bf16)

    @pl.loop(0, 4)
    def _(tile):
        at = lane_range(256 * tile, 256)
        weight = weight_tiles(blocks, where_ref, QKV, 0, 8, 2 * tile, 2)
        product = jnp.dot(normed_own, weight, preferred_element_type=jnp.float32)
        query_ref[:, at] = (product + vec_ref[2:3, at]).astype(bf16)

    @pl.loop(0, 4)
    def _(tile):
        at = lane_range(256 * tile, 256)
        weight = weight_tiles(blocks, where_ref, QKV, 0, 8, 8 + 2 * tile, 2)
        product = jnp.dot(normed_one, weight, preferred_element_type=jnp.float32)
        kv_ref[:, at] = product.astype(bf16)

    @pl.loop(0, 4)
    def _(tile):
        weight = weight_tiles(blocks, where_ref, QKV, 0, 8, 16 + 2 * tile, 2)
        product = jnp.dot(normed_one, weight, preferred_element_type=jnp.float32)
        bias = vec_ref[3:4, lane_range(256 * tile, 256)]
        kv_ref[:, lane_range(D + 256 * tile, 256)] = (product + bias).astype(bf16)

    own_lanes = pair_masks(count)
    pairs = HEADS // 2
    seq_len = hidden_ref.shape[0]
    row = lax.broadcasted_iota(jnp.int32, (count, seq_len), 0)
    key = lax.broadcasted_iota(jnp.int32, (count, seq_len), 1)
    last_key = jnp.zeros((count, seq_len), jnp.int32)
    for i in range(count):
        last_key = jnp.where(row == i, jnp.minimum(positions[i], length - 1), last_key)
    allowed = jnp.concatenate([key <= last_key] * 2, 0)
    for pair in range(pairs):
        lanes = slice(128 * pair, 128 * pair + 128)
        values_at = slice(D + 128 * pair, D + 128 * pair + 128)
        scores = dot_nt(doubled(query_ref[:, lanes], own_lanes), kv_ref[:, lanes]) * HEAD_DIM ** (
            -0.5
        )
        scores = jnp.where(allowed, scores, NEG_FILL)
        exps = jnp.exp(scores - jnp.max(scores, -1, keepdims=True))
        probs = exps / jnp.sum(exps, -1, keepdims=True)
        probs_ref[2 * count * pair : 2 * count * (pair + 1)] = probs
        mixed = jnp.dot(
            probs.astype(bf16), kv_ref[:, values_at], preferred_element_type=jnp.float32
        )
        attended_ref[:, lanes] = folded(mixed, count).astype(bf16)

    attended = attended_ref[...]
    middle_ref[...] = selected_rows(hidden_ref, positions) + vec_ref[4:5]

    @pl.loop(0, 4)
    def _(tile):
        weight = weight_tiles(blocks, where_ref, PROJ, 0, 8, 2 * tile, 2)
        middle_ref[:, lane_range(256 * tile, 256)] += jnp.dot(
            attended, weight, preferred_element_type=jnp.float32
        )

    middle = middle_ref[...]
    hat, _ = normalized(middle)
    normed_two = (hat * vec_ref[5:6] + vec_ref[6:7]).astype(bf16)

    @pl.loop(0, 16)
    def _(tile):
        at = lane_range(256 * tile, 256)
        weight = weight_tiles(blocks, where_ref, FC, 0, 8, 2 * tile, 2)
        bias = vec_ref[pl.ds(7 + tile // 4, 1), lane_range(256 * (tile % 4), 256)]
        pre_act = jnp.dot(normed_two, weight, preferred_element_type=jnp.float32) + bias
        pre_act_ref[:, at] = pre_act
        activated[:, at] = gelu(pre_act).astype(bf16)

    last_ref[...] = middle + vec_ref[11:12]

    @pl.loop(0, 16)
    def _(index):
        tile, depth = index // 4, index % 4
        weight = weight_tiles(blocks, where_ref, OUT, 8 * depth, 8, 2 * tile, 2)
        last_ref[:, lane_range(256 * tile, 256)] += jnp.dot(
            activated[:, lane_range(1024 * depth, 1024)],
            weight,
            preferred_element_type=jnp.float32,
        )

    hat, _ = normalized(last_ref[...])
    head_in_ref[...] = (hat * vec_ref[12:13] + vec_ref[13:14]).astype(bf16)


def forward_kernel(
    where_ref,
    at_smem_ref,
    length_smem_ref,
    ids_ref,
    target_ref,
    at_ref,
    length_ref,
    matrices_ref,
    table_ref,
    positions_ref,
    vec_ref,
    full_ref,
    hidden_ref,
    query_ref,
    kv_ref,
    probs_ref,
    attended_ref,
    middle_ref,
    pre_act_ref,
    last_ref,
    d_head_ref,
    table_grad_ref,
    loss_ref,
    blocks,
    table,
    own_low,
    table_pad,
    ids_all,
    parts,
    sibling_in,
    half_in,
    whole_in,
    landing,
    ready,
    arrived,
    normed_rows,
    activated,
    head_in,
    pieces,
    rows_in,
    logits,
    d_logits,
    stats,
    d_rows,
    d_sibling,
    d_first,
    d_second,
    send_sems,
    recv_sems,
    local_sems,
):
    place = coordinates()
    wires = Wires(send_sems, recv_sems)
    vocab_group = [
        moved(moved(moved(place, Y, near), Z, far), CORE, side)
        for near in range(SIDE)
        for far in range(SIDE)
        for side in range(2)
    ][1:]
    others = vocab_group + [moved(place, X, step) for step in (1, 2, 3)]
    greet(others)
    table_ring = gather_phase(
        place,
        wires,
        others,
        ids_ref,
        matrices_ref,
        table_ref,
        positions_ref,
        blocks,
        table,
        hidden_ref,
        own_low,
        table_pad,
        ids_all,
        parts,
        sibling_in,
        half_in,
        whole_in,
        landing,
        ready,
        arrived,
        local_sems,
    )
    keep = pltpu.make_async_copy(blocks, full_ref, local_sems.at[4])
    keep.start()
    forward_phase(
        where_ref,
        at_smem_ref,
        length_smem_ref,
        hidden_ref,
        vec_ref,
        head_in,
        query_ref,
        kv_ref,
        probs_ref,
        attended_ref,
        middle_ref,
        pre_act_ref,
        last_ref,
        blocks,
        normed_rows,
        activated,
    )
    stores = head_phase(
        place,
        wires,
        vocab_group,
        table_ring,
        head_in,
        table,
        target_ref,
        at_ref,
        length_ref,
        d_head_ref,
        table_grad_ref,
        loss_ref,
        parts,
        pieces,
        rows_in,
        logits,
        d_logits,
        stats,
        d_rows,
        d_sibling,
        d_first,
        d_second,
        local_sems,
    )
    wires.settle()
    keep.wait()
    for copy in stores:
        copy.wait()


def forward_call(where, positions, lengths, token_ids, target_ids, matrices, vocab_table, positions_table, vectors):
    rows, width = vocab_table.shape
    padded = -(-rows // 128) * 128
    own, seqs = positions.shape
    seq_len = positions_table.shape[0]
    count, half = own * seqs, D // 2
    bf16, f32 = jnp.bfloat16, jnp.float32
    shape = jax.ShapeDtypeStruct
    slots = where.shape[0]
    smem = pl.BlockSpec(memory_space=pltpu.SMEM)
    return pl.pallas_call(
        forward_kernel,
        name="forward_and_head",
        out_shape=(
            shape((slots, BLOCK, BLOCK), bf16),
            shape((seq_len, D), f32),
            shape((own, D), bf16),
            shape((seq_len, 2 * D), bf16),
            shape((HEADS * own, seq_len), f32),
            shape((own, D), bf16),
            shape((own, D), f32),
            shape((own, FF), f32),
            shape((own, D), f32),
            shape((own, D), f32),
            shape((N_DP * rows, width), bf16),
            shape((1, count), f32),
        ),
        in_specs=[smem] * 3 + [VMEM] * 8,
        out_specs=(ANY,) + (VMEM,) * 9 + (ANY, VMEM),
        scratch_shapes=[
            pltpu.VMEM((slots, BLOCK, BLOCK), bf16),
            pltpu.VMEM((N_DP, rows, width), bf16),
            pltpu.VMEM((3, 2, BLOCK, BLOCK), bf16),
            pltpu.VMEM((padded, width), bf16),
            pltpu.VMEM((N_DP,) + token_ids.shape, jnp.int32),
            pltpu.VMEM((128 * 128, width), bf16),
            pltpu.VMEM((2, 32 * 128, width), bf16),
            pltpu.VMEM((2, 2, 4 * 128, width), bf16),
            pltpu.VMEM((2, 2, 8 * 128, width), bf16),
            pltpu.VMEM((2, 3, 2 * 128, width), bf16),
            pltpu.VMEM((N_DP, 128, width), bf16),
            pltpu.VMEM((N_DP, 128, width), bf16),
            pltpu.VMEM((seq_len, D), f32),
            pltpu.VMEM((own, FF), bf16),
            pltpu.VMEM((own, D), bf16),
            pltpu.VMEM((2, 2, SIDE, SIDE, own, half), bf16),
            pltpu.VMEM((count, D), bf16),
            pltpu.VMEM((rows, count), f32),
            pltpu.VMEM((rows, count), bf16),
            pltpu.VMEM((N_VOCAB, 8, count // 4), f32),
            pltpu.VMEM((2, 2, SIDE, SIDE, own, half), bf16),
            pltpu.VMEM((2, SIDE, SIDE, own, half), bf16),
            pltpu.VMEM((2, 3, SIDE, own, half), bf16),
            pltpu.VMEM((2, 3, own, half), bf16),
            pltpu.SemaphoreType.DMA((200,)),
            pltpu.SemaphoreType.DMA((200,)),
            pltpu.SemaphoreType.DMA((5,)),
        ],
        compiler_params=pltpu.CompilerParams(
            collective_id=1, has_side_effects=True, vmem_limit_bytes=VMEM_BYTES
        ),
    )(
        where,
        positions,
        lengths,
        token_ids,
        target_ids,
        positions,
        lengths.reshape(1, -1),
        matrices,
        vocab_table,
        positions_table,
        vectors,
    )


def gelu_slope(values):
    cube = 0.044715 * values * values
    bent = jnp.tanh(GELU_C * (values + cube * values))
    return 0.5 * (1.0 + bent) + 0.5 * values * (1.0 - bent * bent) * GELU_C * (1.0 + 3.0 * cube)


def backward_kernel(
    where_ref,
    at_ref,
    full_ref,
    hidden_ref,
    vec_ref,
    query_ref,
    kv_ref,
    probs_ref,
    attended_ref,
    middle_ref,
    pre_act_ref,
    last_ref,
    d_head_ref,
    grads_ref,
    small_ref,
    d_embed_ref,
    blocks,
    grad_blocks,
    activated,
    d_pre,
    normed,
    rows_out,
    d_qkv,
    spread,
    query_grads,
    vec_grads,
    sems,
    grad_sem,
):
    copies = load_blocks(full_ref, blocks, sems)
    count = d_head_ref.shape[0]
    bf16 = jnp.bfloat16
    own = lax.axis_index("vocab")
    positions = [at_ref[i, own] for i in range(count)]

    def weight_grad(matrix, rows, left_ref, right, together=4):
        first, in_row = matrix

        @pl.loop(0, rows // together)
        def _(group):
            left = left_ref[:, lane_range(128 * together * group, 128 * together)]
            for column in range(0, in_row, 2):
                product = dot_tn(left, right[:, 128 * column : 128 * column + 256]).astype(bf16)
                for inner in range(2 * together):
                    row, side = inner // 2, inner % 2
                    index = first + (group * together + row) * in_row + column + side
                    grad_blocks[index] = product[
                        128 * row : 128 * row + 128, 128 * side : 128 * side + 128
                    ]
                    pltpu.make_async_copy(
                        grad_blocks.at[index], grads_ref.at[where_ref[index]], grad_sem
                    ).start()

    hat, scale = normalized(last_ref[...])
    d_last, vec_grads[12:13], vec_grads[13:14] = norm_backward(
        d_head_ref[...], hat, scale, vec_ref[12:13]
    )
    d_branch = d_last.astype(bf16)
    vec_grads[11:12] = jnp.sum(d_branch.astype(jnp.float32), 0, keepdims=True)
    activated[...] = gelu(pre_act_ref[...]).astype(bf16)
    weight_grad(OUT, 32, activated, d_branch)
    for copy in copies:
        copy.wait()

    @pl.loop(0, 16)
    def _(tile):
        at = lane_range(256 * tile, 256)
        weight = weight_tiles(blocks, where_ref, OUT, 2 * tile, 2, 0, 8)
        lowered = (dot_nt(d_branch, weight) * gelu_slope(pre_act_ref[:, at])).astype(bf16)
        d_pre[:, at] = lowered
        vec_grads[pl.ds(7 + tile // 4, 1), lane_range(256 * (tile % 4), 256)] = jnp.sum(
            lowered.astype(jnp.float32), 0, keepdims=True
        )

    hat, scale = normalized(middle_ref[...])
    normed[pl.ds(0, count)] = (hat * vec_ref[5:6] + vec_ref[6:7]).astype(bf16)
    weight_grad(FC, 8, normed.at[pl.ds(0, count)], d_pre[...])
    rows_out[...] = jnp.zeros(rows_out.shape, jnp.float32)

    @pl.loop(0, 16)
    def _(index):
        tile, depth = index // 4, index % 4
        weight = weight_tiles(blocks, where_ref, FC, 2 * tile, 2, 8 * depth, 8)
        rows_out[pl.ds(0, count), lane_range(256 * tile, 256)] += dot_nt(
            d_pre[:, lane_range(1024 * depth, 1024)], weight
        )

    d_middle, vec_grads[5:6], vec_grads[6:7] = norm_backward(
        rows_out[pl.ds(0, count)], hat, scale, vec_ref[5:6]
    )
    d_middle = d_middle + d_last
    d_proj = d_middle.astype(bf16)
    vec_grads[4:5] = jnp.sum(d_proj.astype(jnp.float32), 0, keepdims=True)
    weight_grad(PROJ, 8, attended_ref, d_proj)

    @pl.loop(0, 4)
    def _(tile):
        weight = weight_tiles(blocks, where_ref, PROJ, 2 * tile, 2, 0, 8)
        rows_out[pl.ds(0, count), lane_range(256 * tile, 256)] = dot_nt(d_proj, weight)

    own_lanes = pair_masks(count)
    spread[...] = jnp.zeros(spread.shape, jnp.float32)
    for pair in range(HEADS // 2):
        lanes = slice(128 * pair, 128 * pair + 128)
        values_at = slice(D + 128 * pair, D + 128 * pair + 128)
        d_mixed = doubled(rows_out[0:count, lanes].astype(bf16), own_lanes)
        probs = probs_ref[2 * count * pair : 2 * count * (pair + 1)]
        d_probs = dot_nt(d_mixed, kv_ref[:, values_at])
        inner = jnp.sum(probs * d_probs, -1, keepdims=True)
        d_scores = (probs * (d_probs - inner)).astype(bf16)
        d_values = dot_tn(probs.astype(bf16), d_mixed).astype(bf16)
        d_keys = dot_tn(d_scores, doubled(query_ref[:, lanes], own_lanes)) * HEAD_DIM ** (-0.5)
        d_query = jnp.dot(d_scores, kv_ref[:, lanes], preferred_element_type=jnp.float32)
        d_query = (folded(d_query, count) * HEAD_DIM ** (-0.5)).astype(bf16).astype(jnp.float32)
        vec_grads[2:3, lanes] = jnp.sum(d_query, 0, keepdims=True)
        vec_grads[3:4, lanes] = jnp.sum(d_values.astype(jnp.float32), 0, keepdims=True)
        query_grads[:, lanes] = d_query
        d_qkv[:, D + 128 * pair : D + 128 * pair + 128] = d_keys.astype(bf16)
        d_qkv[:, 2 * D + 128 * pair : 2 * D + 128 * pair + 128] = d_values
    for i in range(count):
        spread[pl.ds(positions[i], 1), :] = query_grads[i : i + 1, :]
    d_qkv[:, :D] = spread[...].astype(bf16)
    hat, scale = normalized(hidden_ref[...])
    normed[...] = (hat * vec_ref[0:1] + vec_ref[1:2]).astype(bf16)
    weight_grad(QKV, 8, normed, d_qkv)
    rows_out[...] = jnp.zeros(rows_out.shape, jnp.float32)

    @pl.loop(0, 12)
    def _(index):
        tile, depth = index // 3, index % 3
        weight = weight_tiles(blocks, where_ref, QKV, 2 * tile, 2, 8 * depth, 8)
        rows_out[:, lane_range(256 * tile, 256)] += dot_nt(
            d_qkv[:, lane_range(1024 * depth, 1024)], weight
        )

    d_hidden, vec_grads[0:1], vec_grads[1:2] = norm_backward(
        rows_out[...], hat, scale, vec_ref[0:1]
    )
    rows_out[...] = d_hidden
    for i in range(count):
        rows_out[pl.ds(positions[i], 1), :] += d_middle[i : i + 1]
    d_embed_ref[...] = rows_out[...].astype(bf16)
    vec_rows = vec_ref.shape[0]
    for index in range(small_ref.shape[0]):
        group, tile = index // 8, index % 8
        lanes = slice(128 * tile, 128 * tile + 128)
        vec_row = (
            vec_grads[group : group + 1, lanes]
            if group < vec_rows
            else jnp.zeros((1, 128), jnp.float32)
        )
        small_ref[index] = jnp.concatenate(
            [rows_out[8 * group : 8 * group + 8, lanes], vec_row, jnp.zeros((7, 128), jnp.float32)],
            0,
        ).astype(bf16)
    pltpu.make_async_copy(grad_blocks, grads_ref, grad_sem).wait()


def backward_call(where, positions, full, hidden, vectors, cache, d_head):
    count = positions.shape[0]
    bf16 = jnp.bfloat16
    shape = jax.ShapeDtypeStruct
    return pl.pallas_call(
        backward_kernel,
        name="layer_backward",
        out_shape=(
            shape(full.shape, bf16),
            shape((N_DP * N_VOCAB, 16, 128), bf16),
            shape(hidden.shape, bf16),
        ),
        grid_spec=pltpu.PrefetchScalarGridSpec(
            num_scalar_prefetch=2,
            grid=(),
            in_specs=[ANY] + [VMEM] * 10,
            out_specs=(ANY, VMEM, VMEM),
            scratch_shapes=[
                pltpu.VMEM(full.shape, bf16),
                pltpu.VMEM(full.shape, bf16),
                pltpu.VMEM((count, FF), bf16),
                pltpu.VMEM((count, FF), bf16),
                pltpu.VMEM(hidden.shape, bf16),
                pltpu.VMEM(hidden.shape, jnp.float32),
                pltpu.VMEM((hidden.shape[0], 3 * D), bf16),
                pltpu.VMEM(hidden.shape, jnp.float32),
                pltpu.VMEM((count, D), jnp.float32),
                pltpu.VMEM((16, D), jnp.float32),
                pltpu.SemaphoreType.DMA((8,)),
                pltpu.SemaphoreType.DMA,
            ],
        ),
        compiler_params=pltpu.CompilerParams(vmem_limit_bytes=VMEM_BYTES),
    )(where, positions, full, hidden, vectors, *cache, d_head)


def adam_step(weight, moment_one, moment_two, grad_in, rate, decay):
    new_one = BETA_ONE * moment_one + (1.0 - BETA_ONE) * grad_in
    new_two = BETA_TWO * moment_two + (1.0 - BETA_TWO) * grad_in * grad_in
    hat_one = new_one * (1.0 / (1.0 - BETA_ONE**STEP))
    hat_two = new_two * (1.0 / (1.0 - BETA_TWO**STEP))
    change = hat_one / (jnp.sqrt(hat_two) + ADAM_EPS)
    if decay:
        change = change + decay * weight
    return weight - rate * change, new_one, new_two


def high_dot(left, right, contract=((1,), (0,))):
    return lax.dot_general(
        left, right, (contract, ((), ())), precision=HIGH, preferred_element_type=jnp.float32
    )


def update_kernel(*refs):
    names = 18
    sources, (loss_ref, norm_ref, *targets) = refs[:names], refs[names : names + 15]
    buffers = refs[names + 15 : 2 * names + 15]
    results = refs[2 * names + 15 : 2 * names + 28]
    vec_grad, load_sems, store_sems = refs[2 * names + 28 :]
    loads = [
        pltpu.make_async_copy(source, buffer, load_sems.at[index])
        for index, (source, buffer) in enumerate(zip(sources, buffers))
    ]
    for copy in loads:
        copy.start()
    stores = []

    def store(index, at=None):
        source, target = results[index], targets[index]
        if at is not None:
            source, target = source.at[at], target.at[at]
        copy = pltpu.make_async_copy(source, target, store_sems.at[len(stores)])
        copy.start()
        stores.append(copy)

    totals, final, grads, matrices, left_stats, right_stats, left_roots, right_roots = buffers[:8]
    table_grad, table, table_m, table_v = buffers[8:12]
    positions, pos_m, pos_v, vectors, vectors_m, vectors_v = buffers[12:]
    matrices_new, left_new, right_new, matrices_grad = results[:4]
    for copy in loads[:2]:
        copy.wait()
    row_squares = jnp.zeros((8, 128), jnp.float32)
    for part in range(2):
        for core in range(2):
            values = final[part, core].reshape(SIDE**3, 8, 128)
            row_squares += jnp.sum(values * values, 0)
    squares = jnp.sum(totals[0:1]) + jnp.sum(row_squares)
    loss = jnp.sum(totals[1:2])
    norm = jnp.sqrt(jnp.full((1, 128), squares, jnp.float32))
    clip = CLIP_LEVEL / jnp.maximum(norm, CLIP_LEVEL)
    loss_ref[0, 0] = loss
    norm_ref[0, 0] = jnp.max(norm)
    for copy in loads[2:8]:
        copy.wait()

    @pl.loop(0, SLOTS, unroll=3)
    def _(slot):
        grad = grads[slot // 2, slot % 2] * clip
        matrices_grad[slot] = grad
        left_new[slot] = STAT_DECAY * left_stats[slot] + (1.0 - STAT_DECAY) * high_dot(
            grad, grad, ((1,), (1,))
        )
        right_new[slot] = STAT_DECAY * right_stats[slot] + (1.0 - STAT_DECAY) * high_dot(
            grad, grad, ((0,), (0,))
        )
        stepped = high_dot(high_dot(left_roots[slot], grad), right_roots[slot])
        weight = matrices[slot]
        matrices_new[slot] = weight - SHAMPOO_RATE * (stepped + DECAY_RATE * weight)

    for index in range(4):
        store(index)
    for copy in loads[8:12]:
        copy.wait()
    rows, width = table.shape
    wide_clip = jnp.concatenate([clip] * (width // 128), 1)
    chunk = rows // 4
    for index in range(4):

        @pl.loop(0, chunk // 80)
        def _(inner):
            at = pl.ds(pl.multiple_of(index * chunk + inner * 80, 80), 80)
            grad = table_grad[at] * wide_clip
            stepped = adam_step(
                table[at], table_m[at], table_v[at], grad, TABLE_RATE, DECAY_RATE
            )
            for order, value in enumerate(stepped):
                results[4 + order][at] = value

        for order in range(3):
            store(4 + order, pl.ds(index * chunk, chunk))
    for copy in loads[12:]:
        copy.wait()
    tiles = D // 128
    for index in range(N_DP * N_VOCAB):
        at_core, rest = index // 64, index % 64
        at_z, at_y, at_x = rest // 16, rest // 4 % 4, rest % 4
        group, lanes = index // tiles, slice(128 * (index % tiles), 128 * (index % tiles) + 128)
        at = slice(8 * group, 8 * group + 8)
        stepped = adam_step(
            positions[at, lanes],
            pos_m[at, lanes],
            pos_v[at, lanes],
            final[0, at_core, at_z, at_y, at_x] * clip,
            POS_RATE,
            DECAY_RATE,
        )
        for order, value in enumerate(stepped):
            results[7 + order][at, lanes] = value
        if group < vectors.shape[0]:
            vec_grad[group : group + 1, lanes] = (
                final[1, at_core, at_x, at_z, at_y, 0:1] * clip
            )
    for index in range(7, 10):
        store(index)
    stepped = adam_step(
        vectors[...], vectors_m[...], vectors_v[...], vec_grad[...], VECTOR_RATE, 0.0
    )
    for order, value in enumerate(stepped):
        results[10 + order][...] = value
        store(10 + order)
    for copy in stores:
        copy.wait()


def update_call(totals, final, grads, blocks, table_grad, table, positions, vectors):
    sources = [totals, final, grads, *blocks, table_grad, *table, *positions, *vectors]
    shape = lambda array: jax.ShapeDtypeStruct(array.shape, jnp.float32)
    targets = [shape(blocks[0])] * 4
    targets += [shape(array) for array in (*table, *positions, *vectors)]
    scalar = jax.ShapeDtypeStruct((1, 1), jnp.float32)
    smem = pl.BlockSpec(memory_space=pltpu.SMEM)
    return pl.pallas_call(
        update_kernel,
        name="optimizer_update",
        out_shape=(scalar, scalar, *targets),
        in_specs=[ANY] * len(sources),
        out_specs=(smem, smem) + (ANY,) * len(targets),
        scratch_shapes=[pltpu.VMEM(array.shape, jnp.float32) for array in sources]
        + [pltpu.VMEM(target.shape, jnp.float32) for target in targets]
        + [
            pltpu.VMEM(vectors[0].shape, jnp.float32),
            pltpu.SemaphoreType.DMA((len(sources),)),
            pltpu.SemaphoreType.DMA((len(targets) + 9,)),
        ],
        compiler_params=pltpu.CompilerParams(vmem_limit_bytes=VMEM_BYTES),
    )(*sources)


def slot_places():
    slot = np.arange(N_DP * N_VOCAB * SLOTS)
    device, own = slot // SLOTS, slot % SLOTS
    inner = device % N_VOCAB
    place = (device // N_VOCAB, inner // 2 % SIDE, inner // (2 * SIDE), inner % 2)
    part = own // 2
    result = np.zeros_like(slot)
    for which, (first, second, third) in enumerate(ORDERS):
        index = which * 2 + place[CORE]
        for axis in (third, second, first):
            index = index * SIDE + place[axis]
        result = np.where(part == which, index * 2 + own % 2, result)
    return result.astype(np.int32)


def per_device(
    token_ids,
    seq_lengths,
    loss_positions,
    target_ids,
    block_of_slot,
    matrices,
    left_stats,
    right_stats,
    left_roots,
    right_roots,
    vocab_table,
    table_m,
    table_v,
    positions_table,
    pos_m,
    pos_v,
    vectors,
    vectors_m,
    vectors_v,
):
    block_iota = jnp.arange(block_of_slot.shape[0], dtype=jnp.int32)
    where = jnp.sum(
        jnp.where(block_of_slot[None, :] == block_iota[:, None], slot_places()[None, :], 0),
        1,
        dtype=jnp.int32,
    )
    positions = loss_positions.T
    full, hidden, *cache, d_head_in, head_grad, loss_row = forward_call(
        where,
        positions,
        seq_lengths,
        token_ids,
        target_ids.T,
        matrices,
        vocab_table,
        positions_table,
        vectors,
    )
    grad_blocks, small, d_embed = backward_call(
        where, positions, full, hidden, vectors, cache, d_head_in
    )
    owned_grads, table_grad_own, final, totals = finish_call(
        grad_blocks.reshape(3, 2, SIDE, 32, BLOCK, BLOCK),
        small.reshape(2, SIDE, 16, 16, 128),
        head_grad.reshape(N_DP, TABLE_CHUNKS, -1, head_grad.shape[1]),
        d_embed,
        token_ids,
        loss_row,
    )
    loss, norm, *updated = update_call(
        totals,
        final,
        owned_grads,
        (matrices, left_stats, right_stats, left_roots, right_roots),
        table_grad_own,
        (vocab_table, table_m, table_v),
        (positions_table, pos_m, pos_v),
        (vectors, vectors_m, vectors_v),
    )
    return (loss.reshape(()), norm.reshape(()), *updated)


def solution(mesh):
    in_specs = (
        P("dp", None),
        P("dp"),
        P("dp", None),
        P("dp", None),
        P(),
        P(("dp", "vocab"), None, None),
        P(("dp", "vocab"), None, None),
        P(("dp", "vocab"), None, None),
        P(("dp", "vocab"), None, None),
        P(("dp", "vocab"), None, None),
        P("vocab", "dp"),
        P("vocab", "dp"),
        P("vocab", "dp"),
        P(),
        P(),
        P(),
        P(),
        P(),
        P(),
    )
    out_specs = (
        P(),
        P(),
        P(("dp", "vocab"), None, None),
        P(("dp", "vocab"), None, None),
        P(("dp", "vocab"), None, None),
        P(("dp", "vocab"), None, None),
        P("vocab", "dp"),
        P("vocab", "dp"),
        P("vocab", "dp"),
        P(),
        P(),
        P(),
        P(),
        P(),
        P(),
    )
    return jax.shard_map(
        per_device, mesh=mesh, in_specs=in_specs, out_specs=out_specs, check_vma=False
    )
```

```python
import math

import jax
import jax.numpy as jnp
import numpy as np
from jax import lax
from jax.experimental import pallas as pl
from jax.experimental.pallas import tpu as pltpu
from jax.sharding import PartitionSpec as P

D = 1024
HEADS = 16
HEAD_DIM = 64
FF = 4096
VOCAB_REAL = 50257
LAYERS = 1
BLOCK = 128
STEP = 10


LN_EPS = 1e-05
CLIP_LEVEL = 0.05
BETA_ONE = 0.9
BETA_TWO = 0.999
ADAM_EPS = 1e-08
STAT_DECAY = 0.95
SHAMPOO_RATE = 0.03
TABLE_RATE = 0.15
POS_RATE = 0.05
VECTOR_RATE = 0.25
DECAY_RATE = 0.1
NEG_FILL = -1e30
GELU_C = 0.7978845608028654
HIGH = lax.Precision.HIGHEST


def gelu(values):
    return 0.5 * values * (1.0 + jnp.tanh(GELU_C * (values + 0.044715 * values * values * values)))


def dot_nt(left, right):
    return lax.dot_general(
        left, right, (((1,), (1,)), ((), ())), preferred_element_type=jnp.float32
    )


def dot_tn(left, right):
    return lax.dot_general(
        left, right, (((0,), (0,)), ((), ())), preferred_element_type=jnp.float32
    )


VMEM_BYTES = 63 << 20
TABLE_CHUNKS = 20
MESH_IDS = pl.DeviceIdType.MESH
ANY = pl.BlockSpec(memory_space=pl.ANY)
VMEM = pl.BlockSpec(memory_space=pltpu.VMEM)
N_DP = 4
N_VOCAB = 32
SIDE = 4
X, Y, Z, CORE = range(4)
ORDERS = ((X, Y, Z), (Y, Z, X), (Z, X, Y))
SLOTS = 6


def coordinates():
    across = lax.axis_index("dp")
    inner = lax.axis_index("vocab")
    return (across, (inner // 2) % SIDE, inner // (2 * SIDE), inner % 2)


def moved(place, axis, step):
    shifted = list(place)
    shifted[axis] = (place[axis] + step) % (2 if axis == CORE else SIDE)
    return tuple(shifted)


def device_of(place):
    return (place[X], (place[Z] * SIDE + place[Y]) * 2 + place[CORE])


def rings_of(place, axes):
    others = [moved(place, CORE, 1)]
    return others + [moved(place, axis, step) for axis in axes for step in (1, 2, 3)]


def greet(others):
    for other in others:
        pl.semaphore_signal(
            pltpu.get_barrier_semaphore(),
            inc=1,
            device_id=device_of(other),
            device_id_type=MESH_IDS,
        )


def await_greetings(others):
    pl.semaphore_wait(pltpu.get_barrier_semaphore(), len(others))


class Wires:
    def __init__(self, send_sems, recv_sems):
        self.send_sems, self.recv_sems = send_sems, recv_sems
        self.send_slots, self.recv_slots, self.sent = 0, 0, []

    def send_slot(self):
        self.send_slots += 1
        return self.send_slots - 1

    def recv_slot(self):
        self.recv_slots += 1
        return self.recv_slots - 1

    def copy(self, source, target, place, send_slot, recv_slot):
        return pltpu.make_async_remote_copy(
            src_ref=source,
            dst_ref=target,
            send_sem=self.send_sems.at[send_slot],
            recv_sem=self.recv_sems.at[recv_slot],
            device_id=device_of(place),
            device_id_type=MESH_IDS,
        )

    def send(self, source, target, place, send_slot=None):
        slot = self.send_slot() if send_slot is None else send_slot
        copy = self.copy(source, target, place, slot, self.recv_slot())
        copy.start()
        if send_slot is None:
            self.sent.append(copy)
        return copy

    def bundle(self):
        return self.send_slot(), self.recv_slot()

    def send_all(self, source, target, place, bundle):
        self.copy(source, target, place, *bundle).start()

    def whole(self, ref, place, bundle):
        return self.copy(ref, ref, place, *bundle)

    def await_sent(self, ref, place, send_slot):
        self.copy(ref, ref, place, send_slot, 0).wait_send()

    def settle(self, latest=0):
        done = len(self.sent) - latest
        for copy in self.sent[:done]:
            copy.wait_send()
        self.sent = self.sent[done:]


def lane_range(first, count):
    return pl.ds(pl.multiple_of(first, 128), count)


class Group:
    def __init__(self, wires, place):
        self.wires, self.place, self.slot, self.size = wires, place, wires.send_slot(), 0

    def send(self, source, target, place):
        self.size += math.prod(source.shape) * jnp.dtype(source.dtype).itemsize
        return self.wires.send(source, target, place, self.slot)

    def settle(self, blocks):
        count, rest = divmod(self.size, math.prod(blocks.shape[1:]) * 2)
        assert rest == 0 and count <= blocks.shape[0]
        self.wires.await_sent(blocks.at[pl.ds(0, count)], self.place, self.slot)


def add_blocks(target, sources, count):
    @pl.loop(0, count)
    def _(i):
        at = i if len(target.shape) == 3 else lane_range(128 * i, 128)
        total = target[at].astype(jnp.float32)
        for source in sources:
            total += source[at].astype(jnp.float32)
        target[at] = total.astype(target.dtype)


class RingGather:
    def __init__(self, wires, place, axis, piece, half, own=None):
        self.wires, self.place, self.axis = wires, place, axis
        self.piece, self.half = piece, half
        self.mine = place[axis]
        self.own = self.piece(self.mine) if own is None else own

    def start(self):
        mine = self.piece(self.mine)
        self.up = self.wires.send(self.own, mine, moved(self.place, self.axis, 1))
        self.down = self.wires.send(self.own, mine, moved(self.place, self.axis, -1))

    def forward(self):
        self.up.wait_recv()
        lower = self.half((self.mine + 3) % SIDE, 0)
        self.far_up = self.wires.send(lower, lower, moved(self.place, self.axis, 1))
        self.down.wait_recv()
        upper = self.half((self.mine + 1) % SIDE, 1)
        self.far_down = self.wires.send(upper, upper, moved(self.place, self.axis, -1))

    def finish(self):
        self.far_up.wait_recv()
        self.far_down.wait_recv()


class DirectGather:
    def __init__(self, wires, place, axis, piece, own=None):
        self.wires, self.place, self.axis, self.piece = wires, place, axis, piece
        self.own = self.piece(place[axis]) if own is None else own

    def start(self):
        mine = self.piece(self.place[self.axis])
        self.copies = [
            self.wires.send(self.own, mine, moved(self.place, self.axis, step))
            for step in (1, 2, 3)
        ]

    def finish(self):
        for copy in self.copies:
            copy.wait_recv()


class RingReduce:
    def __init__(self, wires, place, axis, piece, half, count, half_in, whole_in):
        self.wires, self.place, self.axis = wires, place, axis
        self.piece, self.half, self.count = piece, half, count
        self.half_in, self.whole_in = half_in, whole_in
        self.mine = place[axis]

    def start(self):
        far = (self.mine + 2) % SIDE
        up, down = moved(self.place, self.axis, 1), moved(self.place, self.axis, -1)
        self.far_up = self.wires.send(self.half(far, 0), self.half_in.at[0], up)
        self.far_down = self.wires.send(self.half(far, 1), self.half_in.at[1], down)

    def forward(self):
        after, before = (self.mine + 1) % SIDE, (self.mine + 3) % SIDE
        up, down = moved(self.place, self.axis, 1), moved(self.place, self.axis, -1)
        self.far_up.wait_recv()
        add_blocks(self.half(after, 0), [self.half_in.at[0]], self.count // 2)
        self.up = self.wires.send(self.piece(after), self.whole_in.at[0], up)
        self.far_down.wait_recv()
        add_blocks(self.half(before, 1), [self.half_in.at[1]], self.count // 2)
        self.down = self.wires.send(self.piece(before), self.whole_in.at[1], down)

    def arrive(self):
        self.up.wait_recv()
        self.down.wait_recv()

    def finish(self):
        self.arrive()
        add_blocks(
            self.piece(self.mine), [self.whole_in.at[0], self.whole_in.at[1]], self.count
        )


class DirectReduce:
    def __init__(self, wires, place, axis, piece, count, landing):
        self.wires, self.place, self.axis = wires, place, axis
        self.piece, self.count, self.landing = piece, count, landing

    def start(self):
        mine = self.place[self.axis]
        self.copies = [
            self.wires.send(
                self.piece((mine + step) % SIDE),
                self.landing.at[step - 1],
                moved(self.place, self.axis, step),
            )
            for step in (1, 2, 3)
        ]

    def arrive(self):
        for copy in self.copies:
            copy.wait_recv()

    def finish(self):
        self.arrive()
        add_blocks(
            self.piece(self.place[self.axis]),
            [self.landing.at[step] for step in range(3)],
            self.count,
        )


class RowGather:
    def __init__(self, wires, place, axis, first, row):
        self.wires, self.place, self.axis = wires, place, axis
        self.row, self.mine, self.first = row, place[axis], first
        self.up, self.down, self.far = [], [], {}
        self.bundles = [wires.send_slot() for _ in range(3)]

    def of(self, piece, index):
        return self.row((self.mine + piece) % SIDE, (self.first + (0, 1, 3, 2)[index]) % SIDE)

    def send(self, index):
        mine = self.of(0, index)
        up, down = moved(self.place, self.axis, 1), moved(self.place, self.axis, -1)
        self.up.append(self.wires.send(mine, mine, up, self.bundles[0]))
        self.down.append(self.wires.send(mine, mine, down, self.bundles[1]))

    def forward(self, index):
        upward = index < 2
        (self.up if upward else self.down)[index].wait_recv()
        passed = self.of(3 if upward else 1, index)
        step = 1 if upward else -1
        target = moved(self.place, self.axis, step)
        self.far[index] = self.wires.send(passed, passed, target, self.bundles[2])
        return passed

    def take(self, index):
        (self.down if index < 2 else self.up)[index].wait_recv()
        return self.of(1 if index < 2 else 3, index)

    def take_far(self, index):
        self.far[index].wait_recv()
        return self.of(2, index)

    def settle(self, piece):
        for bundle in self.bundles:
            self.wires.await_sent(piece, self.place, bundle)


class QuarterReduce(RingReduce):
    def start(self, chunk):
        far = (self.mine + 2) % SIDE
        up, down = moved(self.place, self.axis, 1), moved(self.place, self.axis, -1)
        size = self.count // 4
        landing = pl.ds(chunk * size, size)
        if chunk == 0:
            self.far_ups, self.far_downs, self.wholes = [], [], []
        self.far_ups.append(
            self.wires.send(self.half(far, 2 * chunk), self.half_in.at[0, landing], up)
        )
        self.far_downs.append(
            self.wires.send(self.half(far, 2 * chunk + 1), self.half_in.at[1, landing], down)
        )

    def send_quarter(self, piece, quarter, side):
        size = self.count // 4
        landing = self.whole_in.at[side, pl.ds(quarter * size, size)]
        there = moved(self.place, self.axis, 1 if side == 0 else -1)
        self.wholes.append(self.wires.send(self.half(piece, quarter), landing, there))

    def start_near(self):
        after, before = (self.mine + 1) % SIDE, (self.mine + 3) % SIDE
        for quarter in (0, 2):
            self.send_quarter(after, quarter + 1, 0)
            self.send_quarter(before, quarter, 1)

    def forward(self):
        after, before = (self.mine + 1) % SIDE, (self.mine + 3) % SIDE
        size = self.count // 4
        for chunk in range(2):
            landed = pl.ds(chunk * size, size)
            self.far_ups[chunk].wait_recv()
            add_blocks(self.half(after, 2 * chunk), [self.half_in.at[0, landed]], size)
            self.send_quarter(after, 2 * chunk, 0)
            self.far_downs[chunk].wait_recv()
            add_blocks(self.half(before, 2 * chunk + 1), [self.half_in.at[1, landed]], size)
            self.send_quarter(before, 2 * chunk + 1, 1)

    def arrive(self):
        for copy in self.wholes:
            copy.wait_recv()


def block_ring(place, part, phase, at):
    first_axis, second_axis, third_axis = ORDERS[part]
    k1, k2, k3 = place[first_axis], place[second_axis], place[third_axis]
    if phase == 0:
        return (
            lambda j: at(k3, 8 * k2 + 2 * j, 2),
            lambda j, h: at(k3, 8 * k2 + 2 * j + h, 1),
        )
    if phase == 1:
        return (lambda j: at(k3, 8 * j, 8), lambda j, h: at(k3, 8 * j + 4 * h, 4))
    return (lambda j: at(j, 0, 32), lambda j, q: at(j, 8 * q, 8))


def gather_phase(
    place,
    wires,
    others,
    ids_ref,
    matrices_ref,
    table_ref,
    positions_ref,
    blocks,
    table,
    hidden_ref,
    own_low,
    table_pad,
    ids_all,
    parts,
    sibling_in,
    half_in,
    whole_in,
    landing,
    ready,
    arrived,
    local_sems,
):
    core = place[CORE]
    across = place[X]
    sibling = moved(place, CORE, 1)
    group = Group(wires, place)

    def blocks_at(part, side, k3, first, count):
        start = ((2 * part + side) * SIDE + k3) * 32 + first
        return blocks.at[pl.ds(start, count)]

    own_low[...] = matrices_ref[...].astype(jnp.bfloat16).reshape(own_low.shape)
    for part in range(3):
        k1, k2, k3 = (place[axis] for axis in ORDERS[part])
        first = ((2 * part + core) * SIDE + k3) * 32 + 8 * k2 + 2 * k1
        for which in range(2):
            blocks[first + which] = own_low[part, which]
    ids_all[across] = ids_ref[...]
    table[across] = table_ref[...].astype(jnp.bfloat16)
    rings = [[], [], []]
    for part in range(3):

        def at(k3, first, count, part=part):
            return blocks_at(part, core, k3, first, count)

        first_axis, second_axis, third_axis = ORDERS[part]
        piece, _ = block_ring(place, part, 0, at)
        rings[0].append(DirectGather(group, place, first_axis, piece, own_low.at[part]))
        piece, half = block_ring(place, part, 1, at)
        rings[1].append(RingGather(group, place, second_axis, piece, half))
        rings[2].append(
            RowGather(
                wires,
                place,
                third_axis,
                place[second_axis],
                lambda j, row, at=at: at(j, 8 * row, 8),
            )
        )
    on_z, on_x, on_y = rings[2]
    ids_ring = DirectGather(wires, place, X, lambda j: ids_all.at[j])
    rows = table_ref.shape[0]
    table_pad[pl.ds(0, rows)] = table_ref[...].astype(jnp.bfloat16)
    padding = table_pad.shape[0] - rows
    table_pad[pl.ds(rows, padding)] = jnp.zeros((padding, table_pad.shape[1]), jnp.bfloat16)
    table_ring = RowGather(
        wires,
        place,
        X,
        0,
        lambda j, row: table.at[j, pl.ds(rows // SIDE * row, rows // SIDE)],
    )
    base = (lax.axis_index("vocab") * rows).astype(jnp.float32)
    tiles = table_pad.shape[0] // 128
    lane = lax.broadcasted_iota(jnp.int32, (128, 128), 1).astype(jnp.float32)

    def group_of(part, which):
        return 2 * ((across // 2 + part) % 2) + which

    def look_up(part, side, half):
        dp_group = group_of(part, side)

        @pl.loop(4 * half, 4 * half + 4)
        def _(quad):
            hot_rows = []
            for which in range(4):
                ids = ids_all[dp_group, pl.ds(4 * quad + which, 1), :].astype(jnp.float32) - base
                column = jnp.transpose(jnp.broadcast_to(ids, (128, 128)))
                hot_rows.append(
                    jnp.concatenate(
                        [
                            jnp.where(column == lane + 128.0 * tile, 1.0, 0.0).astype(jnp.bfloat16)
                            for tile in range(tiles)
                        ],
                        1,
                    )
                )
            found = jnp.dot(
                jnp.concatenate(hot_rows, 0), table_pad[...], preferred_element_type=jnp.float32
            ).astype(jnp.bfloat16)
            at_z = quad // 2
            for which in range(4):
                at_y = 2 * (quad % 2) + which // 2
                first, second = (at_z, at_y) if part == 0 else (at_y, at_z)
                at = lookup_rows(part, which % 2, first, 2 * second + side, 1)
                parts[at] = found[128 * which : 128 * which + 128]

    def lookup_rows(part, side, first, index, count):
        start = ((2 * part + side) * SIDE + first) * 8 + index
        return lane_range(128 * start, 128 * count)

    def to_sibling(part):
        crossing = parts.at[lookup_rows(part, 1 - core, 0, 0, 32)]
        return group.send(crossing, sibling_in.at[part], sibling)

    lookup_axes = ((Z, Y), (Y, Z))
    lookup_rings, lookup_ends = [], []
    for part in range(2):
        first_axis, second_axis = lookup_axes[part]
        lookup_rings.append(
            RingReduce(
                group,
                place,
                first_axis,
                lambda j, part=part: parts.at[lookup_rows(part, core, j, 0, 8)],
                lambda j, h, part=part: parts.at[lookup_rows(part, core, j, 4 * h, 4)],
                8,
                half_in.at[part],
                whole_in.at[part],
            )
        )
        lookup_ends.append(
            DirectReduce(
                group,
                place,
                second_axis,
                lambda j, part=part, k=place[first_axis]: parts.at[
                    lookup_rows(part, core, k, 2 * j, 2)
                ],
                2,
                landing.at[part],
            )
        )

    def add_sibling(part):
        siblings[part].wait_recv()
        add_blocks(parts.at[lookup_rows(part, core, 0, 0, 32)], [sibling_in.at[part]], 32)
        lookup_rings[part].start()

    def take_result(part):
        lookup_ends[part].arrive()
        first_axis, second_axis = lookup_axes[part]
        for which in range(2):
            at = lookup_rows(part, core, place[first_axis], 2 * place[second_axis] + which, 1)
            total = parts[at].astype(jnp.float32)
            for step in range(3):
                total += landing[part, step, 128 * which : 128 * which + 128].astype(jnp.float32)
            ready[group_of(part, which)] = total.astype(jnp.bfloat16)

    shares = [wires.bundle() for _ in range(3)]

    def share(part, ref):
        wires.send_all(ref, ref, sibling, shares[part])

    own_side = across % 2
    await_greetings(others)
    ids_ring.start()
    for ring in rings[0]:
        ring.start()
    table_ring.send(0)
    look_up(0, own_side, 0)
    look_up(0, own_side, 1)
    for ring, later in zip(rings[0], rings[1]):
        ring.finish()
        later.start()
    for ring in rings[2]:
        ring.send(0)
    ids_ring.finish()
    look_up(0, 1 - own_side, 0)
    look_up(0, 1 - own_side, 1)
    siblings = [to_sibling(0)]
    look_up(1, 0, 0)
    for ring in rings[1]:
        ring.forward()
    look_up(1, 0, 1)
    add_sibling(0)
    for ring in (on_y, on_x, on_z):
        ring.send(1)
    look_up(1, 1, 0)
    look_up(1, 1, 1)
    siblings.append(to_sibling(1))
    for ring in rings[1]:
        ring.finish()
    on_y.send(2)
    on_x.send(2)
    lookup_rings[0].forward()
    add_sibling(1)
    on_z.send(2)
    on_x.send(3)
    table_ring.send(1)
    for part in range(3):
        share(part, blocks_at(part, core, place[ORDERS[part][2]], 0, 32))
    lookup_rings[1].forward()
    share(1, on_x.forward(0))
    share(1, on_x.forward(2))
    lookup_rings[0].finish()
    lookup_ends[0].start()
    on_z.send(3)
    on_y.send(3)
    share(1, on_x.forward(1))
    share(1, on_x.forward(3))
    table_ring.send(2)
    table_ring.send(3)
    lookup_rings[1].finish()
    lookup_ends[1].start()
    for ring_part, ring in ((0, on_z), (2, on_y)):
        for index in (0, 2):
            share(ring_part, ring.forward(index))
    take_result(0)
    for ring_part, ring in ((0, on_z), (2, on_y)):
        for index in (1, 3):
            share(ring_part, ring.forward(index))
    take_result(1)
    swaps = []
    for step in (1, 2, 3):
        there = moved(place, X, step)
        swaps.append(group.send(ready.at[there[X]], arrived.at[across], there))
    arrived[across] = ready[across]
    for part in range(3):
        for index in range(4):
            share(part, rings[2][part].take(index))
    for copy in swaps:
        copy.wait_recv()
    for source in range(4):
        columns = pl.ds(256 * source, 256)
        hidden_ref[:, columns] = (
            arrived[source].astype(jnp.float32) + positions_ref[:, columns]
        )
    table_ring.forward(0)
    table_ring.forward(2)
    for index in (0, 2, 1, 3):
        for part in range(3):
            share(part, rings[2][part].take_far(index))
    for index in (1, 3):
        table_ring.forward(index)
    group.settle(blocks)
    wires.settle()
    for part in range(3):
        rings[2][part].settle(blocks.at[pl.ds(0, 32)])
        wires.whole(blocks.at[pl.ds(0, 128)], sibling, shares[part]).wait()
    return table_ring


def head_phase(
    place,
    wires,
    vocab_group,
    table_ring,
    head_in_ref,
    table,
    target_ref,
    at_ref,
    length_ref,
    d_head_ref,
    table_grad_ref,
    loss_ref,
    table_grads,
    pieces,
    logits,
    stats,
    d_rows,
    d_sibling,
    d_first,
    d_second,
    local_sems,
    arrange_out,
):
    core = place[CORE]
    sibling = moved(place, CORE, 1)
    own, width = head_in_ref.shape
    half_width = width // 2
    sends = Group(wires, place)
    feature_axes = ((Y, Z), (Z, Y))
    for part in range(2):
        near, far = (place[axis] for axis in feature_axes[part])
        pieces[part, core, far, near] = head_in_ref[
            :, part * half_width : (part + 1) * half_width
        ]
    first_rings, second_rings = [], []
    for part in range(2):
        near_axis, far_axis = feature_axes[part]
        first_rings.append(
            DirectGather(
                sends,
                place,
                near_axis,
                lambda j, part=part, k=place[far_axis]: pieces.at[part, core, k, j],
            )
        )
        second_rings.append(
            DirectGather(sends, place, far_axis, lambda j, part=part: pieces.at[part, core, j])
        )
    for ring in first_rings:
        ring.start()
    seqs = target_ref.shape[1]
    column = lax.broadcasted_iota(jnp.int32, (seqs, seqs * own), 1)
    row = lax.broadcasted_iota(jnp.int32, (seqs, seqs * own), 0)
    own_seq = jnp.where(column // own == row, 1.0, 0.0)
    slot = lax.broadcasted_iota(jnp.int32, (own, seqs * own), 0)
    slot_column = lax.broadcasted_iota(jnp.int32, (own, seqs * own), 1)
    own_slot = slot_column % own == slot

    def laid_end_to_end(values):
        wide = jnp.dot(
            values.astype(jnp.float32), own_seq, precision=HIGH, preferred_element_type=jnp.float32
        )
        return jnp.sum(jnp.where(own_slot, wide, 0.0), 0, keepdims=True)

    target = laid_end_to_end(target_ref[...]).astype(jnp.int32)
    lengths = jnp.dot(
        length_ref[...].astype(jnp.float32),
        own_seq,
        precision=HIGH,
        preferred_element_type=jnp.float32,
    )
    counted = (laid_end_to_end(at_ref[...]) < lengths).astype(jnp.float32)
    for index in range(8):
        arrange_out(index)
    for ring, later in zip(first_rings, second_rings):
        ring.finish()
        later.start()
    for index in range(8, 16):
        arrange_out(index)
    crossing = []
    for part in range(2):
        second_rings[part].finish()
        mine = pieces.at[part, core]
        crossing.append(sends.send(mine, mine, sibling))
    for copy in crossing:
        copy.wait_recv()
    for index in range(4):
        table_ring.take(index)
        table_ring.take_far(index)
    table_ring.settle(table.at[0])
    groups, rows, group_width = table.shape
    count = own * N_VOCAB
    exp_sums, hit_sums = groups * rows, groups * (rows + count)
    rows_first = groups * (rows + 2 * count)
    for index in range(N_VOCAB):
        at_z, at_y, at_core = index // 8, index // 2 % SIDE, index % 2
        halves = (pieces[0, at_core, at_z, at_y], pieces[1, at_core, at_y, at_z])
        for group in range(groups):
            column = group % 2 * group_width
            table_grads[pl.ds(rows_first + group * count + own * index, own)] = halves[group // 2][
                :, column : column + group_width
            ]

    def rows_in(group):
        return table_grads[pl.ds(rows_first + group * count, count)]

    half_count = count // 2
    lowered_first = groups * (rows + 3 * count)

    def lower(index, values):
        values = values.astype(jnp.bfloat16)
        for side in range(2):
            first = pl.multiple_of(lowered_first + side * rows + index * chunk, 16)
            table_grads[pl.ds(first, chunk)] = values[
                :, side * half_count : (side + 1) * half_count
            ]

    chunk = rows // 4
    base = lax.axis_index("vocab") * rows
    row_iota = lax.broadcasted_iota(jnp.int32, (chunk, count), 0)

    def logit_chunk(index, top):
        at = pl.ds(pl.multiple_of(index * chunk, chunk), chunk)
        total = jnp.zeros((chunk, count), jnp.float32)
        for group in range(groups):
            total += lax.dot_general(
                table[group, at],
                rows_in(group),
                (((1,), (1,)), ((), ())),
                preferred_element_type=jnp.float32,
            )
        total = jnp.where(row_iota + (base + index * chunk) < VOCAB_REAL, total, NEG_FILL)
        logits[at] = total
        return jnp.maximum(top, jnp.max(total, 0, keepdims=True))

    local_top = lax.fori_loop(
        0, 4, logit_chunk, jnp.full((1, count), NEG_FILL, jnp.float32)
    )

    def exp_chunk(index, carry):
        total, pick = carry
        at = pl.ds(pl.multiple_of(index * chunk, chunk), chunk)
        values = logits[at]
        hits = row_iota + (base + index * chunk) == target
        pick += jnp.sum(jnp.where(hits, values, 0.0), 0, keepdims=True)
        values = jnp.exp(values - local_top)
        logits[at] = values
        lower(index, values)
        return total + jnp.sum(values, 0, keepdims=True), pick

    zero_row = jnp.zeros((1, count), jnp.float32)
    local_total, pick = lax.fori_loop(0, 4, exp_chunk, (zero_row, zero_row))
    lanes = count // 4
    top = jnp.concatenate([local_top[:, lanes * i : lanes * (i + 1)] for i in range(4)], 0)
    total = jnp.concatenate([local_total[:, lanes * i : lanes * (i + 1)] for i in range(4)], 0)
    mine = stats.at[lax.axis_index("vocab")]
    mine[...] = jnp.concatenate([top, total], 0)
    bundle = wires.bundle()
    for other in vocab_group:
        wires.send_all(mine, mine, other, bundle)
    def table_products(first):
        for side in range(2):
            lowered = table_grads[pl.ds(lowered_first + side * rows, rows)]
            for group in range(groups):
                product = dot_tn(lowered, table[group]).astype(jnp.bfloat16)
                at = pl.ds(first + group * count + half_count * side, half_count)
                table_grads[at] = product

    table_products(exp_sums)

    @pl.loop(0, 4)
    def _(index):
        hits = row_iota + (base + index * chunk) == target
        lower(index, jnp.where(hits, 1.0, 0.0))

    table_products(hit_sums)
    wires.whole(stats.at[pl.ds(0, len(vocab_group))], sibling, bundle).wait()
    top = jnp.max(stats[:, :4], 0)
    total = jnp.sum(stats[:, 4:] * jnp.exp(stats[:, :4] - top[None]), 0)
    log_total = top + jnp.log(total)
    log_total = jnp.concatenate([log_total[i : i + 1] for i in range(4)], 1)
    first_device = (lax.axis_index("vocab") == 0).astype(jnp.float32)
    loss_ref[...] = (first_device * log_total - pick) * counted
    weight = counted / (N_DP * N_VOCAB * own)
    scale = jnp.exp(local_top - log_total) * weight

    def down_rows(values, index):
        return jnp.transpose(
            jnp.broadcast_to(values[:, 128 * index : 128 * index + 128], (128, 128))
        )

    for tile in range(count // 128):
        tile_scale = jnp.concatenate([down_rows(scale, tile)] * 2, 1)
        tile_weight = jnp.concatenate([down_rows(weight, tile)] * 2, 1)
        for group in range(groups):
            at = group * count + 128 * tile
            exp_part = table_grads[pl.ds(exp_sums + at, 128)].astype(jnp.float32)
            hit_part = table_grads[pl.ds(hit_sums + at, 128)].astype(jnp.float32)
            rows_grad = (exp_part * tile_scale - hit_part * tile_weight).astype(jnp.bfloat16)
            part, column = group // 2, group % 2 * group_width
            for index in range(128 // own):
                inner = 128 // own * tile + index
                at_z, at_y, at_core = inner // 8, inner // 2 % SIDE, inner % 2
                first, second = (at_z, at_y) if part == 0 else (at_y, at_z)
                d_rows[part, at_core, first, second, :, column : column + group_width] = (
                    rows_grad[own * index : own * (index + 1)]
                )
    crossing = [
        sends.send(d_rows.at[part, 1 - core], d_sibling.at[part], sibling) for part in range(2)
    ]
    reduce_axes = ((Z, Y), (Y, Z))
    first_rings, second_rings = [], []
    for part in range(2):
        first_axis, second_axis = reduce_axes[part]
        crossing[part].wait_recv()
        for j in range(4):
            add_blocks(d_rows.at[part, core, j], [d_sibling.at[part, j]], 4)
        first_rings.append(
            DirectReduce(
                sends,
                place,
                first_axis,
                lambda j, part=part: d_rows.at[part, core, j],
                4,
                d_first.at[part],
            )
        )
        second_rings.append(
            DirectReduce(
                sends,
                place,
                second_axis,
                lambda j, part=part, k=place[first_axis]: d_rows.at[part, core, k, j],
                1,
                d_second.at[part],
            )
        )
        first_rings[part].start()

    stores = []

    @pl.loop(0, 4)
    def _(index):
        at = pl.ds(pl.multiple_of(index * chunk, chunk), chunk)
        hits = row_iota + (base + index * chunk) == target
        lower(index, logits[at] * scale - jnp.where(hits, weight, 0.0))

    def table_grad(group):
        @pl.loop(0, 4)
        def _(index):
            product = jnp.zeros((chunk, group_width), jnp.float32)
            for side in range(2):
                first = pl.multiple_of(lowered_first + side * rows + index * chunk, 16)
                product += jnp.dot(
                    table_grads[pl.ds(first, chunk)],
                    rows_in(group)[side * half_count : (side + 1) * half_count],
                    preferred_element_type=jnp.float32,
                )
            product = product.astype(jnp.bfloat16)
            table_grads[pl.ds(pl.multiple_of(group * rows + index * chunk, chunk), chunk)] = product

        at = pl.ds(group * rows, rows)
        stores.append(
            pltpu.make_async_copy(table_grads.at[at], table_grad_ref.at[at], local_sems.at[group])
        )
        stores[-1].start()

    table_grad(0)
    table_grad(1)
    for ring, later in zip(first_rings, second_rings):
        ring.finish()
        later.start()
    table_grad(2)
    table_grad(3)
    for part in range(2):
        second_rings[part].arrive()
        first_axis, second_axis = reduce_axes[part]
        total = d_rows[part, core, place[first_axis], place[second_axis]].astype(jnp.float32)
        for step in range(3):
            total += d_second[part, step].astype(jnp.float32)
        d_head_ref[:, part * half_width : (part + 1) * half_width] = total
    return stores, sends


def split(values):
    high = values.astype(jnp.bfloat16)
    return high, (values - high.astype(jnp.float32)).astype(jnp.bfloat16)


def fine_dot(left, right, contract=((1,), (0,))):
    (left_high, left_low), (right_high, right_low) = split(left), split(right)

    def product(one, other):
        return lax.dot_general(
            one, other, (contract, ((), ())), preferred_element_type=jnp.float32
        )

    return product(left_high, right_high) + (
        product(left_high, right_low) + product(left_low, right_high)
    )


def clip_for(squares):
    norm = jnp.sqrt(jnp.full((1, 128), squares, jnp.float32))
    return norm, CLIP_LEVEL / jnp.maximum(norm, CLIP_LEVEL)


def finish_kernel(
    grads_ref,
    small_ref,
    head_grad_ref,
    d_embed_ref,
    left_roots_ref,
    ids_ref,
    loss_ref,
    grads_out_target,
    table_grad_target,
    final_target,
    left_gram_target,
    right_gram_target,
    left_part_target,
    totals_ref,
    grads_out_ref,
    table_grad_ref,
    final_ref,
    left_gram,
    right_gram,
    left_part,
    left_roots,
    sums,
    sibling_in,
    half_a,
    whole_a,
    half_b,
    whole_b,
    whole_c,
    small_sums,
    small_sibling,
    small_a,
    small_b,
    small_c,
    table_sums,
    table_half,
    table_whole,
    embeds,
    ids_all,
    totals_all,
    send_sems,
    recv_sems,
    local_sems,
):
    place = coordinates()
    core = place[CORE]
    across = place[X]
    sibling = moved(place, CORE, 1)
    wires = Wires(send_sems, recv_sems)
    to_sibling, to_owners, to_table, later_sends = (Group(wires, place) for _ in range(4))

    def sums_at(part, k3, first, count):
        return sums.at[pl.ds((SIDE * part + k3) * 32 + first, count)]

    loads = []

    def load(source, target):
        copy = pltpu.make_async_copy(source, target, local_sems.at[len(loads)])
        copy.start()
        loads.append(copy)
        return copy

    width = table_grad_ref.shape[1]
    embed_axes = ((Y, Z), (Z, Y))
    source_part = across // 2
    near = place[Y] * (1 - source_part) + place[Z] * source_part
    far = place[Z] * (1 - source_part) + place[Y] * source_part
    landing = embeds.at[source_part, core, far, 2 * near + across % 2]
    own_columns = pl.ds(pl.multiple_of(across * width, width), width)
    embed_load = load(d_embed_ref.at[:, own_columns], landing)
    third = [place[ORDERS[part][2]] for part in range(3)]
    small_load = load(small_ref.at[core], small_sums)
    block_loads = {}
    for step in (2, 1, 3, 0):
        for part in range(3):
            j = (third[part] + step) % SIDE
            block_loads[part, step] = load(grads_ref.at[part, core, j], sums_at(part, j, 0, 32))
    table_load = load(head_grad_ref, table_sums)
    roots_load = load(left_roots_ref, left_roots)

    ids_all[across] = ids_ref[...]
    line = [
        moved(moved(place, X, step), CORE, side) for step in range(SIDE) for side in range(2)
    ][1:]
    plane = [
        moved(moved(place, Y, step), Z, other) for step in range(SIDE) for other in range(SIDE)
    ][1:]
    greet(line + plane)
    await_greetings(line + plane)
    swaps = []
    for step in (1, 2, 3):
        there = moved(place, X, step)
        columns = pl.ds(pl.multiple_of(there[X] * width, width), width)
        swaps.append(wires.send(d_embed_ref.at[:, columns], landing, there))
    ids_ring = DirectGather(wires, place, X, lambda j: ids_all.at[j])
    ids_ring.start()
    small_crossing = wires.send(small_ref.at[1 - core], small_sibling, sibling)
    crossings = {}
    for step, half in ((2, 0), (2, 1), (1, None), (3, None), (0, None)):
        for part in range(3):
            j = (third[part] + step) % SIDE
            source, target = grads_ref.at[part, 1 - core, j], sibling_in.at[part, j]
            if half is not None:
                source, target = source.at[pl.ds(16 * half, 16)], target.at[pl.ds(16 * half, 16)]
            crossings[part, step, half] = to_sibling.send(source, target, sibling)

    embed_first, embed_second = [], []
    for part in range(2):
        near_axis, far_axis = embed_axes[part]
        embed_first.append(
            RingGather(
                to_owners,
                place,
                near_axis,
                lambda j, part=part, k=place[far_axis]: embeds.at[part, core, k, pl.ds(2 * j, 2)],
                lambda j, h, part=part, k=place[far_axis]: embeds.at[
                    part, core, k, pl.ds(2 * j + h, 1)
                ],
            )
        )
        embed_second.append(
            RingGather(
                later_sends,
                place,
                far_axis,
                lambda j, part=part: embeds.at[part, core, j],
                lambda j, h, part=part: embeds.at[part, core, j, pl.ds(4 * h, 4)],
            )
        )
    first_rings, middle_rings, last_rings = [], [], []
    for part in range(3):

        def at(k3, first, count, part=part):
            return sums_at(part, k3, first, count)

        last_axis, middle_axis, first_axis = ORDERS[part]
        piece, half = block_ring(place, part, 2, at)
        first_rings.append(
            QuarterReduce(
                to_owners, place, first_axis, piece, half, 32, half_a.at[part], whole_a.at[part]
            )
        )
        piece, half = block_ring(place, part, 1, at)
        middle_rings.append(
            RingReduce(
                later_sends, place, middle_axis, piece, half, 8, half_b.at[part], whole_b.at[part]
            )
        )
        piece, _ = block_ring(place, part, 0, at)
        last_rings.append(DirectReduce(later_sends, place, last_axis, piece, 2, whole_c.at[part]))
    table_ring = QuarterReduce(
        to_table,
        place,
        X,
        lambda j: table_sums.at[j],
        lambda j, q: table_sums.at[j, pl.ds(TABLE_CHUNKS // 4 * q, TABLE_CHUNKS // 4)],
        TABLE_CHUNKS,
        table_half,
        table_whole,
    )
    small_rings = [
        DirectReduce(wires, place, Z, lambda j: small_sums.at[j], 16, small_a),
        DirectReduce(
            wires, place, Y, lambda j: small_sums.at[place[Z], pl.ds(4 * j, 4)], 4, small_b
        ),
        DirectReduce(
            wires, place, X, lambda j: small_sums.at[place[Z], pl.ds(4 * place[Y] + j, 1)], 1, small_c
        ),
    ]

    def add_crossing(part, step, half=None):
        j = (third[part] + step) % SIDE
        if not half:
            block_loads[part, step].wait()
        crossings[part, step, half].wait_recv()
        first, count = (0, 32) if half is None else (16 * half, 16)
        landed = sibling_in.at[part, j, pl.ds(first, count)]
        add_blocks(sums_at(part, j, first, count), [landed], count)

    embed_siblings = []

    def share(part, step):
        piece = embeds.at[part, core, (place[embed_axes[part][1]] + step) % SIDE]
        embed_siblings.append(later_sends.send(piece, piece, sibling))

    rows = table_grad_ref.shape[0]
    chunk = rows // 4
    base = lax.axis_index("vocab") * rows
    row_iota = lax.broadcasted_iota(jnp.int32, (chunk, 512), 0)

    def scatter_rows(part, at_core, step):
        at_far = (place[embed_axes[part][1]] + step) % SIDE

        @pl.loop(0, 2)
        def _(pair):
            values = embeds[part, at_core, at_far, pl.ds(4 * pair, 4)].reshape(512, width)
            ids = []
            for which in range(4):
                at_near = 2 * pair + which // 2
                at_z, at_y = (at_far, at_near) if part == 0 else (at_near, at_far)
                inner = (at_z * SIDE + at_y) * 2 + at_core
                ids.append(ids_all[2 * part + which % 2, pl.ds(inner, 1), :])
            ids = jnp.concatenate(ids, 1) - base

            @pl.loop(0, 4)
            def _(row):
                at = pl.ds(pl.multiple_of(row * chunk, chunk), chunk)
                hot = jnp.where(row_iota + row * chunk == ids, 1.0, 0.0).astype(jnp.bfloat16)
                table_grad_ref[at] += jnp.dot(hot, values, preferred_element_type=jnp.float32)

    lead = ((0, core), (1, core))
    orders = ((X, Y, Z), (Y, Z, X))
    gathers = []
    for phase in range(3):
        row = []
        for part in range(2):
            _, second_axis, third_axis = orders[part]
            keys = (place[third_axis], place[second_axis])[: 2 - phase]
            row.append(
                DirectGather(
                    wires,
                    place,
                    orders[part][phase],
                    lambda j, key=lead[part] + keys: final_ref.at[key + (j,)],
                )
            )
        gathers.append(row)

    for part in range(3):
        add_crossing(part, 2, 0)
        first_rings[part].start(0)
    for copy in swaps:
        copy.wait_recv()
    embed_load.wait()
    for ring in embed_first:
        ring.start()
    table_load.wait()
    table_ring.start(0)
    table_ring.start(1)
    small_load.wait()
    small_crossing.wait_recv()
    for j in range(4):
        add_blocks(small_sums.at[j], [small_sibling.at[j]], 16)
    small_rings[0].start()
    for part in range(3):
        add_crossing(part, 2, 1)
    for ring in embed_first:
        ring.forward()
    for part in range(3):
        first_rings[part].start(1)
    for part in range(3):
        add_crossing(part, 1)
    for ring, later in zip(embed_first, embed_second):
        ring.finish()
        later.start()
    small_rings[0].finish()
    small_rings[1].start()
    share(0, 0)
    share(1, 0)
    for part in range(3):
        add_crossing(part, 3)
    for part in range(3):
        first_rings[part].start_near()
    table_ring.start_near()
    ids_ring.finish()

    @pl.loop(0, 4)
    def _(index):
        at = pl.ds(pl.multiple_of(index * chunk, chunk), chunk)
        table_grad_ref[at] = jnp.zeros((chunk, width), jnp.float32)

    scatter_rows(0, core, 0)
    scatter_rows(1, core, 0)
    for ring in first_rings:
        ring.forward()
    for part in range(3):
        add_crossing(part, 0)
    for copy in embed_siblings:
        copy.wait_recv()
    embed_siblings.clear()
    scatter_rows(0, 1 - core, 0)
    scatter_rows(1, 1 - core, 0)
    for part in range(2):
        embed_second[part].forward()
        share(part, 1)
        share(part, 3)
    small_rings[1].finish()
    small_rings[2].start()
    table_ring.forward()
    for part in range(2):
        scatter_rows(part, core, 1)
        scatter_rows(part, core, 3)
    for copy in embed_siblings:
        copy.wait_recv()
    embed_siblings.clear()
    for part in range(2):
        scatter_rows(part, 1 - core, 1)
        scatter_rows(part, 1 - core, 3)
    to_sibling.settle(sums)
    for ring, later in zip(first_rings, middle_rings):
        ring.finish()
        later.start()
    small_rings[2].finish()
    own_small = small_sums[place[Z], 4 * place[Y] + across].astype(jnp.float32)
    final_ref[0, core, place[Z], place[Y], across] = own_small[:8]
    final_ref[1, core, across, place[Z], place[Y]] = jnp.concatenate(
        [own_small[8:9], jnp.zeros((7, 128), jnp.float32)], 0
    )
    for gather in gathers[0]:
        gather.start()
    for part in range(2):
        embed_second[part].finish()
        share(part, 2)
    scatter_rows(0, core, 2)
    for ring in middle_rings:
        ring.forward()
    for gather, later in zip(gathers[0], gathers[1]):
        gather.finish()
        later.start()
    scatter_rows(1, core, 2)
    for copy in embed_siblings:
        copy.wait_recv()
    scatter_rows(0, 1 - core, 2)
    to_owners.settle(sums)
    wires.settle(6)
    for ring, later in zip(middle_rings, last_rings):
        ring.finish()
        later.start()
    for gather, later in zip(gathers[1], gathers[2]):
        gather.finish()
        later.start()
    scatter_rows(1, 1 - core, 2)
    table_ring.arrive()
    table_block = rows // TABLE_CHUNKS

    @pl.loop(0, TABLE_CHUNKS)
    def _(index):
        at = pl.ds(pl.multiple_of(index * table_block, table_block), table_block)
        table_grad_ref[at] += (
            table_sums[across, index].astype(jnp.float32)
            + table_whole[0, index].astype(jnp.float32)
            + table_whole[1, index].astype(jnp.float32)
        )

    table_squares = jnp.zeros((1, width), jnp.float32)
    for index in range(4):
        values = table_grad_ref[index * chunk : (index + 1) * chunk]
        table_squares += jnp.sum(values * values, 0, keepdims=True)
    squares = jnp.zeros((1, 128), jnp.float32)
    to_table.settle(sums)
    for part in range(3):
        last_rings[part].arrive()
        k1, k2, k3 = (place[axis] for axis in ORDERS[part])
        for which in range(2):
            total = sums_at(part, k3, 8 * k2 + 2 * k1 + which, 1)[0].astype(jnp.float32)
            for step in range(3):
                total += whole_c[part, step, which].astype(jnp.float32)
            grads_out_ref[part, which] = total
            squares += jnp.sum(total * total, 0, keepdims=True)
    final_siblings = []
    for part in range(2):
        gathers[2][part].finish()
        mine = final_ref.at[part, core]
        final_siblings.append(wires.send(mine, mine, sibling))
    stores = []

    def store(source, target):
        stores.append(pltpu.make_async_copy(source, target, local_sems.at[17 + len(stores)]))
        stores[-1].start()

    own_clip = clip_for(jnp.sum(squares))[1]
    squares += table_squares[:, :128] + table_squares[:, 128:]
    roots_load.wait()

    def products(slots):
        for slot in slots:
            grad = grads_out_ref[slot // 2, slot % 2] * own_clip
            left_gram[slot] = fine_dot(grad, grad, ((1,), (1,)))
            right_gram[slot] = fine_dot(grad, grad, ((0,), (0,)))
            left_part[slot] = fine_dot(left_roots[slot], grad)

    store(table_grad_ref, table_grad_target)
    store(grads_out_ref, grads_out_target)
    loss = sum(loss_ref[:, 128 * index : 128 * (index + 1)] for index in range(4))
    totals = jnp.concatenate([squares, loss, jnp.zeros((6, 128), jnp.float32)], 0)
    for copy in final_siblings:
        copy.wait_recv()
    store(final_ref, final_target)
    for phase, (own, others) in enumerate(
        ((2 * across + core, line), (SIDE * place[Z] + place[Y], plane))
    ):
        mine = totals_all.at[phase, own]
        mine[...] = totals
        bundle = wires.bundle()
        for other in others:
            wires.send_all(mine, mine, other, bundle)
        products(range(3 * phase, 3 * phase + 3))
        wires.whole(totals_all.at[phase, pl.ds(0, len(others))], sibling, bundle).wait()
        totals = totals_all[phase, 0]
        for index in range(1, len(others) + 1):
            totals += totals_all[phase, index]
    totals_ref[...] = totals
    store(left_gram, left_gram_target)
    store(right_gram, right_gram_target)
    store(left_part, left_part_target)
    later_sends.settle(sums)
    wires.settle()
    for copy in stores:
        copy.wait()


def finish_call(grads, small, head_grad, d_embed, left_roots, token_ids, loss_row):
    bf16 = jnp.bfloat16
    _, chunks, chunk_rows, width = head_grad.shape
    rows = chunks * chunk_rows
    block = (BLOCK, BLOCK)
    return pl.pallas_call(
        finish_kernel,
        name="reduce_and_scatter",
        out_shape=(
            jax.ShapeDtypeStruct((3, 2) + block, jnp.float32),
            jax.ShapeDtypeStruct((rows, width), jnp.float32),
            jax.ShapeDtypeStruct((2, 2, SIDE, SIDE, SIDE, 8, 128), jnp.float32),
            *[jax.ShapeDtypeStruct(left_roots.shape, jnp.float32)] * 3,
            jax.ShapeDtypeStruct((8, 128), jnp.float32),
        ),
        in_specs=[ANY] * 5 + [VMEM] * 2,
        out_specs=(ANY,) * 6 + (VMEM,),
        scratch_shapes=[
            pltpu.VMEM((3, 2) + block, jnp.float32),
            pltpu.VMEM((rows, width), jnp.float32),
            pltpu.VMEM((2, 2, SIDE, SIDE, SIDE, 8, 128), jnp.float32),
            *[pltpu.VMEM(left_roots.shape, jnp.float32)] * 4,
            pltpu.VMEM((3 * SIDE * 32,) + block, bf16),
            pltpu.VMEM((3, SIDE, 32) + block, bf16),
            pltpu.VMEM((3, 2, 16) + block, bf16),
            pltpu.VMEM((3, 2, 32) + block, bf16),
            pltpu.VMEM((3, 2, 4) + block, bf16),
            pltpu.VMEM((3, 2, 8) + block, bf16),
            pltpu.VMEM((3, 3, 2) + block, bf16),
            pltpu.VMEM((SIDE, 16, 16, 128), bf16),
            pltpu.VMEM((SIDE, 16, 16, 128), bf16),
            pltpu.VMEM((3, 16, 16, 128), bf16),
            pltpu.VMEM((3, 4, 16, 128), bf16),
            pltpu.VMEM((3, 1, 16, 128), bf16),
            pltpu.VMEM(head_grad.shape, bf16),
            pltpu.VMEM((2, chunks // 2, chunk_rows, width), bf16),
            pltpu.VMEM((2, chunks, chunk_rows, width), bf16),
            pltpu.VMEM((2, 2, SIDE, 8, 128, width), bf16),
            pltpu.VMEM((N_DP,) + token_ids.shape, jnp.int32),
            pltpu.VMEM((2, SIDE * SIDE, 8, 128), jnp.float32),
            pltpu.SemaphoreType.DMA((42,)),
            pltpu.SemaphoreType.DMA((146,)),
            pltpu.SemaphoreType.DMA((23,)),
        ],
        compiler_params=pltpu.CompilerParams(
            collective_id=3, has_side_effects=True, vmem_limit_bytes=VMEM_BYTES
        ),
    )(grads, small, head_grad, d_embed, left_roots, token_ids, loss_row)


def row_mean(values):
    return jnp.mean(values, -1, keepdims=True)


def normalized(values):
    center = values - row_mean(values)
    scale = lax.rsqrt(row_mean(center * center) + LN_EPS)
    return center * scale, scale


def norm_backward(d_normed, hat, scale, gain):
    d_hat = d_normed * gain
    d_values = scale * (d_hat - row_mean(d_hat) - hat * row_mean(d_hat * hat))
    d_gain = jnp.sum(d_normed * hat, 0, keepdims=True)
    return d_values, d_gain, jnp.sum(d_normed, 0, keepdims=True)


QKV, PROJ, FC, OUT = (0, 24), (192, 8), (256, 32), (512, 8)


def load_blocks(full_ref, blocks, sems):
    share = blocks.shape[0] // 8
    copies = []
    for index in range(8):
        part = pl.ds(index * share, share)
        copies.append(pltpu.make_async_copy(full_ref.at[part], blocks.at[part], sems.at[index]))
        copies[-1].start()
    return copies


def weight_tiles(blocks, where_ref, matrix, row, rows, column, columns):
    first, in_row = matrix
    return jnp.concatenate(
        [
            jnp.concatenate(
                [
                    blocks[where_ref[first + (row + i) * in_row + column + j]]
                    for j in range(columns)
                ],
                1,
            )
            for i in range(rows)
        ],
        0,
    )


def selected_rows(ref, positions):
    return jnp.concatenate([ref[pl.ds(position, 1), :] for position in positions], 0)


def pair_masks(count):
    lane = lax.broadcasted_iota(jnp.int32, (2 * count, 2 * HEAD_DIM), 1)
    row = lax.broadcasted_iota(jnp.int32, (2 * count, 2 * HEAD_DIM), 0)
    return (lane < HEAD_DIM) == (row < count)


def doubled(values, own_lanes):
    both = jnp.concatenate([values, values], 0)
    return jnp.where(own_lanes, both.astype(jnp.float32), 0.0).astype(jnp.bfloat16)


def folded(values, count):
    lane = lax.broadcasted_iota(jnp.int32, (count, 2 * HEAD_DIM), 1)
    return jnp.where(lane < HEAD_DIM, values[:count], values[count:])


def forward_phase(
    where_ref,
    at_ref,
    length_ref,
    hidden_ref,
    vec_ref,
    head_in_ref,
    query_ref,
    kv_ref,
    probs_ref,
    attended_ref,
    middle_ref,
    pre_act_ref,
    last_ref,
    blocks,
    normed_rows,
    activated,
):
    count = head_in_ref.shape[0]
    bf16 = jnp.bfloat16
    own = lax.axis_index("vocab")
    positions = [at_ref[i, own] for i in range(count)]
    length = length_ref[own]
    hat, _ = normalized(hidden_ref[...])
    normed_rows[...] = hat * vec_ref[0:1] + vec_ref[1:2]
    normed_one = normed_rows[...].astype(bf16)
    normed_own = selected_rows(normed_rows, positions).astype(bf16)

    @pl.loop(0, 4)
    def _(tile):
        at = lane_range(256 * tile, 256)
        weight = weight_tiles(blocks, where_ref, QKV, 0, 8, 2 * tile, 2)
        product = jnp.dot(normed_own, weight, preferred_element_type=jnp.float32)
        query_ref[:, at] = (product + vec_ref[2:3, at]).astype(bf16)

    @pl.loop(0, 4)
    def _(tile):
        at = lane_range(256 * tile, 256)
        weight = weight_tiles(blocks, where_ref, QKV, 0, 8, 8 + 2 * tile, 2)
        product = jnp.dot(normed_one, weight, preferred_element_type=jnp.float32)
        kv_ref[:, at] = product.astype(bf16)

    @pl.loop(0, 4)
    def _(tile):
        weight = weight_tiles(blocks, where_ref, QKV, 0, 8, 16 + 2 * tile, 2)
        product = jnp.dot(normed_one, weight, preferred_element_type=jnp.float32)
        bias = vec_ref[3:4, lane_range(256 * tile, 256)]
        kv_ref[:, lane_range(D + 256 * tile, 256)] = (product + bias).astype(bf16)

    own_lanes = pair_masks(count)
    pairs = HEADS // 2
    seq_len = hidden_ref.shape[0]
    row = lax.broadcasted_iota(jnp.int32, (count, seq_len), 0)
    key = lax.broadcasted_iota(jnp.int32, (count, seq_len), 1)
    last_key = jnp.zeros((count, seq_len), jnp.int32)
    for i in range(count):
        last_key = jnp.where(row == i, jnp.minimum(positions[i], length - 1), last_key)
    allowed = jnp.concatenate([key <= last_key] * 2, 0)
    for pair in range(pairs):
        lanes = slice(128 * pair, 128 * pair + 128)
        values_at = slice(D + 128 * pair, D + 128 * pair + 128)
        scores = dot_nt(doubled(query_ref[:, lanes], own_lanes), kv_ref[:, lanes]) * HEAD_DIM ** (
            -0.5
        )
        scores = jnp.where(allowed, scores, NEG_FILL)
        exps = jnp.exp(scores - jnp.max(scores, -1, keepdims=True))
        probs = exps / jnp.sum(exps, -1, keepdims=True)
        probs_ref[2 * count * pair : 2 * count * (pair + 1)] = probs
        mixed = jnp.dot(
            probs.astype(bf16), kv_ref[:, values_at], preferred_element_type=jnp.float32
        )
        attended_ref[:, lanes] = folded(mixed, count).astype(bf16)

    attended = attended_ref[...]
    middle_ref[...] = selected_rows(hidden_ref, positions) + vec_ref[4:5]

    @pl.loop(0, 4)
    def _(tile):
        weight = weight_tiles(blocks, where_ref, PROJ, 0, 8, 2 * tile, 2)
        middle_ref[:, lane_range(256 * tile, 256)] += jnp.dot(
            attended, weight, preferred_element_type=jnp.float32
        )

    middle = middle_ref[...]
    hat, _ = normalized(middle)
    normed_two = (hat * vec_ref[5:6] + vec_ref[6:7]).astype(bf16)

    @pl.loop(0, 16)
    def _(tile):
        at = lane_range(256 * tile, 256)
        weight = weight_tiles(blocks, where_ref, FC, 0, 8, 2 * tile, 2)
        bias = vec_ref[pl.ds(7 + tile // 4, 1), lane_range(256 * (tile % 4), 256)]
        pre_act = jnp.dot(normed_two, weight, preferred_element_type=jnp.float32) + bias
        pre_act_ref[:, at] = pre_act
        activated[:, at] = gelu(pre_act).astype(bf16)

    last_ref[...] = middle + vec_ref[11:12]

    @pl.loop(0, 16)
    def _(index):
        tile, depth = index // 4, index % 4
        weight = weight_tiles(blocks, where_ref, OUT, 8 * depth, 8, 2 * tile, 2)
        last_ref[:, lane_range(256 * tile, 256)] += jnp.dot(
            activated[:, lane_range(1024 * depth, 1024)],
            weight,
            preferred_element_type=jnp.float32,
        )

    hat, _ = normalized(last_ref[...])
    head_in_ref[...] = (hat * vec_ref[12:13] + vec_ref[13:14]).astype(bf16)


def forward_kernel(
    where_ref,
    at_smem_ref,
    length_smem_ref,
    ids_ref,
    target_ref,
    at_ref,
    length_ref,
    *refs,
):
    sources, refs = refs[:4], refs[4:]
    (full_ref, out_blocks_ref), targets, refs = refs[:2], refs[2:10], refs[10:]
    (d_head_ref, table_grad_ref, loss_ref), refs = refs[:3], refs[3:]
    held, kept, refs = refs[:4], refs[4:12], refs[12:]
    matrices_ref, table_ref, positions_ref, vec_ref = held
    (
        hidden_ref,
        query_ref,
        kv_ref,
        probs_ref,
        attended_ref,
        middle_ref,
        pre_act_ref,
        last_ref,
    ) = kept
    (
    blocks,
    table,
    own_low,
    table_pad,
    ids_all,
    parts,
    sibling_in,
    half_in,
    whole_in,
    landing,
    ready,
    arrived,
    normed_rows,
    activated,
    head_in,
    pieces,
    logits,
    stats,
    d_rows,
    d_sibling,
    d_first,
    d_second,
    out_staging,
    send_sems,
    recv_sems,
    local_sems,
    ) = refs
    place = coordinates()
    wires = Wires(send_sems, recv_sems)
    loads = [
        pltpu.make_async_copy(source, target, local_sems.at[5 + index])
        for index, (source, target) in enumerate(zip(sources, held))
    ]
    for copy in loads:
        copy.start()
    vocab_group = [
        moved(moved(moved(place, Y, near), Z, far), CORE, side)
        for near in range(SIDE)
        for far in range(SIDE)
        for side in range(2)
    ][1:]
    others = vocab_group + [moved(place, X, step) for step in (1, 2, 3)]
    greet(others)
    for copy in loads:
        copy.wait()
    table_ring = gather_phase(
        place,
        wires,
        others,
        ids_ref,
        matrices_ref,
        table_ref,
        positions_ref,
        blocks,
        table,
        hidden_ref,
        own_low,
        table_pad,
        ids_all,
        parts,
        sibling_in,
        half_in,
        whole_in,
        landing,
        ready,
        arrived,
        local_sems,
    )
    keep = pltpu.make_async_copy(blocks, full_ref, local_sems.at[4])
    keep.start()
    forward_phase(
        where_ref,
        at_smem_ref,
        length_smem_ref,
        hidden_ref,
        vec_ref,
        head_in,
        query_ref,
        kv_ref,
        probs_ref,
        attended_ref,
        middle_ref,
        pre_act_ref,
        last_ref,
        blocks,
        normed_rows,
        activated,
    )
    keeps = [keep]
    for index, (source, target) in enumerate(zip(kept, targets)):
        keeps.append(pltpu.make_async_copy(source, target, local_sems.at[9 + index]))
        keeps[-1].start()

    def arrange_out(chunk):
        if chunk >= 2:
            keeps[len(keeps) - 2].wait()
            del keeps[len(keeps) - 2]
        slot = out_staging.at[chunk % 2]

        @pl.loop(0, 16, unroll=4)
        def _(index):
            slot[index] = blocks[where_ref[OUT[0] + 16 * chunk + index]]

        target = out_blocks_ref.at[pl.ds(16 * chunk, 16)]
        keeps.append(pltpu.make_async_copy(slot, target, local_sems.at[17 + chunk % 2]))
        keeps[-1].start()

    stores, sends = head_phase(
        place,
        wires,
        vocab_group,
        table_ring,
        head_in,
        table,
        target_ref,
        at_ref,
        length_ref,
        d_head_ref,
        table_grad_ref,
        loss_ref,
        parts,
        pieces,
        logits,
        stats,
        d_rows,
        d_sibling,
        d_first,
        d_second,
        local_sems,
        arrange_out,
    )
    sends.settle(blocks)
    for copy in keeps + stores:
        copy.wait()


def forward_call(where, positions, lengths, token_ids, target_ids, matrices, vocab_table, positions_table, vectors):
    rows, width = vocab_table.shape
    padded = -(-rows // 128) * 128
    own, seqs = positions.shape
    seq_len = positions_table.shape[0]
    count, half = own * seqs, D // 2
    bf16, f32 = jnp.bfloat16, jnp.float32
    shape = jax.ShapeDtypeStruct
    slots = where.shape[0]
    cache = (
        shape((seq_len, D), f32),
        shape((own, D), bf16),
        shape((seq_len, 2 * D), bf16),
        shape((HEADS * own, seq_len), f32),
        shape((own, D), bf16),
        shape((own, D), f32),
        shape((own, FF), f32),
        shape((own, D), f32),
    )
    states = (matrices, vocab_table, positions_table, vectors)
    smem = pl.BlockSpec(memory_space=pltpu.SMEM)
    return pl.pallas_call(
        forward_kernel,
        name="forward_and_head",
        out_shape=(
            shape((slots, BLOCK, BLOCK), bf16),
            shape((slots // 3, BLOCK, BLOCK), bf16),
            *cache,
            shape((own, D), f32),
            shape((N_DP * rows, width), bf16),
            shape((1, count), f32),
        ),
        in_specs=[smem] * 3 + [VMEM] * 4 + [ANY] * 4,
        out_specs=(ANY,) * 10 + (VMEM, ANY, VMEM),
        scratch_shapes=[
            *[pltpu.VMEM(array.shape, array.dtype) for array in (*states, *cache)],
            pltpu.VMEM((slots, BLOCK, BLOCK), bf16),
            pltpu.VMEM((N_DP, rows, width), bf16),
            pltpu.VMEM((3, 2, BLOCK, BLOCK), bf16),
            pltpu.VMEM((padded, width), bf16),
            pltpu.VMEM((N_DP,) + token_ids.shape, jnp.int32),
            pltpu.VMEM((128 * 128, width), bf16),
            pltpu.VMEM((2, 32 * 128, width), bf16),
            pltpu.VMEM((2, 2, 4 * 128, width), bf16),
            pltpu.VMEM((2, 2, 8 * 128, width), bf16),
            pltpu.VMEM((2, 3, 2 * 128, width), bf16),
            pltpu.VMEM((N_DP, 128, width), bf16),
            pltpu.VMEM((N_DP, 128, width), bf16),
            pltpu.VMEM((seq_len, D), f32),
            pltpu.VMEM((own, FF), bf16),
            pltpu.VMEM((own, D), bf16),
            pltpu.VMEM((2, 2, SIDE, SIDE, own, half), bf16),
            pltpu.VMEM((rows, count), f32),
            pltpu.VMEM((N_VOCAB, 8, count // 4), f32),
            pltpu.VMEM((2, 2, SIDE, SIDE, own, half), bf16),
            pltpu.VMEM((2, SIDE, SIDE, own, half), bf16),
            pltpu.VMEM((2, 3, SIDE, own, half), bf16),
            pltpu.VMEM((2, 3, own, half), bf16),
            pltpu.VMEM((2, 16, BLOCK, BLOCK), bf16),
            pltpu.SemaphoreType.DMA((21,)),
            pltpu.SemaphoreType.DMA((123,)),
            pltpu.SemaphoreType.DMA((19,)),
        ],
        compiler_params=pltpu.CompilerParams(
            collective_id=1, has_side_effects=True, vmem_limit_bytes=VMEM_BYTES
        ),
    )(
        where,
        positions,
        lengths,
        token_ids,
        target_ids,
        positions,
        lengths.reshape(1, -1),
        *states,
    )


def gelu_slope(values):
    cube = 0.044715 * values * values
    bent = jnp.tanh(GELU_C * (values + cube * values))
    return 0.5 * (1.0 + bent) + 0.5 * values * (1.0 - bent * bent) * GELU_C * (1.0 + 3.0 * cube)


def backward_kernel(
    where_ref,
    at_ref,
    full_ref,
    out_blocks_ref,
    *refs,
):
    sources, (grads_ref, small_ref, d_embed_ref), refs = refs[:10], refs[10:13], refs[13:]
    held, refs = refs[:10], refs[10:]
    (
        d_head_ref,
        last_ref,
        vec_ref,
        pre_act_ref,
        middle_ref,
        attended_ref,
        query_ref,
        kv_ref,
        probs_ref,
        hidden_ref,
    ) = held
    (
    blocks,
    grad_blocks,
    activated,
    d_pre,
    normed,
    rows_out,
    d_qkv,
    spread,
    query_grads,
    vec_grads,
    sems,
    grad_sem,
    ) = refs
    loads = [
        pltpu.make_async_copy(source, target, sems.at[9 + index])
        for index, (source, target) in enumerate(zip(sources, held))
    ]
    for copy in loads:
        copy.start()
    out_blocks = grad_blocks.at[pl.ds(0, out_blocks_ref.shape[0])]
    out_load = pltpu.make_async_copy(out_blocks_ref, out_blocks, sems.at[8])
    out_load.start()
    copies = load_blocks(full_ref, blocks, sems)
    for copy in loads:
        copy.wait()
    count = d_head_ref.shape[0]
    bf16 = jnp.bfloat16
    own = lax.axis_index("vocab")
    positions = [at_ref[i, own] for i in range(count)]

    def weight_grad(matrix, rows, left_ref, right, together=4):
        first, in_row = matrix

        @pl.loop(0, rows // together)
        def _(group):
            left = left_ref[:, lane_range(128 * together * group, 128 * together)]
            for column in range(0, in_row, 2):
                product = dot_tn(left, right[:, 128 * column : 128 * column + 256]).astype(bf16)
                for inner in range(2 * together):
                    row, side = inner // 2, inner % 2
                    index = first + (group * together + row) * in_row + column + side
                    grad_blocks[index] = product[
                        128 * row : 128 * row + 128, 128 * side : 128 * side + 128
                    ]
                    pltpu.make_async_copy(
                        grad_blocks.at[index], grads_ref.at[where_ref[index]], grad_sem
                    ).start()

    hat, scale = normalized(last_ref[...])
    d_last, vec_grads[12:13], vec_grads[13:14] = norm_backward(
        d_head_ref[...], hat, scale, vec_ref[12:13]
    )
    d_branch = d_last.astype(bf16)
    vec_grads[11:12] = jnp.sum(d_branch.astype(jnp.float32), 0, keepdims=True)
    activated[...] = gelu(pre_act_ref[...]).astype(bf16)
    weight_grad(OUT, 32, activated, d_branch)
    out_load.wait()

    @pl.loop(0, 16)
    def _(tile):
        at = lane_range(256 * tile, 256)
        weight = jnp.concatenate(
            [
                jnp.concatenate([out_blocks[16 * tile + 8 * row + j] for j in range(8)], 1)
                for row in range(2)
            ],
            0,
        )
        lowered = (dot_nt(d_branch, weight) * gelu_slope(pre_act_ref[:, at])).astype(bf16)
        d_pre[:, at] = lowered
        vec_grads[pl.ds(7 + tile // 4, 1), lane_range(256 * (tile % 4), 256)] = jnp.sum(
            lowered.astype(jnp.float32), 0, keepdims=True
        )

    hat, scale = normalized(middle_ref[...])
    normed[pl.ds(0, count)] = (hat * vec_ref[5:6] + vec_ref[6:7]).astype(bf16)
    weight_grad(FC, 8, normed.at[pl.ds(0, count)], d_pre[...])
    rows_out[...] = jnp.zeros(rows_out.shape, jnp.float32)
    for copy in copies:
        copy.wait()

    @pl.loop(0, 16)
    def _(index):
        tile, depth = index // 4, index % 4
        weight = weight_tiles(blocks, where_ref, FC, 2 * tile, 2, 8 * depth, 8)
        rows_out[pl.ds(0, count), lane_range(256 * tile, 256)] += dot_nt(
            d_pre[:, lane_range(1024 * depth, 1024)], weight
        )

    d_middle, vec_grads[5:6], vec_grads[6:7] = norm_backward(
        rows_out[pl.ds(0, count)], hat, scale, vec_ref[5:6]
    )
    d_middle = d_middle + d_last
    d_proj = d_middle.astype(bf16)
    vec_grads[4:5] = jnp.sum(d_proj.astype(jnp.float32), 0, keepdims=True)
    weight_grad(PROJ, 8, attended_ref, d_proj)

    @pl.loop(0, 4)
    def _(tile):
        weight = weight_tiles(blocks, where_ref, PROJ, 2 * tile, 2, 0, 8)
        rows_out[pl.ds(0, count), lane_range(256 * tile, 256)] = dot_nt(d_proj, weight)

    own_lanes = pair_masks(count)
    spread[...] = jnp.zeros(spread.shape, jnp.float32)
    for pair in range(HEADS // 2):
        lanes = slice(128 * pair, 128 * pair + 128)
        values_at = slice(D + 128 * pair, D + 128 * pair + 128)
        d_mixed = doubled(rows_out[0:count, lanes].astype(bf16), own_lanes)
        probs = probs_ref[2 * count * pair : 2 * count * (pair + 1)]
        d_probs = dot_nt(d_mixed, kv_ref[:, values_at])
        inner = jnp.sum(probs * d_probs, -1, keepdims=True)
        d_scores = (probs * (d_probs - inner)).astype(bf16)
        d_values = dot_tn(probs.astype(bf16), d_mixed).astype(bf16)
        d_keys = dot_tn(d_scores, doubled(query_ref[:, lanes], own_lanes)) * HEAD_DIM ** (-0.5)
        d_query = jnp.dot(d_scores, kv_ref[:, lanes], preferred_element_type=jnp.float32)
        d_query = (folded(d_query, count) * HEAD_DIM ** (-0.5)).astype(bf16).astype(jnp.float32)
        vec_grads[2:3, lanes] = jnp.sum(d_query, 0, keepdims=True)
        vec_grads[3:4, lanes] = jnp.sum(d_values.astype(jnp.float32), 0, keepdims=True)
        query_grads[:, lanes] = d_query
        d_qkv[:, D + 128 * pair : D + 128 * pair + 128] = d_keys.astype(bf16)
        d_qkv[:, 2 * D + 128 * pair : 2 * D + 128 * pair + 128] = d_values
    for i in range(count):
        spread[pl.ds(positions[i], 1), :] = query_grads[i : i + 1, :]
    d_qkv[:, :D] = spread[...].astype(bf16)
    hat, scale = normalized(hidden_ref[...])
    normed[...] = (hat * vec_ref[0:1] + vec_ref[1:2]).astype(bf16)
    weight_grad(QKV, 8, normed, d_qkv)
    rows_out[...] = jnp.zeros(rows_out.shape, jnp.float32)

    @pl.loop(0, 12)
    def _(index):
        tile, depth = index // 3, index % 3
        weight = weight_tiles(blocks, where_ref, QKV, 2 * tile, 2, 8 * depth, 8)
        rows_out[:, lane_range(256 * tile, 256)] += dot_nt(
            d_qkv[:, lane_range(1024 * depth, 1024)], weight
        )

    d_hidden, vec_grads[0:1], vec_grads[1:2] = norm_backward(
        rows_out[...], hat, scale, vec_ref[0:1]
    )
    rows_out[...] = d_hidden
    for i in range(count):
        rows_out[pl.ds(positions[i], 1), :] += d_middle[i : i + 1]
    d_embed_ref[...] = rows_out[...].astype(bf16)
    vec_rows = vec_ref.shape[0]
    for index in range(small_ref.shape[0]):
        group, tile = index // 8, index % 8
        lanes = slice(128 * tile, 128 * tile + 128)
        vec_row = (
            vec_grads[group : group + 1, lanes]
            if group < vec_rows
            else jnp.zeros((1, 128), jnp.float32)
        )
        small_ref[index] = jnp.concatenate(
            [rows_out[8 * group : 8 * group + 8, lanes], vec_row, jnp.zeros((7, 128), jnp.float32)],
            0,
        ).astype(bf16)
    pltpu.make_async_copy(grad_blocks, grads_ref, grad_sem).wait()


def backward_call(where, positions, full, out_blocks, states):
    count = positions.shape[0]
    hidden = states[-1]
    bf16 = jnp.bfloat16
    shape = jax.ShapeDtypeStruct
    return pl.pallas_call(
        backward_kernel,
        name="layer_backward",
        out_shape=(
            shape(full.shape, bf16),
            shape((N_DP * N_VOCAB, 16, 128), bf16),
            shape(hidden.shape, bf16),
        ),
        grid_spec=pltpu.PrefetchScalarGridSpec(
            num_scalar_prefetch=2,
            grid=(),
            in_specs=[ANY] * 12,
            out_specs=(ANY, VMEM, VMEM),
            scratch_shapes=[
                *[pltpu.VMEM(array.shape, array.dtype) for array in states],
                pltpu.VMEM(full.shape, bf16),
                pltpu.VMEM(full.shape, bf16),
                pltpu.VMEM((count, FF), bf16),
                pltpu.VMEM((count, FF), bf16),
                pltpu.VMEM(hidden.shape, bf16),
                pltpu.VMEM(hidden.shape, jnp.float32),
                pltpu.VMEM((hidden.shape[0], 3 * D), bf16),
                pltpu.VMEM(hidden.shape, jnp.float32),
                pltpu.VMEM((count, D), jnp.float32),
                pltpu.VMEM((16, D), jnp.float32),
                pltpu.SemaphoreType.DMA((19,)),
                pltpu.SemaphoreType.DMA,
            ],
        ),
        compiler_params=pltpu.CompilerParams(vmem_limit_bytes=VMEM_BYTES),
    )(where, positions, full, out_blocks, *states)


def adam_step(weight, moment_one, moment_two, grad_in, rate, decay):
    new_one = BETA_ONE * moment_one + (1.0 - BETA_ONE) * grad_in
    new_two = BETA_TWO * moment_two + (1.0 - BETA_TWO) * grad_in * grad_in
    hat_one = new_one * (1.0 / (1.0 - BETA_ONE**STEP))
    hat_two = new_two * (1.0 / (1.0 - BETA_TWO**STEP))
    change = hat_one / (jnp.sqrt(hat_two) + ADAM_EPS)
    if decay:
        change = change + decay * weight
    return weight - rate * change, new_one, new_two


TABLE_PIECES = 2


def update_kernel(*refs):
    names = 20
    sources, (loss_ref, norm_ref, *targets) = refs[:names], refs[names : names + 15]
    buffers = refs[names + 15 : 2 * names + 15]
    results = refs[2 * names + 15 : 2 * names + 28]
    vec_grad, load_sems, store_sems = refs[2 * names + 28 :]
    loads, stores = [], []

    def load(index, at=None):
        source, target = sources[index], buffers[index]
        if at is not None:
            source, target = source.at[at], target.at[at]
        loads.append(pltpu.make_async_copy(source, target, load_sems.at[len(loads)]))
        loads[-1].start()

    def store(index, at=None):
        source, target = results[index], targets[index]
        if at is not None:
            source, target = source.at[at], target.at[at]
        stores.append(pltpu.make_async_copy(source, target, store_sems.at[len(stores)]))
        stores[-1].start()

    def await_loads(count):
        for copy in loads[:count]:
            copy.wait()
        del loads[:count]

    totals, final, table_grad, table, table_m, table_v = buffers[:6]
    grads, left_gram, right_gram, left_part = buffers[6:10]
    matrices, left_stats, right_stats, right_roots = buffers[10:14]
    positions, pos_m, pos_v, vectors, vectors_m, vectors_v = buffers[14:]
    matrices_new, left_new, right_new, matrices_grad = results[:4]
    rows, width = table.shape
    chunk = rows // TABLE_PIECES
    for index in range(2):
        load(index)
    for piece in range(TABLE_PIECES):
        for index in range(2, 6):
            load(index, pl.ds(piece * chunk, chunk))
    for index in range(6, names):
        load(index)
    await_loads(2)
    row_squares = jnp.zeros((8, 128), jnp.float32)
    for part in range(2):
        for core in range(2):
            values = final[part, core].reshape(SIDE**3, 8, 128)
            row_squares += jnp.sum(values * values, 0)
    norm, clip = clip_for(jnp.sum(totals[0:1]) + jnp.sum(row_squares))
    loss_ref[0, 0] = jnp.sum(totals[1:2])
    norm_ref[0, 0] = jnp.max(norm)
    wide_clip = jnp.concatenate([clip] * (width // 128), 1)
    for piece in range(TABLE_PIECES):
        await_loads(4)

        @pl.loop(0, chunk // 80)
        def _(inner):
            at = pl.ds(pl.multiple_of(piece * chunk + inner * 80, 80), 80)
            grad = table_grad[at] * wide_clip
            stepped = adam_step(
                table[at], table_m[at], table_v[at], grad, TABLE_RATE, DECAY_RATE
            )
            for order, value in enumerate(stepped):
                results[4 + order][at] = value

        for order in range(3):
            store(4 + order, pl.ds(piece * chunk, chunk))
    await_loads(8)
    own_squares = jnp.zeros((1, 128), jnp.float32)
    for slot in range(SLOTS):
        grad = grads[slot // 2, slot % 2]
        own_squares += jnp.sum(grad * grad, 0, keepdims=True)
    own_clip = clip_for(jnp.sum(own_squares))[1]
    ratio = jnp.where(own_clip > 0.0, clip / own_clip, 0.0)

    @pl.loop(0, SLOTS, unroll=3)
    def _(slot):
        matrices_grad[slot] = grads[slot // 2, slot % 2] * clip
        left_new[slot] = STAT_DECAY * left_stats[slot] + (1.0 - STAT_DECAY) * (
            left_gram[slot] * ratio * ratio
        )
        right_new[slot] = STAT_DECAY * right_stats[slot] + (1.0 - STAT_DECAY) * (
            right_gram[slot] * ratio * ratio
        )
        stepped = fine_dot(left_part[slot] * ratio, right_roots[slot])
        weight = matrices[slot]
        matrices_new[slot] = weight - SHAMPOO_RATE * (stepped + DECAY_RATE * weight)

    for index in range(4):
        store(index)
    await_loads(6)
    tiles = D // 128
    for index in range(N_DP * N_VOCAB):
        at_core, rest = index // 64, index % 64
        at_z, at_y, at_x = rest // 16, rest // 4 % 4, rest % 4
        group, lanes = index // tiles, slice(128 * (index % tiles), 128 * (index % tiles) + 128)
        at = slice(8 * group, 8 * group + 8)
        stepped = adam_step(
            positions[at, lanes],
            pos_m[at, lanes],
            pos_v[at, lanes],
            final[0, at_core, at_z, at_y, at_x] * clip,
            POS_RATE,
            DECAY_RATE,
        )
        for order, value in enumerate(stepped):
            results[7 + order][at, lanes] = value
        if group < vectors.shape[0]:
            vec_grad[group : group + 1, lanes] = (
                final[1, at_core, at_x, at_z, at_y, 0:1] * clip
            )
    for index in range(7, 10):
        store(index)
    stepped = adam_step(
        vectors[...], vectors_m[...], vectors_v[...], vec_grad[...], VECTOR_RATE, 0.0
    )
    for order, value in enumerate(stepped):
        results[10 + order][...] = value
        store(10 + order)
    for copy in stores:
        copy.wait()


def update_call(totals, final, grads, products, blocks, table_grad, table, positions, vectors):
    sources = [totals, final, table_grad, *table, grads, *products, *blocks, *positions, *vectors]
    shape = lambda array: jax.ShapeDtypeStruct(array.shape, jnp.float32)
    targets = [shape(blocks[0])] * 4
    targets += [shape(array) for array in (*table, *positions, *vectors)]
    scalar = jax.ShapeDtypeStruct((1, 1), jnp.float32)
    smem = pl.BlockSpec(memory_space=pltpu.SMEM)
    return pl.pallas_call(
        update_kernel,
        name="optimizer_update",
        out_shape=(scalar, scalar, *targets),
        in_specs=[ANY] * len(sources),
        out_specs=(smem, smem) + (ANY,) * len(targets),
        scratch_shapes=[pltpu.VMEM(array.shape, jnp.float32) for array in sources]
        + [pltpu.VMEM(target.shape, jnp.float32) for target in targets]
        + [
            pltpu.VMEM(vectors[0].shape, jnp.float32),
            pltpu.SemaphoreType.DMA((len(sources) + 4 * (TABLE_PIECES - 1),)),
            pltpu.SemaphoreType.DMA((len(targets) + 3 * (TABLE_PIECES - 1),)),
        ],
        compiler_params=pltpu.CompilerParams(vmem_limit_bytes=VMEM_BYTES),
    )(*sources)


def slot_places():
    slot = np.arange(N_DP * N_VOCAB * SLOTS)
    device, own = slot // SLOTS, slot % SLOTS
    inner = device % N_VOCAB
    place = (device // N_VOCAB, inner // 2 % SIDE, inner // (2 * SIDE), inner % 2)
    part = own // 2
    result = np.zeros_like(slot)
    for which, (first, second, third) in enumerate(ORDERS):
        index = which * 2 + place[CORE]
        for axis in (third, second, first):
            index = index * SIDE + place[axis]
        result = np.where(part == which, index * 2 + own % 2, result)
    return result.astype(np.int32)


def per_device(
    token_ids,
    seq_lengths,
    loss_positions,
    target_ids,
    block_of_slot,
    matrices,
    left_stats,
    right_stats,
    left_roots,
    right_roots,
    vocab_table,
    table_m,
    table_v,
    positions_table,
    pos_m,
    pos_v,
    vectors,
    vectors_m,
    vectors_v,
):
    block_iota = jnp.arange(block_of_slot.shape[0], dtype=jnp.int32)
    where = jnp.sum(
        jnp.where(block_of_slot[None, :] == block_iota[:, None], slot_places()[None, :], 0),
        1,
        dtype=jnp.int32,
    )
    positions = loss_positions.T
    full, out_blocks, *cache, d_head_in, head_grad, loss_row = forward_call(
        where,
        positions,
        seq_lengths,
        token_ids,
        target_ids.T,
        matrices,
        vocab_table,
        positions_table,
        vectors,
    )
    hidden, query, key_value, probs, attended, middle, pre_act, last = cache
    grad_blocks, small, d_embed = backward_call(
        where,
        positions,
        full,
        out_blocks,
        (d_head_in, last, vectors, pre_act, middle, attended, query, key_value, probs, hidden),
    )
    owned_grads, table_grad_own, final, *products, totals = finish_call(
        grad_blocks.reshape(3, 2, SIDE, 32, BLOCK, BLOCK),
        small.reshape(2, SIDE, 16, 16, 128),
        head_grad.reshape(N_DP, TABLE_CHUNKS, -1, head_grad.shape[1]),
        d_embed,
        left_roots,
        token_ids,
        loss_row,
    )
    loss, norm, *updated = update_call(
        totals,
        final,
        owned_grads,
        products,
        (matrices, left_stats, right_stats, right_roots),
        table_grad_own,
        (vocab_table, table_m, table_v),
        (positions_table, pos_m, pos_v),
        (vectors, vectors_m, vectors_v),
    )
    return (loss.reshape(()), norm.reshape(()), *updated)


def solution(mesh):
    in_specs = (
        P("dp", None),
        P("dp"),
        P("dp", None),
        P("dp", None),
        P(),
        P(("dp", "vocab"), None, None),
        P(("dp", "vocab"), None, None),
        P(("dp", "vocab"), None, None),
        P(("dp", "vocab"), None, None),
        P(("dp", "vocab"), None, None),
        P("vocab", "dp"),
        P("vocab", "dp"),
        P("vocab", "dp"),
        P(),
        P(),
        P(),
        P(),
        P(),
        P(),
    )
    out_specs = (
        P(),
        P(),
        P(("dp", "vocab"), None, None),
        P(("dp", "vocab"), None, None),
        P(("dp", "vocab"), None, None),
        P(("dp", "vocab"), None, None),
        P("vocab", "dp"),
        P("vocab", "dp"),
        P("vocab", "dp"),
        P(),
        P(),
        P(),
        P(),
        P(),
        P(),
    )
    return jax.shard_map(
        per_device, mesh=mesh, in_specs=in_specs, out_specs=out_specs, check_vma=False
    )
```

```python
import math

import jax
import jax.numpy as jnp
import numpy as np
from jax import lax
from jax.experimental import pallas as pl
from jax.experimental.pallas import tpu as pltpu
from jax.sharding import PartitionSpec as P

D = 1024
HEADS = 16
HEAD_DIM = 64
FF = 4096
VOCAB_REAL = 50257
LAYERS = 1
BLOCK = 128
STEP = 10


LN_EPS = 1e-05
CLIP_LEVEL = 0.05
BETA_ONE = 0.9
BETA_TWO = 0.999
ADAM_EPS = 1e-08
STAT_DECAY = 0.95
SHAMPOO_RATE = 0.03
TABLE_RATE = 0.15
POS_RATE = 0.05
VECTOR_RATE = 0.25
DECAY_RATE = 0.1
NEG_FILL = -1e30
GELU_C = 0.7978845608028654
HIGH = lax.Precision.HIGHEST


def gelu(values):
    return 0.5 * values * (1.0 + jnp.tanh(GELU_C * (values + 0.044715 * values * values * values)))


def dot_nt(left, right):
    return lax.dot_general(
        left, right, (((1,), (1,)), ((), ())), preferred_element_type=jnp.float32
    )


def dot_tn(left, right):
    return lax.dot_general(
        left, right, (((0,), (0,)), ((), ())), preferred_element_type=jnp.float32
    )


VMEM_BYTES = 63 << 20
TABLE_CHUNKS = 20
MESH_IDS = pl.DeviceIdType.MESH
ANY = pl.BlockSpec(memory_space=pl.ANY)
VMEM = pl.BlockSpec(memory_space=pltpu.VMEM)
N_DP = 4
N_VOCAB = 32
SIDE = 4
X, Y, Z, CORE = range(4)
ORDERS = ((X, Y, Z), (Y, Z, X), (Z, X, Y))
SLOTS = 6


def coordinates():
    across = lax.axis_index("dp")
    inner = lax.axis_index("vocab")
    return (across, (inner // 2) % SIDE, inner // (2 * SIDE), inner % 2)


def moved(place, axis, step):
    shifted = list(place)
    shifted[axis] = (place[axis] + step) % (2 if axis == CORE else SIDE)
    return tuple(shifted)


def device_of(place):
    return (place[X], (place[Z] * SIDE + place[Y]) * 2 + place[CORE])


def rings_of(place, axes):
    others = [moved(place, CORE, 1)]
    return others + [moved(place, axis, step) for axis in axes for step in (1, 2, 3)]


def greet(others):
    for other in others:
        pl.semaphore_signal(
            pltpu.get_barrier_semaphore(),
            inc=1,
            device_id=device_of(other),
            device_id_type=MESH_IDS,
        )


def await_greetings(others):
    pl.semaphore_wait(pltpu.get_barrier_semaphore(), len(others))


class Wires:
    def __init__(self, send_sems, recv_sems):
        self.send_sems, self.recv_sems = send_sems, recv_sems
        self.send_slots, self.recv_slots, self.sent = 0, 0, []

    def send_slot(self):
        self.send_slots += 1
        return self.send_slots - 1

    def recv_slot(self):
        self.recv_slots += 1
        return self.recv_slots - 1

    def copy(self, source, target, place, send_slot, recv_slot):
        return pltpu.make_async_remote_copy(
            src_ref=source,
            dst_ref=target,
            send_sem=self.send_sems.at[send_slot],
            recv_sem=self.recv_sems.at[recv_slot],
            device_id=device_of(place),
            device_id_type=MESH_IDS,
        )

    def send(self, source, target, place, send_slot=None):
        slot = self.send_slot() if send_slot is None else send_slot
        copy = self.copy(source, target, place, slot, self.recv_slot())
        copy.start()
        if send_slot is None:
            self.sent.append(copy)
        return copy

    def bundle(self):
        return self.send_slot(), self.recv_slot()

    def send_all(self, source, target, place, bundle):
        self.copy(source, target, place, *bundle).start()

    def whole(self, ref, place, bundle):
        return self.copy(ref, ref, place, *bundle)

    def await_sent(self, ref, place, send_slot):
        self.copy(ref, ref, place, send_slot, 0).wait_send()

    def settle(self, latest=0):
        done = len(self.sent) - latest
        for copy in self.sent[:done]:
            copy.wait_send()
        self.sent = self.sent[done:]


def lane_range(first, count):
    return pl.ds(pl.multiple_of(first, 128), count)


class Group:
    def __init__(self, wires, place):
        self.wires, self.place, self.slot, self.size = wires, place, wires.send_slot(), 0

    def send(self, source, target, place):
        self.size += math.prod(source.shape) * jnp.dtype(source.dtype).itemsize
        return self.wires.send(source, target, place, self.slot)

    def settle(self, blocks):
        count, rest = divmod(self.size, math.prod(blocks.shape[1:]) * 2)
        assert rest == 0 and count <= blocks.shape[0]
        self.wires.await_sent(blocks.at[pl.ds(0, count)], self.place, self.slot)


def add_blocks(target, sources, count):
    @pl.loop(0, count)
    def _(i):
        at = i if len(target.shape) == 3 else lane_range(128 * i, 128)
        total = target[at].astype(jnp.float32)
        for source in sources:
            total += source[at].astype(jnp.float32)
        target[at] = total.astype(target.dtype)


class RingGather:
    def __init__(self, wires, place, axis, piece, half, own=None):
        self.wires, self.place, self.axis = wires, place, axis
        self.piece, self.half = piece, half
        self.mine = place[axis]
        self.own = self.piece(self.mine) if own is None else own

    def start(self):
        mine = self.piece(self.mine)
        self.up = self.wires.send(self.own, mine, moved(self.place, self.axis, 1))
        self.down = self.wires.send(self.own, mine, moved(self.place, self.axis, -1))

    def forward(self):
        self.up.wait_recv()
        lower = self.half((self.mine + 3) % SIDE, 0)
        self.far_up = self.wires.send(lower, lower, moved(self.place, self.axis, 1))
        self.down.wait_recv()
        upper = self.half((self.mine + 1) % SIDE, 1)
        self.far_down = self.wires.send(upper, upper, moved(self.place, self.axis, -1))

    def finish(self):
        self.far_up.wait_recv()
        self.far_down.wait_recv()


class DirectGather:
    def __init__(self, wires, place, axis, piece, own=None):
        self.wires, self.place, self.axis, self.piece = wires, place, axis, piece
        self.own = self.piece(place[axis]) if own is None else own

    def start(self):
        mine = self.piece(self.place[self.axis])
        self.copies = [
            self.wires.send(self.own, mine, moved(self.place, self.axis, step))
            for step in (1, 2, 3)
        ]

    def finish(self):
        for copy in self.copies:
            copy.wait_recv()


class RingReduce:
    def __init__(self, wires, place, axis, piece, half, count, half_in, whole_in):
        self.wires, self.place, self.axis = wires, place, axis
        self.piece, self.half, self.count = piece, half, count
        self.half_in, self.whole_in = half_in, whole_in
        self.mine = place[axis]

    def start(self):
        far = (self.mine + 2) % SIDE
        up, down = moved(self.place, self.axis, 1), moved(self.place, self.axis, -1)
        self.far_up = self.wires.send(self.half(far, 0), self.half_in.at[0], up)
        self.far_down = self.wires.send(self.half(far, 1), self.half_in.at[1], down)

    def forward(self):
        after, before = (self.mine + 1) % SIDE, (self.mine + 3) % SIDE
        up, down = moved(self.place, self.axis, 1), moved(self.place, self.axis, -1)
        self.far_up.wait_recv()
        add_blocks(self.half(after, 0), [self.half_in.at[0]], self.count // 2)
        self.up = self.wires.send(self.piece(after), self.whole_in.at[0], up)
        self.far_down.wait_recv()
        add_blocks(self.half(before, 1), [self.half_in.at[1]], self.count // 2)
        self.down = self.wires.send(self.piece(before), self.whole_in.at[1], down)

    def arrive(self):
        self.up.wait_recv()
        self.down.wait_recv()

    def finish(self):
        self.arrive()
        add_blocks(
            self.piece(self.mine), [self.whole_in.at[0], self.whole_in.at[1]], self.count
        )


class DirectReduce:
    def __init__(self, wires, place, axis, piece, count, landing):
        self.wires, self.place, self.axis = wires, place, axis
        self.piece, self.count, self.landing = piece, count, landing

    def start(self):
        mine = self.place[self.axis]
        self.copies = [
            self.wires.send(
                self.piece((mine + step) % SIDE),
                self.landing.at[step - 1],
                moved(self.place, self.axis, step),
            )
            for step in (1, 2, 3)
        ]

    def arrive(self):
        for copy in self.copies:
            copy.wait_recv()

    def finish(self):
        self.arrive()
        add_blocks(
            self.piece(self.place[self.axis]),
            [self.landing.at[step] for step in range(3)],
            self.count,
        )


class RowGather:
    def __init__(self, wires, place, axis, first, row):
        self.wires, self.place, self.axis = wires, place, axis
        self.row, self.mine, self.first = row, place[axis], first
        self.up, self.down, self.far = [], [], {}
        self.bundles = [wires.send_slot() for _ in range(3)]

    def of(self, piece, index):
        return self.row((self.mine + piece) % SIDE, (self.first + (0, 1, 3, 2)[index]) % SIDE)

    def send(self, index):
        mine = self.of(0, index)
        up, down = moved(self.place, self.axis, 1), moved(self.place, self.axis, -1)
        self.up.append(self.wires.send(mine, mine, up, self.bundles[0]))
        self.down.append(self.wires.send(mine, mine, down, self.bundles[1]))

    def forward(self, index):
        upward = index < 2
        (self.up if upward else self.down)[index].wait_recv()
        passed = self.of(3 if upward else 1, index)
        step = 1 if upward else -1
        target = moved(self.place, self.axis, step)
        self.far[index] = self.wires.send(passed, passed, target, self.bundles[2])
        return passed

    def take(self, index):
        (self.down if index < 2 else self.up)[index].wait_recv()
        return self.of(1 if index < 2 else 3, index)

    def take_far(self, index):
        self.far[index].wait_recv()
        return self.of(2, index)

    def settle(self, piece):
        for bundle in self.bundles:
            self.wires.await_sent(piece, self.place, bundle)


class QuarterReduce(RingReduce):
    def start(self, chunk):
        far = (self.mine + 2) % SIDE
        up, down = moved(self.place, self.axis, 1), moved(self.place, self.axis, -1)
        size = self.count // 4
        landing = pl.ds(chunk * size, size)
        if chunk == 0:
            self.far_ups, self.far_downs, self.wholes = [], [], []
        self.far_ups.append(
            self.wires.send(self.half(far, 2 * chunk), self.half_in.at[0, landing], up)
        )
        self.far_downs.append(
            self.wires.send(self.half(far, 2 * chunk + 1), self.half_in.at[1, landing], down)
        )

    def send_quarter(self, piece, quarter, side):
        size = self.count // 4
        landing = self.whole_in.at[side, pl.ds(quarter * size, size)]
        there = moved(self.place, self.axis, 1 if side == 0 else -1)
        self.wholes.append(self.wires.send(self.half(piece, quarter), landing, there))

    def start_near(self):
        after, before = (self.mine + 1) % SIDE, (self.mine + 3) % SIDE
        for quarter in (0, 2):
            self.send_quarter(after, quarter + 1, 0)
            self.send_quarter(before, quarter, 1)

    def forward(self):
        after, before = (self.mine + 1) % SIDE, (self.mine + 3) % SIDE
        size = self.count // 4
        for chunk in range(2):
            landed = pl.ds(chunk * size, size)
            self.far_ups[chunk].wait_recv()
            add_blocks(self.half(after, 2 * chunk), [self.half_in.at[0, landed]], size)
            self.send_quarter(after, 2 * chunk, 0)
            self.far_downs[chunk].wait_recv()
            add_blocks(self.half(before, 2 * chunk + 1), [self.half_in.at[1, landed]], size)
            self.send_quarter(before, 2 * chunk + 1, 1)

    def arrive(self):
        for copy in self.wholes:
            copy.wait_recv()


def block_ring(place, part, phase, at):
    first_axis, second_axis, third_axis = ORDERS[part]
    k1, k2, k3 = place[first_axis], place[second_axis], place[third_axis]
    if phase == 0:
        return (
            lambda j: at(k3, 8 * k2 + 2 * j, 2),
            lambda j, h: at(k3, 8 * k2 + 2 * j + h, 1),
        )
    if phase == 1:
        return (lambda j: at(k3, 8 * j, 8), lambda j, h: at(k3, 8 * j + 4 * h, 4))
    return (lambda j: at(j, 0, 32), lambda j, q: at(j, 8 * q, 8))


def gather_phase(
    place,
    wires,
    others,
    ids_ref,
    matrices_ref,
    table_ref,
    positions_ref,
    blocks,
    table,
    hidden_ref,
    own_low,
    table_pad,
    ids_all,
    parts,
    sibling_in,
    half_in,
    whole_in,
    landing,
    ready,
    arrived,
    local_sems,
):
    core = place[CORE]
    across = place[X]
    sibling = moved(place, CORE, 1)
    group = Group(wires, place)

    def blocks_at(part, side, k3, first, count):
        start = ((2 * part + side) * SIDE + k3) * 32 + first
        return blocks.at[pl.ds(start, count)]

    own_low[...] = matrices_ref[...].astype(jnp.bfloat16).reshape(own_low.shape)
    for part in range(3):
        k1, k2, k3 = (place[axis] for axis in ORDERS[part])
        first = ((2 * part + core) * SIDE + k3) * 32 + 8 * k2 + 2 * k1
        for which in range(2):
            blocks[first + which] = own_low[part, which]
    ids_all[across] = ids_ref[...]
    table[across] = table_ref[...].astype(jnp.bfloat16)
    rings = [[], [], []]
    for part in range(3):

        def at(k3, first, count, part=part):
            return blocks_at(part, core, k3, first, count)

        first_axis, second_axis, third_axis = ORDERS[part]
        piece, _ = block_ring(place, part, 0, at)
        rings[0].append(DirectGather(group, place, first_axis, piece, own_low.at[part]))
        piece, half = block_ring(place, part, 1, at)
        rings[1].append(RingGather(group, place, second_axis, piece, half))
        rings[2].append(
            RowGather(
                wires,
                place,
                third_axis,
                place[second_axis],
                lambda j, row, at=at: at(j, 8 * row, 8),
            )
        )
    on_z, on_x, on_y = rings[2]
    ids_ring = DirectGather(wires, place, X, lambda j: ids_all.at[j])
    rows = table_ref.shape[0]
    table_pad[pl.ds(0, rows)] = table_ref[...].astype(jnp.bfloat16)
    padding = table_pad.shape[0] - rows
    table_pad[pl.ds(rows, padding)] = jnp.zeros((padding, table_pad.shape[1]), jnp.bfloat16)
    table_ring = RowGather(
        wires,
        place,
        X,
        0,
        lambda j, row: table.at[j, pl.ds(rows // SIDE * row, rows // SIDE)],
    )
    base = (lax.axis_index("vocab") * rows).astype(jnp.float32)
    tiles = table_pad.shape[0] // 128
    lane = lax.broadcasted_iota(jnp.int32, (128, 128), 1).astype(jnp.float32)

    def group_of(part, which):
        return 2 * ((across // 2 + part) % 2) + which

    def look_up(part, side, half):
        dp_group = group_of(part, side)

        @pl.loop(4 * half, 4 * half + 4)
        def _(quad):
            hot_rows = []
            for which in range(4):
                ids = ids_all[dp_group, pl.ds(4 * quad + which, 1), :].astype(jnp.float32) - base
                column = jnp.transpose(jnp.broadcast_to(ids, (128, 128)))
                hot_rows.append(
                    jnp.concatenate(
                        [
                            jnp.where(column == lane + 128.0 * tile, 1.0, 0.0).astype(jnp.bfloat16)
                            for tile in range(tiles)
                        ],
                        1,
                    )
                )
            found = jnp.dot(
                jnp.concatenate(hot_rows, 0), table_pad[...], preferred_element_type=jnp.float32
            ).astype(jnp.bfloat16)
            at_z = quad // 2
            for which in range(4):
                at_y = 2 * (quad % 2) + which // 2
                first, second = (at_z, at_y) if part == 0 else (at_y, at_z)
                at = lookup_rows(part, which % 2, first, 2 * second + side, 1)
                parts[at] = found[128 * which : 128 * which + 128]

    def lookup_rows(part, side, first, index, count):
        start = ((2 * part + side) * SIDE + first) * 8 + index
        return lane_range(128 * start, 128 * count)

    def to_sibling(part):
        crossing = parts.at[lookup_rows(part, 1 - core, 0, 0, 32)]
        return group.send(crossing, sibling_in.at[part], sibling)

    lookup_axes = ((Z, Y), (Y, Z))
    lookup_rings, lookup_ends = [], []
    for part in range(2):
        first_axis, second_axis = lookup_axes[part]
        lookup_rings.append(
            RingReduce(
                group,
                place,
                first_axis,
                lambda j, part=part: parts.at[lookup_rows(part, core, j, 0, 8)],
                lambda j, h, part=part: parts.at[lookup_rows(part, core, j, 4 * h, 4)],
                8,
                half_in.at[part],
                whole_in.at[part],
            )
        )
        lookup_ends.append(
            DirectReduce(
                group,
                place,
                second_axis,
                lambda j, part=part, k=place[first_axis]: parts.at[
                    lookup_rows(part, core, k, 2 * j, 2)
                ],
                2,
                landing.at[part],
            )
        )

    def add_sibling(part):
        siblings[part].wait_recv()
        add_blocks(parts.at[lookup_rows(part, core, 0, 0, 32)], [sibling_in.at[part]], 32)
        lookup_rings[part].start()

    def take_result(part):
        lookup_ends[part].arrive()
        first_axis, second_axis = lookup_axes[part]
        for which in range(2):
            at = lookup_rows(part, core, place[first_axis], 2 * place[second_axis] + which, 1)
            total = parts[at].astype(jnp.float32)
            for step in range(3):
                total += landing[part, step, 128 * which : 128 * which + 128].astype(jnp.float32)
            ready[group_of(part, which)] = total.astype(jnp.bfloat16)

    shares = [wires.bundle() for _ in range(3)]

    def share(part, ref):
        wires.send_all(ref, ref, sibling, shares[part])

    own_side = across % 2
    await_greetings(others)
    ids_ring.start()
    for ring in rings[0]:
        ring.start()
    table_ring.send(0)
    look_up(0, own_side, 0)
    look_up(0, own_side, 1)
    for ring, later in zip(rings[0], rings[1]):
        ring.finish()
        later.start()
    for ring in rings[2]:
        ring.send(0)
    ids_ring.finish()
    look_up(0, 1 - own_side, 0)
    look_up(0, 1 - own_side, 1)
    siblings = [to_sibling(0)]
    look_up(1, 0, 0)
    for ring in rings[1]:
        ring.forward()
    look_up(1, 0, 1)
    add_sibling(0)
    for ring in (on_y, on_x, on_z):
        ring.send(1)
    look_up(1, 1, 0)
    look_up(1, 1, 1)
    siblings.append(to_sibling(1))
    for ring in rings[1]:
        ring.finish()
    on_y.send(2)
    on_x.send(2)
    lookup_rings[0].forward()
    add_sibling(1)
    on_z.send(2)
    on_x.send(3)
    table_ring.send(1)
    for part in range(3):
        share(part, blocks_at(part, core, place[ORDERS[part][2]], 0, 32))
    lookup_rings[1].forward()
    share(1, on_x.forward(0))
    share(1, on_x.forward(2))
    lookup_rings[0].finish()
    lookup_ends[0].start()
    on_z.send(3)
    on_y.send(3)
    share(1, on_x.forward(1))
    share(1, on_x.forward(3))
    table_ring.send(2)
    table_ring.send(3)
    lookup_rings[1].finish()
    lookup_ends[1].start()
    for ring_part, ring in ((0, on_z), (2, on_y)):
        for index in (0, 2):
            share(ring_part, ring.forward(index))
    take_result(0)
    for ring_part, ring in ((0, on_z), (2, on_y)):
        for index in (1, 3):
            share(ring_part, ring.forward(index))
    take_result(1)
    swaps = []
    for step in (1, 2, 3):
        there = moved(place, X, step)
        swaps.append(group.send(ready.at[there[X]], arrived.at[across], there))
    arrived[across] = ready[across]
    for part in range(3):
        for index in range(4):
            share(part, rings[2][part].take(index))
    for copy in swaps:
        copy.wait_recv()
    for source in range(4):
        columns = pl.ds(256 * source, 256)
        hidden_ref[:, columns] = (
            arrived[source].astype(jnp.float32) + positions_ref[:, columns]
        )
    table_ring.forward(0)
    table_ring.forward(2)
    for index in (0, 2, 1, 3):
        for part in range(3):
            share(part, rings[2][part].take_far(index))
    for index in (1, 3):
        table_ring.forward(index)
    group.settle(blocks)
    wires.settle()
    for part in range(3):
        rings[2][part].settle(blocks.at[pl.ds(0, 32)])
        wires.whole(blocks.at[pl.ds(0, 128)], sibling, shares[part]).wait()
    return table_ring


def head_phase(
    place,
    wires,
    vocab_group,
    table_ring,
    head_in_ref,
    table,
    target_ref,
    at_ref,
    length_ref,
    d_head_ref,
    table_grad_ref,
    loss_ref,
    table_grads,
    pieces,
    logits,
    stats,
    d_rows,
    d_sibling,
    d_first,
    d_second,
    local_sems,
    arrange_out,
    keeps,
):
    core = place[CORE]
    sibling = moved(place, CORE, 1)
    own, width = head_in_ref.shape
    half_width = width // 2
    sends = Group(wires, place)
    feature_axes = ((Y, Z), (Z, Y))
    for part in range(2):
        near, far = (place[axis] for axis in feature_axes[part])
        pieces[part, core, far, near] = head_in_ref[
            :, part * half_width : (part + 1) * half_width
        ]
    first_rings, second_rings = [], []
    for part in range(2):
        near_axis, far_axis = feature_axes[part]
        first_rings.append(
            DirectGather(
                sends,
                place,
                near_axis,
                lambda j, part=part, k=place[far_axis]: pieces.at[part, core, k, j],
            )
        )
        second_rings.append(
            DirectGather(sends, place, far_axis, lambda j, part=part: pieces.at[part, core, j])
        )
    for ring in first_rings:
        ring.start()
    seqs = target_ref.shape[1]
    column = lax.broadcasted_iota(jnp.int32, (seqs, seqs * own), 1)
    row = lax.broadcasted_iota(jnp.int32, (seqs, seqs * own), 0)
    own_seq = jnp.where(column // own == row, 1.0, 0.0)
    slot = lax.broadcasted_iota(jnp.int32, (own, seqs * own), 0)
    slot_column = lax.broadcasted_iota(jnp.int32, (own, seqs * own), 1)
    own_slot = slot_column % own == slot

    def laid_end_to_end(values):
        wide = jnp.dot(
            values.astype(jnp.float32), own_seq, precision=HIGH, preferred_element_type=jnp.float32
        )
        return jnp.sum(jnp.where(own_slot, wide, 0.0), 0, keepdims=True)

    target = laid_end_to_end(target_ref[...]).astype(jnp.int32)
    lengths = jnp.dot(
        length_ref[...].astype(jnp.float32),
        own_seq,
        precision=HIGH,
        preferred_element_type=jnp.float32,
    )
    counted = (laid_end_to_end(at_ref[...]) < lengths).astype(jnp.float32)
    for index in range(8):
        arrange_out(index)
    for ring, later in zip(first_rings, second_rings):
        ring.finish()
        later.start()
    for index in range(8, 16):
        arrange_out(index)
    crossing = []
    for part in range(2):
        second_rings[part].finish()
        mine = pieces.at[part, core]
        crossing.append(sends.send(mine, mine, sibling))
    for copy in crossing:
        copy.wait_recv()
    for index in range(4):
        table_ring.take(index)
        table_ring.take_far(index)
    table_ring.settle(table.at[0])
    groups, rows, group_width = table.shape
    count = own * N_VOCAB
    exp_sums, hit_sums = groups * rows, groups * (rows + count)
    rows_first = groups * (rows + 2 * count)
    for index in range(N_VOCAB):
        at_z, at_y, at_core = index // 8, index // 2 % SIDE, index % 2
        halves = (pieces[0, at_core, at_z, at_y], pieces[1, at_core, at_y, at_z])
        for group in range(groups):
            column = group % 2 * group_width
            table_grads[pl.ds(rows_first + group * count + own * index, own)] = halves[group // 2][
                :, column : column + group_width
            ]

    def rows_in(group):
        return table_grads[pl.ds(rows_first + group * count, count)]

    half_count = count // 2
    lowered_first = groups * (rows + 3 * count)

    def lower(index, values):
        values = values.astype(jnp.bfloat16)
        for side in range(2):
            first = pl.multiple_of(lowered_first + side * rows + index * chunk, 16)
            table_grads[pl.ds(first, chunk)] = values[
                :, side * half_count : (side + 1) * half_count
            ]

    chunk = rows // 4
    base = lax.axis_index("vocab") * rows
    row_iota = lax.broadcasted_iota(jnp.int32, (chunk, count), 0)

    def logit_chunk(index, top):
        at = pl.ds(pl.multiple_of(index * chunk, chunk), chunk)
        total = jnp.zeros((chunk, count), jnp.float32)
        for group in range(groups):
            total += lax.dot_general(
                table[group, at],
                rows_in(group),
                (((1,), (1,)), ((), ())),
                preferred_element_type=jnp.float32,
            )
        total = jnp.where(row_iota + (base + index * chunk) < VOCAB_REAL, total, NEG_FILL)
        logits[at] = total
        return jnp.maximum(top, jnp.max(total, 0, keepdims=True))

    local_top = lax.fori_loop(
        0, 4, logit_chunk, jnp.full((1, count), NEG_FILL, jnp.float32)
    )

    def exp_chunk(index, carry):
        total, pick = carry
        at = pl.ds(pl.multiple_of(index * chunk, chunk), chunk)
        values = logits[at]
        hits = row_iota + (base + index * chunk) == target
        pick += jnp.sum(jnp.where(hits, values, 0.0), 0, keepdims=True)
        values = jnp.exp(values - local_top)
        logits[at] = values
        lower(index, values)
        return total + jnp.sum(values, 0, keepdims=True), pick

    zero_row = jnp.zeros((1, count), jnp.float32)
    local_total, pick = lax.fori_loop(0, 4, exp_chunk, (zero_row, zero_row))
    lanes = count // 4
    top = jnp.concatenate([local_top[:, lanes * i : lanes * (i + 1)] for i in range(4)], 0)
    total = jnp.concatenate([local_total[:, lanes * i : lanes * (i + 1)] for i in range(4)], 0)
    mine = stats.at[lax.axis_index("vocab")]
    mine[...] = jnp.concatenate([top, total], 0)
    bundle = wires.bundle()
    for other in vocab_group:
        wires.send_all(mine, mine, other, bundle)
    def table_products(first):
        for side in range(2):
            lowered = table_grads[pl.ds(lowered_first + side * rows, rows)]
            for group in range(groups):
                product = dot_tn(lowered, table[group]).astype(jnp.bfloat16)
                at = pl.ds(first + group * count + half_count * side, half_count)
                table_grads[at] = product

    table_products(exp_sums)

    @pl.loop(0, 4)
    def _(index):
        hits = row_iota + (base + index * chunk) == target
        lower(index, jnp.where(hits, 1.0, 0.0))

    table_products(hit_sums)
    wires.whole(stats.at[pl.ds(0, len(vocab_group))], sibling, bundle).wait()
    top = jnp.max(stats[:, :4], 0)
    total = jnp.sum(stats[:, 4:] * jnp.exp(stats[:, :4] - top[None]), 0)
    log_total = top + jnp.log(total)
    log_total = jnp.concatenate([log_total[i : i + 1] for i in range(4)], 1)
    first_device = (lax.axis_index("vocab") == 0).astype(jnp.float32)
    loss_ref[...] = (first_device * log_total - pick) * counted
    weight = counted / (N_DP * N_VOCAB * own)
    scale = jnp.exp(local_top - log_total) * weight

    def down_rows(values, index):
        return jnp.transpose(
            jnp.broadcast_to(values[:, 128 * index : 128 * index + 128], (128, 128))
        )

    for tile in range(count // 128):
        tile_scale = jnp.concatenate([down_rows(scale, tile)] * 2, 1)
        tile_weight = jnp.concatenate([down_rows(weight, tile)] * 2, 1)
        for group in range(groups):
            at = group * count + 128 * tile
            exp_part = table_grads[pl.ds(exp_sums + at, 128)].astype(jnp.float32)
            hit_part = table_grads[pl.ds(hit_sums + at, 128)].astype(jnp.float32)
            rows_grad = (exp_part * tile_scale - hit_part * tile_weight).astype(jnp.bfloat16)
            part, column = group // 2, group % 2 * group_width
            for index in range(128 // own):
                inner = 128 // own * tile + index
                at_z, at_y, at_core = inner // 8, inner // 2 % SIDE, inner % 2
                first, second = (at_z, at_y) if part == 0 else (at_y, at_z)
                d_rows[part, at_core, first, second, :, column : column + group_width] = (
                    rows_grad[own * index : own * (index + 1)]
                )
    crossing = [
        sends.send(d_rows.at[part, 1 - core], d_sibling.at[part], sibling) for part in range(2)
    ]
    reduce_axes = ((Z, Y), (Y, Z))
    first_rings, second_rings = [], []
    for part in range(2):
        first_axis, second_axis = reduce_axes[part]
        crossing[part].wait_recv()
        for j in range(4):
            add_blocks(d_rows.at[part, core, j], [d_sibling.at[part, j]], 4)
        first_rings.append(
            DirectReduce(
                sends,
                place,
                first_axis,
                lambda j, part=part: d_rows.at[part, core, j],
                4,
                d_first.at[part],
            )
        )
        second_rings.append(
            DirectReduce(
                sends,
                place,
                second_axis,
                lambda j, part=part, k=place[first_axis]: d_rows.at[part, core, k, j],
                1,
                d_second.at[part],
            )
        )
        first_rings[part].start()

    stores = []

    @pl.loop(0, 4)
    def _(index):
        at = pl.ds(pl.multiple_of(index * chunk, chunk), chunk)
        hits = row_iota + (base + index * chunk) == target
        lower(index, logits[at] * scale - jnp.where(hits, weight, 0.0))

    def table_grad(group):
        @pl.loop(0, 4)
        def _(index):
            product = jnp.zeros((chunk, group_width), jnp.float32)
            for side in range(2):
                first = pl.multiple_of(lowered_first + side * rows + index * chunk, 16)
                product += jnp.dot(
                    table_grads[pl.ds(first, chunk)],
                    rows_in(group)[side * half_count : (side + 1) * half_count],
                    preferred_element_type=jnp.float32,
                )
            product = product.astype(jnp.bfloat16)
            table_grads[pl.ds(pl.multiple_of(group * rows + index * chunk, chunk), chunk)] = product

        at = pl.ds(group * rows, rows)
        stores.append(
            pltpu.make_async_copy(table_grads.at[at], table_grad_ref.at[at], local_sems.at[group])
        )
        stores[-1].start()

    table_grad(0)
    table_grad(1)
    for ring, later in zip(first_rings, second_rings):
        ring.finish()
        later.start()
    table_grad(2)
    table_grad(3)
    for copy in keeps + stores[:3]:
        copy.wait()
    del stores[:3]
    for part in range(2):
        second_rings[part].arrive()
        first_axis, second_axis = reduce_axes[part]
        total = d_rows[part, core, place[first_axis], place[second_axis]].astype(jnp.float32)
        for step in range(3):
            total += d_second[part, step].astype(jnp.float32)
        d_head_ref[:, part * half_width : (part + 1) * half_width] = total
    return stores, sends


def split(values):
    high = values.astype(jnp.bfloat16)
    return high, (values - high.astype(jnp.float32)).astype(jnp.bfloat16)


def fine_dot(left, right, contract=((1,), (0,))):
    (left_high, left_low), (right_high, right_low) = split(left), split(right)

    def product(one, other):
        return lax.dot_general(
            one, other, (contract, ((), ())), preferred_element_type=jnp.float32
        )

    return product(left_high, right_high) + (
        product(left_high, right_low) + product(left_low, right_high)
    )


def clip_for(squares):
    norm = jnp.sqrt(jnp.full((1, 128), squares, jnp.float32))
    return norm, CLIP_LEVEL / jnp.maximum(norm, CLIP_LEVEL)


def finish_kernel(
    grads_ref,
    small_ref,
    head_grad_ref,
    d_embed_ref,
    left_roots_ref,
    ids_ref,
    loss_ref,
    grads_out_target,
    table_grad_target,
    final_target,
    left_gram_target,
    right_gram_target,
    left_part_target,
    totals_ref,
    grads_out_ref,
    table_grad_ref,
    final_ref,
    left_gram,
    right_gram,
    left_part,
    left_roots,
    sums,
    sibling_in,
    half_a,
    whole_a,
    half_b,
    whole_b,
    whole_c,
    small_sums,
    small_sibling,
    small_a,
    small_b,
    small_c,
    table_sums,
    table_half,
    table_whole,
    embeds,
    ids_all,
    totals_all,
    send_sems,
    recv_sems,
    local_sems,
):
    place = coordinates()
    core = place[CORE]
    across = place[X]
    sibling = moved(place, CORE, 1)
    wires = Wires(send_sems, recv_sems)
    to_sibling, to_owners, to_table, later_sends = (Group(wires, place) for _ in range(4))

    def sums_at(part, k3, first, count):
        return sums.at[pl.ds((SIDE * part + k3) * 32 + first, count)]

    loads = []

    def load(source, target):
        copy = pltpu.make_async_copy(source, target, local_sems.at[len(loads)])
        copy.start()
        loads.append(copy)
        return copy

    width = table_grad_ref.shape[1]
    embed_axes = ((Y, Z), (Z, Y))
    source_part = across // 2
    near = place[Y] * (1 - source_part) + place[Z] * source_part
    far = place[Z] * (1 - source_part) + place[Y] * source_part
    landing = embeds.at[source_part, core, far, 2 * near + across % 2]
    own_columns = pl.ds(pl.multiple_of(across * width, width), width)
    embed_load = load(d_embed_ref.at[:, own_columns], landing)
    third = [place[ORDERS[part][2]] for part in range(3)]
    small_load = load(small_ref.at[core], small_sums)
    block_loads = {}
    for step in (2, 1, 3, 0):
        for part in range(3):
            j = (third[part] + step) % SIDE
            block_loads[part, step] = load(grads_ref.at[part, core, j], sums_at(part, j, 0, 32))
    table_load = load(head_grad_ref, table_sums)
    roots_load = load(left_roots_ref, left_roots)

    ids_all[across] = ids_ref[...]
    line = [
        moved(moved(place, X, step), CORE, side) for step in range(SIDE) for side in range(2)
    ][1:]
    plane = [
        moved(moved(place, Y, step), Z, other) for step in range(SIDE) for other in range(SIDE)
    ][1:]
    greet(line + plane)
    await_greetings(line + plane)
    swaps = []
    for step in (1, 2, 3):
        there = moved(place, X, step)
        columns = pl.ds(pl.multiple_of(there[X] * width, width), width)
        swaps.append(wires.send(d_embed_ref.at[:, columns], landing, there))
    ids_ring = DirectGather(wires, place, X, lambda j: ids_all.at[j])
    ids_ring.start()
    small_crossing = wires.send(small_ref.at[1 - core], small_sibling, sibling)
    crossings = {}
    for step, half in ((2, 0), (2, 1), (1, None), (3, None), (0, None)):
        for part in range(3):
            j = (third[part] + step) % SIDE
            source, target = grads_ref.at[part, 1 - core, j], sibling_in.at[part, j]
            if half is not None:
                source, target = source.at[pl.ds(16 * half, 16)], target.at[pl.ds(16 * half, 16)]
            crossings[part, step, half] = to_sibling.send(source, target, sibling)

    embed_first, embed_second = [], []
    for part in range(2):
        near_axis, far_axis = embed_axes[part]
        embed_first.append(
            RingGather(
                to_owners,
                place,
                near_axis,
                lambda j, part=part, k=place[far_axis]: embeds.at[part, core, k, pl.ds(2 * j, 2)],
                lambda j, h, part=part, k=place[far_axis]: embeds.at[
                    part, core, k, pl.ds(2 * j + h, 1)
                ],
            )
        )
        embed_second.append(
            RingGather(
                later_sends,
                place,
                far_axis,
                lambda j, part=part: embeds.at[part, core, j],
                lambda j, h, part=part: embeds.at[part, core, j, pl.ds(4 * h, 4)],
            )
        )
    first_rings, middle_rings, last_rings = [], [], []
    for part in range(3):

        def at(k3, first, count, part=part):
            return sums_at(part, k3, first, count)

        last_axis, middle_axis, first_axis = ORDERS[part]
        piece, half = block_ring(place, part, 2, at)
        first_rings.append(
            QuarterReduce(
                to_owners, place, first_axis, piece, half, 32, half_a.at[part], whole_a.at[part]
            )
        )
        piece, half = block_ring(place, part, 1, at)
        middle_rings.append(
            RingReduce(
                later_sends, place, middle_axis, piece, half, 8, half_b.at[part], whole_b.at[part]
            )
        )
        piece, _ = block_ring(place, part, 0, at)
        last_rings.append(DirectReduce(later_sends, place, last_axis, piece, 2, whole_c.at[part]))
    table_ring = QuarterReduce(
        to_table,
        place,
        X,
        lambda j: table_sums.at[j],
        lambda j, q: table_sums.at[j, pl.ds(TABLE_CHUNKS // 4 * q, TABLE_CHUNKS // 4)],
        TABLE_CHUNKS,
        table_half,
        table_whole,
    )
    small_rings = [
        DirectReduce(wires, place, Z, lambda j: small_sums.at[j], 16, small_a),
        DirectReduce(
            wires, place, Y, lambda j: small_sums.at[place[Z], pl.ds(4 * j, 4)], 4, small_b
        ),
        DirectReduce(
            wires, place, X, lambda j: small_sums.at[place[Z], pl.ds(4 * place[Y] + j, 1)], 1, small_c
        ),
    ]

    def add_crossing(part, step, half=None):
        j = (third[part] + step) % SIDE
        if not half:
            block_loads[part, step].wait()
        crossings[part, step, half].wait_recv()
        first, count = (0, 32) if half is None else (16 * half, 16)
        landed = sibling_in.at[part, j, pl.ds(first, count)]
        add_blocks(sums_at(part, j, first, count), [landed], count)

    embed_siblings = []

    def share(part, step):
        piece = embeds.at[part, core, (place[embed_axes[part][1]] + step) % SIDE]
        embed_siblings.append(later_sends.send(piece, piece, sibling))

    rows = table_grad_ref.shape[0]
    chunk = rows // 4
    base = lax.axis_index("vocab") * rows
    row_iota = lax.broadcasted_iota(jnp.int32, (chunk, 512), 0)

    def scatter_rows(part, at_core, step):
        at_far = (place[embed_axes[part][1]] + step) % SIDE

        @pl.loop(0, 2)
        def _(pair):
            values = embeds[part, at_core, at_far, pl.ds(4 * pair, 4)].reshape(512, width)
            ids = []
            for which in range(4):
                at_near = 2 * pair + which // 2
                at_z, at_y = (at_far, at_near) if part == 0 else (at_near, at_far)
                inner = (at_z * SIDE + at_y) * 2 + at_core
                ids.append(ids_all[2 * part + which % 2, pl.ds(inner, 1), :])
            ids = jnp.concatenate(ids, 1) - base

            @pl.loop(0, 4)
            def _(row):
                at = pl.ds(pl.multiple_of(row * chunk, chunk), chunk)
                hot = jnp.where(row_iota + row * chunk == ids, 1.0, 0.0).astype(jnp.bfloat16)
                table_grad_ref[at] += jnp.dot(hot, values, preferred_element_type=jnp.float32)

    lead = ((0, core), (1, core))
    orders = ((X, Y, Z), (Y, Z, X))
    gathers = []
    for phase in range(3):
        row = []
        for part in range(2):
            _, second_axis, third_axis = orders[part]
            keys = (place[third_axis], place[second_axis])[: 2 - phase]
            row.append(
                DirectGather(
                    wires,
                    place,
                    orders[part][phase],
                    lambda j, key=lead[part] + keys: final_ref.at[key + (j,)],
                )
            )
        gathers.append(row)

    for part in range(3):
        add_crossing(part, 2, 0)
        first_rings[part].start(0)
    for copy in swaps:
        copy.wait_recv()
    embed_load.wait()
    for ring in embed_first:
        ring.start()
    table_load.wait()
    table_ring.start(0)
    table_ring.start(1)
    small_load.wait()
    small_crossing.wait_recv()
    for j in range(4):
        add_blocks(small_sums.at[j], [small_sibling.at[j]], 16)
    small_rings[0].start()
    for part in range(3):
        add_crossing(part, 2, 1)
    for ring in embed_first:
        ring.forward()
    for part in range(3):
        first_rings[part].start(1)
    for part in range(3):
        add_crossing(part, 1)
    for ring, later in zip(embed_first, embed_second):
        ring.finish()
        later.start()
    small_rings[0].finish()
    small_rings[1].start()
    share(0, 0)
    share(1, 0)
    for part in range(3):
        add_crossing(part, 3)
    for part in range(3):
        first_rings[part].start_near()
    table_ring.start_near()
    ids_ring.finish()

    @pl.loop(0, 4)
    def _(index):
        at = pl.ds(pl.multiple_of(index * chunk, chunk), chunk)
        table_grad_ref[at] = jnp.zeros((chunk, width), jnp.float32)

    scatter_rows(0, core, 0)
    scatter_rows(1, core, 0)
    for ring in first_rings:
        ring.forward()
    for part in range(3):
        add_crossing(part, 0)
    for copy in embed_siblings:
        copy.wait_recv()
    embed_siblings.clear()
    scatter_rows(0, 1 - core, 0)
    scatter_rows(1, 1 - core, 0)
    for part in range(2):
        embed_second[part].forward()
        share(part, 1)
        share(part, 3)
    small_rings[1].finish()
    small_rings[2].start()
    table_ring.forward()
    for part in range(2):
        scatter_rows(part, core, 1)
        scatter_rows(part, core, 3)
    for copy in embed_siblings:
        copy.wait_recv()
    embed_siblings.clear()
    for part in range(2):
        scatter_rows(part, 1 - core, 1)
        scatter_rows(part, 1 - core, 3)
    to_sibling.settle(sums)
    for ring, later in zip(first_rings, middle_rings):
        ring.finish()
        later.start()
    small_rings[2].finish()
    own_small = small_sums[place[Z], 4 * place[Y] + across].astype(jnp.float32)
    final_ref[0, core, place[Z], place[Y], across] = own_small[:8]
    final_ref[1, core, across, place[Z], place[Y]] = jnp.concatenate(
        [own_small[8:9], jnp.zeros((7, 128), jnp.float32)], 0
    )
    for gather in gathers[0]:
        gather.start()
    for part in range(2):
        embed_second[part].finish()
        share(part, 2)
    scatter_rows(0, core, 2)
    for ring in middle_rings:
        ring.forward()
    for gather, later in zip(gathers[0], gathers[1]):
        gather.finish()
        later.start()
    scatter_rows(1, core, 2)
    for copy in embed_siblings:
        copy.wait_recv()
    scatter_rows(0, 1 - core, 2)
    to_owners.settle(sums)
    wires.settle(6)
    for ring, later in zip(middle_rings, last_rings):
        ring.finish()
        later.start()
    for gather, later in zip(gathers[1], gathers[2]):
        gather.finish()
        later.start()
    scatter_rows(1, 1 - core, 2)
    table_ring.arrive()
    table_block = rows // TABLE_CHUNKS

    @pl.loop(0, TABLE_CHUNKS)
    def _(index):
        at = pl.ds(pl.multiple_of(index * table_block, table_block), table_block)
        table_grad_ref[at] += (
            table_sums[across, index].astype(jnp.float32)
            + table_whole[0, index].astype(jnp.float32)
            + table_whole[1, index].astype(jnp.float32)
        )

    table_squares = jnp.zeros((1, width), jnp.float32)
    for index in range(4):
        values = table_grad_ref[index * chunk : (index + 1) * chunk]
        table_squares += jnp.sum(values * values, 0, keepdims=True)
    squares = jnp.zeros((1, 128), jnp.float32)
    to_table.settle(sums)
    for part in range(3):
        last_rings[part].arrive()
        k1, k2, k3 = (place[axis] for axis in ORDERS[part])
        for which in range(2):
            total = sums_at(part, k3, 8 * k2 + 2 * k1 + which, 1)[0].astype(jnp.float32)
            for step in range(3):
                total += whole_c[part, step, which].astype(jnp.float32)
            grads_out_ref[part, which] = total
            squares += jnp.sum(total * total, 0, keepdims=True)
    final_siblings = []
    for part in range(2):
        gathers[2][part].finish()
        mine = final_ref.at[part, core]
        final_siblings.append(wires.send(mine, mine, sibling))
    stores = []

    def store(source, target):
        stores.append(pltpu.make_async_copy(source, target, local_sems.at[17 + len(stores)]))
        stores[-1].start()

    own_clip = clip_for(jnp.sum(squares))[1]
    squares += table_squares[:, :128] + table_squares[:, 128:]
    roots_load.wait()

    def products(slots):
        for slot in slots:
            grad = grads_out_ref[slot // 2, slot % 2] * own_clip
            left_gram[slot] = fine_dot(grad, grad, ((1,), (1,)))
            right_gram[slot] = fine_dot(grad, grad, ((0,), (0,)))
            left_part[slot] = fine_dot(left_roots[slot], grad)

    store(table_grad_ref, table_grad_target)
    store(grads_out_ref, grads_out_target)
    loss = sum(loss_ref[:, 128 * index : 128 * (index + 1)] for index in range(4))
    totals = jnp.concatenate([squares, loss, jnp.zeros((6, 128), jnp.float32)], 0)
    for phase, (own, others) in enumerate(
        ((2 * across + core, line), (SIDE * place[Z] + place[Y], plane))
    ):
        mine = totals_all.at[phase, own]
        mine[...] = totals
        bundle = wires.bundle()
        for other in others:
            wires.send_all(mine, mine, other, bundle)
        products(range(3 * phase, 3 * phase + 3))
        if phase == 0:
            for copy in final_siblings:
                copy.wait_recv()
            store(final_ref, final_target)
            later_sends.settle(sums)
        else:
            store(left_gram, left_gram_target)
            store(right_gram, right_gram_target)
            store(left_part, left_part_target)
            wires.settle()
        wires.whole(totals_all.at[phase, pl.ds(0, len(others))], sibling, bundle).wait()
        totals = totals_all[phase, 0]
        for index in range(1, len(others) + 1):
            totals += totals_all[phase, index]
    totals_ref[...] = totals
    for copy in stores:
        copy.wait()


def finish_call(grads, small, head_grad, d_embed, left_roots, token_ids, loss_row):
    bf16 = jnp.bfloat16
    _, chunks, chunk_rows, width = head_grad.shape
    rows = chunks * chunk_rows
    block = (BLOCK, BLOCK)
    return pl.pallas_call(
        finish_kernel,
        name="reduce_and_scatter",
        out_shape=(
            jax.ShapeDtypeStruct((3, 2) + block, jnp.float32),
            jax.ShapeDtypeStruct((rows, width), jnp.float32),
            jax.ShapeDtypeStruct((2, 2, SIDE, SIDE, SIDE, 8, 128), jnp.float32),
            *[jax.ShapeDtypeStruct(left_roots.shape, jnp.float32)] * 3,
            jax.ShapeDtypeStruct((8, 128), jnp.float32),
        ),
        in_specs=[ANY] * 5 + [VMEM] * 2,
        out_specs=(ANY,) * 6 + (VMEM,),
        scratch_shapes=[
            pltpu.VMEM((3, 2) + block, jnp.float32),
            pltpu.VMEM((rows, width), jnp.float32),
            pltpu.VMEM((2, 2, SIDE, SIDE, SIDE, 8, 128), jnp.float32),
            *[pltpu.VMEM(left_roots.shape, jnp.float32)] * 4,
            pltpu.VMEM((3 * SIDE * 32,) + block, bf16),
            pltpu.VMEM((3, SIDE, 32) + block, bf16),
            pltpu.VMEM((3, 2, 16) + block, bf16),
            pltpu.VMEM((3, 2, 32) + block, bf16),
            pltpu.VMEM((3, 2, 4) + block, bf16),
            pltpu.VMEM((3, 2, 8) + block, bf16),
            pltpu.VMEM((3, 3, 2) + block, bf16),
            pltpu.VMEM((SIDE, 16, 16, 128), bf16),
            pltpu.VMEM((SIDE, 16, 16, 128), bf16),
            pltpu.VMEM((3, 16, 16, 128), bf16),
            pltpu.VMEM((3, 4, 16, 128), bf16),
            pltpu.VMEM((3, 1, 16, 128), bf16),
            pltpu.VMEM(head_grad.shape, bf16),
            pltpu.VMEM((2, chunks // 2, chunk_rows, width), bf16),
            pltpu.VMEM((2, chunks, chunk_rows, width), bf16),
            pltpu.VMEM((2, 2, SIDE, 8, 128, width), bf16),
            pltpu.VMEM((N_DP,) + token_ids.shape, jnp.int32),
            pltpu.VMEM((2, SIDE * SIDE, 8, 128), jnp.float32),
            pltpu.SemaphoreType.DMA((42,)),
            pltpu.SemaphoreType.DMA((146,)),
            pltpu.SemaphoreType.DMA((23,)),
        ],
        compiler_params=pltpu.CompilerParams(
            collective_id=3, has_side_effects=True, vmem_limit_bytes=VMEM_BYTES
        ),
    )(grads, small, head_grad, d_embed, left_roots, token_ids, loss_row)


def row_mean(values):
    return jnp.mean(values, -1, keepdims=True)


def normalized(values):
    center = values - row_mean(values)
    scale = lax.rsqrt(row_mean(center * center) + LN_EPS)
    return center * scale, scale


def norm_backward(d_normed, hat, scale, gain):
    d_hat = d_normed * gain
    d_values = scale * (d_hat - row_mean(d_hat) - hat * row_mean(d_hat * hat))
    d_gain = jnp.sum(d_normed * hat, 0, keepdims=True)
    return d_values, d_gain, jnp.sum(d_normed, 0, keepdims=True)


QKV, PROJ, FC, OUT = (0, 24), (192, 8), (256, 32), (512, 8)


def load_blocks(full_ref, blocks, sems):
    share = blocks.shape[0] // 8
    copies = []
    for index in range(8):
        part = pl.ds(index * share, share)
        copies.append(pltpu.make_async_copy(full_ref.at[part], blocks.at[part], sems.at[index]))
        copies[-1].start()
    return copies


def weight_tiles(blocks, where_ref, matrix, row, rows, column, columns):
    first, in_row = matrix
    return jnp.concatenate(
        [
            jnp.concatenate(
                [
                    blocks[where_ref[first + (row + i) * in_row + column + j]]
                    for j in range(columns)
                ],
                1,
            )
            for i in range(rows)
        ],
        0,
    )


def selected_rows(ref, positions):
    return jnp.concatenate([ref[pl.ds(position, 1), :] for position in positions], 0)


def pair_masks(count):
    lane = lax.broadcasted_iota(jnp.int32, (2 * count, 2 * HEAD_DIM), 1)
    row = lax.broadcasted_iota(jnp.int32, (2 * count, 2 * HEAD_DIM), 0)
    return (lane < HEAD_DIM) == (row < count)


def doubled(values, own_lanes):
    both = jnp.concatenate([values, values], 0)
    return jnp.where(own_lanes, both.astype(jnp.float32), 0.0).astype(jnp.bfloat16)


def folded(values, count):
    lane = lax.broadcasted_iota(jnp.int32, (count, 2 * HEAD_DIM), 1)
    return jnp.where(lane < HEAD_DIM, values[:count], values[count:])


def forward_phase(
    where_ref,
    at_ref,
    length_ref,
    hidden_ref,
    vec_ref,
    head_in_ref,
    query_ref,
    kv_ref,
    probs_ref,
    attended_ref,
    middle_ref,
    pre_act_ref,
    last_ref,
    blocks,
    normed_rows,
    activated,
):
    count = head_in_ref.shape[0]
    bf16 = jnp.bfloat16
    own = lax.axis_index("vocab")
    positions = [at_ref[i, own] for i in range(count)]
    length = length_ref[own]
    hat, _ = normalized(hidden_ref[...])
    normed_rows[...] = hat * vec_ref[0:1] + vec_ref[1:2]
    normed_one = normed_rows[...].astype(bf16)
    normed_own = selected_rows(normed_rows, positions).astype(bf16)

    @pl.loop(0, 4)
    def _(tile):
        at = lane_range(256 * tile, 256)
        weight = weight_tiles(blocks, where_ref, QKV, 0, 8, 2 * tile, 2)
        product = jnp.dot(normed_own, weight, preferred_element_type=jnp.float32)
        query_ref[:, at] = (product + vec_ref[2:3, at]).astype(bf16)

    @pl.loop(0, 4)
    def _(tile):
        at = lane_range(256 * tile, 256)
        weight = weight_tiles(blocks, where_ref, QKV, 0, 8, 8 + 2 * tile, 2)
        product = jnp.dot(normed_one, weight, preferred_element_type=jnp.float32)
        kv_ref[:, at] = product.astype(bf16)

    @pl.loop(0, 4)
    def _(tile):
        weight = weight_tiles(blocks, where_ref, QKV, 0, 8, 16 + 2 * tile, 2)
        product = jnp.dot(normed_one, weight, preferred_element_type=jnp.float32)
        bias = vec_ref[3:4, lane_range(256 * tile, 256)]
        kv_ref[:, lane_range(D + 256 * tile, 256)] = (product + bias).astype(bf16)

    own_lanes = pair_masks(count)
    pairs = HEADS // 2
    seq_len = hidden_ref.shape[0]
    row = lax.broadcasted_iota(jnp.int32, (count, seq_len), 0)
    key = lax.broadcasted_iota(jnp.int32, (count, seq_len), 1)
    last_key = jnp.zeros((count, seq_len), jnp.int32)
    for i in range(count):
        last_key = jnp.where(row == i, jnp.minimum(positions[i], length - 1), last_key)
    allowed = jnp.concatenate([key <= last_key] * 2, 0)
    for pair in range(pairs):
        lanes = slice(128 * pair, 128 * pair + 128)
        values_at = slice(D + 128 * pair, D + 128 * pair + 128)
        scores = dot_nt(doubled(query_ref[:, lanes], own_lanes), kv_ref[:, lanes]) * HEAD_DIM ** (
            -0.5
        )
        scores = jnp.where(allowed, scores, NEG_FILL)
        exps = jnp.exp(scores - jnp.max(scores, -1, keepdims=True))
        probs = exps / jnp.sum(exps, -1, keepdims=True)
        probs_ref[2 * count * pair : 2 * count * (pair + 1)] = probs
        mixed = jnp.dot(
            probs.astype(bf16), kv_ref[:, values_at], preferred_element_type=jnp.float32
        )
        attended_ref[:, lanes] = folded(mixed, count).astype(bf16)

    attended = attended_ref[...]
    middle_ref[...] = selected_rows(hidden_ref, positions) + vec_ref[4:5]

    @pl.loop(0, 4)
    def _(tile):
        weight = weight_tiles(blocks, where_ref, PROJ, 0, 8, 2 * tile, 2)
        middle_ref[:, lane_range(256 * tile, 256)] += jnp.dot(
            attended, weight, preferred_element_type=jnp.float32
        )

    middle = middle_ref[...]
    hat, _ = normalized(middle)
    normed_two = (hat * vec_ref[5:6] + vec_ref[6:7]).astype(bf16)

    @pl.loop(0, 16)
    def _(tile):
        at = lane_range(256 * tile, 256)
        weight = weight_tiles(blocks, where_ref, FC, 0, 8, 2 * tile, 2)
        bias = vec_ref[pl.ds(7 + tile // 4, 1), lane_range(256 * (tile % 4), 256)]
        pre_act = jnp.dot(normed_two, weight, preferred_element_type=jnp.float32) + bias
        pre_act_ref[:, at] = pre_act
        activated[:, at] = gelu(pre_act).astype(bf16)

    last_ref[...] = middle + vec_ref[11:12]

    @pl.loop(0, 16)
    def _(index):
        tile, depth = index // 4, index % 4
        weight = weight_tiles(blocks, where_ref, OUT, 8 * depth, 8, 2 * tile, 2)
        last_ref[:, lane_range(256 * tile, 256)] += jnp.dot(
            activated[:, lane_range(1024 * depth, 1024)],
            weight,
            preferred_element_type=jnp.float32,
        )

    hat, _ = normalized(last_ref[...])
    head_in_ref[...] = (hat * vec_ref[12:13] + vec_ref[13:14]).astype(bf16)


def forward_kernel(
    where_ref,
    at_smem_ref,
    length_smem_ref,
    ids_ref,
    target_ref,
    at_ref,
    length_ref,
    *refs,
):
    sources, refs = refs[:4], refs[4:]
    (full_ref, out_blocks_ref), targets, refs = refs[:2], refs[2:10], refs[10:]
    (d_head_ref, table_grad_ref, loss_ref), refs = refs[:3], refs[3:]
    held, kept, refs = refs[:4], refs[4:12], refs[12:]
    matrices_ref, table_ref, positions_ref, vec_ref = held
    (
        hidden_ref,
        query_ref,
        kv_ref,
        probs_ref,
        attended_ref,
        middle_ref,
        pre_act_ref,
        last_ref,
    ) = kept
    (
    blocks,
    table,
    own_low,
    table_pad,
    ids_all,
    parts,
    sibling_in,
    half_in,
    whole_in,
    landing,
    ready,
    arrived,
    normed_rows,
    activated,
    head_in,
    pieces,
    logits,
    stats,
    d_rows,
    d_sibling,
    d_first,
    d_second,
    out_staging,
    send_sems,
    recv_sems,
    local_sems,
    ) = refs
    place = coordinates()
    wires = Wires(send_sems, recv_sems)
    loads = [
        pltpu.make_async_copy(source, target, local_sems.at[5 + index])
        for index, (source, target) in enumerate(zip(sources, held))
    ]
    for copy in loads:
        copy.start()
    vocab_group = [
        moved(moved(moved(place, Y, near), Z, far), CORE, side)
        for near in range(SIDE)
        for far in range(SIDE)
        for side in range(2)
    ][1:]
    others = vocab_group + [moved(place, X, step) for step in (1, 2, 3)]
    greet(others)
    for copy in loads:
        copy.wait()
    table_ring = gather_phase(
        place,
        wires,
        others,
        ids_ref,
        matrices_ref,
        table_ref,
        positions_ref,
        blocks,
        table,
        hidden_ref,
        own_low,
        table_pad,
        ids_all,
        parts,
        sibling_in,
        half_in,
        whole_in,
        landing,
        ready,
        arrived,
        local_sems,
    )
    keep = pltpu.make_async_copy(blocks, full_ref, local_sems.at[4])
    keep.start()
    forward_phase(
        where_ref,
        at_smem_ref,
        length_smem_ref,
        hidden_ref,
        vec_ref,
        head_in,
        query_ref,
        kv_ref,
        probs_ref,
        attended_ref,
        middle_ref,
        pre_act_ref,
        last_ref,
        blocks,
        normed_rows,
        activated,
    )
    keeps = [keep]
    for index, (source, target) in enumerate(zip(kept, targets)):
        keeps.append(pltpu.make_async_copy(source, target, local_sems.at[9 + index]))
        keeps[-1].start()

    def arrange_out(chunk):
        if chunk >= 2:
            keeps[len(keeps) - 2].wait()
            del keeps[len(keeps) - 2]
        slot = out_staging.at[chunk % 2]

        @pl.loop(0, 16, unroll=4)
        def _(index):
            slot[index] = blocks[where_ref[OUT[0] + 16 * chunk + index]]

        target = out_blocks_ref.at[pl.ds(16 * chunk, 16)]
        keeps.append(pltpu.make_async_copy(slot, target, local_sems.at[17 + chunk % 2]))
        keeps[-1].start()

    stores, sends = head_phase(
        place,
        wires,
        vocab_group,
        table_ring,
        head_in,
        table,
        target_ref,
        at_ref,
        length_ref,
        d_head_ref,
        table_grad_ref,
        loss_ref,
        parts,
        pieces,
        logits,
        stats,
        d_rows,
        d_sibling,
        d_first,
        d_second,
        local_sems,
        arrange_out,
        keeps,
    )
    sends.settle(blocks)
    for copy in stores:
        copy.wait()


def forward_call(where, positions, lengths, token_ids, target_ids, matrices, vocab_table, positions_table, vectors):
    rows, width = vocab_table.shape
    padded = -(-rows // 128) * 128
    own, seqs = positions.shape
    seq_len = positions_table.shape[0]
    count, half = own * seqs, D // 2
    bf16, f32 = jnp.bfloat16, jnp.float32
    shape = jax.ShapeDtypeStruct
    slots = where.shape[0]
    cache = (
        shape((seq_len, D), f32),
        shape((own, D), bf16),
        shape((seq_len, 2 * D), bf16),
        shape((HEADS * own, seq_len), f32),
        shape((own, D), bf16),
        shape((own, D), f32),
        shape((own, FF), f32),
        shape((own, D), f32),
    )
    states = (matrices, vocab_table, positions_table, vectors)
    smem = pl.BlockSpec(memory_space=pltpu.SMEM)
    return pl.pallas_call(
        forward_kernel,
        name="forward_and_head",
        out_shape=(
            shape((slots, BLOCK, BLOCK), bf16),
            shape((slots // 3, BLOCK, BLOCK), bf16),
            *cache,
            shape((own, D), f32),
            shape((N_DP * rows, width), bf16),
            shape((1, count), f32),
        ),
        in_specs=[smem] * 3 + [VMEM] * 4 + [ANY] * 4,
        out_specs=(ANY,) * 10 + (VMEM, ANY, VMEM),
        scratch_shapes=[
            *[pltpu.VMEM(array.shape, array.dtype) for array in (*states, *cache)],
            pltpu.VMEM((slots, BLOCK, BLOCK), bf16),
            pltpu.VMEM((N_DP, rows, width), bf16),
            pltpu.VMEM((3, 2, BLOCK, BLOCK), bf16),
            pltpu.VMEM((padded, width), bf16),
            pltpu.VMEM((N_DP,) + token_ids.shape, jnp.int32),
            pltpu.VMEM((128 * 128, width), bf16),
            pltpu.VMEM((2, 32 * 128, width), bf16),
            pltpu.VMEM((2, 2, 4 * 128, width), bf16),
            pltpu.VMEM((2, 2, 8 * 128, width), bf16),
            pltpu.VMEM((2, 3, 2 * 128, width), bf16),
            pltpu.VMEM((N_DP, 128, width), bf16),
            pltpu.VMEM((N_DP, 128, width), bf16),
            pltpu.VMEM((seq_len, D), f32),
            pltpu.VMEM((own, FF), bf16),
            pltpu.VMEM((own, D), bf16),
            pltpu.VMEM((2, 2, SIDE, SIDE, own, half), bf16),
            pltpu.VMEM((rows, count), f32),
            pltpu.VMEM((N_VOCAB, 8, count // 4), f32),
            pltpu.VMEM((2, 2, SIDE, SIDE, own, half), bf16),
            pltpu.VMEM((2, SIDE, SIDE, own, half), bf16),
            pltpu.VMEM((2, 3, SIDE, own, half), bf16),
            pltpu.VMEM((2, 3, own, half), bf16),
            pltpu.VMEM((2, 16, BLOCK, BLOCK), bf16),
            pltpu.SemaphoreType.DMA((21,)),
            pltpu.SemaphoreType.DMA((123,)),
            pltpu.SemaphoreType.DMA((19,)),
        ],
        compiler_params=pltpu.CompilerParams(
            collective_id=1, has_side_effects=True, vmem_limit_bytes=VMEM_BYTES
        ),
    )(
        where,
        positions,
        lengths,
        token_ids,
        target_ids,
        positions,
        lengths.reshape(1, -1),
        *states,
    )


def gelu_slope(values):
    cube = 0.044715 * values * values
    bent = jnp.tanh(GELU_C * (values + cube * values))
    return 0.5 * (1.0 + bent) + 0.5 * values * (1.0 - bent * bent) * GELU_C * (1.0 + 3.0 * cube)


def backward_kernel(
    where_ref,
    at_ref,
    full_ref,
    out_blocks_ref,
    *refs,
):
    sources, (grads_ref, small_ref, d_embed_ref), refs = refs[:10], refs[10:13], refs[13:]
    held, refs = refs[:10], refs[10:]
    (
        d_head_ref,
        last_ref,
        vec_ref,
        pre_act_ref,
        middle_ref,
        attended_ref,
        query_ref,
        kv_ref,
        probs_ref,
        hidden_ref,
    ) = held
    (
    blocks,
    grad_blocks,
    activated,
    d_pre,
    normed,
    rows_out,
    d_qkv,
    spread,
    query_grads,
    vec_grads,
    sems,
    grad_sem,
    ) = refs
    loads = [
        pltpu.make_async_copy(source, target, sems.at[9 + index])
        for index, (source, target) in enumerate(zip(sources, held))
    ]
    for copy in loads:
        copy.start()
    out_blocks = grad_blocks.at[pl.ds(0, out_blocks_ref.shape[0])]
    out_load = pltpu.make_async_copy(out_blocks_ref, out_blocks, sems.at[8])
    out_load.start()
    copies = load_blocks(full_ref, blocks, sems)
    for copy in loads:
        copy.wait()
    count = d_head_ref.shape[0]
    bf16 = jnp.bfloat16
    own = lax.axis_index("vocab")
    positions = [at_ref[i, own] for i in range(count)]

    def weight_grad(matrix, rows, left_ref, right, together=4):
        first, in_row = matrix

        @pl.loop(0, rows // together)
        def _(group):
            left = left_ref[:, lane_range(128 * together * group, 128 * together)]
            for column in range(0, in_row, 2):
                product = dot_tn(left, right[:, 128 * column : 128 * column + 256]).astype(bf16)
                for inner in range(2 * together):
                    row, side = inner // 2, inner % 2
                    index = first + (group * together + row) * in_row + column + side
                    grad_blocks[index] = product[
                        128 * row : 128 * row + 128, 128 * side : 128 * side + 128
                    ]
                    pltpu.make_async_copy(
                        grad_blocks.at[index], grads_ref.at[where_ref[index]], grad_sem
                    ).start()

    hat, scale = normalized(last_ref[...])
    d_last, vec_grads[12:13], vec_grads[13:14] = norm_backward(
        d_head_ref[...], hat, scale, vec_ref[12:13]
    )
    d_branch = d_last.astype(bf16)
    vec_grads[11:12] = jnp.sum(d_branch.astype(jnp.float32), 0, keepdims=True)
    activated[...] = gelu(pre_act_ref[...]).astype(bf16)
    weight_grad(OUT, 32, activated, d_branch)
    out_load.wait()

    @pl.loop(0, 16)
    def _(tile):
        at = lane_range(256 * tile, 256)
        weight = jnp.concatenate(
            [
                jnp.concatenate([out_blocks[16 * tile + 8 * row + j] for j in range(8)], 1)
                for row in range(2)
            ],
            0,
        )
        lowered = (dot_nt(d_branch, weight) * gelu_slope(pre_act_ref[:, at])).astype(bf16)
        d_pre[:, at] = lowered
        vec_grads[pl.ds(7 + tile // 4, 1), lane_range(256 * (tile % 4), 256)] = jnp.sum(
            lowered.astype(jnp.float32), 0, keepdims=True
        )

    hat, scale = normalized(middle_ref[...])
    normed[pl.ds(0, count)] = (hat * vec_ref[5:6] + vec_ref[6:7]).astype(bf16)
    weight_grad(FC, 8, normed.at[pl.ds(0, count)], d_pre[...])
    rows_out[...] = jnp.zeros(rows_out.shape, jnp.float32)
    for copy in copies:
        copy.wait()

    @pl.loop(0, 16)
    def _(index):
        tile, depth = index // 4, index % 4
        weight = weight_tiles(blocks, where_ref, FC, 2 * tile, 2, 8 * depth, 8)
        rows_out[pl.ds(0, count), lane_range(256 * tile, 256)] += dot_nt(
            d_pre[:, lane_range(1024 * depth, 1024)], weight
        )

    d_middle, vec_grads[5:6], vec_grads[6:7] = norm_backward(
        rows_out[pl.ds(0, count)], hat, scale, vec_ref[5:6]
    )
    d_middle = d_middle + d_last
    d_proj = d_middle.astype(bf16)
    vec_grads[4:5] = jnp.sum(d_proj.astype(jnp.float32), 0, keepdims=True)
    weight_grad(PROJ, 8, attended_ref, d_proj)

    @pl.loop(0, 4)
    def _(tile):
        weight = weight_tiles(blocks, where_ref, PROJ, 2 * tile, 2, 0, 8)
        rows_out[pl.ds(0, count), lane_range(256 * tile, 256)] = dot_nt(d_proj, weight)

    own_lanes = pair_masks(count)
    spread[...] = jnp.zeros(spread.shape, jnp.float32)
    for pair in range(HEADS // 2):
        lanes = slice(128 * pair, 128 * pair + 128)
        values_at = slice(D + 128 * pair, D + 128 * pair + 128)
        d_mixed = doubled(rows_out[0:count, lanes].astype(bf16), own_lanes)
        probs = probs_ref[2 * count * pair : 2 * count * (pair + 1)]
        d_probs = dot_nt(d_mixed, kv_ref[:, values_at])
        inner = jnp.sum(probs * d_probs, -1, keepdims=True)
        d_scores = (probs * (d_probs - inner)).astype(bf16)
        d_values = dot_tn(probs.astype(bf16), d_mixed).astype(bf16)
        d_keys = dot_tn(d_scores, doubled(query_ref[:, lanes], own_lanes)) * HEAD_DIM ** (-0.5)
        d_query = jnp.dot(d_scores, kv_ref[:, lanes], preferred_element_type=jnp.float32)
        d_query = (folded(d_query, count) * HEAD_DIM ** (-0.5)).astype(bf16).astype(jnp.float32)
        vec_grads[2:3, lanes] = jnp.sum(d_query, 0, keepdims=True)
        vec_grads[3:4, lanes] = jnp.sum(d_values.astype(jnp.float32), 0, keepdims=True)
        query_grads[:, lanes] = d_query
        d_qkv[:, D + 128 * pair : D + 128 * pair + 128] = d_keys.astype(bf16)
        d_qkv[:, 2 * D + 128 * pair : 2 * D + 128 * pair + 128] = d_values
    for i in range(count):
        spread[pl.ds(positions[i], 1), :] = query_grads[i : i + 1, :]
    d_qkv[:, :D] = spread[...].astype(bf16)
    hat, scale = normalized(hidden_ref[...])
    normed[...] = (hat * vec_ref[0:1] + vec_ref[1:2]).astype(bf16)
    weight_grad(QKV, 8, normed, d_qkv)
    rows_out[...] = jnp.zeros(rows_out.shape, jnp.float32)

    @pl.loop(0, 12)
    def _(index):
        tile, depth = index // 3, index % 3
        weight = weight_tiles(blocks, where_ref, QKV, 2 * tile, 2, 8 * depth, 8)
        rows_out[:, lane_range(256 * tile, 256)] += dot_nt(
            d_qkv[:, lane_range(1024 * depth, 1024)], weight
        )

    d_hidden, vec_grads[0:1], vec_grads[1:2] = norm_backward(
        rows_out[...], hat, scale, vec_ref[0:1]
    )
    rows_out[...] = d_hidden
    for i in range(count):
        rows_out[pl.ds(positions[i], 1), :] += d_middle[i : i + 1]
    d_embed_ref[...] = rows_out[...].astype(bf16)
    vec_rows = vec_ref.shape[0]
    for index in range(small_ref.shape[0]):
        group, tile = index // 8, index % 8
        lanes = slice(128 * tile, 128 * tile + 128)
        vec_row = (
            vec_grads[group : group + 1, lanes]
            if group < vec_rows
            else jnp.zeros((1, 128), jnp.float32)
        )
        small_ref[index] = jnp.concatenate(
            [rows_out[8 * group : 8 * group + 8, lanes], vec_row, jnp.zeros((7, 128), jnp.float32)],
            0,
        ).astype(bf16)
    pltpu.make_async_copy(grad_blocks, grads_ref, grad_sem).wait()


def backward_call(where, positions, full, out_blocks, states):
    count = positions.shape[0]
    hidden = states[-1]
    bf16 = jnp.bfloat16
    shape = jax.ShapeDtypeStruct
    return pl.pallas_call(
        backward_kernel,
        name="layer_backward",
        out_shape=(
            shape(full.shape, bf16),
            shape((N_DP * N_VOCAB, 16, 128), bf16),
            shape(hidden.shape, bf16),
        ),
        grid_spec=pltpu.PrefetchScalarGridSpec(
            num_scalar_prefetch=2,
            grid=(),
            in_specs=[ANY] * 12,
            out_specs=(ANY, VMEM, VMEM),
            scratch_shapes=[
                *[pltpu.VMEM(array.shape, array.dtype) for array in states],
                pltpu.VMEM(full.shape, bf16),
                pltpu.VMEM(full.shape, bf16),
                pltpu.VMEM((count, FF), bf16),
                pltpu.VMEM((count, FF), bf16),
                pltpu.VMEM(hidden.shape, bf16),
                pltpu.VMEM(hidden.shape, jnp.float32),
                pltpu.VMEM((hidden.shape[0], 3 * D), bf16),
                pltpu.VMEM(hidden.shape, jnp.float32),
                pltpu.VMEM((count, D), jnp.float32),
                pltpu.VMEM((16, D), jnp.float32),
                pltpu.SemaphoreType.DMA((19,)),
                pltpu.SemaphoreType.DMA,
            ],
        ),
        compiler_params=pltpu.CompilerParams(vmem_limit_bytes=VMEM_BYTES),
    )(where, positions, full, out_blocks, *states)


def adam_step(weight, moment_one, moment_two, grad_in, rate, decay):
    new_one = BETA_ONE * moment_one + (1.0 - BETA_ONE) * grad_in
    new_two = BETA_TWO * moment_two + (1.0 - BETA_TWO) * grad_in * grad_in
    hat_one = new_one * (1.0 / (1.0 - BETA_ONE**STEP))
    hat_two = new_two * (1.0 / (1.0 - BETA_TWO**STEP))
    change = hat_one / (jnp.sqrt(hat_two) + ADAM_EPS)
    if decay:
        change = change + decay * weight
    return weight - rate * change, new_one, new_two


TABLE_PIECES = 2


def update_kernel(*refs):
    names = 20
    sources, (loss_ref, norm_ref, *targets) = refs[:names], refs[names : names + 15]
    buffers = refs[names + 15 : 2 * names + 15]
    results = refs[2 * names + 15 : 2 * names + 28]
    vec_grad, load_sems, store_sems = refs[2 * names + 28 :]
    loads, stores = [], []

    def load(index, at=None):
        source, target = sources[index], buffers[index]
        if at is not None:
            source, target = source.at[at], target.at[at]
        loads.append(pltpu.make_async_copy(source, target, load_sems.at[len(loads)]))
        loads[-1].start()

    def store(index, at=None):
        source, target = results[index], targets[index]
        if at is not None:
            source, target = source.at[at], target.at[at]
        stores.append(pltpu.make_async_copy(source, target, store_sems.at[len(stores)]))
        stores[-1].start()

    def await_loads(count):
        for copy in loads[:count]:
            copy.wait()
        del loads[:count]

    totals, final, table_grad, table, table_m, table_v = buffers[:6]
    grads, left_gram, right_gram, left_part = buffers[6:10]
    matrices, left_stats, right_stats, right_roots = buffers[10:14]
    positions, pos_m, pos_v, vectors, vectors_m, vectors_v = buffers[14:]
    matrices_new, left_new, right_new, matrices_grad = results[:4]
    rows, width = table.shape
    chunk = rows // TABLE_PIECES
    for index in range(2):
        load(index)
    for piece in range(TABLE_PIECES):
        for index in range(2, 6):
            load(index, pl.ds(piece * chunk, chunk))
    for index in range(6, names):
        load(index)
    await_loads(2)
    row_squares = jnp.zeros((8, 128), jnp.float32)
    for part in range(2):
        for core in range(2):
            values = final[part, core].reshape(SIDE**3, 8, 128)
            row_squares += jnp.sum(values * values, 0)
    norm, clip = clip_for(jnp.sum(totals[0:1]) + jnp.sum(row_squares))
    loss_ref[0, 0] = jnp.sum(totals[1:2])
    norm_ref[0, 0] = jnp.max(norm)
    wide_clip = jnp.concatenate([clip] * (width // 128), 1)
    for piece in range(TABLE_PIECES):
        await_loads(4)

        @pl.loop(0, chunk // 80)
        def _(inner):
            at = pl.ds(pl.multiple_of(piece * chunk + inner * 80, 80), 80)
            grad = table_grad[at] * wide_clip
            stepped = adam_step(
                table[at], table_m[at], table_v[at], grad, TABLE_RATE, DECAY_RATE
            )
            for order, value in enumerate(stepped):
                results[4 + order][at] = value

        for order in range(3):
            store(4 + order, pl.ds(piece * chunk, chunk))
    await_loads(8)
    own_squares = jnp.zeros((1, 128), jnp.float32)
    for slot in range(SLOTS):
        grad = grads[slot // 2, slot % 2]
        own_squares += jnp.sum(grad * grad, 0, keepdims=True)
    own_clip = clip_for(jnp.sum(own_squares))[1]
    ratio = jnp.where(own_clip > 0.0, clip / own_clip, 0.0)

    @pl.loop(0, SLOTS, unroll=3)
    def _(slot):
        matrices_grad[slot] = grads[slot // 2, slot % 2] * clip
        left_new[slot] = STAT_DECAY * left_stats[slot] + (1.0 - STAT_DECAY) * (
            left_gram[slot] * ratio * ratio
        )
        right_new[slot] = STAT_DECAY * right_stats[slot] + (1.0 - STAT_DECAY) * (
            right_gram[slot] * ratio * ratio
        )
        stepped = fine_dot(left_part[slot] * ratio, right_roots[slot])
        weight = matrices[slot]
        matrices_new[slot] = weight - SHAMPOO_RATE * (stepped + DECAY_RATE * weight)

    for index in range(4):
        store(index)
    await_loads(6)
    tiles = D // 128
    for index in range(N_DP * N_VOCAB):
        at_core, rest = index // 64, index % 64
        at_z, at_y, at_x = rest // 16, rest // 4 % 4, rest % 4
        group, lanes = index // tiles, slice(128 * (index % tiles), 128 * (index % tiles) + 128)
        at = slice(8 * group, 8 * group + 8)
        stepped = adam_step(
            positions[at, lanes],
            pos_m[at, lanes],
            pos_v[at, lanes],
            final[0, at_core, at_z, at_y, at_x] * clip,
            POS_RATE,
            DECAY_RATE,
        )
        for order, value in enumerate(stepped):
            results[7 + order][at, lanes] = value
        if group < vectors.shape[0]:
            vec_grad[group : group + 1, lanes] = (
                final[1, at_core, at_x, at_z, at_y, 0:1] * clip
            )
    for index in range(7, 10):
        store(index)
    stepped = adam_step(
        vectors[...], vectors_m[...], vectors_v[...], vec_grad[...], VECTOR_RATE, 0.0
    )
    for order, value in enumerate(stepped):
        results[10 + order][...] = value
        store(10 + order)
    for copy in stores:
        copy.wait()


def update_call(totals, final, grads, products, blocks, table_grad, table, positions, vectors):
    sources = [totals, final, table_grad, *table, grads, *products, *blocks, *positions, *vectors]
    shape = lambda array: jax.ShapeDtypeStruct(array.shape, jnp.float32)
    targets = [shape(blocks[0])] * 4
    targets += [shape(array) for array in (*table, *positions, *vectors)]
    scalar = jax.ShapeDtypeStruct((1, 1), jnp.float32)
    smem = pl.BlockSpec(memory_space=pltpu.SMEM)
    return pl.pallas_call(
        update_kernel,
        name="optimizer_update",
        out_shape=(scalar, scalar, *targets),
        in_specs=[ANY] * len(sources),
        out_specs=(smem, smem) + (ANY,) * len(targets),
        scratch_shapes=[pltpu.VMEM(array.shape, jnp.float32) for array in sources]
        + [pltpu.VMEM(target.shape, jnp.float32) for target in targets]
        + [
            pltpu.VMEM(vectors[0].shape, jnp.float32),
            pltpu.SemaphoreType.DMA((len(sources) + 4 * (TABLE_PIECES - 1),)),
            pltpu.SemaphoreType.DMA((len(targets) + 3 * (TABLE_PIECES - 1),)),
        ],
        compiler_params=pltpu.CompilerParams(vmem_limit_bytes=VMEM_BYTES),
    )(*sources)


def slot_places():
    slot = np.arange(N_DP * N_VOCAB * SLOTS)
    device, own = slot // SLOTS, slot % SLOTS
    inner = device % N_VOCAB
    place = (device // N_VOCAB, inner // 2 % SIDE, inner // (2 * SIDE), inner % 2)
    part = own // 2
    result = np.zeros_like(slot)
    for which, (first, second, third) in enumerate(ORDERS):
        index = which * 2 + place[CORE]
        for axis in (third, second, first):
            index = index * SIDE + place[axis]
        result = np.where(part == which, index * 2 + own % 2, result)
    return result.astype(np.int32)


def per_device(
    token_ids,
    seq_lengths,
    loss_positions,
    target_ids,
    block_of_slot,
    matrices,
    left_stats,
    right_stats,
    left_roots,
    right_roots,
    vocab_table,
    table_m,
    table_v,
    positions_table,
    pos_m,
    pos_v,
    vectors,
    vectors_m,
    vectors_v,
):
    block_iota = jnp.arange(block_of_slot.shape[0], dtype=jnp.int32)
    where = jnp.sum(
        jnp.where(block_of_slot[None, :] == block_iota[:, None], slot_places()[None, :], 0),
        1,
        dtype=jnp.int32,
    )
    positions = loss_positions.T
    full, out_blocks, *cache, d_head_in, head_grad, loss_row = forward_call(
        where,
        positions,
        seq_lengths,
        token_ids,
        target_ids.T,
        matrices,
        vocab_table,
        positions_table,
        vectors,
    )
    hidden, query, key_value, probs, attended, middle, pre_act, last = cache
    grad_blocks, small, d_embed = backward_call(
        where,
        positions,
        full,
        out_blocks,
        (d_head_in, last, vectors, pre_act, middle, attended, query, key_value, probs, hidden),
    )
    owned_grads, table_grad_own, final, *products, totals = finish_call(
        grad_blocks.reshape(3, 2, SIDE, 32, BLOCK, BLOCK),
        small.reshape(2, SIDE, 16, 16, 128),
        head_grad.reshape(N_DP, TABLE_CHUNKS, -1, head_grad.shape[1]),
        d_embed,
        left_roots,
        token_ids,
        loss_row,
    )
    loss, norm, *updated = update_call(
        totals,
        final,
        owned_grads,
        products,
        (matrices, left_stats, right_stats, right_roots),
        table_grad_own,
        (vocab_table, table_m, table_v),
        (positions_table, pos_m, pos_v),
        (vectors, vectors_m, vectors_v),
    )
    return (loss.reshape(()), norm.reshape(()), *updated)


def solution(mesh):
    in_specs = (
        P("dp", None),
        P("dp"),
        P("dp", None),
        P("dp", None),
        P(),
        P(("dp", "vocab"), None, None),
        P(("dp", "vocab"), None, None),
        P(("dp", "vocab"), None, None),
        P(("dp", "vocab"), None, None),
        P(("dp", "vocab"), None, None),
        P("vocab", "dp"),
        P("vocab", "dp"),
        P("vocab", "dp"),
        P(),
        P(),
        P(),
        P(),
        P(),
        P(),
    )
    out_specs = (
        P(),
        P(),
        P(("dp", "vocab"), None, None),
        P(("dp", "vocab"), None, None),
        P(("dp", "vocab"), None, None),
        P(("dp", "vocab"), None, None),
        P("vocab", "dp"),
        P("vocab", "dp"),
        P("vocab", "dp"),
        P(),
        P(),
        P(),
        P(),
        P(),
        P(),
    )
    return jax.shard_map(
        per_device, mesh=mesh, in_specs=in_specs, out_specs=out_specs, check_vma=False
    )
```

```python
import math

import jax
import jax.numpy as jnp
import numpy as np
from jax import lax
from jax.experimental import pallas as pl
from jax.experimental.pallas import tpu as pltpu
from jax.sharding import PartitionSpec as P

D = 1024
HEADS = 16
HEAD_DIM = 64
FF = 4096
VOCAB_REAL = 50257
LAYERS = 1
BLOCK = 128
STEP = 10


LN_EPS = 1e-05
CLIP_LEVEL = 0.05
BETA_ONE = 0.9
BETA_TWO = 0.999
ADAM_EPS = 1e-08
STAT_DECAY = 0.95
SHAMPOO_RATE = 0.03
TABLE_RATE = 0.15
POS_RATE = 0.05
VECTOR_RATE = 0.25
DECAY_RATE = 0.1
NEG_FILL = -1e30
GELU_C = 0.7978845608028654
HIGH = lax.Precision.HIGHEST


def gelu(values):
    return 0.5 * values * (1.0 + jnp.tanh(GELU_C * (values + 0.044715 * values * values * values)))


def dot_nt(left, right):
    return lax.dot_general(
        left, right, (((1,), (1,)), ((), ())), preferred_element_type=jnp.float32
    )


def dot_tn(left, right):
    return lax.dot_general(
        left, right, (((0,), (0,)), ((), ())), preferred_element_type=jnp.float32
    )


VMEM_BYTES = 63 << 20
TABLE_CHUNKS = 20
MESH_IDS = pl.DeviceIdType.MESH
ANY = pl.BlockSpec(memory_space=pl.ANY)
VMEM = pl.BlockSpec(memory_space=pltpu.VMEM)
N_DP = 4
N_VOCAB = 32
SIDE = 4
X, Y, Z, CORE = range(4)
ORDERS = ((X, Y, Z), (Y, Z, X), (Z, X, Y))
SLOTS = 6


def coordinates():
    across = lax.axis_index("dp")
    inner = lax.axis_index("vocab")
    return (across, (inner // 2) % SIDE, inner // (2 * SIDE), inner % 2)


def moved(place, axis, step):
    shifted = list(place)
    shifted[axis] = (place[axis] + step) % (2 if axis == CORE else SIDE)
    return tuple(shifted)


def device_of(place):
    return (place[X], (place[Z] * SIDE + place[Y]) * 2 + place[CORE])


def rings_of(place, axes):
    others = [moved(place, CORE, 1)]
    return others + [moved(place, axis, step) for axis in axes for step in (1, 2, 3)]


def greet(others):
    for other in others:
        pl.semaphore_signal(
            pltpu.get_barrier_semaphore(),
            inc=1,
            device_id=device_of(other),
            device_id_type=MESH_IDS,
        )


def await_greetings(others):
    pl.semaphore_wait(pltpu.get_barrier_semaphore(), len(others))


class Wires:
    def __init__(self, send_sems, recv_sems):
        self.send_sems, self.recv_sems = send_sems, recv_sems
        self.send_slots, self.recv_slots, self.sent = 0, 0, []

    def send_slot(self):
        self.send_slots += 1
        return self.send_slots - 1

    def recv_slot(self):
        self.recv_slots += 1
        return self.recv_slots - 1

    def copy(self, source, target, place, send_slot, recv_slot):
        return pltpu.make_async_remote_copy(
            src_ref=source,
            dst_ref=target,
            send_sem=self.send_sems.at[send_slot],
            recv_sem=self.recv_sems.at[recv_slot],
            device_id=device_of(place),
            device_id_type=MESH_IDS,
        )

    def send(self, source, target, place, send_slot=None):
        slot = self.send_slot() if send_slot is None else send_slot
        copy = self.copy(source, target, place, slot, self.recv_slot())
        copy.start()
        if send_slot is None:
            self.sent.append(copy)
        return copy

    def bundle(self):
        return self.send_slot(), self.recv_slot()

    def send_all(self, source, target, place, bundle):
        self.copy(source, target, place, *bundle).start()

    def whole(self, ref, place, bundle):
        return self.copy(ref, ref, place, *bundle)

    def await_sent(self, ref, place, send_slot):
        self.copy(ref, ref, place, send_slot, 0).wait_send()

    def settle(self, latest=0):
        done = len(self.sent) - latest
        for copy in self.sent[:done]:
            copy.wait_send()
        self.sent = self.sent[done:]


def lane_range(first, count):
    return pl.ds(pl.multiple_of(first, 128), count)


class Group:
    def __init__(self, wires, place):
        self.wires, self.place, self.slot, self.size = wires, place, wires.send_slot(), 0

    def send(self, source, target, place):
        self.size += math.prod(source.shape) * jnp.dtype(source.dtype).itemsize
        return self.wires.send(source, target, place, self.slot)

    def settle(self, blocks):
        count, rest = divmod(self.size, math.prod(blocks.shape[1:]) * 2)
        assert rest == 0 and count <= blocks.shape[0]
        self.wires.await_sent(blocks.at[pl.ds(0, count)], self.place, self.slot)


def add_blocks(target, sources, count):
    @pl.loop(0, count)
    def _(i):
        at = i if len(target.shape) == 3 else lane_range(128 * i, 128)
        total = target[at].astype(jnp.float32)
        for source in sources:
            total += source[at].astype(jnp.float32)
        target[at] = total.astype(target.dtype)


class RingGather:
    def __init__(self, wires, place, axis, piece, half, own=None):
        self.wires, self.place, self.axis = wires, place, axis
        self.piece, self.half = piece, half
        self.mine = place[axis]
        self.own = self.piece(self.mine) if own is None else own

    def start(self):
        mine = self.piece(self.mine)
        self.up = self.wires.send(self.own, mine, moved(self.place, self.axis, 1))
        self.down = self.wires.send(self.own, mine, moved(self.place, self.axis, -1))

    def forward(self):
        self.up.wait_recv()
        lower = self.half((self.mine + 3) % SIDE, 0)
        self.far_up = self.wires.send(lower, lower, moved(self.place, self.axis, 1))
        self.down.wait_recv()
        upper = self.half((self.mine + 1) % SIDE, 1)
        self.far_down = self.wires.send(upper, upper, moved(self.place, self.axis, -1))

    def finish(self):
        self.far_up.wait_recv()
        self.far_down.wait_recv()


class DirectGather:
    def __init__(self, wires, place, axis, piece, own=None):
        self.wires, self.place, self.axis, self.piece = wires, place, axis, piece
        self.own = self.piece(place[axis]) if own is None else own

    def start(self):
        mine = self.piece(self.place[self.axis])
        self.copies = [
            self.wires.send(self.own, mine, moved(self.place, self.axis, step))
            for step in (1, 2, 3)
        ]

    def finish(self):
        for copy in self.copies:
            copy.wait_recv()


class RingReduce:
    def __init__(self, wires, place, axis, piece, half, count, half_in, whole_in):
        self.wires, self.place, self.axis = wires, place, axis
        self.piece, self.half, self.count = piece, half, count
        self.half_in, self.whole_in = half_in, whole_in
        self.mine = place[axis]

    def start(self):
        far = (self.mine + 2) % SIDE
        up, down = moved(self.place, self.axis, 1), moved(self.place, self.axis, -1)
        self.far_up = self.wires.send(self.half(far, 0), self.half_in.at[0], up)
        self.far_down = self.wires.send(self.half(far, 1), self.half_in.at[1], down)

    def forward(self):
        after, before = (self.mine + 1) % SIDE, (self.mine + 3) % SIDE
        up, down = moved(self.place, self.axis, 1), moved(self.place, self.axis, -1)
        self.far_up.wait_recv()
        add_blocks(self.half(after, 0), [self.half_in.at[0]], self.count // 2)
        self.up = self.wires.send(self.piece(after), self.whole_in.at[0], up)
        self.far_down.wait_recv()
        add_blocks(self.half(before, 1), [self.half_in.at[1]], self.count // 2)
        self.down = self.wires.send(self.piece(before), self.whole_in.at[1], down)

    def arrive(self):
        self.up.wait_recv()
        self.down.wait_recv()

    def finish(self):
        self.arrive()
        add_blocks(
            self.piece(self.mine), [self.whole_in.at[0], self.whole_in.at[1]], self.count
        )


class DirectReduce:
    def __init__(self, wires, place, axis, piece, count, landing):
        self.wires, self.place, self.axis = wires, place, axis
        self.piece, self.count, self.landing = piece, count, landing

    def start(self):
        mine = self.place[self.axis]
        self.copies = [
            self.wires.send(
                self.piece((mine + step) % SIDE),
                self.landing.at[step - 1],
                moved(self.place, self.axis, step),
            )
            for step in (1, 2, 3)
        ]

    def arrive(self):
        for copy in self.copies:
            copy.wait_recv()

    def finish(self):
        self.arrive()
        add_blocks(
            self.piece(self.place[self.axis]),
            [self.landing.at[step] for step in range(3)],
            self.count,
        )


class RowGather:
    def __init__(self, wires, place, axis, first, row):
        self.wires, self.place, self.axis = wires, place, axis
        self.row, self.mine, self.first = row, place[axis], first
        self.up, self.down, self.far = [], [], {}
        self.bundles = [wires.send_slot() for _ in range(3)]

    def of(self, piece, index):
        return self.row((self.mine + piece) % SIDE, (self.first + (0, 1, 3, 2)[index]) % SIDE)

    def send(self, index):
        mine = self.of(0, index)
        up, down = moved(self.place, self.axis, 1), moved(self.place, self.axis, -1)
        self.up.append(self.wires.send(mine, mine, up, self.bundles[0]))
        self.down.append(self.wires.send(mine, mine, down, self.bundles[1]))

    def forward(self, index):
        upward = index < 2
        (self.up if upward else self.down)[index].wait_recv()
        passed = self.of(3 if upward else 1, index)
        step = 1 if upward else -1
        target = moved(self.place, self.axis, step)
        self.far[index] = self.wires.send(passed, passed, target, self.bundles[2])
        return passed

    def take(self, index):
        (self.down if index < 2 else self.up)[index].wait_recv()
        return self.of(1 if index < 2 else 3, index)

    def take_far(self, index):
        self.far[index].wait_recv()
        return self.of(2, index)

    def settle(self, piece):
        for bundle in self.bundles:
            self.wires.await_sent(piece, self.place, bundle)


class QuarterReduce(RingReduce):
    def start(self, chunk):
        far = (self.mine + 2) % SIDE
        up, down = moved(self.place, self.axis, 1), moved(self.place, self.axis, -1)
        size = self.count // 4
        landing = pl.ds(chunk * size, size)
        if chunk == 0:
            self.far_ups, self.far_downs, self.wholes = [], [], []
        self.far_ups.append(
            self.wires.send(self.half(far, 2 * chunk), self.half_in.at[0, landing], up)
        )
        self.far_downs.append(
            self.wires.send(self.half(far, 2 * chunk + 1), self.half_in.at[1, landing], down)
        )

    def send_quarter(self, piece, quarter, side):
        size = self.count // 4
        landing = self.whole_in.at[side, pl.ds(quarter * size, size)]
        there = moved(self.place, self.axis, 1 if side == 0 else -1)
        self.wholes.append(self.wires.send(self.half(piece, quarter), landing, there))

    def start_near(self):
        after, before = (self.mine + 1) % SIDE, (self.mine + 3) % SIDE
        for quarter in (0, 2):
            self.send_quarter(after, quarter + 1, 0)
            self.send_quarter(before, quarter, 1)

    def forward(self):
        after, before = (self.mine + 1) % SIDE, (self.mine + 3) % SIDE
        size = self.count // 4
        for chunk in range(2):
            landed = pl.ds(chunk * size, size)
            self.far_ups[chunk].wait_recv()
            add_blocks(self.half(after, 2 * chunk), [self.half_in.at[0, landed]], size)
            self.send_quarter(after, 2 * chunk, 0)
            self.far_downs[chunk].wait_recv()
            add_blocks(self.half(before, 2 * chunk + 1), [self.half_in.at[1, landed]], size)
            self.send_quarter(before, 2 * chunk + 1, 1)

    def arrive(self):
        for copy in self.wholes:
            copy.wait_recv()


def block_ring(place, part, phase, at):
    first_axis, second_axis, third_axis = ORDERS[part]
    k1, k2, k3 = place[first_axis], place[second_axis], place[third_axis]
    if phase == 0:
        return (
            lambda j: at(k3, 8 * k2 + 2 * j, 2),
            lambda j, h: at(k3, 8 * k2 + 2 * j + h, 1),
        )
    if phase == 1:
        return (lambda j: at(k3, 8 * j, 8), lambda j, h: at(k3, 8 * j + 4 * h, 4))
    return (lambda j: at(j, 0, 32), lambda j, q: at(j, 8 * q, 8))


def gather_phase(
    place,
    wires,
    others,
    ids_ref,
    matrices_ref,
    table_ref,
    positions_ref,
    blocks,
    table,
    hidden_ref,
    own_low,
    table_pad,
    ids_all,
    parts,
    sibling_in,
    half_in,
    whole_in,
    landing,
    ready,
    arrived,
    local_sems,
):
    core = place[CORE]
    across = place[X]
    sibling = moved(place, CORE, 1)
    group = Group(wires, place)

    def blocks_at(part, side, k3, first, count):
        start = ((2 * part + side) * SIDE + k3) * 32 + first
        return blocks.at[pl.ds(start, count)]

    own_low[...] = matrices_ref[...].astype(jnp.bfloat16).reshape(own_low.shape)
    for part in range(3):
        k1, k2, k3 = (place[axis] for axis in ORDERS[part])
        first = ((2 * part + core) * SIDE + k3) * 32 + 8 * k2 + 2 * k1
        for which in range(2):
            blocks[first + which] = own_low[part, which]
    ids_all[across] = ids_ref[...]
    table[across] = table_ref[...].astype(jnp.bfloat16)
    rings = [[], [], []]
    for part in range(3):

        def at(k3, first, count, part=part):
            return blocks_at(part, core, k3, first, count)

        first_axis, second_axis, third_axis = ORDERS[part]
        piece, _ = block_ring(place, part, 0, at)
        rings[0].append(DirectGather(group, place, first_axis, piece, own_low.at[part]))
        piece, half = block_ring(place, part, 1, at)
        rings[1].append(RingGather(group, place, second_axis, piece, half))
        rings[2].append(
            RowGather(
                wires,
                place,
                third_axis,
                place[second_axis],
                lambda j, row, at=at: at(j, 8 * row, 8),
            )
        )
    on_z, on_x, on_y = rings[2]
    ids_ring = DirectGather(wires, place, X, lambda j: ids_all.at[j])
    rows = table_ref.shape[0]
    table_pad[pl.ds(0, rows)] = table_ref[...].astype(jnp.bfloat16)
    padding = table_pad.shape[0] - rows
    table_pad[pl.ds(rows, padding)] = jnp.zeros((padding, table_pad.shape[1]), jnp.bfloat16)
    table_ring = RowGather(
        wires,
        place,
        X,
        0,
        lambda j, row: table.at[j, pl.ds(rows // SIDE * row, rows // SIDE)],
    )
    base = (lax.axis_index("vocab") * rows).astype(jnp.float32)
    tiles = table_pad.shape[0] // 128
    lane = lax.broadcasted_iota(jnp.int32, (128, 128), 1).astype(jnp.float32)

    def group_of(part, which):
        return 2 * ((across // 2 + part) % 2) + which

    def look_up(part, side, half):
        dp_group = group_of(part, side)

        @pl.loop(4 * half, 4 * half + 4)
        def _(quad):
            hot_rows = []
            for which in range(4):
                ids = ids_all[dp_group, pl.ds(4 * quad + which, 1), :].astype(jnp.float32) - base
                column = jnp.transpose(jnp.broadcast_to(ids, (128, 128)))
                hot_rows.append(
                    jnp.concatenate(
                        [
                            jnp.where(column == lane + 128.0 * tile, 1.0, 0.0).astype(jnp.bfloat16)
                            for tile in range(tiles)
                        ],
                        1,
                    )
                )
            found = jnp.dot(
                jnp.concatenate(hot_rows, 0), table_pad[...], preferred_element_type=jnp.float32
            ).astype(jnp.bfloat16)
            at_z = quad // 2
            for which in range(4):
                at_y = 2 * (quad % 2) + which // 2
                first, second = (at_z, at_y) if part == 0 else (at_y, at_z)
                at = lookup_rows(part, which % 2, first, 2 * second + side, 1)
                parts[at] = found[128 * which : 128 * which + 128]

    def lookup_rows(part, side, first, index, count):
        start = ((2 * part + side) * SIDE + first) * 8 + index
        return lane_range(128 * start, 128 * count)

    def to_sibling(part):
        crossing = parts.at[lookup_rows(part, 1 - core, 0, 0, 32)]
        return group.send(crossing, sibling_in.at[part], sibling)

    lookup_axes = ((Z, Y), (Y, Z))
    lookup_rings, lookup_ends = [], []
    for part in range(2):
        first_axis, second_axis = lookup_axes[part]
        lookup_rings.append(
            RingReduce(
                group,
                place,
                first_axis,
                lambda j, part=part: parts.at[lookup_rows(part, core, j, 0, 8)],
                lambda j, h, part=part: parts.at[lookup_rows(part, core, j, 4 * h, 4)],
                8,
                half_in.at[part],
                whole_in.at[part],
            )
        )
        lookup_ends.append(
            DirectReduce(
                group,
                place,
                second_axis,
                lambda j, part=part, k=place[first_axis]: parts.at[
                    lookup_rows(part, core, k, 2 * j, 2)
                ],
                2,
                landing.at[part],
            )
        )

    def add_sibling(part):
        siblings[part].wait_recv()
        add_blocks(parts.at[lookup_rows(part, core, 0, 0, 32)], [sibling_in.at[part]], 32)
        lookup_rings[part].start()

    def take_result(part):
        lookup_ends[part].arrive()
        first_axis, second_axis = lookup_axes[part]
        for which in range(2):
            at = lookup_rows(part, core, place[first_axis], 2 * place[second_axis] + which, 1)
            total = parts[at].astype(jnp.float32)
            for step in range(3):
                total += landing[part, step, 128 * which : 128 * which + 128].astype(jnp.float32)
            ready[group_of(part, which)] = total.astype(jnp.bfloat16)

    shares = [wires.bundle() for _ in range(3)]

    def share(part, ref):
        wires.send_all(ref, ref, sibling, shares[part])

    own_side = across % 2
    await_greetings(others)
    ids_ring.start()
    for ring in rings[0]:
        ring.start()
    table_ring.send(0)
    look_up(0, own_side, 0)
    look_up(0, own_side, 1)
    for ring, later in zip(rings[0], rings[1]):
        ring.finish()
        later.start()
    for ring in rings[2]:
        ring.send(0)
    ids_ring.finish()
    look_up(0, 1 - own_side, 0)
    look_up(0, 1 - own_side, 1)
    siblings = [to_sibling(0)]
    look_up(1, 0, 0)
    for ring in rings[1]:
        ring.forward()
    look_up(1, 0, 1)
    add_sibling(0)
    for ring in (on_y, on_x, on_z):
        ring.send(1)
    look_up(1, 1, 0)
    look_up(1, 1, 1)
    siblings.append(to_sibling(1))
    for ring in rings[1]:
        ring.finish()
    on_y.send(2)
    on_x.send(2)
    lookup_rings[0].forward()
    add_sibling(1)
    on_z.send(2)
    on_x.send(3)
    table_ring.send(1)
    for part in range(3):
        share(part, blocks_at(part, core, place[ORDERS[part][2]], 0, 32))
    lookup_rings[1].forward()
    share(1, on_x.forward(0))
    share(1, on_x.forward(2))
    lookup_rings[0].finish()
    lookup_ends[0].start()
    on_z.send(3)
    on_y.send(3)
    share(1, on_x.forward(1))
    share(1, on_x.forward(3))
    table_ring.send(2)
    table_ring.send(3)
    lookup_rings[1].finish()
    lookup_ends[1].start()
    for ring_part, ring in ((0, on_z), (2, on_y)):
        for index in (0, 2):
            share(ring_part, ring.forward(index))
    take_result(0)
    for ring_part, ring in ((0, on_z), (2, on_y)):
        for index in (1, 3):
            share(ring_part, ring.forward(index))
    take_result(1)
    swaps = []
    for step in (1, 2, 3):
        there = moved(place, X, step)
        swaps.append(group.send(ready.at[there[X]], arrived.at[across], there))
    arrived[across] = ready[across]
    for part in range(3):
        for index in range(4):
            share(part, rings[2][part].take(index))
    for copy in swaps:
        copy.wait_recv()
    for source in range(4):
        columns = pl.ds(256 * source, 256)
        hidden_ref[:, columns] = (
            arrived[source].astype(jnp.float32) + positions_ref[:, columns]
        )
    table_ring.forward(0)
    table_ring.forward(2)
    for index in (0, 2, 1, 3):
        for part in range(3):
            share(part, rings[2][part].take_far(index))
    for index in (1, 3):
        table_ring.forward(index)
    group.settle(blocks)
    wires.settle()
    for part in range(3):
        rings[2][part].settle(blocks.at[pl.ds(0, 32)])
        wires.whole(blocks.at[pl.ds(0, 128)], sibling, shares[part]).wait()
    return table_ring


def head_phase(
    place,
    wires,
    vocab_group,
    table_ring,
    head_in_ref,
    table,
    target_ref,
    at_ref,
    length_ref,
    d_head_ref,
    table_grad_ref,
    loss_ref,
    table_grads,
    pieces,
    logits,
    stats,
    d_rows,
    d_sibling,
    d_first,
    d_second,
    local_sems,
    arrange_out,
    keeps,
):
    core = place[CORE]
    sibling = moved(place, CORE, 1)
    own, width = head_in_ref.shape
    half_width = width // 2
    sends = Group(wires, place)
    feature_axes = ((Y, Z), (Z, Y))
    for part in range(2):
        near, far = (place[axis] for axis in feature_axes[part])
        pieces[part, core, far, near] = head_in_ref[
            :, part * half_width : (part + 1) * half_width
        ]
    first_rings, second_rings = [], []
    for part in range(2):
        near_axis, far_axis = feature_axes[part]
        first_rings.append(
            DirectGather(
                sends,
                place,
                near_axis,
                lambda j, part=part, k=place[far_axis]: pieces.at[part, core, k, j],
            )
        )
        second_rings.append(
            DirectGather(sends, place, far_axis, lambda j, part=part: pieces.at[part, core, j])
        )
    for ring in first_rings:
        ring.start()
    seqs = target_ref.shape[1]
    column = lax.broadcasted_iota(jnp.int32, (seqs, seqs * own), 1)
    row = lax.broadcasted_iota(jnp.int32, (seqs, seqs * own), 0)
    own_seq = jnp.where(column // own == row, 1.0, 0.0)
    slot = lax.broadcasted_iota(jnp.int32, (own, seqs * own), 0)
    slot_column = lax.broadcasted_iota(jnp.int32, (own, seqs * own), 1)
    own_slot = slot_column % own == slot

    def laid_end_to_end(values):
        wide = jnp.dot(
            values.astype(jnp.float32), own_seq, precision=HIGH, preferred_element_type=jnp.float32
        )
        return jnp.sum(jnp.where(own_slot, wide, 0.0), 0, keepdims=True)

    target = laid_end_to_end(target_ref[...]).astype(jnp.int32)
    lengths = jnp.dot(
        length_ref[...].astype(jnp.float32),
        own_seq,
        precision=HIGH,
        preferred_element_type=jnp.float32,
    )
    counted = (laid_end_to_end(at_ref[...]) < lengths).astype(jnp.float32)
    for index in range(8):
        arrange_out(index)
    for ring, later in zip(first_rings, second_rings):
        ring.finish()
        later.start()
    for index in range(8, 16):
        arrange_out(index)
    crossing = []
    for part in range(2):
        second_rings[part].finish()
        mine = pieces.at[part, core]
        crossing.append(sends.send(mine, mine, sibling))
    for copy in crossing:
        copy.wait_recv()
    for index in range(4):
        table_ring.take(index)
        table_ring.take_far(index)
    table_ring.settle(table.at[0])
    groups, rows, group_width = table.shape
    count = own * N_VOCAB
    exp_sums, hit_sums = groups * rows, groups * (rows + count)
    rows_first = groups * (rows + 2 * count)
    for index in range(N_VOCAB):
        at_z, at_y, at_core = index // 8, index // 2 % SIDE, index % 2
        halves = (pieces[0, at_core, at_z, at_y], pieces[1, at_core, at_y, at_z])
        for group in range(groups):
            column = group % 2 * group_width
            table_grads[pl.ds(rows_first + group * count + own * index, own)] = halves[group // 2][
                :, column : column + group_width
            ]

    def rows_in(group):
        return table_grads[pl.ds(rows_first + group * count, count)]

    half_count = count // 2
    lowered_first = groups * (rows + 3 * count)

    def lower(index, values):
        values = values.astype(jnp.bfloat16)
        for side in range(2):
            first = pl.multiple_of(lowered_first + side * rows + index * chunk, 16)
            table_grads[pl.ds(first, chunk)] = values[
                :, side * half_count : (side + 1) * half_count
            ]

    chunk = rows // 4
    base = lax.axis_index("vocab") * rows
    row_iota = lax.broadcasted_iota(jnp.int32, (chunk, count), 0)

    def logit_chunk(index, top):
        at = pl.ds(pl.multiple_of(index * chunk, chunk), chunk)
        total = jnp.zeros((chunk, count), jnp.float32)
        for group in range(groups):
            total += lax.dot_general(
                table[group, at],
                rows_in(group),
                (((1,), (1,)), ((), ())),
                preferred_element_type=jnp.float32,
            )
        total = jnp.where(row_iota + (base + index * chunk) < VOCAB_REAL, total, NEG_FILL)
        logits[at] = total
        return jnp.maximum(top, jnp.max(total, 0, keepdims=True))

    local_top = lax.fori_loop(
        0, 4, logit_chunk, jnp.full((1, count), NEG_FILL, jnp.float32)
    )

    def exp_chunk(index, carry):
        total, pick = carry
        at = pl.ds(pl.multiple_of(index * chunk, chunk), chunk)
        values = logits[at]
        hits = row_iota + (base + index * chunk) == target
        pick += jnp.sum(jnp.where(hits, values, 0.0), 0, keepdims=True)
        values = jnp.exp(values - local_top)
        logits[at] = values
        lower(index, values)
        return total + jnp.sum(values, 0, keepdims=True), pick

    zero_row = jnp.zeros((1, count), jnp.float32)
    local_total, pick = lax.fori_loop(0, 4, exp_chunk, (zero_row, zero_row))
    lanes = count // 4
    top = jnp.concatenate([local_top[:, lanes * i : lanes * (i + 1)] for i in range(4)], 0)
    total = jnp.concatenate([local_total[:, lanes * i : lanes * (i + 1)] for i in range(4)], 0)
    mine = stats.at[lax.axis_index("vocab")]
    mine[...] = jnp.concatenate([top, total], 0)
    bundle = wires.bundle()
    for other in vocab_group:
        wires.send_all(mine, mine, other, bundle)
    def table_products(first):
        for side in range(2):
            lowered = table_grads[pl.ds(lowered_first + side * rows, rows)]
            for group in range(groups):
                product = dot_tn(lowered, table[group]).astype(jnp.bfloat16)
                at = pl.ds(first + group * count + half_count * side, half_count)
                table_grads[at] = product

    table_products(exp_sums)

    @pl.loop(0, 4)
    def _(index):
        hits = row_iota + (base + index * chunk) == target
        lower(index, jnp.where(hits, 1.0, 0.0))

    table_products(hit_sums)
    wires.whole(stats.at[pl.ds(0, len(vocab_group))], sibling, bundle).wait()
    top = jnp.max(stats[:, :4], 0)
    total = jnp.sum(stats[:, 4:] * jnp.exp(stats[:, :4] - top[None]), 0)
    log_total = top + jnp.log(total)
    log_total = jnp.concatenate([log_total[i : i + 1] for i in range(4)], 1)
    first_device = (lax.axis_index("vocab") == 0).astype(jnp.float32)
    loss_ref[...] = (first_device * log_total - pick) * counted
    weight = counted / (N_DP * N_VOCAB * own)
    scale = jnp.exp(local_top - log_total) * weight

    def down_rows(values, index):
        return jnp.transpose(
            jnp.broadcast_to(values[:, 128 * index : 128 * index + 128], (128, 128))
        )

    for tile in range(count // 128):
        tile_scale = jnp.concatenate([down_rows(scale, tile)] * 2, 1)
        tile_weight = jnp.concatenate([down_rows(weight, tile)] * 2, 1)
        for group in range(groups):
            at = group * count + 128 * tile
            exp_part = table_grads[pl.ds(exp_sums + at, 128)].astype(jnp.float32)
            hit_part = table_grads[pl.ds(hit_sums + at, 128)].astype(jnp.float32)
            rows_grad = (exp_part * tile_scale - hit_part * tile_weight).astype(jnp.bfloat16)
            part, column = group // 2, group % 2 * group_width
            for index in range(128 // own):
                inner = 128 // own * tile + index
                at_z, at_y, at_core = inner // 8, inner // 2 % SIDE, inner % 2
                first, second = (at_z, at_y) if part == 0 else (at_y, at_z)
                d_rows[part, at_core, first, second, :, column : column + group_width] = (
                    rows_grad[own * index : own * (index + 1)]
                )
    crossing = [
        sends.send(d_rows.at[part, 1 - core], d_sibling.at[part], sibling) for part in range(2)
    ]
    reduce_axes = ((Z, Y), (Y, Z))
    first_rings, second_rings = [], []
    for part in range(2):
        first_axis, second_axis = reduce_axes[part]
        crossing[part].wait_recv()
        for j in range(4):
            add_blocks(d_rows.at[part, core, j], [d_sibling.at[part, j]], 4)
        first_rings.append(
            DirectReduce(
                sends,
                place,
                first_axis,
                lambda j, part=part: d_rows.at[part, core, j],
                4,
                d_first.at[part],
            )
        )
        second_rings.append(
            DirectReduce(
                sends,
                place,
                second_axis,
                lambda j, part=part, k=place[first_axis]: d_rows.at[part, core, k, j],
                1,
                d_second.at[part],
            )
        )
        first_rings[part].start()

    stores = []

    @pl.loop(0, 4)
    def _(index):
        at = pl.ds(pl.multiple_of(index * chunk, chunk), chunk)
        hits = row_iota + (base + index * chunk) == target
        lower(index, logits[at] * scale - jnp.where(hits, weight, 0.0))

    def table_grad(group):
        @pl.loop(0, 4)
        def _(index):
            product = jnp.zeros((chunk, group_width), jnp.float32)
            for side in range(2):
                first = pl.multiple_of(lowered_first + side * rows + index * chunk, 16)
                product += jnp.dot(
                    table_grads[pl.ds(first, chunk)],
                    rows_in(group)[side * half_count : (side + 1) * half_count],
                    preferred_element_type=jnp.float32,
                )
            product = product.astype(jnp.bfloat16)
            table_grads[pl.ds(pl.multiple_of(group * rows + index * chunk, chunk), chunk)] = product

        at = pl.ds(group * rows, rows)
        stores.append(
            pltpu.make_async_copy(table_grads.at[at], table_grad_ref.at[at], local_sems.at[group])
        )
        stores[-1].start()

    table_grad(0)
    table_grad(1)
    for ring, later in zip(first_rings, second_rings):
        ring.finish()
        later.start()
    table_grad(2)
    table_grad(3)
    for copy in keeps + stores[:3]:
        copy.wait()
    del stores[:3]
    for part in range(2):
        second_rings[part].arrive()
        first_axis, second_axis = reduce_axes[part]
        total = d_rows[part, core, place[first_axis], place[second_axis]].astype(jnp.float32)
        for step in range(3):
            total += d_second[part, step].astype(jnp.float32)
        d_head_ref[:, part * half_width : (part + 1) * half_width] = total
    return stores, sends


def split(values):
    high = values.astype(jnp.bfloat16)
    return high, (values - high.astype(jnp.float32)).astype(jnp.bfloat16)


def fine_dot(left, right, contract=((1,), (0,))):
    (left_high, left_low), (right_high, right_low) = split(left), split(right)

    def product(one, other):
        return lax.dot_general(
            one, other, (contract, ((), ())), preferred_element_type=jnp.float32
        )

    return product(left_high, right_high) + (
        product(left_high, right_low) + product(left_low, right_high)
    )


def clip_for(squares):
    norm = jnp.sqrt(jnp.full((1, 128), squares, jnp.float32))
    return norm, CLIP_LEVEL / jnp.maximum(norm, CLIP_LEVEL)


def finish_kernel(
    grads_ref,
    small_ref,
    head_grad_ref,
    d_embed_ref,
    left_roots_ref,
    ids_ref,
    loss_ref,
    grads_out_target,
    table_grad_target,
    final_target,
    left_gram_target,
    right_gram_target,
    left_part_target,
    totals_ref,
    grads_out_ref,
    table_grad_ref,
    final_ref,
    left_gram,
    right_gram,
    left_part,
    left_roots,
    sums,
    sibling_in,
    half_a,
    whole_a,
    half_b,
    whole_b,
    whole_c,
    small_sums,
    small_sibling,
    small_a,
    small_b,
    small_c,
    table_sums,
    table_half,
    table_whole,
    embeds,
    ids_all,
    totals_all,
    send_sems,
    recv_sems,
    local_sems,
):
    place = coordinates()
    core = place[CORE]
    across = place[X]
    sibling = moved(place, CORE, 1)
    wires = Wires(send_sems, recv_sems)
    to_sibling, to_owners, to_table, later_sends = (Group(wires, place) for _ in range(4))

    def sums_at(part, k3, first, count):
        return sums.at[pl.ds((SIDE * part + k3) * 32 + first, count)]

    loads = []

    def load(source, target):
        copy = pltpu.make_async_copy(source, target, local_sems.at[len(loads)])
        copy.start()
        loads.append(copy)
        return copy

    width = table_grad_ref.shape[1]
    embed_axes = ((Y, Z), (Z, Y))
    source_part = across // 2
    near = place[Y] * (1 - source_part) + place[Z] * source_part
    far = place[Z] * (1 - source_part) + place[Y] * source_part
    landing = embeds.at[source_part, core, far, 2 * near + across % 2]
    own_columns = pl.ds(pl.multiple_of(across * width, width), width)
    embed_load = load(d_embed_ref.at[:, own_columns], landing)
    third = [place[ORDERS[part][2]] for part in range(3)]
    small_load = load(small_ref.at[core], small_sums)
    block_loads = {}
    for step in (2, 1, 3, 0):
        for part in range(3):
            j = (third[part] + step) % SIDE
            block_loads[part, step] = load(grads_ref.at[part, core, j], sums_at(part, j, 0, 32))
    table_load = load(head_grad_ref, table_sums)
    roots_load = load(left_roots_ref, left_roots)

    ids_all[across] = ids_ref[...]
    line = [
        moved(moved(place, X, step), CORE, side) for step in range(SIDE) for side in range(2)
    ][1:]
    plane = [
        moved(moved(place, Y, step), Z, other) for step in range(SIDE) for other in range(SIDE)
    ][1:]
    greet(line + plane)
    await_greetings(line + plane)
    swaps = []
    for step in (1, 2, 3):
        there = moved(place, X, step)
        columns = pl.ds(pl.multiple_of(there[X] * width, width), width)
        swaps.append(wires.send(d_embed_ref.at[:, columns], landing, there))
    ids_ring = DirectGather(wires, place, X, lambda j: ids_all.at[j])
    ids_ring.start()
    small_crossing = wires.send(small_ref.at[1 - core], small_sibling, sibling)
    crossings = {}
    for step, half in ((2, 0), (2, 1), (1, None), (3, None), (0, None)):
        for part in range(3):
            j = (third[part] + step) % SIDE
            source, target = grads_ref.at[part, 1 - core, j], sibling_in.at[part, j]
            if half is not None:
                source, target = source.at[pl.ds(16 * half, 16)], target.at[pl.ds(16 * half, 16)]
            crossings[part, step, half] = to_sibling.send(source, target, sibling)

    embed_first, embed_second = [], []
    for part in range(2):
        near_axis, far_axis = embed_axes[part]
        embed_first.append(
            RingGather(
                to_owners,
                place,
                near_axis,
                lambda j, part=part, k=place[far_axis]: embeds.at[part, core, k, pl.ds(2 * j, 2)],
                lambda j, h, part=part, k=place[far_axis]: embeds.at[
                    part, core, k, pl.ds(2 * j + h, 1)
                ],
            )
        )
        embed_second.append(
            RingGather(
                later_sends,
                place,
                far_axis,
                lambda j, part=part: embeds.at[part, core, j],
                lambda j, h, part=part: embeds.at[part, core, j, pl.ds(4 * h, 4)],
            )
        )
    first_rings, middle_rings, last_rings = [], [], []
    for part in range(3):

        def at(k3, first, count, part=part):
            return sums_at(part, k3, first, count)

        last_axis, middle_axis, first_axis = ORDERS[part]
        piece, half = block_ring(place, part, 2, at)
        first_rings.append(
            QuarterReduce(
                to_owners, place, first_axis, piece, half, 32, half_a.at[part], whole_a.at[part]
            )
        )
        piece, half = block_ring(place, part, 1, at)
        middle_rings.append(
            RingReduce(
                later_sends, place, middle_axis, piece, half, 8, half_b.at[part], whole_b.at[part]
            )
        )
        piece, _ = block_ring(place, part, 0, at)
        last_rings.append(DirectReduce(later_sends, place, last_axis, piece, 2, whole_c.at[part]))
    table_ring = QuarterReduce(
        to_table,
        place,
        X,
        lambda j: table_sums.at[j],
        lambda j, q: table_sums.at[j, pl.ds(TABLE_CHUNKS // 4 * q, TABLE_CHUNKS // 4)],
        TABLE_CHUNKS,
        table_half,
        table_whole,
    )
    small_rings = [
        DirectReduce(wires, place, Z, lambda j: small_sums.at[j], 16, small_a),
        DirectReduce(
            wires, place, Y, lambda j: small_sums.at[place[Z], pl.ds(4 * j, 4)], 4, small_b
        ),
        DirectReduce(
            wires, place, X, lambda j: small_sums.at[place[Z], pl.ds(4 * place[Y] + j, 1)], 1, small_c
        ),
    ]

    def add_crossing(part, step, half=None):
        j = (third[part] + step) % SIDE
        if not half:
            block_loads[part, step].wait()
        crossings[part, step, half].wait_recv()
        first, count = (0, 32) if half is None else (16 * half, 16)
        landed = sibling_in.at[part, j, pl.ds(first, count)]
        add_blocks(sums_at(part, j, first, count), [landed], count)

    embed_siblings = []

    def share(part, step):
        piece = embeds.at[part, core, (place[embed_axes[part][1]] + step) % SIDE]
        embed_siblings.append(later_sends.send(piece, piece, sibling))

    rows = table_grad_ref.shape[0]
    chunk = rows // 4
    base = lax.axis_index("vocab") * rows
    row_iota = lax.broadcasted_iota(jnp.int32, (chunk, 512), 0)

    def scatter_rows(part, at_core, step):
        at_far = (place[embed_axes[part][1]] + step) % SIDE

        @pl.loop(0, 2)
        def _(pair):
            values = embeds[part, at_core, at_far, pl.ds(4 * pair, 4)].reshape(512, width)
            ids = []
            for which in range(4):
                at_near = 2 * pair + which // 2
                at_z, at_y = (at_far, at_near) if part == 0 else (at_near, at_far)
                inner = (at_z * SIDE + at_y) * 2 + at_core
                ids.append(ids_all[2 * part + which % 2, pl.ds(inner, 1), :])
            ids = jnp.concatenate(ids, 1) - base

            @pl.loop(0, 4)
            def _(row):
                at = pl.ds(pl.multiple_of(row * chunk, chunk), chunk)
                hot = jnp.where(row_iota + row * chunk == ids, 1.0, 0.0).astype(jnp.bfloat16)
                table_grad_ref[at] += jnp.dot(hot, values, preferred_element_type=jnp.float32)

    lead = ((0, core), (1, core))
    orders = ((X, Y, Z), (Y, Z, X))
    gathers = []
    for phase in range(3):
        row = []
        for part in range(2):
            _, second_axis, third_axis = orders[part]
            keys = (place[third_axis], place[second_axis])[: 2 - phase]
            row.append(
                DirectGather(
                    wires,
                    place,
                    orders[part][phase],
                    lambda j, key=lead[part] + keys: final_ref.at[key + (j,)],
                )
            )
        gathers.append(row)

    for part in range(3):
        add_crossing(part, 2, 0)
        first_rings[part].start(0)
    for copy in swaps:
        copy.wait_recv()
    embed_load.wait()
    for ring in embed_first:
        ring.start()
    table_load.wait()
    table_ring.start(0)
    table_ring.start(1)
    small_load.wait()
    small_crossing.wait_recv()
    for j in range(4):
        add_blocks(small_sums.at[j], [small_sibling.at[j]], 16)
    small_rings[0].start()
    for part in range(3):
        add_crossing(part, 2, 1)
    for ring in embed_first:
        ring.forward()
    for part in range(3):
        first_rings[part].start(1)
    for part in range(3):
        add_crossing(part, 1)
    for ring, later in zip(embed_first, embed_second):
        ring.finish()
        later.start()
    small_rings[0].finish()
    small_rings[1].start()
    share(0, 0)
    share(1, 0)
    for part in range(3):
        add_crossing(part, 3)
    for part in range(3):
        first_rings[part].start_near()
    table_ring.start_near()
    ids_ring.finish()

    @pl.loop(0, 4)
    def _(index):
        at = pl.ds(pl.multiple_of(index * chunk, chunk), chunk)
        table_grad_ref[at] = jnp.zeros((chunk, width), jnp.float32)

    scatter_rows(0, core, 0)
    scatter_rows(1, core, 0)
    for ring in first_rings:
        ring.forward()
    for part in range(3):
        add_crossing(part, 0)
    for copy in embed_siblings:
        copy.wait_recv()
    embed_siblings.clear()
    scatter_rows(0, 1 - core, 0)
    scatter_rows(1, 1 - core, 0)
    for part in range(2):
        embed_second[part].forward()
        share(part, 1)
        share(part, 3)
    small_rings[1].finish()
    small_rings[2].start()
    table_ring.forward()
    for part in range(2):
        scatter_rows(part, core, 1)
        scatter_rows(part, core, 3)
    for copy in embed_siblings:
        copy.wait_recv()
    embed_siblings.clear()
    for part in range(2):
        scatter_rows(part, 1 - core, 1)
        scatter_rows(part, 1 - core, 3)
    to_sibling.settle(sums)
    for ring, later in zip(first_rings, middle_rings):
        ring.finish()
        later.start()
    small_rings[2].finish()
    own_small = small_sums[place[Z], 4 * place[Y] + across].astype(jnp.float32)
    final_ref[0, core, place[Z], place[Y], across] = own_small[:8]
    final_ref[1, core, across, place[Z], place[Y]] = jnp.concatenate(
        [own_small[8:9], jnp.zeros((7, 128), jnp.float32)], 0
    )
    for gather in gathers[0]:
        gather.start()
    for part in range(2):
        embed_second[part].finish()
        share(part, 2)
    scatter_rows(0, core, 2)
    for ring in middle_rings:
        ring.forward()
    for gather, later in zip(gathers[0], gathers[1]):
        gather.finish()
        later.start()
    scatter_rows(1, core, 2)
    for copy in embed_siblings:
        copy.wait_recv()
    scatter_rows(0, 1 - core, 2)
    to_owners.settle(sums)
    wires.settle(6)
    for ring, later in zip(middle_rings, last_rings):
        ring.finish()
        later.start()
    for gather, later in zip(gathers[1], gathers[2]):
        gather.finish()
        later.start()
    scatter_rows(1, 1 - core, 2)
    table_ring.arrive()
    table_block = rows // TABLE_CHUNKS

    @pl.loop(0, TABLE_CHUNKS)
    def _(index):
        at = pl.ds(pl.multiple_of(index * table_block, table_block), table_block)
        table_grad_ref[at] += (
            table_sums[across, index].astype(jnp.float32)
            + table_whole[0, index].astype(jnp.float32)
            + table_whole[1, index].astype(jnp.float32)
        )

    table_squares = jnp.zeros((1, width), jnp.float32)
    for index in range(4):
        values = table_grad_ref[index * chunk : (index + 1) * chunk]
        table_squares += jnp.sum(values * values, 0, keepdims=True)
    squares = jnp.zeros((1, 128), jnp.float32)
    to_table.settle(sums)
    for part in range(3):
        last_rings[part].arrive()
        k1, k2, k3 = (place[axis] for axis in ORDERS[part])
        for which in range(2):
            total = sums_at(part, k3, 8 * k2 + 2 * k1 + which, 1)[0].astype(jnp.float32)
            for step in range(3):
                total += whole_c[part, step, which].astype(jnp.float32)
            grads_out_ref[part, which] = total
            squares += jnp.sum(total * total, 0, keepdims=True)
    final_siblings = []
    for part in range(2):
        gathers[2][part].finish()
        mine = final_ref.at[part, core]
        final_siblings.append(wires.send(mine, mine, sibling))
    stores = []

    def store(source, target):
        stores.append(pltpu.make_async_copy(source, target, local_sems.at[17 + len(stores)]))
        stores[-1].start()

    own_clip = clip_for(jnp.sum(squares))[1]
    squares += table_squares[:, :128] + table_squares[:, 128:]
    roots_load.wait()

    def products(slots):
        for slot in slots:
            grad = grads_out_ref[slot // 2, slot % 2] * own_clip
            left_gram[slot] = fine_dot(grad, grad, ((1,), (1,)))
            right_gram[slot] = fine_dot(grad, grad, ((0,), (0,)))
            left_part[slot] = fine_dot(left_roots[slot], grad)

    store(table_grad_ref, table_grad_target)
    store(grads_out_ref, grads_out_target)
    loss = sum(loss_ref[:, 128 * index : 128 * (index + 1)] for index in range(4))
    totals = jnp.concatenate([squares, loss, jnp.zeros((6, 128), jnp.float32)], 0)
    for phase, (own, others) in enumerate(
        ((2 * across + core, line), (SIDE * place[Z] + place[Y], plane))
    ):
        mine = totals_all.at[phase, own]
        mine[...] = totals
        bundle = wires.bundle()
        for other in others:
            wires.send_all(mine, mine, other, bundle)
        products(range(3 * phase, 3 * phase + 3))
        if phase == 0:
            for copy in final_siblings:
                copy.wait_recv()
            store(final_ref, final_target)
            later_sends.settle(sums)
        else:
            store(left_gram, left_gram_target)
            store(right_gram, right_gram_target)
            store(left_part, left_part_target)
            wires.settle()
        wires.whole(totals_all.at[phase, pl.ds(0, len(others))], sibling, bundle).wait()
        totals = totals_all[phase, 0]
        for index in range(1, len(others) + 1):
            totals += totals_all[phase, index]
    totals_ref[...] = totals
    for copy in stores:
        copy.wait()


def finish_call(grads, small, head_grad, d_embed, left_roots, token_ids, loss_row):
    bf16 = jnp.bfloat16
    _, chunks, chunk_rows, width = head_grad.shape
    rows = chunks * chunk_rows
    block = (BLOCK, BLOCK)
    return pl.pallas_call(
        finish_kernel,
        name="reduce_and_scatter",
        out_shape=(
            jax.ShapeDtypeStruct((3, 2) + block, jnp.float32),
            jax.ShapeDtypeStruct((rows, width), jnp.float32),
            jax.ShapeDtypeStruct((2, 2, SIDE, SIDE, SIDE, 8, 128), jnp.float32),
            *[jax.ShapeDtypeStruct(left_roots.shape, jnp.float32)] * 3,
            jax.ShapeDtypeStruct((8, 128), jnp.float32),
        ),
        in_specs=[ANY] * 5 + [VMEM] * 2,
        out_specs=(ANY,) * 6 + (VMEM,),
        scratch_shapes=[
            pltpu.VMEM((3, 2) + block, jnp.float32),
            pltpu.VMEM((rows, width), jnp.float32),
            pltpu.VMEM((2, 2, SIDE, SIDE, SIDE, 8, 128), jnp.float32),
            *[pltpu.VMEM(left_roots.shape, jnp.float32)] * 4,
            pltpu.VMEM((3 * SIDE * 32,) + block, bf16),
            pltpu.VMEM((3, SIDE, 32) + block, bf16),
            pltpu.VMEM((3, 2, 16) + block, bf16),
            pltpu.VMEM((3, 2, 32) + block, bf16),
            pltpu.VMEM((3, 2, 4) + block, bf16),
            pltpu.VMEM((3, 2, 8) + block, bf16),
            pltpu.VMEM((3, 3, 2) + block, bf16),
            pltpu.VMEM((SIDE, 16, 16, 128), bf16),
            pltpu.VMEM((SIDE, 16, 16, 128), bf16),
            pltpu.VMEM((3, 16, 16, 128), bf16),
            pltpu.VMEM((3, 4, 16, 128), bf16),
            pltpu.VMEM((3, 1, 16, 128), bf16),
            pltpu.VMEM(head_grad.shape, bf16),
            pltpu.VMEM((2, chunks // 2, chunk_rows, width), bf16),
            pltpu.VMEM((2, chunks, chunk_rows, width), bf16),
            pltpu.VMEM((2, 2, SIDE, 8, 128, width), bf16),
            pltpu.VMEM((N_DP,) + token_ids.shape, jnp.int32),
            pltpu.VMEM((2, SIDE * SIDE, 8, 128), jnp.float32),
            pltpu.SemaphoreType.DMA((42,)),
            pltpu.SemaphoreType.DMA((146,)),
            pltpu.SemaphoreType.DMA((23,)),
        ],
        compiler_params=pltpu.CompilerParams(
            collective_id=3, has_side_effects=True, vmem_limit_bytes=VMEM_BYTES
        ),
    )(grads, small, head_grad, d_embed, left_roots, token_ids, loss_row)


def row_mean(values):
    return jnp.mean(values, -1, keepdims=True)


def normalized(values):
    center = values - row_mean(values)
    scale = lax.rsqrt(row_mean(center * center) + LN_EPS)
    return center * scale, scale


def norm_backward(d_normed, hat, scale, gain):
    d_hat = d_normed * gain
    d_values = scale * (d_hat - row_mean(d_hat) - hat * row_mean(d_hat * hat))
    d_gain = jnp.sum(d_normed * hat, 0, keepdims=True)
    return d_values, d_gain, jnp.sum(d_normed, 0, keepdims=True)


QKV, PROJ, FC, OUT = (0, 24), (192, 8), (256, 32), (512, 8)


def load_blocks(full_ref, blocks, sems):
    share = blocks.shape[0] // 8
    copies = []
    for index in range(8):
        part = pl.ds(index * share, share)
        copies.append(pltpu.make_async_copy(full_ref.at[part], blocks.at[part], sems.at[index]))
        copies[-1].start()
    return copies


def weight_tiles(blocks, where_ref, matrix, row, rows, column, columns):
    first, in_row = matrix
    return jnp.concatenate(
        [
            jnp.concatenate(
                [
                    blocks[where_ref[first + (row + i) * in_row + column + j]]
                    for j in range(columns)
                ],
                1,
            )
            for i in range(rows)
        ],
        0,
    )


def selected_rows(ref, positions):
    return jnp.concatenate([ref[pl.ds(position, 1), :] for position in positions], 0)


def pair_masks(count):
    lane = lax.broadcasted_iota(jnp.int32, (2 * count, 2 * HEAD_DIM), 1)
    row = lax.broadcasted_iota(jnp.int32, (2 * count, 2 * HEAD_DIM), 0)
    return (lane < HEAD_DIM) == (row < count)


def doubled(values, own_lanes):
    both = jnp.concatenate([values, values], 0)
    return jnp.where(own_lanes, both.astype(jnp.float32), 0.0).astype(jnp.bfloat16)


def folded(values, count):
    lane = lax.broadcasted_iota(jnp.int32, (count, 2 * HEAD_DIM), 1)
    return jnp.where(lane < HEAD_DIM, values[:count], values[count:])


def forward_phase(
    where_ref,
    at_ref,
    length_ref,
    hidden_ref,
    vec_ref,
    head_in_ref,
    query_ref,
    kv_ref,
    probs_ref,
    attended_ref,
    middle_ref,
    pre_act_ref,
    last_ref,
    blocks,
    normed_rows,
    activated,
):
    count = head_in_ref.shape[0]
    bf16 = jnp.bfloat16
    own = lax.axis_index("vocab")
    positions = [at_ref[i, own] for i in range(count)]
    length = length_ref[own]
    hat, _ = normalized(hidden_ref[...])
    normed_rows[...] = hat * vec_ref[0:1] + vec_ref[1:2]
    normed_one = normed_rows[...].astype(bf16)
    normed_own = selected_rows(normed_rows, positions).astype(bf16)

    @pl.loop(0, 4)
    def _(tile):
        at = lane_range(256 * tile, 256)
        weight = weight_tiles(blocks, where_ref, QKV, 0, 8, 2 * tile, 2)
        product = jnp.dot(normed_own, weight, preferred_element_type=jnp.float32)
        query_ref[:, at] = (product + vec_ref[2:3, at]).astype(bf16)

    @pl.loop(0, 4)
    def _(tile):
        at = lane_range(256 * tile, 256)
        weight = weight_tiles(blocks, where_ref, QKV, 0, 8, 8 + 2 * tile, 2)
        product = jnp.dot(normed_one, weight, preferred_element_type=jnp.float32)
        kv_ref[:, at] = product.astype(bf16)

    @pl.loop(0, 4)
    def _(tile):
        weight = weight_tiles(blocks, where_ref, QKV, 0, 8, 16 + 2 * tile, 2)
        product = jnp.dot(normed_one, weight, preferred_element_type=jnp.float32)
        bias = vec_ref[3:4, lane_range(256 * tile, 256)]
        kv_ref[:, lane_range(D + 256 * tile, 256)] = (product + bias).astype(bf16)

    own_lanes = pair_masks(count)
    pairs = HEADS // 2
    seq_len = hidden_ref.shape[0]
    row = lax.broadcasted_iota(jnp.int32, (count, seq_len), 0)
    key = lax.broadcasted_iota(jnp.int32, (count, seq_len), 1)
    last_key = jnp.zeros((count, seq_len), jnp.int32)
    for i in range(count):
        last_key = jnp.where(row == i, jnp.minimum(positions[i], length - 1), last_key)
    allowed = jnp.concatenate([key <= last_key] * 2, 0)
    for pair in range(pairs):
        lanes = slice(128 * pair, 128 * pair + 128)
        values_at = slice(D + 128 * pair, D + 128 * pair + 128)
        scores = dot_nt(doubled(query_ref[:, lanes], own_lanes), kv_ref[:, lanes]) * HEAD_DIM ** (
            -0.5
        )
        scores = jnp.where(allowed, scores, NEG_FILL)
        exps = jnp.exp(scores - jnp.max(scores, -1, keepdims=True))
        probs = exps / jnp.sum(exps, -1, keepdims=True)
        probs_ref[2 * count * pair : 2 * count * (pair + 1)] = probs
        mixed = jnp.dot(
            probs.astype(bf16), kv_ref[:, values_at], preferred_element_type=jnp.float32
        )
        attended_ref[:, lanes] = folded(mixed, count).astype(bf16)

    attended = attended_ref[...]
    middle_ref[...] = selected_rows(hidden_ref, positions) + vec_ref[4:5]

    @pl.loop(0, 4)
    def _(tile):
        weight = weight_tiles(blocks, where_ref, PROJ, 0, 8, 2 * tile, 2)
        middle_ref[:, lane_range(256 * tile, 256)] += jnp.dot(
            attended, weight, preferred_element_type=jnp.float32
        )

    middle = middle_ref[...]
    hat, _ = normalized(middle)
    normed_two = (hat * vec_ref[5:6] + vec_ref[6:7]).astype(bf16)

    @pl.loop(0, 16)
    def _(tile):
        at = lane_range(256 * tile, 256)
        weight = weight_tiles(blocks, where_ref, FC, 0, 8, 2 * tile, 2)
        bias = vec_ref[pl.ds(7 + tile // 4, 1), lane_range(256 * (tile % 4), 256)]
        pre_act = jnp.dot(normed_two, weight, preferred_element_type=jnp.float32) + bias
        pre_act_ref[:, at] = pre_act
        activated[:, at] = gelu(pre_act).astype(bf16)

    last_ref[...] = middle + vec_ref[11:12]

    @pl.loop(0, 16)
    def _(index):
        tile, depth = index // 4, index % 4
        weight = weight_tiles(blocks, where_ref, OUT, 8 * depth, 8, 2 * tile, 2)
        last_ref[:, lane_range(256 * tile, 256)] += jnp.dot(
            activated[:, lane_range(1024 * depth, 1024)],
            weight,
            preferred_element_type=jnp.float32,
        )

    hat, _ = normalized(last_ref[...])
    head_in_ref[...] = (hat * vec_ref[12:13] + vec_ref[13:14]).astype(bf16)


def forward_kernel(
    where_ref,
    at_smem_ref,
    length_smem_ref,
    ids_ref,
    target_ref,
    at_ref,
    length_ref,
    *refs,
):
    sources, refs = refs[:4], refs[4:]
    (full_ref, out_blocks_ref), targets, refs = refs[:2], refs[2:10], refs[10:]
    (d_head_ref, table_grad_ref, loss_ref), refs = refs[:3], refs[3:]
    held, kept, refs = refs[:4], refs[4:12], refs[12:]
    matrices_ref, table_ref, positions_ref, vec_ref = held
    (
        hidden_ref,
        query_ref,
        kv_ref,
        probs_ref,
        attended_ref,
        middle_ref,
        pre_act_ref,
        last_ref,
    ) = kept
    (
    blocks,
    table,
    own_low,
    table_pad,
    ids_all,
    parts,
    sibling_in,
    half_in,
    whole_in,
    landing,
    ready,
    arrived,
    normed_rows,
    activated,
    head_in,
    pieces,
    logits,
    stats,
    d_rows,
    d_sibling,
    d_first,
    d_second,
    out_staging,
    send_sems,
    recv_sems,
    local_sems,
    ) = refs
    place = coordinates()
    wires = Wires(send_sems, recv_sems)
    loads = [
        pltpu.make_async_copy(source, target, local_sems.at[5 + index])
        for index, (source, target) in enumerate(zip(sources, held))
    ]
    for copy in loads:
        copy.start()
    vocab_group = [
        moved(moved(moved(place, Y, near), Z, far), CORE, side)
        for near in range(SIDE)
        for far in range(SIDE)
        for side in range(2)
    ][1:]
    others = vocab_group + [moved(place, X, step) for step in (1, 2, 3)]
    greet(others)
    for copy in loads:
        copy.wait()
    table_ring = gather_phase(
        place,
        wires,
        others,
        ids_ref,
        matrices_ref,
        table_ref,
        positions_ref,
        blocks,
        table,
        hidden_ref,
        own_low,
        table_pad,
        ids_all,
        parts,
        sibling_in,
        half_in,
        whole_in,
        landing,
        ready,
        arrived,
        local_sems,
    )
    keep = pltpu.make_async_copy(blocks, full_ref, local_sems.at[4])
    keep.start()
    forward_phase(
        where_ref,
        at_smem_ref,
        length_smem_ref,
        hidden_ref,
        vec_ref,
        head_in,
        query_ref,
        kv_ref,
        probs_ref,
        attended_ref,
        middle_ref,
        pre_act_ref,
        last_ref,
        blocks,
        normed_rows,
        activated,
    )
    keeps = [keep]
    for index, (source, target) in enumerate(zip(kept, targets)):
        keeps.append(pltpu.make_async_copy(source, target, local_sems.at[9 + index]))
        keeps[-1].start()

    def arrange_out(chunk):
        if chunk >= 2:
            keeps[len(keeps) - 2].wait()
            del keeps[len(keeps) - 2]
        slot = out_staging.at[chunk % 2]

        @pl.loop(0, 16, unroll=4)
        def _(index):
            slot[index] = blocks[where_ref[OUT[0] + 16 * chunk + index]]

        target = out_blocks_ref.at[pl.ds(16 * chunk, 16)]
        keeps.append(pltpu.make_async_copy(slot, target, local_sems.at[17 + chunk % 2]))
        keeps[-1].start()

    stores, sends = head_phase(
        place,
        wires,
        vocab_group,
        table_ring,
        head_in,
        table,
        target_ref,
        at_ref,
        length_ref,
        d_head_ref,
        table_grad_ref,
        loss_ref,
        parts,
        pieces,
        logits,
        stats,
        d_rows,
        d_sibling,
        d_first,
        d_second,
        local_sems,
        arrange_out,
        keeps,
    )
    sends.settle(blocks)
    for copy in stores:
        copy.wait()


def forward_call(where, positions, lengths, token_ids, target_ids, matrices, vocab_table, positions_table, vectors):
    rows, width = vocab_table.shape
    padded = -(-rows // 128) * 128
    own, seqs = positions.shape
    seq_len = positions_table.shape[0]
    count, half = own * seqs, D // 2
    bf16, f32 = jnp.bfloat16, jnp.float32
    shape = jax.ShapeDtypeStruct
    slots = where.shape[0]
    cache = (
        shape((seq_len, D), f32),
        shape((own, D), bf16),
        shape((seq_len, 2 * D), bf16),
        shape((HEADS * own, seq_len), f32),
        shape((own, D), bf16),
        shape((own, D), f32),
        shape((own, FF), f32),
        shape((own, D), f32),
    )
    states = (matrices, vocab_table, positions_table, vectors)
    smem = pl.BlockSpec(memory_space=pltpu.SMEM)
    return pl.pallas_call(
        forward_kernel,
        name="forward_and_head",
        out_shape=(
            shape((slots, BLOCK, BLOCK), bf16),
            shape((slots // 3, BLOCK, BLOCK), bf16),
            *cache,
            shape((own, D), f32),
            shape((N_DP * rows, width), bf16),
            shape((1, count), f32),
        ),
        in_specs=[smem] * 3 + [VMEM] * 4 + [ANY] * 4,
        out_specs=(ANY,) * 10 + (VMEM, ANY, VMEM),
        scratch_shapes=[
            *[pltpu.VMEM(array.shape, array.dtype) for array in (*states, *cache)],
            pltpu.VMEM((slots, BLOCK, BLOCK), bf16),
            pltpu.VMEM((N_DP, rows, width), bf16),
            pltpu.VMEM((3, 2, BLOCK, BLOCK), bf16),
            pltpu.VMEM((padded, width), bf16),
            pltpu.VMEM((N_DP,) + token_ids.shape, jnp.int32),
            pltpu.VMEM((128 * 128, width), bf16),
            pltpu.VMEM((2, 32 * 128, width), bf16),
            pltpu.VMEM((2, 2, 4 * 128, width), bf16),
            pltpu.VMEM((2, 2, 8 * 128, width), bf16),
            pltpu.VMEM((2, 3, 2 * 128, width), bf16),
            pltpu.VMEM((N_DP, 128, width), bf16),
            pltpu.VMEM((N_DP, 128, width), bf16),
            pltpu.VMEM((seq_len, D), f32),
            pltpu.VMEM((own, FF), bf16),
            pltpu.VMEM((own, D), bf16),
            pltpu.VMEM((2, 2, SIDE, SIDE, own, half), bf16),
            pltpu.VMEM((rows, count), f32),
            pltpu.VMEM((N_VOCAB, 8, count // 4), f32),
            pltpu.VMEM((2, 2, SIDE, SIDE, own, half), bf16),
            pltpu.VMEM((2, SIDE, SIDE, own, half), bf16),
            pltpu.VMEM((2, 3, SIDE, own, half), bf16),
            pltpu.VMEM((2, 3, own, half), bf16),
            pltpu.VMEM((2, 16, BLOCK, BLOCK), bf16),
            pltpu.SemaphoreType.DMA((21,)),
            pltpu.SemaphoreType.DMA((123,)),
            pltpu.SemaphoreType.DMA((19,)),
        ],
        compiler_params=pltpu.CompilerParams(
            collective_id=1, has_side_effects=True, vmem_limit_bytes=VMEM_BYTES
        ),
    )(
        where,
        positions,
        lengths,
        token_ids,
        target_ids,
        positions,
        lengths.reshape(1, -1),
        *states,
    )


def gelu_slope(values):
    cube = 0.044715 * values * values
    bent = jnp.tanh(GELU_C * (values + cube * values))
    return 0.5 * (1.0 + bent) + 0.5 * values * (1.0 - bent * bent) * GELU_C * (1.0 + 3.0 * cube)


def backward_kernel(
    where_ref,
    at_ref,
    full_ref,
    out_blocks_ref,
    *refs,
):
    sources, (grads_ref, small_ref, d_embed_ref), refs = refs[:10], refs[10:13], refs[13:]
    held, refs = refs[:10], refs[10:]
    (
        d_head_ref,
        last_ref,
        vec_ref,
        pre_act_ref,
        middle_ref,
        attended_ref,
        query_ref,
        kv_ref,
        probs_ref,
        hidden_ref,
    ) = held
    (
    blocks,
    grad_blocks,
    activated,
    d_pre,
    normed,
    rows_out,
    d_qkv,
    spread,
    query_grads,
    vec_grads,
    sems,
    grad_sem,
    ) = refs
    loads = [
        pltpu.make_async_copy(source, target, sems.at[9 + index])
        for index, (source, target) in enumerate(zip(sources, held))
    ]
    for copy in loads:
        copy.start()
    out_blocks = grad_blocks.at[pl.ds(0, out_blocks_ref.shape[0])]
    out_load = pltpu.make_async_copy(out_blocks_ref, out_blocks, sems.at[8])
    out_load.start()
    copies = load_blocks(full_ref, blocks, sems)
    for copy in loads:
        copy.wait()
    count = d_head_ref.shape[0]
    bf16 = jnp.bfloat16
    own = lax.axis_index("vocab")
    positions = [at_ref[i, own] for i in range(count)]

    def weight_grad(matrix, rows, left_ref, right, together=8):
        first, in_row = matrix

        @pl.loop(0, rows // together)
        def _(group):
            left = left_ref[:, lane_range(128 * together * group, 128 * together)]
            for column in range(0, in_row, 2):
                product = dot_tn(left, right[:, 128 * column : 128 * column + 256]).astype(bf16)
                for inner in range(2 * together):
                    row, side = inner // 2, inner % 2
                    index = first + (group * together + row) * in_row + column + side
                    grad_blocks[index] = product[
                        128 * row : 128 * row + 128, 128 * side : 128 * side + 128
                    ]
                    pltpu.make_async_copy(
                        grad_blocks.at[index], grads_ref.at[where_ref[index]], grad_sem
                    ).start()

    hat, scale = normalized(last_ref[...])
    d_last, vec_grads[12:13], vec_grads[13:14] = norm_backward(
        d_head_ref[...], hat, scale, vec_ref[12:13]
    )
    d_branch = d_last.astype(bf16)
    vec_grads[11:12] = jnp.sum(d_branch.astype(jnp.float32), 0, keepdims=True)
    activated[...] = gelu(pre_act_ref[...]).astype(bf16)
    weight_grad(OUT, 32, activated, d_branch)
    out_load.wait()

    @pl.loop(0, 16)
    def _(tile):
        at = lane_range(256 * tile, 256)
        weight = jnp.concatenate(
            [
                jnp.concatenate([out_blocks[16 * tile + 8 * row + j] for j in range(8)], 1)
                for row in range(2)
            ],
            0,
        )
        lowered = (dot_nt(d_branch, weight) * gelu_slope(pre_act_ref[:, at])).astype(bf16)
        d_pre[:, at] = lowered
        vec_grads[pl.ds(7 + tile // 4, 1), lane_range(256 * (tile % 4), 256)] = jnp.sum(
            lowered.astype(jnp.float32), 0, keepdims=True
        )

    hat, scale = normalized(middle_ref[...])
    normed[pl.ds(0, count)] = (hat * vec_ref[5:6] + vec_ref[6:7]).astype(bf16)
    weight_grad(FC, 8, normed.at[pl.ds(0, count)], d_pre[...])
    rows_out[...] = jnp.zeros(rows_out.shape, jnp.float32)
    for copy in copies:
        copy.wait()

    @pl.loop(0, 16)
    def _(index):
        tile, depth = index // 4, index % 4
        weight = weight_tiles(blocks, where_ref, FC, 2 * tile, 2, 8 * depth, 8)
        rows_out[pl.ds(0, count), lane_range(256 * tile, 256)] += dot_nt(
            d_pre[:, lane_range(1024 * depth, 1024)], weight
        )

    d_middle, vec_grads[5:6], vec_grads[6:7] = norm_backward(
        rows_out[pl.ds(0, count)], hat, scale, vec_ref[5:6]
    )
    d_middle = d_middle + d_last
    d_proj = d_middle.astype(bf16)
    vec_grads[4:5] = jnp.sum(d_proj.astype(jnp.float32), 0, keepdims=True)
    weight_grad(PROJ, 8, attended_ref, d_proj)

    @pl.loop(0, 4)
    def _(tile):
        weight = weight_tiles(blocks, where_ref, PROJ, 2 * tile, 2, 0, 8)
        rows_out[pl.ds(0, count), lane_range(256 * tile, 256)] = dot_nt(d_proj, weight)

    own_lanes = pair_masks(count)
    spread[...] = jnp.zeros(spread.shape, jnp.float32)
    for pair in range(HEADS // 2):
        lanes = slice(128 * pair, 128 * pair + 128)
        values_at = slice(D + 128 * pair, D + 128 * pair + 128)
        d_mixed = doubled(rows_out[0:count, lanes].astype(bf16), own_lanes)
        probs = probs_ref[2 * count * pair : 2 * count * (pair + 1)]
        d_probs = dot_nt(d_mixed, kv_ref[:, values_at])
        inner = jnp.sum(probs * d_probs, -1, keepdims=True)
        d_scores = (probs * (d_probs - inner)).astype(bf16)
        d_values = dot_tn(probs.astype(bf16), d_mixed).astype(bf16)
        d_keys = dot_tn(d_scores, doubled(query_ref[:, lanes], own_lanes)) * HEAD_DIM ** (-0.5)
        d_query = jnp.dot(d_scores, kv_ref[:, lanes], preferred_element_type=jnp.float32)
        d_query = (folded(d_query, count) * HEAD_DIM ** (-0.5)).astype(bf16).astype(jnp.float32)
        vec_grads[2:3, lanes] = jnp.sum(d_query, 0, keepdims=True)
        vec_grads[3:4, lanes] = jnp.sum(d_values.astype(jnp.float32), 0, keepdims=True)
        query_grads[:, lanes] = d_query
        d_qkv[:, D + 128 * pair : D + 128 * pair + 128] = d_keys.astype(bf16)
        d_qkv[:, 2 * D + 128 * pair : 2 * D + 128 * pair + 128] = d_values
    for i in range(count):
        spread[pl.ds(positions[i], 1), :] = query_grads[i : i + 1, :]
    d_qkv[:, :D] = spread[...].astype(bf16)
    hat, scale = normalized(hidden_ref[...])
    normed[...] = (hat * vec_ref[0:1] + vec_ref[1:2]).astype(bf16)
    weight_grad(QKV, 8, normed, d_qkv)
    rows_out[...] = jnp.zeros(rows_out.shape, jnp.float32)

    @pl.loop(0, 12)
    def _(index):
        tile, depth = index // 3, index % 3
        weight = weight_tiles(blocks, where_ref, QKV, 2 * tile, 2, 8 * depth, 8)
        rows_out[:, lane_range(256 * tile, 256)] += dot_nt(
            d_qkv[:, lane_range(1024 * depth, 1024)], weight
        )

    d_hidden, vec_grads[0:1], vec_grads[1:2] = norm_backward(
        rows_out[...], hat, scale, vec_ref[0:1]
    )
    rows_out[...] = d_hidden
    for i in range(count):
        rows_out[pl.ds(positions[i], 1), :] += d_middle[i : i + 1]
    d_embed_ref[...] = rows_out[...].astype(bf16)
    vec_rows = vec_ref.shape[0]
    for index in range(small_ref.shape[0]):
        group, tile = index // 8, index % 8
        lanes = slice(128 * tile, 128 * tile + 128)
        vec_row = (
            vec_grads[group : group + 1, lanes]
            if group < vec_rows
            else jnp.zeros((1, 128), jnp.float32)
        )
        small_ref[index] = jnp.concatenate(
            [rows_out[8 * group : 8 * group + 8, lanes], vec_row, jnp.zeros((7, 128), jnp.float32)],
            0,
        ).astype(bf16)
    pltpu.make_async_copy(grad_blocks, grads_ref, grad_sem).wait()


def backward_call(where, positions, full, out_blocks, states):
    count = positions.shape[0]
    hidden = states[-1]
    bf16 = jnp.bfloat16
    shape = jax.ShapeDtypeStruct
    return pl.pallas_call(
        backward_kernel,
        name="layer_backward",
        out_shape=(
            shape(full.shape, bf16),
            shape((N_DP * N_VOCAB, 16, 128), bf16),
            shape(hidden.shape, bf16),
        ),
        grid_spec=pltpu.PrefetchScalarGridSpec(
            num_scalar_prefetch=2,
            grid=(),
            in_specs=[ANY] * 12,
            out_specs=(ANY, VMEM, VMEM),
            scratch_shapes=[
                *[pltpu.VMEM(array.shape, array.dtype) for array in states],
                pltpu.VMEM(full.shape, bf16),
                pltpu.VMEM(full.shape, bf16),
                pltpu.VMEM((count, FF), bf16),
                pltpu.VMEM((count, FF), bf16),
                pltpu.VMEM(hidden.shape, bf16),
                pltpu.VMEM(hidden.shape, jnp.float32),
                pltpu.VMEM((hidden.shape[0], 3 * D), bf16),
                pltpu.VMEM(hidden.shape, jnp.float32),
                pltpu.VMEM((count, D), jnp.float32),
                pltpu.VMEM((16, D), jnp.float32),
                pltpu.SemaphoreType.DMA((19,)),
                pltpu.SemaphoreType.DMA,
            ],
        ),
        compiler_params=pltpu.CompilerParams(vmem_limit_bytes=VMEM_BYTES),
    )(where, positions, full, out_blocks, *states)


def adam_step(weight, moment_one, moment_two, grad_in, rate, decay):
    new_one = BETA_ONE * moment_one + (1.0 - BETA_ONE) * grad_in
    new_two = BETA_TWO * moment_two + (1.0 - BETA_TWO) * grad_in * grad_in
    hat_one = new_one * (1.0 / (1.0 - BETA_ONE**STEP))
    hat_two = new_two * (1.0 / (1.0 - BETA_TWO**STEP))
    change = hat_one / (jnp.sqrt(hat_two) + ADAM_EPS)
    if decay:
        change = change + decay * weight
    return weight - rate * change, new_one, new_two


TABLE_PIECES = 2


def update_kernel(*refs):
    names = 20
    sources, (loss_ref, norm_ref, *targets) = refs[:names], refs[names : names + 15]
    buffers = refs[names + 15 : 2 * names + 15]
    results = refs[2 * names + 15 : 2 * names + 28]
    vec_grad, load_sems, store_sems = refs[2 * names + 28 :]
    loads, stores = [], []

    def load(index, at=None):
        source, target = sources[index], buffers[index]
        if at is not None:
            source, target = source.at[at], target.at[at]
        loads.append(pltpu.make_async_copy(source, target, load_sems.at[len(loads)]))
        loads[-1].start()

    def store(index, at=None):
        source, target = results[index], targets[index]
        if at is not None:
            source, target = source.at[at], target.at[at]
        stores.append(pltpu.make_async_copy(source, target, store_sems.at[len(stores)]))
        stores[-1].start()

    def await_loads(count):
        for copy in loads[:count]:
            copy.wait()
        del loads[:count]

    totals, final, table_grad, table, table_m, table_v = buffers[:6]
    grads, left_gram, right_gram, left_part = buffers[6:10]
    matrices, left_stats, right_stats, right_roots = buffers[10:14]
    positions, pos_m, pos_v, vectors, vectors_m, vectors_v = buffers[14:]
    matrices_new, left_new, right_new, matrices_grad = results[:4]
    rows, width = table.shape
    chunk = rows // TABLE_PIECES
    for index in range(2):
        load(index)
    for piece in range(TABLE_PIECES):
        for index in range(2, 6):
            load(index, pl.ds(piece * chunk, chunk))
    for index in range(6, names):
        load(index)
    await_loads(2)
    row_squares = jnp.zeros((8, 128), jnp.float32)
    for part in range(2):
        for core in range(2):
            values = final[part, core].reshape(SIDE**3, 8, 128)
            row_squares += jnp.sum(values * values, 0)
    norm, clip = clip_for(jnp.sum(totals[0:1]) + jnp.sum(row_squares))
    loss_ref[0, 0] = jnp.sum(totals[1:2])
    norm_ref[0, 0] = jnp.max(norm)
    wide_clip = jnp.concatenate([clip] * (width // 128), 1)
    for piece in range(TABLE_PIECES):
        await_loads(4)

        @pl.loop(0, chunk // 80)
        def _(inner):
            at = pl.ds(pl.multiple_of(piece * chunk + inner * 80, 80), 80)
            grad = table_grad[at] * wide_clip
            stepped = adam_step(
                table[at], table_m[at], table_v[at], grad, TABLE_RATE, DECAY_RATE
            )
            for order, value in enumerate(stepped):
                results[4 + order][at] = value

        for order in range(3):
            store(4 + order, pl.ds(piece * chunk, chunk))
    await_loads(8)
    own_squares = jnp.zeros((1, 128), jnp.float32)
    for slot in range(SLOTS):
        grad = grads[slot // 2, slot % 2]
        own_squares += jnp.sum(grad * grad, 0, keepdims=True)
    own_clip = clip_for(jnp.sum(own_squares))[1]
    ratio = jnp.where(own_clip > 0.0, clip / own_clip, 0.0)

    @pl.loop(0, SLOTS, unroll=3)
    def _(slot):
        matrices_grad[slot] = grads[slot // 2, slot % 2] * clip
        left_new[slot] = STAT_DECAY * left_stats[slot] + (1.0 - STAT_DECAY) * (
            left_gram[slot] * ratio * ratio
        )
        right_new[slot] = STAT_DECAY * right_stats[slot] + (1.0 - STAT_DECAY) * (
            right_gram[slot] * ratio * ratio
        )
        stepped = fine_dot(left_part[slot] * ratio, right_roots[slot])
        weight = matrices[slot]
        matrices_new[slot] = weight - SHAMPOO_RATE * (stepped + DECAY_RATE * weight)

    for index in range(4):
        store(index)
    await_loads(6)
    tiles = D // 128
    for index in range(N_DP * N_VOCAB):
        at_core, rest = index // 64, index % 64
        at_z, at_y, at_x = rest // 16, rest // 4 % 4, rest % 4
        group, lanes = index // tiles, slice(128 * (index % tiles), 128 * (index % tiles) + 128)
        at = slice(8 * group, 8 * group + 8)
        stepped = adam_step(
            positions[at, lanes],
            pos_m[at, lanes],
            pos_v[at, lanes],
            final[0, at_core, at_z, at_y, at_x] * clip,
            POS_RATE,
            DECAY_RATE,
        )
        for order, value in enumerate(stepped):
            results[7 + order][at, lanes] = value
        if group < vectors.shape[0]:
            vec_grad[group : group + 1, lanes] = (
                final[1, at_core, at_x, at_z, at_y, 0:1] * clip
            )
    for index in range(7, 10):
        store(index)
    stepped = adam_step(
        vectors[...], vectors_m[...], vectors_v[...], vec_grad[...], VECTOR_RATE, 0.0
    )
    for order, value in enumerate(stepped):
        results[10 + order][...] = value
        store(10 + order)
    for copy in stores:
        copy.wait()


def update_call(totals, final, grads, products, blocks, table_grad, table, positions, vectors):
    sources = [totals, final, table_grad, *table, grads, *products, *blocks, *positions, *vectors]
    shape = lambda array: jax.ShapeDtypeStruct(array.shape, jnp.float32)
    targets = [shape(blocks[0])] * 4
    targets += [shape(array) for array in (*table, *positions, *vectors)]
    scalar = jax.ShapeDtypeStruct((1, 1), jnp.float32)
    smem = pl.BlockSpec(memory_space=pltpu.SMEM)
    return pl.pallas_call(
        update_kernel,
        name="optimizer_update",
        out_shape=(scalar, scalar, *targets),
        in_specs=[ANY] * len(sources),
        out_specs=(smem, smem) + (ANY,) * len(targets),
        scratch_shapes=[pltpu.VMEM(array.shape, jnp.float32) for array in sources]
        + [pltpu.VMEM(target.shape, jnp.float32) for target in targets]
        + [
            pltpu.VMEM(vectors[0].shape, jnp.float32),
            pltpu.SemaphoreType.DMA((len(sources) + 4 * (TABLE_PIECES - 1),)),
            pltpu.SemaphoreType.DMA((len(targets) + 3 * (TABLE_PIECES - 1),)),
        ],
        compiler_params=pltpu.CompilerParams(vmem_limit_bytes=VMEM_BYTES),
    )(*sources)


def slot_places():
    slot = np.arange(N_DP * N_VOCAB * SLOTS)
    device, own = slot // SLOTS, slot % SLOTS
    inner = device % N_VOCAB
    place = (device // N_VOCAB, inner // 2 % SIDE, inner // (2 * SIDE), inner % 2)
    part = own // 2
    result = np.zeros_like(slot)
    for which, (first, second, third) in enumerate(ORDERS):
        index = which * 2 + place[CORE]
        for axis in (third, second, first):
            index = index * SIDE + place[axis]
        result = np.where(part == which, index * 2 + own % 2, result)
    return result.astype(np.int32)


def per_device(
    token_ids,
    seq_lengths,
    loss_positions,
    target_ids,
    block_of_slot,
    matrices,
    left_stats,
    right_stats,
    left_roots,
    right_roots,
    vocab_table,
    table_m,
    table_v,
    positions_table,
    pos_m,
    pos_v,
    vectors,
    vectors_m,
    vectors_v,
):
    block_iota = jnp.arange(block_of_slot.shape[0], dtype=jnp.int32)
    where = jnp.sum(
        jnp.where(block_of_slot[None, :] == block_iota[:, None], slot_places()[None, :], 0),
        1,
        dtype=jnp.int32,
    )
    positions = loss_positions.T
    full, out_blocks, *cache, d_head_in, head_grad, loss_row = forward_call(
        where,
        positions,
        seq_lengths,
        token_ids,
        target_ids.T,
        matrices,
        vocab_table,
        positions_table,
        vectors,
    )
    hidden, query, key_value, probs, attended, middle, pre_act, last = cache
    grad_blocks, small, d_embed = backward_call(
        where,
        positions,
        full,
        out_blocks,
        (d_head_in, last, vectors, pre_act, middle, attended, query, key_value, probs, hidden),
    )
    owned_grads, table_grad_own, final, *products, totals = finish_call(
        grad_blocks.reshape(3, 2, SIDE, 32, BLOCK, BLOCK),
        small.reshape(2, SIDE, 16, 16, 128),
        head_grad.reshape(N_DP, TABLE_CHUNKS, -1, head_grad.shape[1]),
        d_embed,
        left_roots,
        token_ids,
        loss_row,
    )
    loss, norm, *updated = update_call(
        totals,
        final,
        owned_grads,
        products,
        (matrices, left_stats, right_stats, right_roots),
        table_grad_own,
        (vocab_table, table_m, table_v),
        (positions_table, pos_m, pos_v),
        (vectors, vectors_m, vectors_v),
    )
    return (loss.reshape(()), norm.reshape(()), *updated)


def solution(mesh):
    in_specs = (
        P("dp", None),
        P("dp"),
        P("dp", None),
        P("dp", None),
        P(),
        P(("dp", "vocab"), None, None),
        P(("dp", "vocab"), None, None),
        P(("dp", "vocab"), None, None),
        P(("dp", "vocab"), None, None),
        P(("dp", "vocab"), None, None),
        P("vocab", "dp"),
        P("vocab", "dp"),
        P("vocab", "dp"),
        P(),
        P(),
        P(),
        P(),
        P(),
        P(),
    )
    out_specs = (
        P(),
        P(),
        P(("dp", "vocab"), None, None),
        P(("dp", "vocab"), None, None),
        P(("dp", "vocab"), None, None),
        P(("dp", "vocab"), None, None),
        P("vocab", "dp"),
        P("vocab", "dp"),
        P("vocab", "dp"),
        P(),
        P(),
        P(),
        P(),
        P(),
        P(),
    )
    return jax.shard_map(
        per_device, mesh=mesh, in_specs=in_specs, out_specs=out_specs, check_vma=False
    )
```
